128 devices in a mesh: rep: 8 (over x_lo, z), shard: 16 (over y, x_hi, core).
Axes of the slice: x: 4 (x_hi: 2, x_lo: 2; x = x_hi * 2 + x_lo), y: 4, z: 4, core: 2. Of those that a mesh axis runs over, the one named last changes fastest.
Arguments:
- hidden_in: bfloat16 [32768, 2048], P(('rep', 'shard')), may hold values from -6 to 6
- cotangent: bfloat16 [32768, 2048], P(('rep', 'shard')), may hold values from -6 to 6
- segment_ids: int32 [32768], P('rep'), may hold values from 0 to 2, as said below
- positions: int32 [32768], P('rep'), may hold values from 0 to 3583, as said below
- attn_gain: float32 [2048], P('shard'), may hold values from 0.25 to 1.75
- query_gain: float32 [128], replicated, may hold values from 0.25 to 1.75
- key_gain: float32 [128], replicated, may hold values from 0.25 to 1.75
- query_weight: float32 [2048, 2048], P('shard'), may hold values from -0.125 to 0.125
- key_weight: float32 [2048, 1024], P('shard'), may hold values from -0.125 to 0.125
- value_weight: float32 [2048, 1024], P('shard'), may hold values from -0.125 to 0.125
- out_weight: float32 [2048, 2048], P('shard'), may hold values from -3 to 3
- mlp_gain: float32 [2048], P('shard'), may hold values from 0.25 to 1.75
- gate_weight: float32 [2048, 6144], P('shard'), may hold values from -0.125 to 0.125
- up_weight: float32 [2048, 6144], P('shard'), may hold values from -0.125 to 0.125
- down_weight: float32 [2048, 6144], P('shard'), may hold values from -0.078125 to 0.078125
Outputs:
- output: bfloat16 [32768, 2048], P(('rep', 'shard'))
- hidden_grad: bfloat16 [32768, 2048], P(('rep', 'shard'))
- attn_gain_grad: float32 [2048], P('shard')
- query_gain_grad: float32 [128], replicated
- key_gain_grad: float32 [128], replicated
- query_weight_grad: float32 [2048, 2048], P('shard')
- key_weight_grad: float32 [2048, 1024], P('shard')
- value_weight_grad: float32 [2048, 1024], P('shard')
- out_weight_grad: float32 [2048, 2048], P('shard')
- mlp_gain_grad: float32 [2048], P('shard')
- gate_weight_grad: float32 [2048, 6144], P('shard')
- up_weight_grad: float32 [2048, 6144], P('shard')
- down_weight_grad: float32 [2048, 6144], P('shard')
The draws below stay inside these ranges and needn't reach their ends.
Inputs may be any that keep to these rules, and one draw needn't show every extreme that they name: `segment_ids`: within the 4096 rows of each index of rep, one prompt of 3072 rows (segment 0) and 2 continuations of 512 rows (segments 1 to 2) are laid out; each index of shard holds 256 consecutive rows of the order prompt, continuation 1, ..., and these runs are placed on the devices in a drawn order. Prompt rows have positions 0 to 3071 in order; continuation rows have positions 3072 to 3583 in order, in the layout of segment_ids.
All inputs are finite; a program needn't handle non-finite values.
Results may differ from the reference program's by a relative error of at most 0.025.
Values may be sent and summed in bfloat16 or wider, within the bound.
No kernel may reach another device: no remote copies, remote signals or barrier semaphores. Data moves between devices by JAX's collectives and lax.ppermute only.
A program may use at most 384 MiB of HBM per device.

```python
import jax
import jax.numpy as jnp
from jax import lax

D = 2048
HEADS = 16
KV_HEADS = 8
HEAD_DIM = 128
FF = 6144
TOK_DEV = 256
CONT_LEN = 512
Q_DIM = 2048
KV_DIM = 1024
GROUP = 4096
PROMPT = 3072
TOKENS = 32768
N_REP = 8


def layout_rows(key):
    stream = jax.random.fold_in(key, 11)
    group_count = TOKENS // GROUP
    slot_count = GROUP // TOK_DEV
    orders = jax.vmap(lambda sub_key: jax.random.permutation(sub_key, slot_count))(jax.random.split(stream, group_count))
    logical = orders.astype(jnp.int32)[:, :, None] * TOK_DEV + jnp.arange(TOK_DEV, dtype=jnp.int32)[None, None, :]
    logical = logical.reshape(-1)
    beyond = logical - PROMPT
    segments = jnp.where(logical < PROMPT, 0, beyond // CONT_LEN + 1)
    places = jnp.where(logical < PROMPT, logical, PROMPT + beyond % CONT_LEN)
    return (segments.astype(jnp.int32), places.astype(jnp.int32))


def draw_segment_ids(key, part):
    return layout_rows(key)[0]


def draw_positions(key, part):
    return layout_rows(key)[1]


def steps_of(key, extent, cuts, smallest, top_value):
    gain = 1.0
    for axis_at, parts in cuts:
        draws = jax.random.uniform(jax.random.fold_in(jax.random.fold_in(key, 6), axis_at), (parts,), jnp.float32, smallest / len(cuts), top_value / len(cuts))
        gain = gain * jnp.repeat(jnp.exp(draws), extent[axis_at] // parts).reshape((-1,) + (1,) * (len(extent) - 1 - axis_at))
    return gain


def gaussian(key, dims, width, most, cuts=(), held_as=jnp.bfloat16):
    loudness = steps_of(key, dims, cuts, -0.22, 0.18) if cuts else 1.0
    entries = jax.random.normal(key, dims, jnp.float32) * width * loudness
    return jnp.minimum(jnp.maximum(entries, -most), most).astype(held_as)


def setup_inputs(seed: int = 0) -> dict:
    key_list = jax.random.split(jax.random.key(seed), 16)
    return {
        "hidden_in": gaussian(key_list[0], (TOKENS, D), 1.0, 6.0, ((0, 128),)),
        "cotangent": gaussian(key_list[1], (TOKENS, D), 1.0, 6.0, ((0, 128),)),
        "segment_ids": draw_segment_ids(jax.random.fold_in(key_list[15], 71), 0),
        "positions": draw_positions(jax.random.fold_in(key_list[15], 71), 0),
        "attn_gain": jnp.clip(1.0 + 0.15 * jax.random.normal(key_list[4], (D,), jnp.float32), 0.25, 1.75),
        "query_gain": jnp.clip(1.0 + 0.15 * jax.random.normal(key_list[5], (HEAD_DIM,), jnp.float32), 0.25, 1.75),
        "key_gain": jnp.clip(1.0 + 0.15 * jax.random.normal(key_list[6], (HEAD_DIM,), jnp.float32), 0.25, 1.75),
        "query_weight": gaussian(key_list[7], (D, Q_DIM), D ** -0.5, 0.125, ((0, 16),), jnp.float32),
        "key_weight": gaussian(key_list[8], (D, KV_DIM), D ** -0.5, 0.125, ((0, 16),), jnp.float32),
        "value_weight": gaussian(key_list[9], (D, KV_DIM), D ** -0.5, 0.125, ((0, 16),), jnp.float32),
        "out_weight": gaussian(key_list[10], (D, Q_DIM), (max(2, Q_DIM // 512)) ** -0.5, 3.0, ((0, 16),), jnp.float32),
        "mlp_gain": jnp.clip(1.0 + 0.15 * jax.random.normal(key_list[11], (D,), jnp.float32), 0.25, 1.75),
        "gate_weight": gaussian(key_list[12], (D, FF), D ** -0.5, 0.125, ((0, 16),), jnp.float32),
        "up_weight": gaussian(key_list[13], (D, FF), D ** -0.5, 0.125, ((0, 16),), jnp.float32),
        "down_weight": gaussian(key_list[14], (D, FF), FF ** -0.5, 0.078125, ((0, 16),), jnp.float32),
    }


norm_eps = 1e-06
rope_base = 1000000.0
masked_score = -1e+30

@jax.custom_vjp
def low(v):
    return lax.optimization_barrier(v.astype(jnp.bfloat16)).astype(jnp.float32)

@jax.custom_vjp
def low_back(v):
    return v

def low_keep(v):
    return (low(v), None)

def low_pass(kept, grad):
    return (grad,)

def back_keep(v):
    return (v, None)

def back_low(kept, grad):
    return (low(grad),)
low.defvjp(low_keep, low_pass)
low_back.defvjp(back_keep, back_low)

def normalize(values):
    return values * lax.rsqrt(lax.optimization_barrier(jnp.mean(values * values, axis=-1, keepdims=True)) + norm_eps)

def rotate(values, places):
    half_dim = values.shape[-1] // 2
    frequency = rope_base ** (-2.0 * jnp.arange(half_dim, dtype=jnp.float32) / values.shape[-1])
    angles = places.astype(jnp.float32)[:, None] * frequency[None, :]
    cosine = jnp.cos(angles)[:, None, :]
    sine_part = jnp.sin(angles)[:, None, :]
    first_half = values[..., :half_dim]
    second_half = values[..., half_dim:]
    return jnp.concatenate([first_half * cosine - second_half * sine_part, second_half * cosine + first_half * sine_part], axis=-1)

def matmul(left, right):
    return jnp.dot(left, right, precision=lax.Precision.HIGHEST, preferred_element_type=jnp.float32)

def group_layer(inputs, params):
    hidden, segments, places = inputs
    attn_gain, query_gain, key_gain, query_weight, key_weight, value_weight, out_weight, mlp_gain, gate_weight, up_weight, down_weight = params
    row_count = hidden.shape[0]
    first_in = low(normalize(hidden) * attn_gain)
    query_pre = low_back(matmul(first_in, query_weight))
    key_pre = low_back(matmul(first_in, key_weight))
    value_pre = low_back(matmul(first_in, value_weight))
    queries = low(rotate(normalize(query_pre.reshape(row_count, HEADS, HEAD_DIM)) * query_gain, places))
    key_act = low(rotate(normalize(key_pre.reshape(row_count, KV_HEADS, HEAD_DIM)) * key_gain, places))
    values = low(value_pre.reshape(row_count, KV_HEADS, HEAD_DIM))
    visible = (places[None, :] <= places[:, None]) & ((segments[None, :] == 0) | (segments[None, :] == segments[:, None]))
    group_size = HEADS // KV_HEADS
    tiled_mask = jnp.tile(visible, (group_size, 1))
    score_scale = HEAD_DIM ** (-0.5)
    query_heads = queries.reshape(row_count, KV_HEADS, group_size, HEAD_DIM).transpose(1, 2, 0, 3).reshape(KV_HEADS, group_size * row_count, HEAD_DIM)
    key_heads = key_act.transpose(1, 0, 2)
    value_heads = values.transpose(1, 0, 2)

    def one_head(operands):
        head_queries, head_keys, head_values = operands
        scores = low_back(matmul(head_queries, head_keys.T) * score_scale)
        scores = jnp.where(tiled_mask, scores, masked_score)
        probabilities = jax.nn.softmax(scores, axis=-1)
        return matmul(low(probabilities), head_values)
    mixed_out = lax.map(jax.checkpoint(one_head), (query_heads, key_heads, value_heads))
    mixed_out = mixed_out.reshape(KV_HEADS, group_size, row_count, HEAD_DIM).transpose(2, 0, 1, 3).reshape(row_count, Q_DIM)
    mixed_out = low_back(low(mixed_out))
    attn_out = low_back(matmul(mixed_out, out_weight.T))
    middle = hidden + attn_out
    second_in = low(normalize(middle) * mlp_gain)
    gate_act = low_back(matmul(second_in, gate_weight))
    up_act = low_back(matmul(second_in, up_weight))
    inner_act = low(jax.nn.silu(gate_act) * up_act)
    return middle + low_back(matmul(inner_act, down_weight.T))

def reference(hidden_in, cotangent, segment_ids, positions, attn_gain, query_gain, key_gain, query_weight, key_weight, value_weight, out_weight, mlp_gain, gate_weight, up_weight, down_weight):
    hidden = hidden_in.astype(jnp.float32)
    cot_float = cotangent.astype(jnp.float32)
    params = (attn_gain, query_gain, key_gain, query_weight, key_weight, value_weight, out_weight, mlp_gain, gate_weight, up_weight, down_weight)
    segment_groups = segment_ids.reshape(N_REP, GROUP)
    place_groups = positions.reshape(N_REP, GROUP)

    def forward(hidden_all, weights):
        rounded = (low(weights[0]), weights[1], weights[2], low(weights[3]), low(weights[4]), low(weights[5]), low(weights[6]), low(weights[7]), low(weights[8]), low(weights[9]), low(weights[10]))
        layer_fn = jax.checkpoint(group_layer)
        result = lax.map(lambda pieces: layer_fn(pieces, rounded), (hidden_all.reshape(N_REP, GROUP, D), segment_groups, place_groups))
        return result.reshape(TOKENS, D)
    output, pullback = jax.vjp(forward, hidden, params)
    hidden_grad, grads = pullback(cot_float)
    return (output.astype(jnp.bfloat16), hidden_grad.astype(jnp.bfloat16), grads[0], grads[1], grads[2], grads[3], grads[4], grads[5], grads[6], grads[7], grads[8], grads[9], grads[10])
```

```python
import jax
import jax.numpy as jnp
from jax import lax
from jax.experimental import pallas as pl
from jax.experimental.pallas import tpu as pltpu
from jax.sharding import Mesh
from jax.sharding import PartitionSpec as P

HEAD_DIM = 128
RING = 4
BLOCK = 256
BLOCKS = 16
TILE = 512
TILES = 8
PROMPT_TILES = 6

norm_eps = 1e-06
rope_base = 1000000.0
score_scale = HEAD_DIM ** (-0.5)
score_scale_log2 = score_scale * 1.4426950408889634
contract_first = (((0,), (0,)), ((), ()))
contract_last = (((1,), (1,)), ((), ()))
GROUP_AXES = ("y", "x_hi", "core")
ALL_AXES = ("x_lo", "z", "y", "x_hi", "core")
low = jnp.bfloat16


def inverse_rms(values):
    return lax.rsqrt(jnp.mean(values * values, axis=-1, keepdims=True) + norm_eps)


def normalize(values):
    return values * inverse_rms(values)


def shift(values, axis, by, size=RING):
    return lax.ppermute(values, axis, [(i, (i + by) % size) for i in range(size)])


def gather_z(values):
    return jnp.concatenate(
        [values, shift(values, "z", 1), shift(values, "z", 2), shift(values, "z", 3)], axis=0
    )


def scatter_z(partial):
    rows = partial.shape[0] // RING
    blocks = [partial[r * rows : (r + 1) * rows] for r in range(RING)]
    total = blocks[0].astype(jnp.float32)
    for r in range(1, RING):
        total = total + shift(blocks[r].astype(low), "z", -r).astype(jnp.float32)
    return total


def forward_kernel(order, q_ref, k_ref, v_ref, mixed_ref, mixed_t_ref, log_ref, k_all, v_t, acc, total):
    tile = pl.program_id(0)

    @pl.when(tile == 0)
    def _():
        for at in range(BLOCKS):
            k_all[at * BLOCK : (at + 1) * BLOCK, :] = k_ref[order[at]]
            v_t[at // 2, :, (at % 2) * BLOCK : (at % 2 + 1) * BLOCK] = (
                v_ref[order[at]].astype(jnp.float32).T.astype(low)
            )

    queries = jnp.concatenate([q_ref[order[2 * tile]], q_ref[order[2 * tile + 1]]], axis=0)
    acc[...] = jnp.zeros_like(acc)
    total[...] = jnp.zeros_like(total)

    def chunk(at, masked):
        keys = k_all[pl.ds(pl.multiple_of(at * TILE, TILE), TILE), :]
        scores = lax.dot_general(keys, queries, contract_last, preferred_element_type=jnp.float32)
        weights = jnp.exp2(scores * score_scale_log2)
        if masked:
            key_row = lax.broadcasted_iota(jnp.int32, (TILE, TILE), 0)
            query_row = lax.broadcasted_iota(jnp.int32, (TILE, TILE), 1)
            weights = jnp.where(key_row <= query_row, weights, 0.0)
        total[...] += jnp.sum(weights, axis=0, keepdims=True)
        acc[...] += jnp.dot(v_t[at], weights.astype(low), preferred_element_type=jnp.float32)

    @pl.loop(0, jnp.minimum(tile, PROMPT_TILES))
    def _(at):
        chunk(at, False)

    chunk(tile, True)
    mixed_t = acc[...] / total[...]
    mixed_t_ref[tile] = mixed_t
    log_ref[tile] = jnp.log2(total[...])
    mixed = mixed_t.T.astype(low)
    mixed_ref[order[2 * tile]] = mixed[:BLOCK]
    mixed_ref[order[2 * tile + 1]] = mixed[BLOCK:]


def attention_forward(order, queries, keys, values):
    whole = pl.BlockSpec(memory_space=pltpu.VMEM)
    return pl.pallas_call(
        forward_kernel,
        out_shape=(
            jax.ShapeDtypeStruct((BLOCKS, BLOCK, HEAD_DIM), low),
            jax.ShapeDtypeStruct((TILES, HEAD_DIM, TILE), jnp.float32),
            jax.ShapeDtypeStruct((TILES, 1, TILE), jnp.float32),
        ),
        grid_spec=pltpu.PrefetchScalarGridSpec(
            num_scalar_prefetch=1,
            grid=(TILES,),
            in_specs=[whole] * 3,
            out_specs=(whole, whole, whole),
            scratch_shapes=[
                pltpu.VMEM((BLOCKS * BLOCK, HEAD_DIM), low),
                pltpu.VMEM((TILES, HEAD_DIM, TILE), low),
                pltpu.VMEM((HEAD_DIM, TILE), jnp.float32),
                pltpu.VMEM((1, TILE), jnp.float32),
            ],
        ),
        compiler_params=pltpu.CompilerParams(vmem_limit_bytes=40 * 1024 * 1024),
        cost_estimate=pl.CostEstimate(
            flops=1024, bytes_accessed=1024, transcendentals=0
        ),
    )(order, queries, keys, values)


def backward_kernel(
    order,
    q_ref,
    k_ref,
    v_ref,
    g_ref,
    mixed_t_ref,
    log_ref,
    q_out,
    k_out,
    v_out,
    k_all,
    v_all,
    k_t,
    q_acc,
    k_acc,
    v_acc,
):
    tile = pl.program_id(0)

    @pl.when(tile == 0)
    def _():
        for at in range(BLOCKS):
            rows = slice(at * BLOCK, (at + 1) * BLOCK)
            keys = k_ref[order[at]]
            k_all[rows, :] = keys
            v_all[rows, :] = v_ref[order[at]]
            k_t[at // 2, :, (at % 2) * BLOCK : (at % 2 + 1) * BLOCK] = (
                keys.astype(jnp.float32).T.astype(low)
            )
        k_acc[...] = jnp.zeros_like(k_acc)
        v_acc[...] = jnp.zeros_like(v_acc)

    queries = jnp.concatenate([q_ref[order[2 * tile]], q_ref[order[2 * tile + 1]]], axis=0)
    grads = jnp.concatenate([g_ref[order[2 * tile]], g_ref[order[2 * tile + 1]]], axis=0)
    grads_t = grads.astype(jnp.float32).T
    shared = jnp.sum(grads_t * mixed_t_ref[tile], axis=0, keepdims=True)
    logs = log_ref[tile]
    q_acc[...] = jnp.zeros_like(q_acc)

    def chunk(at, masked):
        rows = pl.ds(pl.multiple_of(at * TILE, TILE), TILE)
        scores = lax.dot_general(
            k_all[rows, :], queries, contract_last, preferred_element_type=jnp.float32
        )
        probs = jnp.exp2(scores * score_scale_log2 - logs)
        if masked:
            key_row = lax.broadcasted_iota(jnp.int32, (TILE, TILE), 0)
            query_row = lax.broadcasted_iota(jnp.int32, (TILE, TILE), 1)
            probs = jnp.where(key_row <= query_row, probs, 0.0)
        prob_grads = lax.dot_general(
            v_all[rows, :], grads, contract_last, preferred_element_type=jnp.float32
        )
        score_grads = (probs * (prob_grads - shared)).astype(low)
        v_acc[rows, :] += jnp.dot(probs.astype(low), grads, preferred_element_type=jnp.float32)
        k_acc[rows, :] += jnp.dot(score_grads, queries, preferred_element_type=jnp.float32)
        q_acc[...] += jnp.dot(k_t[at], score_grads, preferred_element_type=jnp.float32)

    @pl.loop(0, jnp.minimum(tile, PROMPT_TILES))
    def _(at):
        chunk(at, False)

    chunk(tile, True)
    query_grad = (q_acc[...] * score_scale).T.astype(low)
    q_out[order[2 * tile]] = query_grad[:BLOCK]
    q_out[order[2 * tile + 1]] = query_grad[BLOCK:]

    @pl.when(tile == TILES - 1)
    def _():
        for at in range(BLOCKS):
            rows = slice(at * BLOCK, (at + 1) * BLOCK)
            k_out[order[at]] = (k_acc[rows, :] * score_scale).astype(low)
            v_out[order[at]] = v_acc[rows, :].astype(low)


def attention_backward(order, queries, keys, values, grads, mixed_t, logs):
    whole = pl.BlockSpec(memory_space=pltpu.VMEM)
    rows = BLOCKS * BLOCK
    return pl.pallas_call(
        backward_kernel,
        out_shape=(jax.ShapeDtypeStruct((BLOCKS, BLOCK, HEAD_DIM), low),) * 3,
        grid_spec=pltpu.PrefetchScalarGridSpec(
            num_scalar_prefetch=1,
            grid=(TILES,),
            in_specs=[whole] * 6,
            out_specs=(whole, whole, whole),
            scratch_shapes=[
                pltpu.VMEM((rows, HEAD_DIM), low),
                pltpu.VMEM((rows, HEAD_DIM), low),
                pltpu.VMEM((TILES, HEAD_DIM, TILE), low),
                pltpu.VMEM((HEAD_DIM, TILE), jnp.float32),
                pltpu.VMEM((rows, HEAD_DIM), jnp.float32),
                pltpu.VMEM((rows, HEAD_DIM), jnp.float32),
            ],
        ),
        compiler_params=pltpu.CompilerParams(vmem_limit_bytes=48 * 1024 * 1024),
        cost_estimate=pl.CostEstimate(
            flops=1024, bytes_accessed=1024, transcendentals=0
        ),
    )(order, queries, keys, values, grads, mixed_t, logs)


def mlp_kernel(second_ref, cot_ref, gate_ref, up_ref, down_ref, *refs):
    inner_ref, both_ref, grad_ref, acc = refs[-4:]
    at = pl.program_id(0)
    step = gate_ref.shape[1]
    second = second_ref[...]
    gate_weight = gate_ref[...]
    up_weight = up_ref[...]
    gate_act = jnp.dot(second, gate_weight, preferred_element_type=jnp.float32)
    up_act = jnp.dot(second, up_weight, preferred_element_type=jnp.float32)
    inner_grad = jnp.dot(cot_ref[...], down_ref[...], preferred_element_type=jnp.float32)
    sigmoid = 1.0 / (1.0 + jnp.exp(-gate_act))
    silu = gate_act * sigmoid
    inner_ref[0] = (silu * up_act).astype(low)
    gate_grad = (inner_grad * up_act * (sigmoid * (1.0 + gate_act * (1.0 - sigmoid)))).astype(low)
    up_grad = (inner_grad * silu).astype(low)
    both_ref[0, :, pl.ds(pl.multiple_of(at * step, step), step)] = gate_grad
    up_at = (pl.num_programs(0) + at) * step
    both_ref[0, :, pl.ds(pl.multiple_of(up_at, step), step)] = up_grad
    part = lax.dot_general(
        gate_grad, gate_weight, contract_last, preferred_element_type=jnp.float32
    ) + lax.dot_general(up_grad, up_weight, contract_last, preferred_element_type=jnp.float32)

    @pl.when(at == 0)
    def _():
        acc[...] = part

    @pl.when(at > 0)
    def _():
        acc[...] += part

    @pl.when(at == pl.num_programs(0) - 1)
    def _():
        grad_ref[...] = acc[...].astype(low)


def mlp_block(block, second, cot, weights, held):
    rows, width = second.shape
    hidden_width = weights.shape[1] // 3
    step = 256
    steps = hidden_width // step
    whole = pl.BlockSpec((rows, width), lambda c: (0, 0))
    kept = pl.BlockSpec((1, rows, step), lambda c: (block, 0, c))
    kept_both = pl.BlockSpec((1, rows, 2 * hidden_width), lambda c: (block, 0, 0))
    return pl.pallas_call(
        mlp_kernel,
        grid=(steps,),
        in_specs=[
            whole,
            whole,
            pl.BlockSpec((width, step), lambda c: (0, c)),
            pl.BlockSpec((width, step), lambda c: (0, steps + c)),
            pl.BlockSpec((width, step), lambda c: (0, 2 * steps + c)),
        ]
        + [pl.BlockSpec(memory_space=pl.ANY)] * len(held),
        out_specs=(kept, kept_both, whole),
        out_shape=(
            jax.ShapeDtypeStruct((RING, rows, hidden_width), low),
            jax.ShapeDtypeStruct((RING, rows, 2 * hidden_width), low),
            jax.ShapeDtypeStruct((rows, width), low),
        ),
        scratch_shapes=[pltpu.VMEM((rows, width), jnp.float32)],
        input_output_aliases={5 + i: i for i in range(len(held))},
        compiler_params=pltpu.CompilerParams(vmem_limit_bytes=40 * 1024 * 1024),
        cost_estimate=pl.CostEstimate(
            flops=2 * 5 * rows * width * hidden_width,
            bytes_accessed=2 * 3 * width * hidden_width,
            transcendentals=rows * hidden_width,
        ),
    )(second, cot, weights, weights, weights, *held)


def first_kernel(
    hidden_ref, gain_ref, weight_ref, cos_ref, sin_ref, query_gain, key_gain, first_ref, pre_ref, send_ref
):
    first = (normalize(hidden_ref[0].astype(jnp.float32)) * gain_ref[...]).astype(low)
    first_ref[0] = first
    pre = jnp.dot(first, weight_ref[...], preferred_element_type=jnp.float32)
    pre_ref[0] = pre
    cosine = cos_ref[0]
    sine = sin_ref[0]

    def turned(head, gain):
        values = normalize(pre[:, head * HEAD_DIM : (head + 1) * HEAD_DIM]) * gain
        return (values * cosine + pltpu.roll(values, HEAD_DIM // 2, 1) * sine).astype(low)

    for head in range(4):
        send_ref[head, 0] = turned(head, query_gain[...])
    for head in range(2):
        send_ref[2 * head, 1] = turned(4 + head, key_gain[...])
        send_ref[2 * head + 1, 1] = pre[:, (6 + head) * HEAD_DIM : (7 + head) * HEAD_DIM].astype(low)


def first_part(hidden_all, gain, weights, cosine, sine, query_gain, key_gain):
    _, rows, width = hidden_all.shape
    row = pl.BlockSpec((1, HEAD_DIM), lambda r: (0, 0))
    turn = pl.BlockSpec((1, rows, HEAD_DIM), lambda r: (r, 0, 0))
    return pl.pallas_call(
        first_kernel,
        grid=(RING,),
        in_specs=[
            pl.BlockSpec((1, rows, width), lambda r: (r, 0, 0)),
            pl.BlockSpec((1, width), lambda r: (0, 0)),
            pl.BlockSpec((width, 1024), lambda r: (0, 0)),
            turn,
            turn,
            row,
            row,
        ],
        out_specs=(
            pl.BlockSpec((1, rows, width), lambda r: (r, 0, 0)),
            pl.BlockSpec((1, rows, 1024), lambda r: (r, 0, 0)),
            pl.BlockSpec((4, 2, rows, HEAD_DIM), lambda r: (r, 0, 0, 0)),
        ),
        out_shape=(
            jax.ShapeDtypeStruct((RING, rows, width), low),
            jax.ShapeDtypeStruct((RING, rows, 1024), jnp.float32),
            jax.ShapeDtypeStruct((BLOCKS, 2, rows, HEAD_DIM), low),
        ),
        compiler_params=pltpu.CompilerParams(vmem_limit_bytes=40 * 1024 * 1024),
        cost_estimate=pl.CostEstimate(
            flops=2 * RING * rows * width * 1024,
            bytes_accessed=20 * 1024 * 1024,
            transcendentals=0,
        ),
    )(hidden_all, gain, weights, cosine, sine, query_gain, key_gain)


def first_back_kernel(
    back_ref, pre_ref, cos_ref, sin_ref, query_gain, key_gain, grad_ref, query_sum, key_sum
):
    cosine = cos_ref[0]
    sine = sin_ref[0]

    @pl.when(pl.program_id(0) == 0)
    def _():
        query_sum[...] = jnp.zeros_like(query_sum)
        key_sum[...] = jnp.zeros_like(key_sum)

    def back(grads, head, gain, sums):
        columns = slice(head * HEAD_DIM, (head + 1) * HEAD_DIM)
        values = pre_ref[0, :, columns]
        grads = grads.astype(jnp.float32)
        grads = grads * cosine - pltpu.roll(grads, HEAD_DIM // 2, 1) * sine
        scale = inverse_rms(values)
        normed = values * scale
        sums[...] += jnp.sum(grads * normed, axis=0, keepdims=True)
        scaled = grads * gain
        out = scale * (scaled - normed * jnp.mean(scaled * normed, axis=-1, keepdims=True))
        grad_ref[0, :, columns] = out.astype(low)

    for head in range(4):
        back(back_ref[head, 0], head, query_gain[...], query_sum)
    for head in range(2):
        back(back_ref[2 * head, 1], 4 + head, key_gain[...], key_sum)
        grad_ref[0, :, (6 + head) * HEAD_DIM : (7 + head) * HEAD_DIM] = back_ref[2 * head + 1, 1]


def first_back(returned, pre, cosine, sine, query_gain, key_gain):
    _, rows, _ = pre.shape
    row = pl.BlockSpec((1, HEAD_DIM), lambda r: (0, 0))
    turn = pl.BlockSpec((1, rows, HEAD_DIM), lambda r: (r, 0, 0))
    wide = pl.BlockSpec((1, rows, 1024), lambda r: (r, 0, 0))
    return pl.pallas_call(
        first_back_kernel,
        grid=(RING,),
        in_specs=[
            pl.BlockSpec((4, 2, rows, HEAD_DIM), lambda r: (r, 0, 0, 0)),
            wide,
            turn,
            turn,
            row,
            row,
        ],
        out_specs=(wide, row, row),
        out_shape=(
            jax.ShapeDtypeStruct((RING, rows, 1024), low),
            jax.ShapeDtypeStruct((1, HEAD_DIM), jnp.float32),
            jax.ShapeDtypeStruct((1, HEAD_DIM), jnp.float32),
        ),
        compiler_params=pltpu.CompilerParams(vmem_limit_bytes=40 * 1024 * 1024),
        cost_estimate=pl.CostEstimate(
            flops=1024, bytes_accessed=1024, transcendentals=0
        ),
    )(returned, pre, cosine, sine, query_gain, key_gain)


def to_heads(send):
    return lax.all_to_all(send, GROUP_AXES, 0, 0, tiled=True)


def after(value, *others):
    return lax.optimization_barrier((value, others))[0]


def ring_blocks(values):
    half = values.shape[0] // 2
    left = shift(values, "z", 1)
    right = shift(values, "z", 3)
    opposite = jnp.concatenate(
        [shift(left[:half], "z", 1), shift(right[half:], "z", 3)], axis=0
    )
    return [values, left, opposite, right]


def together(*values):
    return lax.optimization_barrier(values)


def place_kernel(z_ref, *refs):
    blocks, outs = refs[:RING], refs[RING:]
    for r in range(RING):
        slot = lax.rem(z_ref[0] - r + RING, RING)
        start = 0
        for out in outs:
            part = out.shape[1] // RING
            at = pl.multiple_of(slot * part, part)
            out[:, pl.ds(at, part)] = blocks[r][:, start : start + part].astype(jnp.float32)
            start += part


def place(z_at, blocks, widths):
    rows = blocks[0].shape[0]
    whole = pl.BlockSpec(memory_space=pltpu.VMEM)
    return pl.pallas_call(
        place_kernel,
        in_specs=[pl.BlockSpec(memory_space=pltpu.SMEM)] + [whole] * RING,
        out_specs=tuple(whole for _ in widths),
        out_shape=tuple(jax.ShapeDtypeStruct((rows, RING * part), jnp.float32) for part in widths),
        compiler_params=pltpu.CompilerParams(vmem_limit_bytes=24 * 1024 * 1024),
        cost_estimate=pl.CostEstimate(
            flops=0, bytes_accessed=rows * sum(widths) * 24, transcendentals=0
        ),
    )(z_at[None], *blocks)


def send_back(block, r):
    return shift(block, "z", -r)


def local(
    hidden_in,
    cotangent,
    segment_ids,
    positions,
    attn_gain,
    query_gain,
    key_gain,
    query_weight,
    key_weight,
    value_weight,
    out_weight,
    mlp_gain,
    gate_weight,
    up_weight,
    down_weight,
):
    f32 = jnp.float32
    rows, width = hidden_in.shape
    ring_rows = RING * rows
    z_at = lax.axis_index("z")
    y_at = lax.axis_index("y")
    core_at = lax.axis_index("core")
    my_index = (y_at * 2 + lax.axis_index("x_hi")) * 2 + core_at

    def columns(weight):
        part = weight.shape[1] // RING
        return lax.dynamic_slice_in_dim(weight, z_at * part, part, 1).astype(low)

    def gather(block):
        return lax.all_gather(block, GROUP_AXES, axis=0, tiled=True)

    own_places = lax.dynamic_slice_in_dim(positions, my_index * rows, rows)
    firsts = positions.reshape(BLOCKS, BLOCK)[:, 0]
    segments = segment_ids.reshape(BLOCKS, BLOCK)[:, 0]
    logical = firsts // BLOCK + jnp.maximum(segments - 1, 0) * 2
    numbers = jnp.arange(BLOCKS, dtype=jnp.int32)
    order = jnp.sum(jnp.where(logical[:, None] == numbers[None, :], numbers[:, None], 0), axis=0)
    notes = gather_z(jnp.concatenate([own_places, order, jnp.zeros((112,), jnp.int32)])[None])
    places = notes[:, :rows]
    order = lax.dynamic_index_in_dim(notes, y_at, 0, keepdims=False)[rows : rows + BLOCKS]

    gains = jnp.pad(
        jnp.stack([attn_gain, mlp_gain], axis=1).astype(low), ((0, 0), (0, HEAD_DIM - 2))
    )
    first_weights = gather(
        jnp.concatenate(
            [
                columns(query_weight),
                columns(key_weight),
                columns(value_weight),
                columns(out_weight),
                gains,
            ],
            axis=1,
        )
    )
    out_full = first_weights[:, 1024:1536]
    attn_scale = first_weights[:, 1536].astype(f32)[None]
    mlp_scale = first_weights[:, 1537].astype(f32)[None]
    mlp_weights = gather(
        jnp.concatenate([columns(gate_weight), columns(up_weight), columns(down_weight)], axis=1)
    )
    down_full = mlp_weights[:, 3072:]

    hidden_blocks = ring_blocks(hidden_in)
    cot_blocks = ring_blocks(after(cotangent, *hidden_blocks))
    frequency = rope_base ** (-2.0 * jnp.arange(HEAD_DIM // 2, dtype=f32) / HEAD_DIM)
    angles = places.astype(f32)[:, :, None] * frequency[None, None, :]
    cosine = jnp.cos(angles)
    sine = jnp.sin(angles)
    cosine = jnp.concatenate([cosine, cosine], axis=-1)
    sine = jnp.concatenate([-sine, sine], axis=-1)
    query_row = query_gain[None]
    key_row = key_gain[None]

    first_in, qkv_pre, send = first_part(
        jnp.stack(hidden_blocks), attn_scale, first_weights, cosine, sine, query_row, key_row
    )
    arrived = to_heads(send)
    head_queries = arrived[:, 0]
    own_pair = arrived[:, 1]
    other_pair = shift(own_pair, "core", 1, 2)
    head_keys = jnp.where(core_at == 0, own_pair, other_pair)
    head_values = jnp.where(core_at == 0, other_pair, own_pair)
    head_mixed, head_mixed_t, head_logs = attention_forward(
        order, head_queries, head_keys, head_values
    )
    head_mixed = after(head_mixed, *cot_blocks)

    def from_heads(values):
        return values.reshape(RING, 4, rows, HEAD_DIM).transpose(0, 2, 1, 3).reshape(ring_rows, 512)

    mixed = from_heads(to_heads(head_mixed))
    attn_out = lax.dot_general(mixed, out_full, contract_last, preferred_element_type=f32)
    hidden = hidden_in.astype(f32)
    middle = hidden + scatter_z(attn_out)
    middle_rms = inverse_rms(middle)
    second_norm = middle * middle_rms
    second_in = (second_norm * mlp_scale).astype(low)
    left = shift(second_in, "z", 1)
    right = shift(second_in, "z", 3)
    *held, own_part = mlp_block(0, second_in, cot_blocks[0], mlp_weights, ())
    held, own_part, left, right = together(held, own_part, left, right)
    half = rows // 2
    top = shift(left[:half], "z", 1)
    bottom = shift(right[half:], "z", 3)
    *held, left_part = mlp_block(1, left, cot_blocks[1], mlp_weights, held)
    left_back = send_back(left_part, 1)
    *held, right_part = mlp_block(3, right, cot_blocks[3], mlp_weights, held)
    right_back = send_back(right_part, 3)
    held, top, bottom = together(held, top, bottom)
    opposite = jnp.concatenate([top, bottom], axis=0)
    *held, opposite_part = mlp_block(2, opposite, cot_blocks[2], mlp_weights, held)
    opposite_back = send_back(opposite_part, 2)
    inner = held[0].reshape(ring_rows, 1536)
    both_grad = held[1].reshape(ring_rows, 3072)

    def weight_grad(left, right):
        return lax.dot_general(left, right, contract_first, preferred_element_type=f32).astype(low)

    def pair_start(term):
        term = term.reshape(8, 2, 128, term.shape[1])
        keep = lax.dynamic_index_in_dim(term, core_at, 1, keepdims=False)
        give = lax.dynamic_index_in_dim(term, 1 - core_at, 1, keepdims=False)
        return keep, shift(give, "core", 1, 2)

    def pair_sum(keep, come):
        return (keep.astype(f32) + come.astype(f32)).astype(low)

    def to_owners(pair):
        terms = lax.all_to_all(pair, ("y", "x_hi"), 0, 0, tiled=True)
        return jnp.sum(terms.astype(f32), axis=0).astype(low)

    def over_x(share):
        return share, shift(share, "x_lo", 1, 2)

    def over_z(pair):
        share = pair_sum(*pair)
        return [share] + [shift(share, "z", r) for r in range(1, RING)]

    second_all = jnp.concatenate([second_in, left, opposite, right], axis=0)
    cot_all = jnp.concatenate(cot_blocks, axis=0)
    down_term = weight_grad(cot_all, inner)
    left_back, right_back, opposite_back, down_term, both_grad = together(
        left_back, right_back, opposite_back, down_term, both_grad
    )
    down_pair = pair_start(down_term)

    second_grad = (
        own_part.astype(f32)
        + left_back.astype(f32)
        + right_back.astype(f32)
        + opposite_back.astype(f32)
    )
    mlp_gain_part = jnp.sum(second_grad * second_norm, axis=0)
    scaled_grad = second_grad * mlp_scale
    middle_grad = cotangent.astype(f32) + middle_rms * (
        scaled_grad - second_norm * jnp.mean(scaled_grad * second_norm, axis=-1, keepdims=True)
    )
    own_low = middle_grad.astype(low)
    left_low = shift(own_low, "z", 1)
    right_low = shift(own_low, "z", 3)
    down_sum = pair_sum(*down_pair)
    gate_term = weight_grad(second_all, both_grad[:, :1536])
    left_low, right_low, gate_term, down_sum, both_grad = together(
        left_low, right_low, gate_term, down_sum, both_grad
    )
    down_share = to_owners(down_sum)
    gate_pair = pair_start(gate_term)
    top_low = shift(left_low[:half], "z", 1)
    bottom_low = shift(right_low[half:], "z", 3)
    up_term = weight_grad(second_all, both_grad[:, 1536:])
    mlp_out = lax.dot_general(
        inner, down_full, contract_last, preferred_element_type=f32
    ).reshape(RING, rows, width)
    mlp_own = mlp_out[0].astype(low)
    mlp_rest = mlp_out[1:].astype(low)
    top_low, bottom_low, up_term, mlp_own, mlp_rest = together(
        top_low, bottom_low, up_term, mlp_own, mlp_rest
    )
    up_pair = pair_start(up_term)
    middle_low = jnp.concatenate([own_low, left_low, top_low, bottom_low, right_low], axis=0)
    mixed_grad = jnp.dot(middle_low, out_full, preferred_element_type=f32).astype(low)
    mixed_grad = mixed_grad.reshape(RING, rows, 4, HEAD_DIM).transpose(0, 2, 1, 3)
    mixed_grad, down_share = together(mixed_grad, down_share)
    head_grads = to_heads(mixed_grad.reshape(BLOCKS, rows, HEAD_DIM))
    down_pair = over_x(down_share)
    mlp_left = send_back(mlp_rest[0], 1)
    mlp_right = send_back(mlp_rest[2], 3)
    out_term = weight_grad(middle_low, mixed)
    gate_sum = pair_sum(*gate_pair)
    head_grads, out_term, gate_sum, down_pair, mlp_left, mlp_right, mlp_opposite = together(
        head_grads, out_term, gate_sum, down_pair, mlp_left, mlp_right, mlp_rest[1]
    )
    gate_share = to_owners(gate_sum)
    down_blocks = over_z(down_pair)
    out_pair = pair_start(out_term)

    query_grad, key_grad, value_grad = attention_backward(
        order, head_queries, head_keys, head_values, head_grads, head_mixed_t, head_logs
    )
    up_sum = pair_sum(*up_pair)
    out_sum = pair_sum(*out_pair)
    query_grad, gate_share, up_sum, out_sum = together(query_grad, gate_share, up_sum, out_sum)
    gate_pair = over_x(gate_share)
    mlp_opposite = send_back(mlp_opposite, 2)
    keep = jnp.where(core_at == 0, key_grad, value_grad)
    give = jnp.where(core_at == 0, value_grad, key_grad)
    pair_grad = (keep.astype(f32) + shift(give, "core", 1, 2).astype(f32)).astype(low)
    returned = to_heads(jnp.stack([query_grad, pair_grad], axis=1))
    returned, up_sum, gate_pair, down_blocks, mlp_opposite = together(
        returned, up_sum, gate_pair, down_blocks, mlp_opposite
    )
    up_share = to_owners(up_sum)
    gate_blocks = over_z(gate_pair)
    output = (
        middle
        + mlp_own.astype(f32)
        + mlp_left.astype(f32)
        + mlp_right.astype(f32)
        + mlp_opposite.astype(f32)
    ).astype(low)
    qkv_grad, query_gain_part, key_gain_part = first_back(
        returned, qkv_pre, cosine, sine, query_row, key_row
    )
    qkv_grad = qkv_grad.reshape(ring_rows, 1024)
    qkv_term = weight_grad(first_in.reshape(ring_rows, width), qkv_grad)
    qkv_pair = pair_start(qkv_term)
    first_partial = lax.dot_general(
        after(qkv_grad, qkv_term),
        first_weights[:, :1024],
        contract_last,
        preferred_element_type=f32,
    )
    qkv_pair, first_partial, up_share, gate_blocks = together(
        qkv_pair, first_partial.astype(low), up_share, gate_blocks
    )
    up_pair = over_x(up_share)
    qkv_share = to_owners(jnp.concatenate([pair_sum(*qkv_pair), out_sum], axis=2))
    first_blocks = [first_partial[r * rows : (r + 1) * rows] for r in range(RING)]
    first_blocks = [first_blocks[0]] + [send_back(first_blocks[r], r) for r in range(1, RING)]
    first_blocks, qkv_share, up_pair = together(first_blocks, qkv_share, up_pair)
    first_grad = sum(block.astype(f32) for block in first_blocks)
    hidden_rms = inverse_rms(hidden)
    own_norm = hidden * hidden_rms
    attn_gain_part = jnp.sum(first_grad * own_norm, axis=0)
    scaled_first = first_grad * attn_scale
    hidden_grad = (
        middle_grad
        + hidden_rms
        * (scaled_first - own_norm * jnp.mean(scaled_first * own_norm, axis=-1, keepdims=True))
    ).astype(low)

    (down_grad_out,) = place(z_at, down_blocks, (1536,))
    (gate_grad_out,) = place(z_at, gate_blocks, (1536,))
    (up_grad_out,) = place(z_at, over_z(up_pair), (1536,))
    query_grad_out, key_grad_out, value_grad_out, out_grad_out = place(
        z_at, over_z(over_x(qkv_share)), (512, 256, 256, 512)
    )

    gain_send = jnp.stack(
        [
            attn_gain_part.reshape(BLOCKS, HEAD_DIM),
            mlp_gain_part.reshape(BLOCKS, HEAD_DIM),
            jnp.broadcast_to(query_gain_part, (BLOCKS, HEAD_DIM)),
            jnp.broadcast_to(key_gain_part, (BLOCKS, HEAD_DIM)),
        ],
        axis=1,
    )
    gain_sum = jnp.sum(to_heads(gain_send), axis=0)
    gain_sum = gain_sum + shift(gain_sum, "x_lo", 1, 2)
    pair_sum = gain_sum + shift(gain_sum, "z", 2)
    gain_sum = pair_sum + shift(pair_sum, "z", 1)

    return (
        output,
        hidden_grad,
        gain_sum[0],
        gain_sum[2],
        gain_sum[3],
        query_grad_out,
        key_grad_out,
        value_grad_out,
        out_grad_out,
        gain_sum[1],
        gate_grad_out,
        up_grad_out,
        down_grad_out,
    )


def solution(mesh):
    fine = Mesh(mesh.devices.reshape(2, 4, 4, 2, 2), ALL_AXES)
    rep = ("x_lo", "z")
    row = P(ALL_AXES, None)
    part = P(GROUP_AXES)
    weight = P(GROUP_AXES, None)
    in_specs = (
        row,
        row,
        P(rep),
        P(rep),
        part,
        P(),
        P(),
        weight,
        weight,
        weight,
        weight,
        part,
        weight,
        weight,
        weight,
    )
    out_specs = (
        row,
        row,
        part,
        P(),
        P(),
        weight,
        weight,
        weight,
        weight,
        part,
        weight,
        weight,
        weight,
    )
    return jax.shard_map(local, mesh=fine, in_specs=in_specs, out_specs=out_specs, check_vma=False)
```

```python
import jax
import jax.numpy as jnp
from jax import lax
from jax.experimental import pallas as pl
from jax.experimental.pallas import tpu as pltpu
from jax.sharding import Mesh
from jax.sharding import PartitionSpec as P

HEAD_DIM = 128
RING = 4
BLOCK = 256
BLOCKS = 16
TILE = 512
TILES = 8
PROMPT_TILES = 6

norm_eps = 1e-06
rope_base = 1000000.0
score_scale = HEAD_DIM ** (-0.5)
score_scale_log2 = score_scale * 1.4426950408889634
contract_first = (((0,), (0,)), ((), ()))
contract_last = (((1,), (1,)), ((), ()))
GROUP_AXES = ("y", "x_hi", "core")
ALL_AXES = ("x_lo", "z", "y", "x_hi", "core")
low = jnp.bfloat16


def inverse_rms(values):
    return lax.rsqrt(jnp.mean(values * values, axis=-1, keepdims=True) + norm_eps)


def normalize(values):
    return values * inverse_rms(values)


def shift(values, axis, by, size=RING):
    return lax.ppermute(values, axis, [(i, (i + by) % size) for i in range(size)])


def gather_z(values):
    return jnp.concatenate(
        [values, shift(values, "z", 1), shift(values, "z", 2), shift(values, "z", 3)], axis=0
    )


def scatter_z(partial):
    rows = partial.shape[0] // RING
    blocks = [partial[r * rows : (r + 1) * rows] for r in range(RING)]
    total = blocks[0].astype(jnp.float32)
    for r in range(1, RING):
        total = total + shift(blocks[r].astype(low), "z", -r).astype(jnp.float32)
    return total


def forward_kernel(order, q_ref, k_ref, v_ref, mixed_ref, mixed_t_ref, log_ref, k_all, v_t, acc, total):
    tile = pl.program_id(0)

    @pl.when(tile == 0)
    def _():
        for at in range(BLOCKS):
            k_all[at * BLOCK : (at + 1) * BLOCK, :] = k_ref[order[at]]
            v_t[at // 2, :, (at % 2) * BLOCK : (at % 2 + 1) * BLOCK] = (
                v_ref[order[at]].astype(jnp.float32).T.astype(low)
            )

    queries = jnp.concatenate([q_ref[order[2 * tile]], q_ref[order[2 * tile + 1]]], axis=0)
    acc[...] = jnp.zeros_like(acc)
    total[...] = jnp.zeros_like(total)

    def chunk(at, masked):
        keys = k_all[pl.ds(pl.multiple_of(at * TILE, TILE), TILE), :]
        scores = lax.dot_general(keys, queries, contract_last, preferred_element_type=jnp.float32)
        weights = jnp.exp2(scores * score_scale_log2)
        if masked:
            key_row = lax.broadcasted_iota(jnp.int32, (TILE, TILE), 0)
            query_row = lax.broadcasted_iota(jnp.int32, (TILE, TILE), 1)
            weights = jnp.where(key_row <= query_row, weights, 0.0)
        total[...] += jnp.sum(weights, axis=0, keepdims=True)
        acc[...] += jnp.dot(v_t[at], weights.astype(low), preferred_element_type=jnp.float32)

    @pl.loop(0, jnp.minimum(tile, PROMPT_TILES))
    def _(at):
        chunk(at, False)

    chunk(tile, True)
    mixed_t = acc[...] / total[...]
    mixed_t_ref[tile] = mixed_t
    log_ref[tile] = jnp.log2(total[...])
    mixed = mixed_t.T.astype(low)
    mixed_ref[order[2 * tile]] = mixed[:BLOCK]
    mixed_ref[order[2 * tile + 1]] = mixed[BLOCK:]


def attention_forward(order, queries, keys, values):
    whole = pl.BlockSpec(memory_space=pltpu.VMEM)
    return pl.pallas_call(
        forward_kernel,
        out_shape=(
            jax.ShapeDtypeStruct((BLOCKS, BLOCK, HEAD_DIM), low),
            jax.ShapeDtypeStruct((TILES, HEAD_DIM, TILE), jnp.float32),
            jax.ShapeDtypeStruct((TILES, 1, TILE), jnp.float32),
        ),
        grid_spec=pltpu.PrefetchScalarGridSpec(
            num_scalar_prefetch=1,
            grid=(TILES,),
            in_specs=[whole] * 3,
            out_specs=(whole, whole, whole),
            scratch_shapes=[
                pltpu.VMEM((BLOCKS * BLOCK, HEAD_DIM), low),
                pltpu.VMEM((TILES, HEAD_DIM, TILE), low),
                pltpu.VMEM((HEAD_DIM, TILE), jnp.float32),
                pltpu.VMEM((1, TILE), jnp.float32),
            ],
        ),
        compiler_params=pltpu.CompilerParams(vmem_limit_bytes=40 * 1024 * 1024),
        cost_estimate=pl.CostEstimate(
            flops=1024, bytes_accessed=1024, transcendentals=0
        ),
    )(order, queries, keys, values)


def backward_kernel(
    order,
    q_ref,
    k_ref,
    v_ref,
    g_ref,
    mixed_t_ref,
    log_ref,
    q_out,
    k_out,
    v_out,
    k_all,
    v_all,
    k_t,
    q_acc,
    k_acc,
    v_acc,
):
    tile = pl.program_id(0)

    @pl.when(tile == 0)
    def _():
        for at in range(BLOCKS):
            rows = slice(at * BLOCK, (at + 1) * BLOCK)
            keys = k_ref[order[at]]
            k_all[rows, :] = keys
            v_all[rows, :] = v_ref[order[at]]
            k_t[at // 2, :, (at % 2) * BLOCK : (at % 2 + 1) * BLOCK] = (
                keys.astype(jnp.float32).T.astype(low)
            )
        k_acc[...] = jnp.zeros_like(k_acc)
        v_acc[...] = jnp.zeros_like(v_acc)

    queries = jnp.concatenate([q_ref[order[2 * tile]], q_ref[order[2 * tile + 1]]], axis=0)
    grads = jnp.concatenate([g_ref[order[2 * tile]], g_ref[order[2 * tile + 1]]], axis=0)
    grads_t = grads.astype(jnp.float32).T
    shared = jnp.sum(grads_t * mixed_t_ref[tile], axis=0, keepdims=True)
    logs = log_ref[tile]
    q_acc[...] = jnp.zeros_like(q_acc)

    def chunk(at, masked):
        rows = pl.ds(pl.multiple_of(at * TILE, TILE), TILE)
        scores = lax.dot_general(
            k_all[rows, :], queries, contract_last, preferred_element_type=jnp.float32
        )
        probs = jnp.exp2(scores * score_scale_log2 - logs)
        if masked:
            key_row = lax.broadcasted_iota(jnp.int32, (TILE, TILE), 0)
            query_row = lax.broadcasted_iota(jnp.int32, (TILE, TILE), 1)
            probs = jnp.where(key_row <= query_row, probs, 0.0)
        prob_grads = lax.dot_general(
            v_all[rows, :], grads, contract_last, preferred_element_type=jnp.float32
        )
        score_grads = (probs * (prob_grads - shared)).astype(low)
        v_acc[rows, :] += jnp.dot(probs.astype(low), grads, preferred_element_type=jnp.float32)
        k_acc[rows, :] += jnp.dot(score_grads, queries, preferred_element_type=jnp.float32)
        q_acc[...] += jnp.dot(k_t[at], score_grads, preferred_element_type=jnp.float32)

    @pl.loop(0, jnp.minimum(tile, PROMPT_TILES))
    def _(at):
        chunk(at, False)

    chunk(tile, True)
    query_grad = (q_acc[...] * score_scale).T.astype(low)
    q_out[order[2 * tile]] = query_grad[:BLOCK]
    q_out[order[2 * tile + 1]] = query_grad[BLOCK:]

    @pl.when(tile == TILES - 1)
    def _():
        for at in range(BLOCKS):
            rows = slice(at * BLOCK, (at + 1) * BLOCK)
            k_out[order[at]] = (k_acc[rows, :] * score_scale).astype(low)
            v_out[order[at]] = v_acc[rows, :].astype(low)


def attention_backward(order, queries, keys, values, grads, mixed_t, logs):
    whole = pl.BlockSpec(memory_space=pltpu.VMEM)
    rows = BLOCKS * BLOCK
    return pl.pallas_call(
        backward_kernel,
        out_shape=(jax.ShapeDtypeStruct((BLOCKS, BLOCK, HEAD_DIM), low),) * 3,
        grid_spec=pltpu.PrefetchScalarGridSpec(
            num_scalar_prefetch=1,
            grid=(TILES,),
            in_specs=[whole] * 6,
            out_specs=(whole, whole, whole),
            scratch_shapes=[
                pltpu.VMEM((rows, HEAD_DIM), low),
                pltpu.VMEM((rows, HEAD_DIM), low),
                pltpu.VMEM((TILES, HEAD_DIM, TILE), low),
                pltpu.VMEM((HEAD_DIM, TILE), jnp.float32),
                pltpu.VMEM((rows, HEAD_DIM), jnp.float32),
                pltpu.VMEM((rows, HEAD_DIM), jnp.float32),
            ],
        ),
        compiler_params=pltpu.CompilerParams(vmem_limit_bytes=48 * 1024 * 1024),
        cost_estimate=pl.CostEstimate(
            flops=1024, bytes_accessed=1024, transcendentals=0
        ),
    )(order, queries, keys, values, grads, mixed_t, logs)


def mlp_kernel(second_ref, cot_ref, gate_ref, up_ref, down_ref, *refs):
    inner_ref, both_ref, second_out, cot_out, grad_ref, acc = refs[-6:]
    at = pl.program_id(0)
    step = gate_ref.shape[1]
    second = second_ref[...]

    @pl.when(at == 0)
    def _():
        second_out[0] = second
        cot_out[0] = cot_ref[...]

    gate_weight = gate_ref[...]
    up_weight = up_ref[...]
    gate_act = jnp.dot(second, gate_weight, preferred_element_type=jnp.float32)
    up_act = jnp.dot(second, up_weight, preferred_element_type=jnp.float32)
    inner_grad = jnp.dot(cot_ref[...], down_ref[...], preferred_element_type=jnp.float32)
    sigmoid = 1.0 / (1.0 + jnp.exp(-gate_act))
    silu = gate_act * sigmoid
    inner_ref[0] = (silu * up_act).astype(low)
    gate_grad = (inner_grad * up_act * (sigmoid * (1.0 + gate_act * (1.0 - sigmoid)))).astype(low)
    up_grad = (inner_grad * silu).astype(low)
    both_ref[0, :, pl.ds(pl.multiple_of(at * step, step), step)] = gate_grad
    up_at = (pl.num_programs(0) + at) * step
    both_ref[0, :, pl.ds(pl.multiple_of(up_at, step), step)] = up_grad
    part = lax.dot_general(
        gate_grad, gate_weight, contract_last, preferred_element_type=jnp.float32
    ) + lax.dot_general(up_grad, up_weight, contract_last, preferred_element_type=jnp.float32)

    @pl.when(at == 0)
    def _():
        acc[...] = part

    @pl.when(at > 0)
    def _():
        acc[...] += part

    @pl.when(at == pl.num_programs(0) - 1)
    def _():
        grad_ref[...] = acc[...].astype(low)


def mlp_block(block, second, cot, weights, held):
    rows, width = second.shape
    hidden_width = weights.shape[1] // 3
    step = 512
    steps = hidden_width // step
    whole = pl.BlockSpec((rows, width), lambda c: (0, 0))
    kept = pl.BlockSpec((1, rows, step), lambda c: (block, 0, c))
    kept_both = pl.BlockSpec((1, rows, 2 * hidden_width), lambda c: (block, 0, 0))
    kept_rows = pl.BlockSpec((1, rows, width), lambda c: (block, 0, 0))
    rows_shape = jax.ShapeDtypeStruct((RING, rows, width), low)
    return pl.pallas_call(
        mlp_kernel,
        grid=(steps,),
        in_specs=[
            whole,
            whole,
            pl.BlockSpec((width, step), lambda c: (0, c)),
            pl.BlockSpec((width, step), lambda c: (0, steps + c)),
            pl.BlockSpec((width, step), lambda c: (0, 2 * steps + c)),
        ]
        + [pl.BlockSpec(memory_space=pl.ANY)] * len(held),
        out_specs=(kept, kept_both, kept_rows, kept_rows, whole),
        out_shape=(
            jax.ShapeDtypeStruct((RING, rows, hidden_width), low),
            jax.ShapeDtypeStruct((RING, rows, 2 * hidden_width), low),
            rows_shape,
            rows_shape,
            jax.ShapeDtypeStruct((rows, width), low),
        ),
        scratch_shapes=[pltpu.VMEM((rows, width), jnp.float32)],
        input_output_aliases={5 + i: i for i in range(len(held))},
        compiler_params=pltpu.CompilerParams(vmem_limit_bytes=48 * 1024 * 1024),
        cost_estimate=pl.CostEstimate(
            flops=2 * 5 * rows * width * hidden_width,
            bytes_accessed=2 * 3 * width * hidden_width,
            transcendentals=rows * hidden_width,
        ),
    )(second, cot, weights, weights, weights, *held)


def first_kernel(
    hidden_ref, gain_ref, weight_ref, cos_ref, sin_ref, query_gain, key_gain, first_ref, pre_ref, send_ref
):
    first = (normalize(hidden_ref[0].astype(jnp.float32)) * gain_ref[...]).astype(low)
    first_ref[0] = first
    pre = jnp.dot(first, weight_ref[...], preferred_element_type=jnp.float32)
    pre_ref[0] = pre
    cosine = cos_ref[0]
    sine = sin_ref[0]

    def turned(head, gain):
        values = normalize(pre[:, head * HEAD_DIM : (head + 1) * HEAD_DIM]) * gain
        return (values * cosine + pltpu.roll(values, HEAD_DIM // 2, 1) * sine).astype(low)

    for head in range(4):
        send_ref[head, 0] = turned(head, query_gain[...])
    for head in range(2):
        send_ref[2 * head, 1] = turned(4 + head, key_gain[...])
        send_ref[2 * head + 1, 1] = pre[:, (6 + head) * HEAD_DIM : (7 + head) * HEAD_DIM].astype(low)


def first_part(hidden_all, gain, weights, cosine, sine, query_gain, key_gain):
    _, rows, width = hidden_all.shape
    row = pl.BlockSpec((1, HEAD_DIM), lambda r: (0, 0))
    turn = pl.BlockSpec((1, rows, HEAD_DIM), lambda r: (r, 0, 0))
    return pl.pallas_call(
        first_kernel,
        grid=(RING,),
        in_specs=[
            pl.BlockSpec((1, rows, width), lambda r: (r, 0, 0)),
            pl.BlockSpec((1, width), lambda r: (0, 0)),
            pl.BlockSpec((width, 1024), lambda r: (0, 0)),
            turn,
            turn,
            row,
            row,
        ],
        out_specs=(
            pl.BlockSpec((1, rows, width), lambda r: (r, 0, 0)),
            pl.BlockSpec((1, rows, 1024), lambda r: (r, 0, 0)),
            pl.BlockSpec((4, 2, rows, HEAD_DIM), lambda r: (r, 0, 0, 0)),
        ),
        out_shape=(
            jax.ShapeDtypeStruct((RING, rows, width), low),
            jax.ShapeDtypeStruct((RING, rows, 1024), jnp.float32),
            jax.ShapeDtypeStruct((BLOCKS, 2, rows, HEAD_DIM), low),
        ),
        compiler_params=pltpu.CompilerParams(vmem_limit_bytes=40 * 1024 * 1024),
        cost_estimate=pl.CostEstimate(
            flops=2 * RING * rows * width * 1024,
            bytes_accessed=20 * 1024 * 1024,
            transcendentals=0,
        ),
    )(hidden_all, gain, weights, cosine, sine, query_gain, key_gain)


def first_back_kernel(
    back_ref, pre_ref, cos_ref, sin_ref, query_gain, key_gain, grad_ref, query_sum, key_sum
):
    cosine = cos_ref[0]
    sine = sin_ref[0]

    @pl.when(pl.program_id(0) == 0)
    def _():
        query_sum[...] = jnp.zeros_like(query_sum)
        key_sum[...] = jnp.zeros_like(key_sum)

    def back(grads, head, gain, sums):
        columns = slice(head * HEAD_DIM, (head + 1) * HEAD_DIM)
        values = pre_ref[0, :, columns]
        grads = grads.astype(jnp.float32)
        grads = grads * cosine - pltpu.roll(grads, HEAD_DIM // 2, 1) * sine
        scale = inverse_rms(values)
        normed = values * scale
        sums[...] += jnp.sum(grads * normed, axis=0, keepdims=True)
        scaled = grads * gain
        out = scale * (scaled - normed * jnp.mean(scaled * normed, axis=-1, keepdims=True))
        grad_ref[0, :, columns] = out.astype(low)

    for head in range(4):
        back(back_ref[head, 0], head, query_gain[...], query_sum)
    for head in range(2):
        back(back_ref[2 * head, 1], 4 + head, key_gain[...], key_sum)
        grad_ref[0, :, (6 + head) * HEAD_DIM : (7 + head) * HEAD_DIM] = back_ref[2 * head + 1, 1]


def first_back(returned, pre, cosine, sine, query_gain, key_gain):
    _, rows, _ = pre.shape
    row = pl.BlockSpec((1, HEAD_DIM), lambda r: (0, 0))
    turn = pl.BlockSpec((1, rows, HEAD_DIM), lambda r: (r, 0, 0))
    wide = pl.BlockSpec((1, rows, 1024), lambda r: (r, 0, 0))
    return pl.pallas_call(
        first_back_kernel,
        grid=(RING,),
        in_specs=[
            pl.BlockSpec((4, 2, rows, HEAD_DIM), lambda r: (r, 0, 0, 0)),
            wide,
            turn,
            turn,
            row,
            row,
        ],
        out_specs=(wide, row, row),
        out_shape=(
            jax.ShapeDtypeStruct((RING, rows, 1024), low),
            jax.ShapeDtypeStruct((1, HEAD_DIM), jnp.float32),
            jax.ShapeDtypeStruct((1, HEAD_DIM), jnp.float32),
        ),
        compiler_params=pltpu.CompilerParams(vmem_limit_bytes=40 * 1024 * 1024),
        cost_estimate=pl.CostEstimate(
            flops=1024, bytes_accessed=1024, transcendentals=0
        ),
    )(returned, pre, cosine, sine, query_gain, key_gain)


def last_kernel(grad_ref, weight_ref, hidden_ref, part_ref, gain_ref):
    part = lax.dot_general(
        grad_ref[0], weight_ref[...], contract_last, preferred_element_type=jnp.float32
    )
    part_ref[0] = part.astype(low)
    normed = normalize(hidden_ref[0].astype(jnp.float32))
    gain = jnp.sum(part * normed, axis=0, keepdims=True)

    @pl.when(pl.program_id(0) == 0)
    def _():
        gain_ref[...] = gain

    @pl.when(pl.program_id(0) > 0)
    def _():
        gain_ref[...] += gain


def last_part(grads, weights, hidden_all):
    _, rows, width = hidden_all.shape
    wide = pl.BlockSpec((1, rows, width), lambda r: (r, 0, 0))
    return pl.pallas_call(
        last_kernel,
        grid=(RING,),
        in_specs=[
            pl.BlockSpec((1, rows, 1024), lambda r: (r, 0, 0)),
            pl.BlockSpec((width, 1024), lambda r: (0, 0)),
            wide,
        ],
        out_specs=(wide, pl.BlockSpec((1, width), lambda r: (0, 0))),
        out_shape=(
            jax.ShapeDtypeStruct((RING, rows, width), low),
            jax.ShapeDtypeStruct((1, width), jnp.float32),
        ),
        compiler_params=pltpu.CompilerParams(vmem_limit_bytes=40 * 1024 * 1024),
        cost_estimate=pl.CostEstimate(flops=1024, bytes_accessed=1024, transcendentals=0),
    )(grads, weights, hidden_all)


def to_heads(send):
    return lax.all_to_all(send, GROUP_AXES, 0, 0, tiled=True)


def after(value, *others):
    return lax.optimization_barrier((value, others))[0]


def ring_blocks(values):
    half = values.shape[0] // 2
    left = shift(values, "z", 1)
    right = shift(values, "z", 3)
    opposite = jnp.concatenate(
        [shift(left[:half], "z", 1), shift(right[half:], "z", 3)], axis=0
    )
    return [values, left, opposite, right]


def together(*values):
    return lax.optimization_barrier(values)


def place_kernel(z_ref, *refs):
    blocks, outs = refs[:RING], refs[RING:]
    for r in range(RING):
        slot = lax.rem(z_ref[0] - r + RING, RING)
        start = 0
        for out in outs:
            if out.shape[1] == HEAD_DIM:
                columns = blocks[r][:, start : start + HEAD_DIM].astype(jnp.float32)
                out[...] = columns if r == 0 else out[...] + columns
                continue
            part = out.shape[1] // RING
            at = pl.multiple_of(slot * part, part)
            out[:, pl.ds(at, part)] = blocks[r][:, start : start + part].astype(jnp.float32)
            start += part


def place(z_at, blocks, widths, summed=False):
    shapes = [RING * part for part in widths] + [HEAD_DIM] * summed
    rows = blocks[0].shape[0]
    whole = pl.BlockSpec(memory_space=pltpu.VMEM)
    return pl.pallas_call(
        place_kernel,
        in_specs=[pl.BlockSpec(memory_space=pltpu.SMEM)] + [whole] * RING,
        out_specs=tuple(whole for _ in shapes),
        out_shape=tuple(jax.ShapeDtypeStruct((rows, part), jnp.float32) for part in shapes),
        compiler_params=pltpu.CompilerParams(vmem_limit_bytes=24 * 1024 * 1024),
        cost_estimate=pl.CostEstimate(
            flops=0, bytes_accessed=rows * sum(widths) * 24, transcendentals=0
        ),
    )(z_at[None], *blocks)


def ring_sum(own, left, opposite, right):
    half = left.shape[0] // 2
    f32 = jnp.float32
    top = shift(opposite[:half], "z", 3)
    bottom = shift(opposite[half:], "z", 1)
    left_top = (left[:half].astype(f32) + top.astype(f32)).astype(low)
    right_bottom = (right[half:].astype(f32) + bottom.astype(f32)).astype(low)
    left = shift(jnp.concatenate([left_top, left[half:]], axis=0), "z", 3)
    right = shift(jnp.concatenate([right[:half], right_bottom], axis=0), "z", 1)
    return own, left, right


def send_back(block, r):
    return shift(block, "z", -r)


def local(
    hidden_in,
    cotangent,
    segment_ids,
    positions,
    attn_gain,
    query_gain,
    key_gain,
    query_weight,
    key_weight,
    value_weight,
    out_weight,
    mlp_gain,
    gate_weight,
    up_weight,
    down_weight,
):
    f32 = jnp.float32
    rows, width = hidden_in.shape
    ring_rows = RING * rows
    z_at = lax.axis_index("z")
    y_at = lax.axis_index("y")
    core_at = lax.axis_index("core")
    my_index = (y_at * 2 + lax.axis_index("x_hi")) * 2 + core_at

    def columns(weight):
        part = weight.shape[1] // RING
        return lax.dynamic_slice_in_dim(weight, z_at * part, part, 1).astype(low)

    def gather(block):
        return lax.all_gather(block, GROUP_AXES, axis=0, tiled=True)

    own_places = lax.dynamic_slice_in_dim(positions, my_index * rows, rows)
    firsts = positions.reshape(BLOCKS, BLOCK)[:, 0]
    segments = segment_ids.reshape(BLOCKS, BLOCK)[:, 0]
    logical = firsts // BLOCK + jnp.maximum(segments - 1, 0) * 2
    numbers = jnp.arange(BLOCKS, dtype=jnp.int32)
    order = jnp.sum(jnp.where(logical[:, None] == numbers[None, :], numbers[:, None], 0), axis=0)
    notes = gather_z(jnp.concatenate([own_places, order, jnp.zeros((112,), jnp.int32)])[None])
    places = notes[:, :rows]
    order = lax.dynamic_index_in_dim(notes, y_at, 0, keepdims=False)[rows : rows + BLOCKS]

    gains = jnp.pad(
        jnp.stack([attn_gain, mlp_gain], axis=1).astype(low), ((0, 0), (0, HEAD_DIM - 2))
    )
    first_weights = gather(
        jnp.concatenate(
            [
                columns(query_weight),
                columns(key_weight),
                columns(value_weight),
                columns(out_weight),
                gains,
            ],
            axis=1,
        )
    )
    out_full = first_weights[:, 1024:1536]
    attn_scale = first_weights[:, 1536].astype(f32)[None]
    mlp_scale = first_weights[:, 1537].astype(f32)[None]
    mlp_weights = gather(
        jnp.concatenate([columns(gate_weight), columns(up_weight), columns(down_weight)], axis=1)
    )
    down_full = mlp_weights[:, 3072:]
    out_all = gather(out_weight.astype(low))

    hidden_blocks = ring_blocks(hidden_in)
    cot_own = after(cotangent, *hidden_blocks)
    cot_left = shift(cot_own, "z", 1)
    cot_right = shift(cot_own, "z", 3)
    frequency = rope_base ** (-2.0 * jnp.arange(HEAD_DIM // 2, dtype=f32) / HEAD_DIM)
    angles = places.astype(f32)[:, :, None] * frequency[None, None, :]
    cosine = jnp.cos(angles)
    sine = jnp.sin(angles)
    cosine = jnp.concatenate([cosine, cosine], axis=-1)
    sine = jnp.concatenate([-sine, sine], axis=-1)
    query_row = query_gain[None]
    key_row = key_gain[None]

    hidden_all = jnp.stack(hidden_blocks)
    first_in, qkv_pre, send = first_part(
        hidden_all, attn_scale, first_weights, cosine, sine, query_row, key_row
    )
    arrived, cot_left, cot_right, cot_own = together(
        to_heads(send), cot_left, cot_right, cot_own
    )
    cot_opposite = shift(cot_own, "z", 2)
    head_queries = arrived[:, 0]
    own_pair = arrived[:, 1]
    other_pair = shift(own_pair, "core", 1, 2)
    head_keys = jnp.where(core_at == 0, own_pair, other_pair)
    head_values = jnp.where(core_at == 0, other_pair, own_pair)
    head_mixed, head_mixed_t, head_logs = attention_forward(
        order, head_queries, head_keys, head_values
    )

    def from_heads(values):
        return values.reshape(RING, 4, rows, HEAD_DIM).transpose(0, 2, 1, 3).reshape(ring_rows, 512)

    mixed_arrived, cot_opposite = together(to_heads(head_mixed), cot_opposite)
    mixed = from_heads(mixed_arrived)
    attn_out = lax.dot_general(mixed, out_full, contract_last, preferred_element_type=f32)
    hidden = hidden_in.astype(f32)
    middle = hidden + scatter_z(attn_out)
    middle_rms = inverse_rms(middle)
    second_norm = middle * middle_rms
    second_in = (second_norm * mlp_scale).astype(low)
    left = shift(second_in, "z", 1)
    right = shift(second_in, "z", 3)
    *held, own_part = mlp_block(0, second_in, cot_own, mlp_weights, ())
    held, own_part, left, right = together(held, own_part, left, right)
    half = rows // 2
    top = shift(left[:half], "z", 1)
    bottom = shift(right[half:], "z", 3)
    *held, left_part = mlp_block(1, left, cot_left, mlp_weights, held)
    left_back = send_back(left_part, 1)
    *held, right_part = mlp_block(3, right, cot_right, mlp_weights, held)
    right_back = send_back(right_part, 3)
    held, top, bottom = together(held, top, bottom)
    opposite = jnp.concatenate([top, bottom], axis=0)
    *held, opposite_part = mlp_block(2, opposite, cot_opposite, mlp_weights, held)
    opposite_back = send_back(opposite_part, 2)
    inner = held[0].reshape(ring_rows, 1536)
    both_grad = held[1].reshape(ring_rows, 3072)
    second_all = held[2].reshape(ring_rows, width)
    cot_all = held[3].reshape(ring_rows, width)

    def weight_grad(left, right):
        return lax.dot_general(left, right, contract_first, preferred_element_type=f32).astype(low)

    def pair_start(term):
        term = term.reshape(8, 2, 128, term.shape[1])
        keep = lax.dynamic_index_in_dim(term, core_at, 1, keepdims=False)
        give = lax.dynamic_index_in_dim(term, 1 - core_at, 1, keepdims=False)
        return keep, shift(give, "core", 1, 2)

    def pair_sum(keep, come):
        return (keep.astype(f32) + come.astype(f32)).astype(low)

    def to_owners(pair):
        terms = lax.all_to_all(pair, ("y", "x_hi"), 0, 0, tiled=True)
        return jnp.sum(terms.astype(f32), axis=0).astype(low)

    def over_x(share):
        return share, shift(share, "x_lo", 1, 2)

    def over_z(pair):
        share = pair_sum(*pair)
        return [share] + [shift(share, "z", r) for r in range(1, RING)]

    both_term = weight_grad(second_all, both_grad)
    mlp_out = lax.dot_general(
        inner, down_full, contract_last, preferred_element_type=f32
    ).reshape(RING, rows, width)
    mlp_own = mlp_out[0].astype(low)
    mlp_rest = mlp_out[1:].astype(low)
    left_back, right_back, opposite_back, both_term, mlp_own, mlp_rest, inner = together(
        left_back, right_back, opposite_back, both_term, mlp_own, mlp_rest, inner
    )
    both_share = lax.psum_scatter(both_term, GROUP_AXES, scatter_dimension=0, tiled=True)

    second_grad = (
        own_part.astype(f32)
        + left_back.astype(f32)
        + right_back.astype(f32)
        + opposite_back.astype(f32)
    )
    mlp_gain_part = jnp.sum(second_grad * second_norm, axis=0)
    scaled_grad = second_grad * mlp_scale
    middle_grad = cotangent.astype(f32) + middle_rms * (
        scaled_grad - second_norm * jnp.mean(scaled_grad * second_norm, axis=-1, keepdims=True)
    )
    own_low = middle_grad.astype(low)
    mixed_grad = jnp.dot(own_low, out_all, preferred_element_type=f32).astype(low)

    def heads_of(r):
        return lax.dynamic_slice_in_dim(mixed_grad, ((z_at + r) & (RING - 1)) * 512, 512, 1)

    grad_blocks = [heads_of(0)] + [shift(heads_of(r), "z", r) for r in range(1, RING)]
    down_term = weight_grad(cot_all, inner)
    grad_blocks, down_term, own_low, mlp_rest = together(grad_blocks, down_term, own_low, mlp_rest)
    down_pair = pair_start(down_term)
    mixed_grad = jnp.stack(grad_blocks).reshape(RING, rows, 4, HEAD_DIM).transpose(0, 2, 1, 3)
    head_grads = to_heads(mixed_grad.reshape(BLOCKS, rows, HEAD_DIM))
    down_sum = pair_sum(*down_pair)
    low_left = shift(own_low, "z", 1)
    low_right = shift(own_low, "z", 3)
    head_grads, down_sum, low_left, low_right, own_low, mlp_rest = together(
        head_grads, down_sum, low_left, low_right, own_low, mlp_rest
    )
    low_opposite = shift(own_low, "z", 2)
    down_share = to_owners(down_sum)

    query_grad, key_grad, value_grad = attention_backward(
        order, head_queries, head_keys, head_values, head_grads, head_mixed_t, head_logs
    )
    query_grad, key_grad, value_grad, low_opposite, mlp_rest = together(
        query_grad, key_grad, value_grad, low_opposite, mlp_rest
    )
    keep = jnp.where(core_at == 0, key_grad, value_grad)
    give = jnp.where(core_at == 0, value_grad, key_grad)
    pair_grad = (keep.astype(f32) + shift(give, "core", 1, 2).astype(f32)).astype(low)
    returned = to_heads(jnp.stack([query_grad, pair_grad], axis=1))
    down_pair = over_x(down_share)
    middle_low = jnp.concatenate([own_low, low_left, low_opposite, low_right], axis=0)
    out_sum = pair_sum(*pair_start(weight_grad(middle_low, mixed)))
    mlp_top = shift(mlp_rest[1][:half], "z", 3)
    mlp_bottom = shift(mlp_rest[1][half:], "z", 1)
    returned, down_pair, out_sum, mlp_top, mlp_bottom = together(
        returned, down_pair, out_sum, mlp_top, mlp_bottom
    )
    out_share = to_owners(out_sum)
    mlp_left = jnp.concatenate(
        [(mlp_rest[0][:half].astype(f32) + mlp_top.astype(f32)).astype(low), mlp_rest[0][half:]],
        axis=0,
    )
    mlp_right = jnp.concatenate(
        [mlp_rest[2][:half], (mlp_rest[2][half:].astype(f32) + mlp_bottom.astype(f32)).astype(low)],
        axis=0,
    )
    mlp_left = shift(mlp_left, "z", 3)
    mlp_right = shift(mlp_right, "z", 1)
    qkv_grad, query_gain_part, key_gain_part = first_back(
        returned, qkv_pre, cosine, sine, query_row, key_row
    )
    qkv_term = weight_grad(
        first_in.reshape(ring_rows, width), qkv_grad.reshape(ring_rows, 1024)
    )
    qkv_pair = pair_start(qkv_term)
    first_partial, attn_gain_part = last_part(
        after(qkv_grad, qkv_term), first_weights, hidden_all
    )
    first_partial, attn_gain_part, out_share = together(first_partial, attn_gain_part, out_share)
    gains_part = jnp.stack(
        [
            attn_gain_part[0],
            mlp_gain_part,
            jnp.tile(query_gain_part[0], BLOCKS),
            jnp.tile(key_gain_part[0], BLOCKS),
        ],
        axis=1,
    )
    gains_part = jnp.pad(gains_part.astype(low), ((0, 0), (0, HEAD_DIM - 4)))
    gains_pair = pair_start(gains_part)
    down_blocks = over_z(down_pair)
    qkv_pair, gains_pair, first_partial = together(qkv_pair, gains_pair, first_partial)
    qkv_share = to_owners(
        jnp.concatenate([pair_sum(*qkv_pair), pair_sum(*gains_pair)], axis=2)
    )
    out_pair = over_x(out_share)
    first_blocks = ring_sum(*[first_partial[r] for r in range(RING)])
    both_pair = over_x(both_share)
    first_blocks, qkv_share, out_pair, both_pair, down_blocks, mlp_left, mlp_right = together(
        first_blocks, qkv_share, out_pair, both_pair, down_blocks, mlp_left, mlp_right
    )
    qkv_pair = over_x(qkv_share)
    both_blocks = over_z(both_pair)
    output = (
        middle + mlp_own.astype(f32) + mlp_left.astype(f32) + mlp_right.astype(f32)
    ).astype(low)
    first_grad = sum(block.astype(f32) for block in first_blocks)
    hidden_rms = inverse_rms(hidden)
    own_norm = hidden * hidden_rms
    scaled_first = first_grad * attn_scale
    hidden_grad = (
        middle_grad
        + hidden_rms
        * (scaled_first - own_norm * jnp.mean(scaled_first * own_norm, axis=-1, keepdims=True))
    ).astype(low)

    (down_grad_out,) = place(z_at, down_blocks, (1536,))
    gate_grad_out, up_grad_out = place(z_at, both_blocks, (1536, 1536))
    (out_grad_out,) = place(z_at, over_z(out_pair), (512,))
    query_grad_out, key_grad_out, value_grad_out, gain_sum = place(
        z_at, over_z(qkv_pair), (512, 256, 256), True
    )
    gain_sum = gain_sum[:, :4].T

    return (
        output,
        hidden_grad,
        gain_sum[0],
        gain_sum[2],
        gain_sum[3],
        query_grad_out,
        key_grad_out,
        value_grad_out,
        out_grad_out,
        gain_sum[1],
        gate_grad_out,
        up_grad_out,
        down_grad_out,
    )


def solution(mesh):
    fine = Mesh(mesh.devices.reshape(2, 4, 4, 2, 2), ALL_AXES)
    rep = ("x_lo", "z")
    row = P(ALL_AXES, None)
    part = P(GROUP_AXES)
    weight = P(GROUP_AXES, None)
    in_specs = (
        row,
        row,
        P(rep),
        P(rep),
        part,
        P(),
        P(),
        weight,
        weight,
        weight,
        weight,
        part,
        weight,
        weight,
        weight,
    )
    out_specs = (
        row,
        row,
        part,
        P(),
        P(),
        weight,
        weight,
        weight,
        weight,
        part,
        weight,
        weight,
        weight,
    )
    return jax.shard_map(local, mesh=fine, in_specs=in_specs, out_specs=out_specs, check_vma=False)
```

```python
import jax
import jax.numpy as jnp
from jax import lax
from jax.experimental import pallas as pl
from jax.experimental.pallas import tpu as pltpu
from jax.sharding import Mesh
from jax.sharding import PartitionSpec as P

HEAD_DIM = 128
RING = 4
BLOCK = 256
BLOCKS = 16
TILE = 512
TILES = 8
PROMPT_TILES = 6
FF_STEP = 512

norm_eps = 1e-06
rope_base = 1000000.0
score_scale = HEAD_DIM ** (-0.5)
score_scale_log2 = score_scale * 1.4426950408889634
contract_first = (((0,), (0,)), ((), ()))
contract_last = (((1,), (1,)), ((), ()))
GROUP_AXES = ("y", "x_hi", "core")
ALL_AXES = ("x_lo", "z", "y", "x_hi", "core")
low = jnp.bfloat16


def inverse_rms(values):
    return lax.rsqrt(jnp.mean(values * values, axis=-1, keepdims=True) + norm_eps)


def normalize(values):
    return values * inverse_rms(values)


def shift(values, axis, by, size=RING):
    return lax.ppermute(values, axis, [(i, (i + by) % size) for i in range(size)])


def gather_z(values):
    return jnp.concatenate(
        [values, shift(values, "z", 1), shift(values, "z", 2), shift(values, "z", 3)], axis=0
    )


def forward_kernel(order, q_ref, k_ref, v_ref, mixed_ref, mixed_t_ref, log_ref, k_all, v_t, acc, total):
    tile = pl.program_id(0)

    @pl.when(tile == 0)
    def _():
        for at in range(BLOCKS):
            k_all[at * BLOCK : (at + 1) * BLOCK, :] = k_ref[order[at]]
            v_t[at // 2, :, (at % 2) * BLOCK : (at % 2 + 1) * BLOCK] = (
                v_ref[order[at]].astype(jnp.float32).T.astype(low)
            )

    queries = jnp.concatenate([q_ref[order[2 * tile]], q_ref[order[2 * tile + 1]]], axis=0)
    acc[...] = jnp.zeros_like(acc)
    total[...] = jnp.zeros_like(total)

    def chunk(at, masked):
        keys = k_all[pl.ds(pl.multiple_of(at * TILE, TILE), TILE), :]
        scores = lax.dot_general(keys, queries, contract_last, preferred_element_type=jnp.float32)
        weights = jnp.exp2(scores * score_scale_log2)
        if masked:
            key_row = lax.broadcasted_iota(jnp.int32, (TILE, TILE), 0)
            query_row = lax.broadcasted_iota(jnp.int32, (TILE, TILE), 1)
            weights = jnp.where(key_row <= query_row, weights, 0.0)
        total[...] += jnp.sum(weights, axis=0, keepdims=True)
        acc[...] += jnp.dot(v_t[at], weights.astype(low), preferred_element_type=jnp.float32)

    @pl.loop(0, jnp.minimum(tile, PROMPT_TILES))
    def _(at):
        chunk(at, False)

    chunk(tile, True)
    mixed_t = acc[...] / total[...]
    mixed_t_ref[tile] = mixed_t
    log_ref[tile] = jnp.log2(total[...])
    mixed = mixed_t.T.astype(low)
    mixed_ref[order[2 * tile]] = mixed[:BLOCK]
    mixed_ref[order[2 * tile + 1]] = mixed[BLOCK:]


def attention_forward(order, queries, keys, values):
    whole = pl.BlockSpec(memory_space=pltpu.VMEM)
    return pl.pallas_call(
        forward_kernel,
        out_shape=(
            jax.ShapeDtypeStruct((BLOCKS, BLOCK, HEAD_DIM), low),
            jax.ShapeDtypeStruct((TILES, HEAD_DIM, TILE), jnp.float32),
            jax.ShapeDtypeStruct((TILES, 1, TILE), jnp.float32),
        ),
        grid_spec=pltpu.PrefetchScalarGridSpec(
            num_scalar_prefetch=1,
            grid=(TILES,),
            in_specs=[whole] * 3,
            out_specs=(whole, whole, whole),
            scratch_shapes=[
                pltpu.VMEM((BLOCKS * BLOCK, HEAD_DIM), low),
                pltpu.VMEM((TILES, HEAD_DIM, TILE), low),
                pltpu.VMEM((HEAD_DIM, TILE), jnp.float32),
                pltpu.VMEM((1, TILE), jnp.float32),
            ],
        ),
        compiler_params=pltpu.CompilerParams(vmem_limit_bytes=40 * 1024 * 1024),
        cost_estimate=pl.CostEstimate(
            flops=1024, bytes_accessed=1024, transcendentals=0
        ),
    )(order, queries, keys, values)


def backward_kernel(
    order,
    q_ref,
    k_ref,
    v_ref,
    g_ref,
    mixed_t_ref,
    log_ref,
    q_out,
    k_out,
    v_out,
    k_all,
    v_all,
    k_t,
    q_acc,
    k_acc,
    v_acc,
):
    tile = pl.program_id(0)

    @pl.when(tile == 0)
    def _():
        for at in range(BLOCKS):
            rows = slice(at * BLOCK, (at + 1) * BLOCK)
            keys = k_ref[order[at]]
            k_all[rows, :] = keys
            v_all[rows, :] = v_ref[order[at]]
            k_t[at // 2, :, (at % 2) * BLOCK : (at % 2 + 1) * BLOCK] = (
                keys.astype(jnp.float32).T.astype(low)
            )
        k_acc[...] = jnp.zeros_like(k_acc)
        v_acc[...] = jnp.zeros_like(v_acc)

    queries = jnp.concatenate([q_ref[order[2 * tile]], q_ref[order[2 * tile + 1]]], axis=0)
    grads = jnp.concatenate([g_ref[order[2 * tile]], g_ref[order[2 * tile + 1]]], axis=0)
    grads_t = grads.astype(jnp.float32).T
    shared = jnp.sum(grads_t * mixed_t_ref[tile], axis=0, keepdims=True)
    logs = log_ref[tile]
    q_acc[...] = jnp.zeros_like(q_acc)

    def chunk(at, masked):
        rows = pl.ds(pl.multiple_of(at * TILE, TILE), TILE)
        scores = lax.dot_general(
            k_all[rows, :], queries, contract_last, preferred_element_type=jnp.float32
        )
        probs = jnp.exp2(scores * score_scale_log2 - logs)
        if masked:
            key_row = lax.broadcasted_iota(jnp.int32, (TILE, TILE), 0)
            query_row = lax.broadcasted_iota(jnp.int32, (TILE, TILE), 1)
            probs = jnp.where(key_row <= query_row, probs, 0.0)
        prob_grads = lax.dot_general(
            v_all[rows, :], grads, contract_last, preferred_element_type=jnp.float32
        )
        score_grads = (probs * (prob_grads - shared)).astype(low)
        v_acc[rows, :] += jnp.dot(probs.astype(low), grads, preferred_element_type=jnp.float32)
        k_acc[rows, :] += jnp.dot(score_grads, queries, preferred_element_type=jnp.float32)
        q_acc[...] += jnp.dot(k_t[at], score_grads, preferred_element_type=jnp.float32)

    @pl.loop(0, jnp.minimum(tile, PROMPT_TILES))
    def _(at):
        chunk(at, False)

    chunk(tile, True)
    query_grad = (q_acc[...] * score_scale).T.astype(low)
    q_out[order[2 * tile]] = query_grad[:BLOCK]
    q_out[order[2 * tile + 1]] = query_grad[BLOCK:]

    @pl.when(tile == TILES - 1)
    def _():
        for at in range(BLOCKS):
            rows = slice(at * BLOCK, (at + 1) * BLOCK)
            k_out[order[at]] = (k_acc[rows, :] * score_scale).astype(low)
            v_out[order[at]] = v_acc[rows, :].astype(low)


def attention_backward(order, queries, keys, values, grads, mixed_t, logs):
    whole = pl.BlockSpec(memory_space=pltpu.VMEM)
    rows = BLOCKS * BLOCK
    return pl.pallas_call(
        backward_kernel,
        out_shape=(jax.ShapeDtypeStruct((BLOCKS, BLOCK, HEAD_DIM), low),) * 3,
        grid_spec=pltpu.PrefetchScalarGridSpec(
            num_scalar_prefetch=1,
            grid=(TILES,),
            in_specs=[whole] * 6,
            out_specs=(whole, whole, whole),
            scratch_shapes=[
                pltpu.VMEM((rows, HEAD_DIM), low),
                pltpu.VMEM((rows, HEAD_DIM), low),
                pltpu.VMEM((TILES, HEAD_DIM, TILE), low),
                pltpu.VMEM((HEAD_DIM, TILE), jnp.float32),
                pltpu.VMEM((rows, HEAD_DIM), jnp.float32),
                pltpu.VMEM((rows, HEAD_DIM), jnp.float32),
            ],
        ),
        compiler_params=pltpu.CompilerParams(vmem_limit_bytes=48 * 1024 * 1024),
        cost_estimate=pl.CostEstimate(
            flops=1024, bytes_accessed=1024, transcendentals=0
        ),
    )(order, queries, keys, values, grads, mixed_t, logs)


def mlp_kernel(second_ref, cot_ref, both_weight_ref, down_ref, *refs):
    inner_ref, both_ref, second_out, cot_out, grad_ref, acc = refs[-6:]
    at = pl.program_id(0)
    step = down_ref.shape[1]
    second = second_ref[...]

    @pl.when(at == 0)
    def _():
        second_out[0] = second
        cot_out[0] = cot_ref[...]

    both_act = jnp.dot(second, both_weight_ref[...], preferred_element_type=jnp.float32)
    inner_grad = jnp.dot(cot_ref[...], down_ref[...], preferred_element_type=jnp.float32)
    gate_act = both_act[:, :step]
    up_act = both_act[:, step:]
    sigmoid = 1.0 / (1.0 + jnp.exp(-gate_act))
    silu = gate_act * sigmoid
    inner_ref[0] = (silu * up_act).astype(low)
    gate_grad = (inner_grad * up_act * (sigmoid * (1.0 + gate_act * (1.0 - sigmoid)))).astype(low)
    both_grad = jnp.concatenate([gate_grad, (inner_grad * silu).astype(low)], axis=1)
    both_ref[0, :, pl.ds(pl.multiple_of(at * 2 * step, 2 * step), 2 * step)] = both_grad
    part = lax.dot_general(
        both_grad, both_weight_ref[...], contract_last, preferred_element_type=jnp.float32
    )
    last = pl.num_programs(0) - 1

    @pl.when(at == 0)
    def _():
        acc[...] = part

    @pl.when((at > 0) & (at < last))
    def _():
        acc[...] += part

    @pl.when(at == last)
    def _():
        grad_ref[...] = (acc[...] + part).astype(low)


def mlp_block(block, second, cot, weights, held):
    rows, width = second.shape
    hidden_width = weights.shape[1] // 3
    step = FF_STEP
    steps = hidden_width // step
    whole = pl.BlockSpec((rows, width), lambda c: (0, 0))
    kept = pl.BlockSpec((1, rows, step), lambda c: (block, 0, c))
    kept_both = pl.BlockSpec((1, rows, 2 * hidden_width), lambda c: (block, 0, 0))
    kept_rows = pl.BlockSpec((1, rows, width), lambda c: (block, 0, 0))
    rows_shape = jax.ShapeDtypeStruct((RING, rows, width), low)
    return pl.pallas_call(
        mlp_kernel,
        grid=(steps,),
        in_specs=[
            whole,
            whole,
            pl.BlockSpec((width, 2 * step), lambda c: (0, c)),
            pl.BlockSpec((width, step), lambda c: (0, 2 * steps + c)),
        ]
        + [pl.BlockSpec(memory_space=pl.ANY)] * len(held),
        out_specs=(kept, kept_both, kept_rows, kept_rows, whole),
        out_shape=(
            jax.ShapeDtypeStruct((RING, rows, hidden_width), low),
            jax.ShapeDtypeStruct((RING, rows, 2 * hidden_width), low),
            rows_shape,
            rows_shape,
            jax.ShapeDtypeStruct((rows, width), low),
        ),
        scratch_shapes=[pltpu.VMEM((rows, width), jnp.float32)],
        input_output_aliases={4 + i: i for i in range(len(held))},
        compiler_params=pltpu.CompilerParams(vmem_limit_bytes=48 * 1024 * 1024),
        cost_estimate=pl.CostEstimate(
            flops=2 * 5 * rows * width * hidden_width,
            bytes_accessed=2 * 3 * width * hidden_width,
            transcendentals=rows * hidden_width,
        ),
    )(second, cot, weights, weights, *held)


def middle_kernel(*refs):
    mixed_refs, weight_refs = refs[:RING], refs[RING : 2 * RING]
    hidden_ref, gain_ref, middle_ref, second_ref = refs[2 * RING :]
    at = pl.program_id(0)
    step = weight_refs[0].shape[0]
    columns = pl.ds(pl.multiple_of(at * step, step), step)
    total = hidden_ref[:, columns].astype(jnp.float32)
    for mixed, weight in zip(mixed_refs, weight_refs):
        rows = jnp.concatenate([mixed[head] for head in range(4)], axis=1)
        total += lax.dot_general(
            rows, weight[...], contract_last, preferred_element_type=jnp.float32
        )
    middle_ref[:, columns] = total

    @pl.when(at == pl.num_programs(0) - 1)
    def _():
        second_ref[...] = (normalize(middle_ref[...]) * gain_ref[...]).astype(low)


def middle_part(mixed_blocks, weights, hidden, gain):
    rows, width = hidden.shape
    steps = 4
    whole = pl.BlockSpec((rows, width), lambda d: (0, 0))
    return pl.pallas_call(
        middle_kernel,
        grid=(steps,),
        in_specs=[pl.BlockSpec((4, rows, HEAD_DIM), lambda d: (0, 0, 0))] * RING
        + [pl.BlockSpec((width // steps, 512), lambda d: (d, 0))] * RING
        + [whole, pl.BlockSpec((1, width), lambda d: (0, 0))],
        out_specs=(whole, whole),
        out_shape=(
            jax.ShapeDtypeStruct((rows, width), jnp.float32),
            jax.ShapeDtypeStruct((rows, width), low),
        ),
        compiler_params=pltpu.CompilerParams(vmem_limit_bytes=32 * 1024 * 1024),
        cost_estimate=pl.CostEstimate(flops=1024, bytes_accessed=1024, transcendentals=0),
    )(*mixed_blocks, *weights, hidden, gain)


def middle_back_kernel(*refs):
    parts, weight_refs = refs[:RING], refs[RING : 2 * RING]
    middle_ref, cot_ref, gain_ref, grad_ref, low_ref, gain_out, *rest = refs[2 * RING :]
    outs, accs = rest[:RING], rest[RING:]
    at = pl.program_id(0)
    step = weight_refs[0].shape[0]

    @pl.when(at == 0)
    def _():
        second_grad = sum(part[...].astype(jnp.float32) for part in parts)
        middle = middle_ref[...]
        scale = inverse_rms(middle)
        normed = middle * scale
        gain_out[...] = jnp.sum(second_grad * normed, axis=0, keepdims=True)
        scaled = second_grad * gain_ref[...]
        grad = cot_ref[...].astype(jnp.float32) + scale * (
            scaled - normed * jnp.mean(scaled * normed, axis=-1, keepdims=True)
        )
        grad_ref[...] = grad
        low_ref[...] = grad.astype(low)
        for acc in accs:
            acc[...] = jnp.zeros_like(acc)

    rows = low_ref[:, pl.ds(pl.multiple_of(at * step, step), step)]
    for weight, acc in zip(weight_refs, accs):
        acc[...] += jnp.dot(rows, weight[...], preferred_element_type=jnp.float32)

    @pl.when(at == pl.num_programs(0) - 1)
    def _():
        for out, acc in zip(outs, accs):
            for head in range(4):
                out[head] = acc[:, head * HEAD_DIM : (head + 1) * HEAD_DIM].astype(low)


def middle_back(parts, weights, middle, cot, gain):
    rows, width = middle.shape
    steps = 4
    whole = pl.BlockSpec((rows, width), lambda d: (0, 0))
    row = pl.BlockSpec((1, width), lambda d: (0, 0))
    heads = pl.BlockSpec((4, rows, HEAD_DIM), lambda d: (0, 0, 0))
    return pl.pallas_call(
        middle_back_kernel,
        grid=(steps,),
        in_specs=[whole] * RING
        + [pl.BlockSpec((width // steps, 512), lambda d: (d, 0))] * RING
        + [whole, whole, row],
        out_specs=(whole, whole, row) + (heads,) * RING,
        out_shape=(
            jax.ShapeDtypeStruct((rows, width), jnp.float32),
            jax.ShapeDtypeStruct((rows, width), low),
            jax.ShapeDtypeStruct((1, width), jnp.float32),
        )
        + (jax.ShapeDtypeStruct((4, rows, HEAD_DIM), low),) * RING,
        scratch_shapes=[pltpu.VMEM((rows, 512), jnp.float32)] * RING,
        compiler_params=pltpu.CompilerParams(vmem_limit_bytes=40 * 1024 * 1024),
        cost_estimate=pl.CostEstimate(flops=1024, bytes_accessed=1024, transcendentals=0),
    )(*parts, *weights, middle, cot, gain)


def first_kernel(
    hidden_ref, gain_ref, weight_ref, cos_ref, sin_ref, query_gain, key_gain, first_ref, pre_ref, send_ref
):
    first = (normalize(hidden_ref[0].astype(jnp.float32)) * gain_ref[...]).astype(low)
    first_ref[0] = first
    pre = jnp.dot(first, weight_ref[...], preferred_element_type=jnp.float32)
    pre_ref[0] = pre
    cosine = cos_ref[0]
    sine = sin_ref[0]

    def turned(head, gain):
        values = normalize(pre[:, head * HEAD_DIM : (head + 1) * HEAD_DIM]) * gain
        return (values * cosine + pltpu.roll(values, HEAD_DIM // 2, 1) * sine).astype(low)

    for head in range(4):
        send_ref[head, 0] = turned(head, query_gain[...])
    for head in range(2):
        send_ref[2 * head, 1] = turned(4 + head, key_gain[...])
        send_ref[2 * head + 1, 1] = pre[:, (6 + head) * HEAD_DIM : (7 + head) * HEAD_DIM].astype(low)


def first_part(hidden_all, gain, weights, cosine, sine, query_gain, key_gain):
    _, rows, width = hidden_all.shape
    row = pl.BlockSpec((1, HEAD_DIM), lambda r: (0, 0))
    turn = pl.BlockSpec((1, rows, HEAD_DIM), lambda r: (r, 0, 0))
    return pl.pallas_call(
        first_kernel,
        grid=(RING,),
        in_specs=[
            pl.BlockSpec((1, rows, width), lambda r: (r, 0, 0)),
            pl.BlockSpec((1, width), lambda r: (0, 0)),
            pl.BlockSpec((width, 1024), lambda r: (0, 0)),
            turn,
            turn,
            row,
            row,
        ],
        out_specs=(
            pl.BlockSpec((1, rows, width), lambda r: (r, 0, 0)),
            pl.BlockSpec((1, rows, 1024), lambda r: (r, 0, 0)),
            pl.BlockSpec((4, 2, rows, HEAD_DIM), lambda r: (r, 0, 0, 0)),
        ),
        out_shape=(
            jax.ShapeDtypeStruct((RING, rows, width), low),
            jax.ShapeDtypeStruct((RING, rows, 1024), jnp.float32),
            jax.ShapeDtypeStruct((BLOCKS, 2, rows, HEAD_DIM), low),
        ),
        compiler_params=pltpu.CompilerParams(vmem_limit_bytes=40 * 1024 * 1024),
        cost_estimate=pl.CostEstimate(
            flops=2 * RING * rows * width * 1024,
            bytes_accessed=20 * 1024 * 1024,
            transcendentals=0,
        ),
    )(hidden_all, gain, weights, cosine, sine, query_gain, key_gain)


def first_back_kernel(
    core_ref, back_ref, pre_ref, cos_ref, sin_ref, query_gain, key_gain, first_ref,
    grad_ref, keep_ref, give_ref, query_sum, key_sum, all_grads,
):
    at = pl.program_id(0)
    rows = grad_ref.shape[1]
    cosine = cos_ref[0]
    sine = sin_ref[0]

    @pl.when(at == 0)
    def _():
        query_sum[...] = jnp.zeros_like(query_sum)
        key_sum[...] = jnp.zeros_like(key_sum)

    def back(grads, head, gain, sums):
        columns = slice(head * HEAD_DIM, (head + 1) * HEAD_DIM)
        values = pre_ref[0, :, columns]
        grads = grads.astype(jnp.float32)
        grads = grads * cosine - pltpu.roll(grads, HEAD_DIM // 2, 1) * sine
        scale = inverse_rms(values)
        normed = values * scale
        sums[...] += jnp.sum(grads * normed, axis=0, keepdims=True)
        scaled = grads * gain
        out = scale * (scaled - normed * jnp.mean(scaled * normed, axis=-1, keepdims=True))
        grad_ref[0, :, columns] = out.astype(low)

    for head in range(4):
        back(back_ref[head, 0], head, query_gain[...], query_sum)
    for head in range(2):
        back(back_ref[2 * head, 1], 4 + head, key_gain[...], key_sum)
        grad_ref[0, :, (6 + head) * HEAD_DIM : (7 + head) * HEAD_DIM] = back_ref[2 * head + 1, 1]
    all_grads[pl.ds(pl.multiple_of(at * rows, rows), rows), :] = grad_ref[0]

    @pl.when(at == RING - 1)
    def _():
        grads = all_grads[...]
        first_core = core_ref[0] == 0
        for pair in range(8):
            inputs = first_ref[:, :, pair * 256 : (pair + 1) * 256].reshape(RING * rows, 256)
            term = lax.dot_general(
                inputs, grads, contract_first, preferred_element_type=jnp.float32
            ).astype(low)
            keep_ref[pair] = jnp.where(first_core, term[:128], term[128:])
            give_ref[pair] = jnp.where(first_core, term[128:], term[:128])


def first_back(core_at, returned, pre, cosine, sine, query_gain, key_gain, first_in):
    _, rows, width = first_in.shape
    row = pl.BlockSpec((1, HEAD_DIM), lambda r: (0, 0))
    turn = pl.BlockSpec((1, rows, HEAD_DIM), lambda r: (r, 0, 0))
    wide = pl.BlockSpec((1, rows, 1024), lambda r: (r, 0, 0))
    half = pl.BlockSpec((8, 128, 1024), lambda r: (0, 0, 0))
    return pl.pallas_call(
        first_back_kernel,
        grid=(RING,),
        in_specs=[
            pl.BlockSpec(memory_space=pltpu.SMEM),
            pl.BlockSpec((4, 2, rows, HEAD_DIM), lambda r: (r, 0, 0, 0)),
            wide,
            turn,
            turn,
            row,
            row,
            pl.BlockSpec((RING, rows, width), lambda r: (0, 0, 0)),
        ],
        out_specs=(wide, half, half, row, row),
        out_shape=(
            jax.ShapeDtypeStruct((RING, rows, 1024), low),
            jax.ShapeDtypeStruct((8, 128, 1024), low),
            jax.ShapeDtypeStruct((8, 128, 1024), low),
            jax.ShapeDtypeStruct((1, HEAD_DIM), jnp.float32),
            jax.ShapeDtypeStruct((1, HEAD_DIM), jnp.float32),
        ),
        scratch_shapes=[pltpu.VMEM((RING * rows, 1024), low)],
        compiler_params=pltpu.CompilerParams(vmem_limit_bytes=48 * 1024 * 1024),
        cost_estimate=pl.CostEstimate(flops=1024, bytes_accessed=1024, transcendentals=0),
    )(core_at[None], returned, pre, cosine, sine, query_gain, key_gain, first_in)


def last_kernel(
    core_ref, grad_ref, weight_ref, hidden_ref, mlp_ref, query_ref, key_ref,
    own_ref, left_ref, opposite_ref, right_ref, keep_ref, give_ref, gain_acc,
):
    at = pl.program_id(0)
    width = hidden_ref.shape[2]
    part = lax.dot_general(
        grad_ref[0], weight_ref[...], contract_last, preferred_element_type=jnp.float32
    )
    for r, out in enumerate((own_ref, left_ref, opposite_ref, right_ref)):

        @pl.when(at == r)
        def _(out=out):
            out[...] = part.astype(low)

    normed = normalize(hidden_ref[0].astype(jnp.float32))
    gain = jnp.sum(part * normed, axis=0, keepdims=True)

    @pl.when(at == 0)
    def _():
        gain_acc[...] = gain

    @pl.when(at > 0)
    def _():
        gain_acc[...] += gain

    @pl.when(at == RING - 1)
    def _():
        lines = [
            gain_acc[...],
            mlp_ref[...],
            jnp.concatenate([query_ref[...]] * BLOCKS, axis=1),
            jnp.concatenate([key_ref[...]] * BLOCKS, axis=1),
            jnp.zeros((HEAD_DIM - 4, width), jnp.float32),
        ]
        turned = jnp.concatenate(lines, axis=0).T.astype(low)
        first_core = core_ref[0] == 0
        for pair in range(8):
            first = turned[pair * 256 : pair * 256 + 128]
            second = turned[pair * 256 + 128 : (pair + 1) * 256]
            keep_ref[pair] = jnp.where(first_core, first, second)
            give_ref[pair] = jnp.where(first_core, second, first)


def last_part(core_at, grads, weights, hidden_all, mlp_part, query_part, key_part):
    _, rows, width = hidden_all.shape
    block = pl.BlockSpec((rows, width), lambda r: (0, 0))
    row = pl.BlockSpec((1, HEAD_DIM), lambda r: (0, 0))
    half = pl.BlockSpec((8, 128, HEAD_DIM), lambda r: (0, 0, 0))
    return pl.pallas_call(
        last_kernel,
        grid=(RING,),
        in_specs=[
            pl.BlockSpec(memory_space=pltpu.SMEM),
            pl.BlockSpec((1, rows, 1024), lambda r: (r, 0, 0)),
            pl.BlockSpec((width, 1024), lambda r: (0, 0)),
            pl.BlockSpec((1, rows, width), lambda r: (r, 0, 0)),
            pl.BlockSpec((1, width), lambda r: (0, 0)),
            row,
            row,
        ],
        out_specs=(block,) * RING + (half, half),
        out_shape=(jax.ShapeDtypeStruct((rows, width), low),) * RING
        + (jax.ShapeDtypeStruct((8, 128, HEAD_DIM), low),) * 2,
        scratch_shapes=[pltpu.VMEM((1, width), jnp.float32)],
        compiler_params=pltpu.CompilerParams(vmem_limit_bytes=40 * 1024 * 1024),
        cost_estimate=pl.CostEstimate(flops=1024, bytes_accessed=1024, transcendentals=0),
    )(core_at[None], grads, weights, hidden_all, mlp_part, query_part, key_part)


def arrange_kernel(at_ref, own_ref, other_ref, out_ref):
    y_at, x_at, core_at = at_ref[0], at_ref[1], at_ref[2]
    for dy in range(RING):
        for dx in range(2):
            first = ((y_at - dy + RING) & 3) * 4 + (x_at ^ dx) * 2
            own = pl.multiple_of((first + core_at) * 128, 128)
            other = pl.multiple_of((first + 1 - core_at) * 128, 128)
            out_ref[pl.ds(own, 128), :] = own_ref[dy, dx]
            out_ref[pl.ds(other, 128), :] = other_ref[dy, dx]


def gather_by_permutes(pair, y_at, x_at, core_at):
    own = jnp.stack([pair] + [shift(pair, "y", r) for r in range(1, RING)])
    other = shift(own, "core", 1, 2)
    whole = pl.BlockSpec(memory_space=pltpu.VMEM)
    return pl.pallas_call(
        arrange_kernel,
        in_specs=[pl.BlockSpec(memory_space=pltpu.SMEM), whole, whole],
        out_specs=whole,
        out_shape=jax.ShapeDtypeStruct((BLOCKS * 128, pair.shape[2]), pair.dtype),
        compiler_params=pltpu.CompilerParams(vmem_limit_bytes=16 * 1024 * 1024),
        cost_estimate=pl.CostEstimate(flops=1024, bytes_accessed=1024, transcendentals=0),
    )(jnp.stack([y_at, x_at, core_at]), own, other)


def to_heads(send):
    return lax.all_to_all(send, GROUP_AXES, 0, 0, tiled=True)


def after(value, *others):
    return lax.optimization_barrier((value, others))[0]


def ring_blocks(values):
    half = values.shape[0] // 2
    left = shift(values, "z", 1)
    right = shift(values, "z", 3)
    opposite = jnp.concatenate(
        [shift(left[:half], "z", 1), shift(right[half:], "z", 3)], axis=0
    )
    return [values, left, opposite, right]


def together(*values):
    return lax.optimization_barrier(values)


def place(z_at, blocks, widths, chunk=None, summed=False):
    rows = blocks[0].shape[0]
    whole = pl.BlockSpec(memory_space=pltpu.VMEM)
    shapes = [RING * part for part in widths] + [HEAD_DIM] * summed

    def kernel(z_ref, *refs):
        ins, outs = refs[:RING], refs[RING:]
        for r in range(RING):
            slot = (z_ref[0] - r + RING) & 3
            start = 0
            for turn in range(widths[0] // chunk if chunk else 1):
                for out, part in zip(outs, widths):
                    size = chunk or part
                    at = pl.multiple_of(slot * part + turn * size, 128)
                    out[:, pl.ds(at, size)] = ins[r][:, start : start + size].astype(jnp.float32)
                    start += size
            if summed:
                columns = ins[r][:, start : start + HEAD_DIM].astype(jnp.float32)
                outs[-1][...] = columns if r == 0 else outs[-1][...] + columns

    return pl.pallas_call(
        kernel,
        in_specs=[pl.BlockSpec(memory_space=pltpu.SMEM)] + [whole] * RING,
        out_specs=tuple(whole for _ in shapes),
        out_shape=tuple(jax.ShapeDtypeStruct((rows, part), jnp.float32) for part in shapes),
        compiler_params=pltpu.CompilerParams(vmem_limit_bytes=24 * 1024 * 1024),
        cost_estimate=pl.CostEstimate(flops=1024, bytes_accessed=1024, transcendentals=0),
    )(z_at[None], *blocks)


def send_back(block, r):
    return shift(block, "z", -r)


def local(
    hidden_in,
    cotangent,
    segment_ids,
    positions,
    attn_gain,
    query_gain,
    key_gain,
    query_weight,
    key_weight,
    value_weight,
    out_weight,
    mlp_gain,
    gate_weight,
    up_weight,
    down_weight,
):
    f32 = jnp.float32
    rows, width = hidden_in.shape
    ring_rows = RING * rows
    z_at = lax.axis_index("z")
    y_at = lax.axis_index("y")
    x_at = lax.axis_index("x_hi")
    core_at = lax.axis_index("core")
    my_index = (y_at * 2 + x_at) * 2 + core_at

    def columns(weight):
        part = weight.shape[1] // RING
        return lax.dynamic_slice_in_dim(weight, z_at * part, part, 1).astype(low)

    def gather(block):
        return lax.all_gather(block, GROUP_AXES, axis=0, tiled=True)

    own_places = lax.dynamic_slice_in_dim(positions, my_index * rows, rows)
    firsts = positions.reshape(BLOCKS, BLOCK)[:, 0]
    segments = segment_ids.reshape(BLOCKS, BLOCK)[:, 0]
    logical = firsts // BLOCK + jnp.maximum(segments - 1, 0) * 2
    numbers = jnp.arange(BLOCKS, dtype=jnp.int32)
    order = jnp.sum(jnp.where(logical[:, None] == numbers[None, :], numbers[:, None], 0), axis=0)
    notes = gather_z(jnp.concatenate([own_places, order, jnp.zeros((112,), jnp.int32)])[None])
    places = notes[:, :rows]
    order = lax.dynamic_index_in_dim(notes, y_at, 0, keepdims=False)[rows : rows + BLOCKS]

    gains = jnp.pad(
        jnp.stack([attn_gain, mlp_gain], axis=1).astype(low), ((0, 0), (0, HEAD_DIM - 2))
    )
    first_weights = gather(
        jnp.concatenate(
            [columns(query_weight), columns(key_weight), columns(value_weight), gains], axis=1
        )
    )
    attn_scale = first_weights[:, 1024].astype(f32)[None]
    mlp_scale = first_weights[:, 1025].astype(f32)[None]
    out_columns = columns(out_weight)
    out_come = shift(out_columns, "x_hi", 1, 2)
    gate_columns, up_columns, down_columns, out_come = together(
        gate_weight, up_weight, down_weight, out_come
    )
    gate_columns, up_columns = columns(gate_columns), columns(up_columns)
    mlp_columns = []
    for start in range(0, gate_columns.shape[1], FF_STEP):
        mlp_columns.append(gate_columns[:, start : start + FF_STEP])
        mlp_columns.append(up_columns[:, start : start + FF_STEP])
    mlp_weights = gather(jnp.concatenate(mlp_columns + [columns(down_columns)], axis=1))
    down_full = mlp_weights[:, 3072:]
    out_slice = gather_by_permutes(jnp.stack([out_columns, out_come]), y_at, x_at, core_at)

    hidden_blocks = ring_blocks(hidden_in)
    out_slice = after(out_slice, *hidden_blocks)
    out_left = shift(out_slice, "z", 1)
    out_right = shift(out_slice, "z", 3)
    frequency = rope_base ** (-2.0 * jnp.arange(HEAD_DIM // 2, dtype=f32) / HEAD_DIM)
    angles = places.astype(f32)[:, :, None] * frequency[None, None, :]
    cosine = jnp.cos(angles)
    sine = jnp.sin(angles)
    cosine = jnp.concatenate([cosine, cosine], axis=-1)
    sine = jnp.concatenate([-sine, sine], axis=-1)
    query_row = query_gain[None]
    key_row = key_gain[None]

    hidden_all = jnp.stack(hidden_blocks)
    first_in, qkv_pre, send = first_part(
        hidden_all, attn_scale, first_weights, cosine, sine, query_row, key_row
    )
    arrived, out_left, out_right, cot_own = together(
        to_heads(send), out_left, out_right, cotangent
    )
    out_top = shift(out_left[: width // 2], "z", 1)
    out_bottom = shift(out_right[width // 2 :], "z", 3)
    cot_left = shift(cot_own, "z", 1)
    cot_right = shift(cot_own, "z", 3)
    head_queries = arrived[:, 0]
    own_pair = arrived[:, 1]
    other_pair = shift(own_pair, "core", 1, 2)
    head_keys = jnp.where(core_at == 0, own_pair, other_pair)
    head_values = jnp.where(core_at == 0, other_pair, own_pair)
    head_mixed, head_mixed_t, head_logs = attention_forward(
        order, head_queries, head_keys, head_values
    )

    def from_heads(values):
        return values.reshape(RING, 4, rows, HEAD_DIM).transpose(0, 2, 1, 3).reshape(ring_rows, 512)

    mixed_arrived, out_top, out_bottom, cot_left, cot_right = together(
        to_heads(head_mixed), out_top, out_bottom, cot_left, cot_right
    )
    half = rows // 2
    cot_top = shift(cot_left[:half], "z", 1)
    cot_bottom = shift(cot_right[half:], "z", 3)
    mixed = from_heads(mixed_arrived)
    mixed_blocks = [mixed_arrived[:4]] + [
        shift(mixed_arrived[4 * (RING - j) : 4 * (RING - j) + 4], "z", j) for j in range(1, RING)
    ]
    out_opposite = jnp.concatenate([out_top, out_bottom], axis=0)
    out_weights = [out_slice, out_left, out_opposite, out_right]
    mixed_blocks, out_weights, cot_top, cot_bottom = together(
        mixed_blocks, out_weights, cot_top, cot_bottom
    )
    middle, second_in = middle_part(mixed_blocks, out_weights, hidden_in, mlp_scale)
    hidden = hidden_in.astype(f32)
    left = shift(second_in, "z", 1)
    right = shift(second_in, "z", 3)
    *held, own_part = mlp_block(0, second_in, cot_own, mlp_weights, ())
    held, own_part, left, right = together(held, own_part, left, right)
    top = shift(left[:half], "z", 1)
    bottom = shift(right[half:], "z", 3)
    *held, left_part = mlp_block(1, left, cot_left, mlp_weights, held)
    left_back = send_back(left_part, 1)
    *held, right_part = mlp_block(3, right, cot_right, mlp_weights, held)
    right_back = send_back(right_part, 3)
    held, top, bottom = together(held, top, bottom)
    opposite = jnp.concatenate([top, bottom], axis=0)
    cot_opposite = jnp.concatenate([cot_top, cot_bottom], axis=0)
    *held, opposite_part = mlp_block(2, opposite, cot_opposite, mlp_weights, held)
    opposite_back = send_back(opposite_part, 2)
    inner = held[0].reshape(ring_rows, 1536)
    both_grad = held[1].reshape(ring_rows, 3072)
    second_all = held[2].reshape(ring_rows, width)
    cot_all = held[3].reshape(ring_rows, width)

    def weight_grad(left, right):
        return lax.dot_general(left, right, contract_first, preferred_element_type=f32).astype(low)

    def pair_start(term):
        term = term.reshape(8, 2, 128, term.shape[1])
        keep = lax.dynamic_index_in_dim(term, core_at, 1, keepdims=False)
        give = lax.dynamic_index_in_dim(term, 1 - core_at, 1, keepdims=False)
        return keep, shift(give, "core", 1, 2)

    def pair_sum(keep, come):
        return (keep.astype(f32) + come.astype(f32)).astype(low)

    def to_owners(pair):
        terms = lax.all_to_all(pair, ("y", "x_hi"), 0, 0, tiled=True)
        return jnp.sum(terms.astype(f32), axis=0).astype(low)

    def over_x(share):
        return share, shift(share, "x_lo", 1, 2)

    def over_z(pair):
        share = pair_sum(*pair)
        return [share] + [shift(share, "z", r) for r in range(1, RING)]

    both_term = weight_grad(second_all, both_grad)
    mlp_out = lax.dot_general(
        inner, down_full, contract_last, preferred_element_type=f32
    ).reshape(RING, rows, width)
    mlp_own = mlp_out[0].astype(low)
    mlp_rest = mlp_out[1:].astype(low)
    left_back, right_back, opposite_back, both_term, mlp_own, mlp_rest, inner = together(
        left_back, right_back, opposite_back, both_term, mlp_own, mlp_rest, inner
    )
    both_share = lax.psum_scatter(both_term, GROUP_AXES, scatter_dimension=0, tiled=True)

    middle_grad, own_low, mlp_gain_part, *grad_blocks = middle_back(
        (own_part, left_back, right_back, opposite_back),
        out_weights,
        middle,
        cotangent,
        mlp_scale,
    )
    grad_blocks = [grad_blocks[0]] + [shift(grad_blocks[RING - r], "z", r) for r in range(1, RING)]
    down_term = weight_grad(cot_all, inner)
    grad_blocks, down_term, own_low, mlp_rest = together(grad_blocks, down_term, own_low, mlp_rest)
    down_pair = pair_start(down_term)
    head_grads = to_heads(jnp.concatenate(grad_blocks, axis=0))
    down_sum = pair_sum(*down_pair)
    low_left = shift(own_low, "z", 1)
    low_right = shift(own_low, "z", 3)
    head_grads, down_sum, low_left, low_right, own_low, mlp_rest = together(
        head_grads, down_sum, low_left, low_right, own_low, mlp_rest
    )
    low_top = shift(low_left[:half], "z", 1)
    low_bottom = shift(low_right[half:], "z", 3)
    down_share = to_owners(down_sum)

    query_grad, key_grad, value_grad = attention_backward(
        order, head_queries, head_keys, head_values, head_grads, head_mixed_t, head_logs
    )
    keep = jnp.where(core_at == 0, key_grad, value_grad)
    give = jnp.where(core_at == 0, value_grad, key_grad)
    pair_grad = (keep.astype(f32) + shift(give, "core", 1, 2).astype(f32)).astype(low)
    grads_send, low_top, low_bottom, down_share, mlp_rest = together(
        jnp.stack([query_grad, pair_grad], axis=1), low_top, low_bottom, down_share, mlp_rest
    )
    down_pair = over_x(down_share)
    returned = to_heads(grads_send)
    middle_low = jnp.concatenate(
        [own_low, low_left, low_top, low_bottom, low_right], axis=0
    )
    out_sum = pair_sum(*pair_start(weight_grad(middle_low, mixed)))
    mlp_top = shift(mlp_rest[1][:half], "z", 3)
    mlp_bottom = shift(mlp_rest[1][half:], "z", 1)
    returned, out_sum, mlp_top, mlp_bottom = together(returned, out_sum, mlp_top, mlp_bottom)
    out_share = to_owners(out_sum)
    mlp_left = jnp.concatenate(
        [(mlp_rest[0][:half].astype(f32) + mlp_top.astype(f32)).astype(low), mlp_rest[0][half:]],
        axis=0,
    )
    mlp_right = jnp.concatenate(
        [mlp_rest[2][:half], (mlp_rest[2][half:].astype(f32) + mlp_bottom.astype(f32)).astype(low)],
        axis=0,
    )
    mlp_left = shift(mlp_left, "z", 3)
    mlp_right = shift(mlp_right, "z", 1)
    qkv_grad, qkv_keep, qkv_give, query_gain_part, key_gain_part = first_back(
        core_at, returned, qkv_pre, cosine, sine, query_row, key_row, first_in
    )
    qkv_come = shift(qkv_give, "core", 1, 2)
    *first_parts, gains_keep, gains_give = last_part(
        core_at,
        qkv_grad,
        first_weights,
        hidden_all,
        mlp_gain_part,
        query_gain_part,
        key_gain_part,
    )
    first_parts, gains_give, qkv_come, out_share, mlp_left, mlp_right, down_pair, both_share = (
        together(
            first_parts, gains_give, qkv_come, out_share, mlp_left, mlp_right, down_pair, both_share
        )
    )
    gains_come = shift(gains_give, "core", 1, 2)
    first_blocks = [first_parts[0]] + [send_back(first_parts[r], r) for r in range(1, RING)]
    qkv_share = to_owners(
        jnp.concatenate([pair_sum(qkv_keep, qkv_come), pair_sum(gains_keep, gains_come)], axis=2)
    )
    out_pair = over_x(out_share)
    both_pair = over_x(both_share)
    down_blocks = over_z(down_pair)
    qkv_share, out_pair, both_pair, down_blocks = together(
        qkv_share, out_pair, both_pair, down_blocks
    )
    both_blocks = over_z(both_pair)
    qkv_pair = over_x(qkv_share)
    output = (
        middle + mlp_own.astype(f32) + mlp_left.astype(f32) + mlp_right.astype(f32)
    ).astype(low)
    first_grad = sum(block.astype(f32) for block in first_blocks)
    hidden_rms = inverse_rms(hidden)
    own_norm = hidden * hidden_rms
    scaled_first = first_grad * attn_scale
    hidden_grad = (
        middle_grad
        + hidden_rms
        * (scaled_first - own_norm * jnp.mean(scaled_first * own_norm, axis=-1, keepdims=True))
    ).astype(low)

    (down_grad_out,) = place(z_at, down_blocks, (1536,))
    gate_grad_out, up_grad_out = place(z_at, both_blocks, (1536, 1536), chunk=FF_STEP)
    (out_grad_out,) = place(z_at, over_z(out_pair), (512,))
    query_grad_out, key_grad_out, value_grad_out, gain_sum = place(
        z_at, over_z(qkv_pair), (512, 256, 256), summed=True
    )
    gain_sum = gain_sum[:, :4].T

    return (
        output,
        hidden_grad,
        gain_sum[0],
        gain_sum[2],
        gain_sum[3],
        query_grad_out,
        key_grad_out,
        value_grad_out,
        out_grad_out,
        gain_sum[1],
        gate_grad_out,
        up_grad_out,
        down_grad_out,
    )


def solution(mesh):
    fine = Mesh(mesh.devices.reshape(2, 4, 4, 2, 2), ALL_AXES)
    rep = ("x_lo", "z")
    row = P(ALL_AXES, None)
    part = P(GROUP_AXES)
    weight = P(GROUP_AXES, None)
    in_specs = (
        row,
        row,
        P(rep),
        P(rep),
        part,
        P(),
        P(),
        weight,
        weight,
        weight,
        weight,
        part,
        weight,
        weight,
        weight,
    )
    out_specs = (
        row,
        row,
        part,
        P(),
        P(),
        weight,
        weight,
        weight,
        weight,
        part,
        weight,
        weight,
        weight,
    )
    return jax.shard_map(local, mesh=fine, in_specs=in_specs, out_specs=out_specs, check_vma=False)
```

```python
import functools

import jax
import jax.numpy as jnp
from jax import lax
from jax.experimental import pallas as pl
from jax.experimental.pallas import tpu as pltpu
from jax.sharding import Mesh
from jax.sharding import PartitionSpec as P

HEAD_DIM = 128
RING = 4
BLOCK = 256
BLOCKS = 16
TILE = 512
TILES = 8
PROMPT_TILES = 6
FF_STEP = 512
VMEM_LIMIT = 60 * 1024 * 1024

norm_eps = 1e-06
rope_base = 1000000.0
score_scale = HEAD_DIM ** (-0.5)
score_scale_log2 = score_scale * 1.4426950408889634
contract_first = (((0,), (0,)), ((), ()))
contract_last = (((1,), (1,)), ((), ()))
GROUP_AXES = ("y", "x_hi", "core")
ALL_AXES = ("x_lo", "z", "y", "x_hi", "core")
low = jnp.bfloat16


def inverse_rms(values):
    return lax.rsqrt(jnp.mean(values * values, axis=-1, keepdims=True) + norm_eps)


def normalize(values):
    return values * inverse_rms(values)


def shift(values, axis, by, size=RING):
    return lax.ppermute(values, axis, [(i, (i + by) % size) for i in range(size)])


def gather_z(values):
    return jnp.concatenate(
        [values, shift(values, "z", 1), shift(values, "z", 2), shift(values, "z", 3)], axis=0
    )


def tile_rows(ref, order, tile, *slot):
    return jnp.concatenate([ref[order[2 * tile + half], *slot] for half in range(2)], axis=0)


def forward_kernel(
    order, core, own_ref, other_ref, mixed_ref, mixed_t_ref, log_ref, k_all, v_t, acc, total
):
    tile = pl.program_id(0)

    def take(keys_of, values_of):
        for at in range(BLOCKS):
            k_all[at * BLOCK : (at + 1) * BLOCK, :] = keys_of(order[at])
            v_t[at // 2, :, (at % 2) * BLOCK : (at % 2 + 1) * BLOCK] = (
                values_of(order[at]).astype(jnp.float32).T.astype(low)
            )

    @pl.when((tile == 0) & (core[0] == 0))
    def _():
        take(lambda at: own_ref[at, 1], lambda at: other_ref[at])

    @pl.when((tile == 0) & (core[0] == 1))
    def _():
        take(lambda at: other_ref[at], lambda at: own_ref[at, 1])

    queries = tile_rows(own_ref, order, tile, 0)
    acc[...] = jnp.zeros_like(acc)
    total[...] = jnp.zeros_like(total)

    def chunk(at, masked):
        keys = k_all[pl.ds(pl.multiple_of(at * TILE, TILE), TILE), :]
        scores = lax.dot_general(keys, queries, contract_last, preferred_element_type=jnp.float32)
        weights = jnp.exp2(scores * score_scale_log2)
        if masked:
            key_row = lax.broadcasted_iota(jnp.int32, (TILE, TILE), 0)
            query_row = lax.broadcasted_iota(jnp.int32, (TILE, TILE), 1)
            weights = jnp.where(key_row <= query_row, weights, 0.0)
        total[...] += jnp.sum(weights, axis=0, keepdims=True)
        acc[...] += jnp.dot(v_t[at], weights.astype(low), preferred_element_type=jnp.float32)

    @pl.loop(0, jnp.minimum(tile, PROMPT_TILES))
    def _(at):
        chunk(at, False)

    chunk(tile, True)
    mixed_t = acc[...] / total[...]
    mixed_t_ref[tile] = mixed_t
    log_ref[tile] = jnp.log2(total[...])
    mixed = mixed_t.T.astype(low)
    mixed_ref[order[2 * tile]] = mixed[:BLOCK]
    mixed_ref[order[2 * tile + 1]] = mixed[BLOCK:]


def attention_forward(order, core_at, arrived, other):
    whole = pl.BlockSpec(memory_space=pltpu.VMEM)
    return pl.pallas_call(
        forward_kernel,
        out_shape=(
            jax.ShapeDtypeStruct((BLOCKS, BLOCK, HEAD_DIM), low),
            jax.ShapeDtypeStruct((TILES, HEAD_DIM, TILE), jnp.float32),
            jax.ShapeDtypeStruct((TILES, 1, TILE), jnp.float32),
        ),
        grid_spec=pltpu.PrefetchScalarGridSpec(
            num_scalar_prefetch=2,
            grid=(TILES,),
            in_specs=[whole] * 2,
            out_specs=(whole, whole, whole),
            scratch_shapes=[
                pltpu.VMEM((BLOCKS * BLOCK, HEAD_DIM), low),
                pltpu.VMEM((TILES, HEAD_DIM, TILE), low),
                pltpu.VMEM((HEAD_DIM, TILE), jnp.float32),
                pltpu.VMEM((1, TILE), jnp.float32),
            ],
        ),
        compiler_params=pltpu.CompilerParams(vmem_limit_bytes=VMEM_LIMIT),
        cost_estimate=pl.CostEstimate(
            flops=1024, bytes_accessed=1024, transcendentals=0
        ),
    )(order, core_at[None], arrived, other)


def backward_kernel(
    order, core, own_ref, other_ref, g_ref, mixed_t_ref, log_ref, q_out, keep_out, give_out,
    k_all, v_all, k_t, q_acc, k_acc, v_acc,
):
    tile = pl.program_id(0)

    def take(keys_of, values_of):
        for at in range(BLOCKS):
            rows = slice(at * BLOCK, (at + 1) * BLOCK)
            keys = keys_of(order[at])
            k_all[rows, :] = keys
            v_all[rows, :] = values_of(order[at])
            k_t[at // 2, :, (at % 2) * BLOCK : (at % 2 + 1) * BLOCK] = (
                keys.astype(jnp.float32).T.astype(low)
            )

    @pl.when((tile == 0) & (core[0] == 0))
    def _():
        take(lambda at: own_ref[at, 1], lambda at: other_ref[at])

    @pl.when((tile == 0) & (core[0] == 1))
    def _():
        take(lambda at: other_ref[at], lambda at: own_ref[at, 1])

    @pl.when(tile == 0)
    def _():
        k_acc[...] = jnp.zeros_like(k_acc)
        v_acc[...] = jnp.zeros_like(v_acc)

    queries = tile_rows(own_ref, order, tile, 0)
    grads = tile_rows(g_ref, order, tile)
    grads_t = grads.astype(jnp.float32).T
    shared = jnp.sum(grads_t * mixed_t_ref[tile], axis=0, keepdims=True)
    logs = log_ref[tile]
    q_acc[...] = jnp.zeros_like(q_acc)

    def chunk(at, masked):
        rows = pl.ds(pl.multiple_of(at * TILE, TILE), TILE)
        scores = lax.dot_general(
            k_all[rows, :], queries, contract_last, preferred_element_type=jnp.float32
        )
        probs = jnp.exp2(scores * score_scale_log2 - logs)
        if masked:
            key_row = lax.broadcasted_iota(jnp.int32, (TILE, TILE), 0)
            query_row = lax.broadcasted_iota(jnp.int32, (TILE, TILE), 1)
            probs = jnp.where(key_row <= query_row, probs, 0.0)
        prob_grads = lax.dot_general(
            v_all[rows, :], grads, contract_last, preferred_element_type=jnp.float32
        )
        score_grads = (probs * (prob_grads - shared)).astype(low)
        v_acc[rows, :] += jnp.dot(probs.astype(low), grads, preferred_element_type=jnp.float32)
        k_acc[rows, :] += jnp.dot(score_grads, queries, preferred_element_type=jnp.float32)
        q_acc[...] += jnp.dot(k_t[at], score_grads, preferred_element_type=jnp.float32)

    @pl.loop(0, jnp.minimum(tile, PROMPT_TILES))
    def _(at):
        chunk(at, False)

    chunk(tile, True)
    query_grad = (q_acc[...] * score_scale).T.astype(low)
    q_out[order[2 * tile], 0] = query_grad[:BLOCK]
    q_out[order[2 * tile + 1], 0] = query_grad[BLOCK:]

    def give(keep_acc, keep_scale, give_acc, give_scale):
        for at in range(BLOCKS):
            rows = slice(at * BLOCK, (at + 1) * BLOCK)
            keep_out[order[at]] = (keep_acc[rows, :] * keep_scale).astype(low)
            give_out[order[at]] = (give_acc[rows, :] * give_scale).astype(low)

    @pl.when((tile == TILES - 1) & (core[0] == 0))
    def _():
        give(k_acc, score_scale, v_acc, 1.0)

    @pl.when((tile == TILES - 1) & (core[0] == 1))
    def _():
        give(v_acc, 1.0, k_acc, score_scale)


def attention_backward(order, core_at, arrived, other, grads, mixed_t, logs):
    whole = pl.BlockSpec(memory_space=pltpu.VMEM)
    rows = BLOCKS * BLOCK
    return pl.pallas_call(
        backward_kernel,
        out_shape=(jax.ShapeDtypeStruct((BLOCKS, 2, BLOCK, HEAD_DIM), low),)
        + (jax.ShapeDtypeStruct((BLOCKS, BLOCK, HEAD_DIM), low),) * 2,
        grid_spec=pltpu.PrefetchScalarGridSpec(
            num_scalar_prefetch=2,
            grid=(TILES,),
            in_specs=[whole] * 5,
            out_specs=(whole, whole, whole),
            scratch_shapes=[
                pltpu.VMEM((rows, HEAD_DIM), low),
                pltpu.VMEM((rows, HEAD_DIM), low),
                pltpu.VMEM((TILES, HEAD_DIM, TILE), low),
                pltpu.VMEM((HEAD_DIM, TILE), jnp.float32),
                pltpu.VMEM((rows, HEAD_DIM), jnp.float32),
                pltpu.VMEM((rows, HEAD_DIM), jnp.float32),
            ],
        ),
        compiler_params=pltpu.CompilerParams(vmem_limit_bytes=VMEM_LIMIT),
        cost_estimate=pl.CostEstimate(
            flops=1024, bytes_accessed=1024, transcendentals=0
        ),
    )(order, core_at[None], arrived, other, grads, mixed_t, logs)


def mlp_kernel(parts, *refs):
    second_refs, cot_refs = refs[:parts], refs[parts : 2 * parts]
    both_weight_ref, down_ref = refs[2 * parts : 2 * parts + 2]
    count = refs[-1].shape[0] // BLOCK
    inner_ref, both_ref, second_out, cot_out = refs[-5 - count : -1 - count]
    grad_refs, acc = refs[-1 - count : -1], refs[-1]
    at = pl.program_id(0)
    step = down_ref.shape[1]
    rows, width = acc.shape

    @pl.when(at == 0)
    def _():
        for ins, out in ((second_refs, second_out), (cot_refs, cot_out)):
            start = 0
            for part in ins:
                size = part.shape[0]
                out[start // BLOCK, start % BLOCK : start % BLOCK + size, :] = part[...]
                start += size

    second = second_out[...].reshape(rows, width)
    both_act = jnp.dot(second, both_weight_ref[...], preferred_element_type=jnp.float32)
    inner_grad = jnp.dot(
        cot_out[...].reshape(rows, width), down_ref[...], preferred_element_type=jnp.float32
    )
    gate_act = both_act[:, :step]
    up_act = both_act[:, step:]
    sigmoid = 1.0 / (1.0 + jnp.exp(-gate_act))
    silu = gate_act * sigmoid
    inner_ref[...] = (silu * up_act).astype(low).reshape(inner_ref.shape)
    gate_grad = (inner_grad * up_act * (sigmoid * (1.0 + gate_act * (1.0 - sigmoid)))).astype(low)
    both_grad = jnp.concatenate([gate_grad, (inner_grad * silu).astype(low)], axis=1)
    both_ref[:, :, pl.ds(pl.multiple_of(at * 2 * step, 2 * step), 2 * step)] = both_grad.reshape(
        count, BLOCK, 2 * step
    )
    part = lax.dot_general(
        both_grad, both_weight_ref[...], contract_last, preferred_element_type=jnp.float32
    )
    last = pl.num_programs(0) - 1

    @pl.when(at == 0)
    def _():
        acc[...] = part

    @pl.when((at > 0) & (at < last))
    def _():
        acc[...] += part

    @pl.when(at == last)
    def _():
        total = (acc[...] + part).astype(low)
        for block, grad in enumerate(grad_refs):
            grad[...] = total[block * BLOCK : (block + 1) * BLOCK]


def mlp_blocks(place_at, seconds, cots, weights, held):
    rows = sum(second.shape[0] for second in seconds)
    width = seconds[0].shape[1]
    count = rows // BLOCK
    hidden_width = weights.shape[1] // 3
    step = FF_STEP
    steps = hidden_width // step
    ins = [
        pl.BlockSpec(value.shape, lambda c: (0, 0), pipeline_mode=pl.Buffered(1))
        for value in (*seconds, *cots)
    ]
    kept = pl.BlockSpec((count, BLOCK, step), lambda c: (place_at, 0, c))
    kept_both = pl.BlockSpec((count, BLOCK, 2 * hidden_width), lambda c: (place_at, 0, 0))
    kept_rows = pl.BlockSpec((count, BLOCK, width), lambda c: (place_at, 0, 0))
    rows_shape = jax.ShapeDtypeStruct((RING, BLOCK, width), low)
    return pl.pallas_call(
        functools.partial(mlp_kernel, len(seconds)),
        grid=(steps,),
        in_specs=ins
        + [
            pl.BlockSpec((width, 2 * step), lambda c: (0, c)),
            pl.BlockSpec((width, step), lambda c: (0, 2 * steps + c)),
        ]
        + [pl.BlockSpec(memory_space=pl.ANY)] * len(held),
        out_specs=(kept, kept_both, kept_rows, kept_rows)
        + (pl.BlockSpec((BLOCK, width), lambda c: (0, 0)),) * count,
        out_shape=(
            jax.ShapeDtypeStruct((RING, BLOCK, hidden_width), low),
            jax.ShapeDtypeStruct((RING, BLOCK, 2 * hidden_width), low),
            rows_shape,
            rows_shape,
        )
        + (jax.ShapeDtypeStruct((BLOCK, width), low),) * count,
        scratch_shapes=[pltpu.VMEM((rows, width), jnp.float32)],
        input_output_aliases={len(ins) + 2 + i: i for i in range(len(held))},
        compiler_params=pltpu.CompilerParams(vmem_limit_bytes=VMEM_LIMIT),
        cost_estimate=pl.CostEstimate(
            flops=2 * 5 * rows * width * hidden_width,
            bytes_accessed=2 * 3 * width * hidden_width,
            transcendentals=rows * hidden_width,
        ),
    )(*seconds, *cots, weights, weights, *held)


def mlp_out_kernel(inner_ref, weight_ref, *outs):
    inner = inner_ref[...].reshape(RING * BLOCK, inner_ref.shape[2])
    part = lax.dot_general(
        inner, weight_ref[...], contract_last, preferred_element_type=jnp.float32
    ).astype(low)
    for block, out in enumerate(outs):
        out[...] = part[block * BLOCK : (block + 1) * BLOCK]


def mlp_out_part(inner, weights):
    _, rows, hidden_width = inner.shape
    width = weights.shape[0]
    steps = 4
    return pl.pallas_call(
        mlp_out_kernel,
        grid=(steps,),
        in_specs=[
            pl.BlockSpec(inner.shape, lambda d: (0, 0, 0)),
            pl.BlockSpec((width // steps, hidden_width), lambda d: (d, 2)),
        ],
        out_specs=(pl.BlockSpec((rows, width // steps), lambda d: (0, d)),) * RING,
        out_shape=(jax.ShapeDtypeStruct((rows, width), low),) * RING,
        compiler_params=pltpu.CompilerParams(vmem_limit_bytes=VMEM_LIMIT),
        cost_estimate=pl.CostEstimate(flops=1024, bytes_accessed=1024, transcendentals=0),
    )(inner, weights)


def pair_grad(core_at, lefts, right, by_heads=False):
    width = lefts[0].shape[-1]
    outs = 512 if by_heads else right.shape[2]
    rows = RING * BLOCK

    def kernel(core_ref, *refs):
        left_refs = refs[: len(lefts)]
        right_ref, keep_ref, give_ref = refs[len(lefts) : len(lefts) + 3]
        if by_heads:
            all_ref = refs[-1]

            @pl.when(pl.program_id(0) == 0)
            def _():
                for r in range(RING):
                    for head in range(4):
                        all_ref[
                            r * BLOCK : (r + 1) * BLOCK, head * HEAD_DIM : (head + 1) * HEAD_DIM
                        ] = right_ref[4 * r + head]

            values = all_ref[...]
        else:
            values = right_ref[...].reshape(rows, outs)
        inputs = [ref[...].reshape(-1, 256) for ref in left_refs]
        inputs = inputs[0] if len(inputs) == 1 else jnp.concatenate(inputs, axis=0)
        term = lax.dot_general(
            inputs, values, contract_first, preferred_element_type=jnp.float32
        ).astype(low)
        first_core = core_ref[0] == 0
        keep_ref[0] = jnp.where(first_core, term[:128], term[128:])
        give_ref[0] = jnp.where(first_core, term[128:], term[:128])

    def columns(value):
        lead = value.shape[:-1]
        return pl.BlockSpec((*lead, 256), lambda i: (0,) * len(lead) + (i,))

    half = pl.BlockSpec((1, 128, outs), lambda i: (i, 0, 0))
    return pl.pallas_call(
        kernel,
        grid=(width // 256,),
        in_specs=[pl.BlockSpec(memory_space=pltpu.SMEM)]
        + [columns(value) for value in lefts]
        + [pl.BlockSpec(right.shape, lambda i: (0, 0, 0))],
        out_specs=(half, half),
        out_shape=(jax.ShapeDtypeStruct((width // 256, 128, outs), low),) * 2,
        scratch_shapes=[pltpu.VMEM((rows, 512), low)] * by_heads,
        compiler_params=pltpu.CompilerParams(vmem_limit_bytes=VMEM_LIMIT),
        cost_estimate=pl.CostEstimate(flops=1024, bytes_accessed=1024, transcendentals=0),
    )(core_at[None], *lefts, right)


def middle_kernel(*refs):
    mixed_refs, weight_refs = refs[:RING], refs[RING : 2 * RING]
    hidden_ref, gain_ref, middle_ref, second_ref = refs[2 * RING :]
    at = pl.program_id(0)
    step = weight_refs[0].shape[0]
    columns = pl.ds(pl.multiple_of(at * step, step), step)
    total = hidden_ref[:, columns].astype(jnp.float32)
    for mixed, weight in zip(mixed_refs, weight_refs):
        rows = jnp.concatenate([mixed[head] for head in range(4)], axis=1)
        total += lax.dot_general(
            rows, weight[...], contract_last, preferred_element_type=jnp.float32
        )
    middle_ref[:, columns] = total

    @pl.when(at == pl.num_programs(0) - 1)
    def _():
        second_ref[...] = (normalize(middle_ref[...]) * gain_ref[...]).astype(low)


def middle_part(mixed_blocks, weights, hidden, gain):
    rows, width = hidden.shape
    steps = 4
    whole = pl.BlockSpec((rows, width), lambda d: (0, 0))
    return pl.pallas_call(
        middle_kernel,
        grid=(steps,),
        in_specs=[pl.BlockSpec((4, rows, HEAD_DIM), lambda d: (0, 0, 0))] * RING
        + [pl.BlockSpec((width // steps, 512), lambda d: (d, 0))] * RING
        + [whole, pl.BlockSpec((1, width), lambda d: (0, 0))],
        out_specs=(whole, whole),
        out_shape=(
            jax.ShapeDtypeStruct((rows, width), jnp.float32),
            jax.ShapeDtypeStruct((rows, width), low),
        ),
        compiler_params=pltpu.CompilerParams(vmem_limit_bytes=VMEM_LIMIT),
        cost_estimate=pl.CostEstimate(flops=1024, bytes_accessed=1024, transcendentals=0),
    )(*mixed_blocks, *weights, hidden, gain)


def middle_back_kernel(*refs):
    parts, weight_refs = refs[:RING], refs[RING : 2 * RING]
    middle_ref, cot_ref, gain_ref, grad_ref, low_ref, gain_out, *rest = refs[2 * RING :]
    outs, accs = rest[:RING], rest[RING:]
    at = pl.program_id(0)
    step = weight_refs[0].shape[0]

    @pl.when(at == 0)
    def _():
        second_grad = sum(part[...].astype(jnp.float32) for part in parts)
        middle = middle_ref[...]
        scale = inverse_rms(middle)
        normed = middle * scale
        gain_out[...] = jnp.sum(second_grad * normed, axis=0, keepdims=True)
        scaled = second_grad * gain_ref[...]
        grad = cot_ref[...].astype(jnp.float32) + scale * (
            scaled - normed * jnp.mean(scaled * normed, axis=-1, keepdims=True)
        )
        grad_ref[...] = grad
        low_ref[...] = grad.astype(low)
        for acc in accs:
            acc[...] = jnp.zeros_like(acc)

    rows = low_ref[:, pl.ds(pl.multiple_of(at * step, step), step)]
    for weight, acc in zip(weight_refs, accs):
        acc[...] += jnp.dot(rows, weight[...], preferred_element_type=jnp.float32)

    @pl.when(at == pl.num_programs(0) - 1)
    def _():
        for out, acc in zip(outs, accs):
            for head in range(4):
                out[head] = acc[:, head * HEAD_DIM : (head + 1) * HEAD_DIM].astype(low)


def middle_back(parts, weights, middle, cot, gain):
    rows, width = middle.shape
    steps = 4
    whole = pl.BlockSpec((rows, width), lambda d: (0, 0))
    row = pl.BlockSpec((1, width), lambda d: (0, 0))
    heads = pl.BlockSpec((4, rows, HEAD_DIM), lambda d: (0, 0, 0))
    return pl.pallas_call(
        middle_back_kernel,
        grid=(steps,),
        in_specs=[whole] * RING
        + [pl.BlockSpec((width // steps, 512), lambda d: (d, 0))] * RING
        + [whole, whole, row],
        out_specs=(whole, whole, row) + (heads,) * RING,
        out_shape=(
            jax.ShapeDtypeStruct((rows, width), jnp.float32),
            jax.ShapeDtypeStruct((rows, width), low),
            jax.ShapeDtypeStruct((1, width), jnp.float32),
        )
        + (jax.ShapeDtypeStruct((4, rows, HEAD_DIM), low),) * RING,
        scratch_shapes=[pltpu.VMEM((rows, 512), jnp.float32)] * RING,
        compiler_params=pltpu.CompilerParams(vmem_limit_bytes=VMEM_LIMIT),
        cost_estimate=pl.CostEstimate(flops=1024, bytes_accessed=1024, transcendentals=0),
    )(*parts, *weights, middle, cot, gain)


def first_kernel(
    hidden_ref, gain_ref, weight_ref, cos_ref, sin_ref, query_gain, key_gain, first_ref, pre_ref, send_ref
):
    first = (normalize(hidden_ref[0].astype(jnp.float32)) * gain_ref[...]).astype(low)
    first_ref[0] = first
    pre = jnp.dot(first, weight_ref[...], preferred_element_type=jnp.float32)
    pre_ref[0] = pre
    cosine = cos_ref[0]
    sine = sin_ref[0]

    def turned(head, gain):
        values = normalize(pre[:, head * HEAD_DIM : (head + 1) * HEAD_DIM]) * gain
        return (values * cosine + pltpu.roll(values, HEAD_DIM // 2, 1) * sine).astype(low)

    for head in range(4):
        send_ref[head, 0] = turned(head, query_gain[...])
    for head in range(2):
        send_ref[2 * head, 1] = turned(4 + head, key_gain[...])
        send_ref[2 * head + 1, 1] = pre[:, (6 + head) * HEAD_DIM : (7 + head) * HEAD_DIM].astype(low)


def first_part(hidden_all, gain, weights, cosine, sine, query_gain, key_gain):
    _, rows, width = hidden_all.shape
    row = pl.BlockSpec((1, HEAD_DIM), lambda r: (0, 0))
    turn = pl.BlockSpec((1, rows, HEAD_DIM), lambda r: (r, 0, 0))
    return pl.pallas_call(
        first_kernel,
        grid=(RING,),
        in_specs=[
            pl.BlockSpec((1, rows, width), lambda r: (r, 0, 0)),
            pl.BlockSpec((1, width), lambda r: (0, 0)),
            pl.BlockSpec((width, 1024), lambda r: (0, 0)),
            turn,
            turn,
            row,
            row,
        ],
        out_specs=(
            pl.BlockSpec((1, rows, width), lambda r: (r, 0, 0)),
            pl.BlockSpec((1, rows, 1024), lambda r: (r, 0, 0)),
            pl.BlockSpec((4, 2, rows, HEAD_DIM), lambda r: (r, 0, 0, 0)),
        ),
        out_shape=(
            jax.ShapeDtypeStruct((RING, rows, width), low),
            jax.ShapeDtypeStruct((RING, rows, 1024), jnp.float32),
            jax.ShapeDtypeStruct((BLOCKS, 2, rows, HEAD_DIM), low),
        ),
        compiler_params=pltpu.CompilerParams(vmem_limit_bytes=VMEM_LIMIT),
        cost_estimate=pl.CostEstimate(
            flops=2 * RING * rows * width * 1024,
            bytes_accessed=20 * 1024 * 1024,
            transcendentals=0,
        ),
    )(hidden_all, gain, weights, cosine, sine, query_gain, key_gain)


def first_back_kernel(
    core_ref, back_ref, pre_ref, cos_ref, sin_ref, query_gain, key_gain, first_ref,
    grad_ref, keep_ref, give_ref, query_sum, key_sum, all_grads,
):
    at = pl.program_id(0)
    rows = grad_ref.shape[1]
    cosine = cos_ref[0]
    sine = sin_ref[0]

    @pl.when(at == 0)
    def _():
        query_sum[...] = jnp.zeros_like(query_sum)
        key_sum[...] = jnp.zeros_like(key_sum)

    def back(grads, head, gain, sums):
        columns = slice(head * HEAD_DIM, (head + 1) * HEAD_DIM)
        values = pre_ref[0, :, columns]
        grads = grads.astype(jnp.float32)
        grads = grads * cosine - pltpu.roll(grads, HEAD_DIM // 2, 1) * sine
        scale = inverse_rms(values)
        normed = values * scale
        sums[...] += jnp.sum(grads * normed, axis=0, keepdims=True)
        scaled = grads * gain
        out = scale * (scaled - normed * jnp.mean(scaled * normed, axis=-1, keepdims=True))
        grad_ref[0, :, columns] = out.astype(low)

    for head in range(4):
        back(back_ref[head, 0], head, query_gain[...], query_sum)
    for head in range(2):
        back(back_ref[2 * head, 1], 4 + head, key_gain[...], key_sum)
        grad_ref[0, :, (6 + head) * HEAD_DIM : (7 + head) * HEAD_DIM] = back_ref[2 * head + 1, 1]
    all_grads[pl.ds(pl.multiple_of(at * rows, rows), rows), :] = grad_ref[0]

    @pl.when(at == RING - 1)
    def _():
        grads = all_grads[...]
        first_core = core_ref[0] == 0
        for pair in range(8):
            inputs = first_ref[:, :, pair * 256 : (pair + 1) * 256].reshape(RING * rows, 256)
            term = lax.dot_general(
                inputs, grads, contract_first, preferred_element_type=jnp.float32
            ).astype(low)
            keep_ref[pair] = jnp.where(first_core, term[:128], term[128:])
            give_ref[pair] = jnp.where(first_core, term[128:], term[:128])


def first_back(core_at, returned, pre, cosine, sine, query_gain, key_gain, first_in):
    _, rows, width = first_in.shape
    row = pl.BlockSpec((1, HEAD_DIM), lambda r: (0, 0))
    turn = pl.BlockSpec((1, rows, HEAD_DIM), lambda r: (r, 0, 0))
    wide = pl.BlockSpec((1, rows, 1024), lambda r: (r, 0, 0))
    half = pl.BlockSpec((8, 128, 1024), lambda r: (0, 0, 0))
    return pl.pallas_call(
        first_back_kernel,
        grid=(RING,),
        in_specs=[
            pl.BlockSpec(memory_space=pltpu.SMEM),
            pl.BlockSpec((4, 2, rows, HEAD_DIM), lambda r: (r, 0, 0, 0)),
            wide,
            turn,
            turn,
            row,
            row,
            pl.BlockSpec((RING, rows, width), lambda r: (0, 0, 0)),
        ],
        out_specs=(wide, half, half, row, row),
        out_shape=(
            jax.ShapeDtypeStruct((RING, rows, 1024), low),
            jax.ShapeDtypeStruct((8, 128, 1024), low),
            jax.ShapeDtypeStruct((8, 128, 1024), low),
            jax.ShapeDtypeStruct((1, HEAD_DIM), jnp.float32),
            jax.ShapeDtypeStruct((1, HEAD_DIM), jnp.float32),
        ),
        scratch_shapes=[pltpu.VMEM((RING * rows, 1024), low)],
        compiler_params=pltpu.CompilerParams(vmem_limit_bytes=VMEM_LIMIT),
        cost_estimate=pl.CostEstimate(flops=1024, bytes_accessed=1024, transcendentals=0),
    )(core_at[None], returned, pre, cosine, sine, query_gain, key_gain, first_in)


def last_kernel(
    core_ref, grad_ref, weight_ref, hidden_ref, mlp_ref, query_ref, key_ref,
    own_ref, left_ref, top_ref, bottom_ref, right_ref, keep_ref, give_ref, gain_acc,
):
    at = pl.program_id(0)
    width = hidden_ref.shape[2]
    part = lax.dot_general(
        grad_ref[0], weight_ref[...], contract_last, preferred_element_type=jnp.float32
    )
    half = top_ref.shape[0]
    for r, out in ((0, own_ref), (1, left_ref), (3, right_ref)):

        @pl.when(at == r)
        def _(out=out):
            out[...] = part.astype(low)

    @pl.when(at == 2)
    def _():
        top_ref[...] = part[:half].astype(low)
        bottom_ref[...] = part[half:].astype(low)

    normed = normalize(hidden_ref[0].astype(jnp.float32))
    gain = jnp.sum(part * normed, axis=0, keepdims=True)

    @pl.when(at == 0)
    def _():
        gain_acc[...] = gain

    @pl.when(at > 0)
    def _():
        gain_acc[...] += gain

    @pl.when(at == RING - 1)
    def _():
        lines = [
            gain_acc[...],
            mlp_ref[...],
            jnp.concatenate([query_ref[...]] * BLOCKS, axis=1),
            jnp.concatenate([key_ref[...]] * BLOCKS, axis=1),
            jnp.zeros((HEAD_DIM - 4, width), jnp.float32),
        ]
        turned = jnp.concatenate(lines, axis=0).T.astype(low)
        first_core = core_ref[0] == 0
        for pair in range(8):
            first = turned[pair * 256 : pair * 256 + 128]
            second = turned[pair * 256 + 128 : (pair + 1) * 256]
            keep_ref[pair] = jnp.where(first_core, first, second)
            give_ref[pair] = jnp.where(first_core, second, first)


def last_part(core_at, grads, weights, hidden_all, mlp_part, query_part, key_part):
    _, rows, width = hidden_all.shape
    block = pl.BlockSpec((rows, width), lambda r: (0, 0))
    small = pl.BlockSpec((rows // 2, width), lambda r: (0, 0))
    whole = jax.ShapeDtypeStruct((rows, width), low)
    part = jax.ShapeDtypeStruct((rows // 2, width), low)
    row = pl.BlockSpec((1, HEAD_DIM), lambda r: (0, 0))
    half = pl.BlockSpec((8, 128, HEAD_DIM), lambda r: (0, 0, 0))
    return pl.pallas_call(
        last_kernel,
        grid=(RING,),
        in_specs=[
            pl.BlockSpec(memory_space=pltpu.SMEM),
            pl.BlockSpec((1, rows, 1024), lambda r: (r, 0, 0)),
            pl.BlockSpec((width, 1024), lambda r: (0, 0)),
            pl.BlockSpec((1, rows, width), lambda r: (r, 0, 0)),
            pl.BlockSpec((1, width), lambda r: (0, 0)),
            row,
            row,
        ],
        out_specs=(block, block, small, small, block, half, half),
        out_shape=(whole, whole, part, part, whole)
        + (jax.ShapeDtypeStruct((8, 128, HEAD_DIM), low),) * 2,
        scratch_shapes=[pltpu.VMEM((1, width), jnp.float32)],
        compiler_params=pltpu.CompilerParams(vmem_limit_bytes=VMEM_LIMIT),
        cost_estimate=pl.CostEstimate(flops=1024, bytes_accessed=1024, transcendentals=0),
    )(core_at[None], grads, weights, hidden_all, mlp_part, query_part, key_part)


def arrange_kernel(at_ref, own_ref, other_ref, out_ref):
    y_at, x_at, core_at = at_ref[0], at_ref[1], at_ref[2]
    for dy in range(RING):
        for dx in range(2):
            first = ((y_at - dy + RING) & 3) * 4 + (x_at ^ dx) * 2
            own = pl.multiple_of((first + core_at) * 128, 128)
            other = pl.multiple_of((first + 1 - core_at) * 128, 128)
            out_ref[pl.ds(own, 128), :] = own_ref[dy, dx]
            out_ref[pl.ds(other, 128), :] = other_ref[dy, dx]


def gather_by_permutes(pair, y_at, x_at, core_at):
    own = jnp.stack([pair] + [shift(pair, "y", r) for r in range(1, RING)])
    other = shift(own, "core", 1, 2)
    whole = pl.BlockSpec(memory_space=pltpu.VMEM)
    return pl.pallas_call(
        arrange_kernel,
        in_specs=[pl.BlockSpec(memory_space=pltpu.SMEM), whole, whole],
        out_specs=whole,
        out_shape=jax.ShapeDtypeStruct((BLOCKS * 128, pair.shape[2]), pair.dtype),
        compiler_params=pltpu.CompilerParams(vmem_limit_bytes=VMEM_LIMIT),
        cost_estimate=pl.CostEstimate(flops=1024, bytes_accessed=1024, transcendentals=0),
    )(jnp.stack([y_at, x_at, core_at]), own, other)


def to_heads(send):
    return lax.all_to_all(send, GROUP_AXES, 0, 0, tiled=True)


def after(value, *others):
    return lax.optimization_barrier((value, others))[0]


def ring_blocks(values):
    half = values.shape[0] // 2
    left = shift(values, "z", 1)
    right = shift(values, "z", 3)
    opposite = jnp.concatenate(
        [shift(left[:half], "z", 1), shift(right[half:], "z", 3)], axis=0
    )
    return [values, left, opposite, right]


def together(*values):
    return lax.optimization_barrier(values)


def place(z_at, blocks, widths, chunk=None, summed=False):
    rows = blocks[0].shape[0]
    whole = pl.BlockSpec(memory_space=pltpu.VMEM)
    shapes = [RING * part for part in widths] + [HEAD_DIM] * summed

    def kernel(z_ref, *refs):
        ins, outs = refs[:RING], refs[RING:]
        for r in range(RING):
            slot = (z_ref[0] - r + RING) & 3
            start = 0
            for turn in range(widths[0] // chunk if chunk else 1):
                for out, part in zip(outs, widths):
                    size = chunk or part
                    at = pl.multiple_of(slot * part + turn * size, 128)
                    out[:, pl.ds(at, size)] = ins[r][:, start : start + size].astype(jnp.float32)
                    start += size
            if summed:
                columns = ins[r][:, start : start + HEAD_DIM].astype(jnp.float32)
                outs[-1][...] = columns if r == 0 else outs[-1][...] + columns

    return pl.pallas_call(
        kernel,
        in_specs=[pl.BlockSpec(memory_space=pltpu.SMEM)] + [whole] * RING,
        out_specs=tuple(whole for _ in shapes),
        out_shape=tuple(jax.ShapeDtypeStruct((rows, part), jnp.float32) for part in shapes),
        compiler_params=pltpu.CompilerParams(vmem_limit_bytes=VMEM_LIMIT),
        cost_estimate=pl.CostEstimate(flops=1024, bytes_accessed=1024, transcendentals=0),
    )(z_at[None], *blocks)


def send_back(block, r):
    return shift(block, "z", -r)


def local(
    hidden_in,
    cotangent,
    segment_ids,
    positions,
    attn_gain,
    query_gain,
    key_gain,
    query_weight,
    key_weight,
    value_weight,
    out_weight,
    mlp_gain,
    gate_weight,
    up_weight,
    down_weight,
):
    f32 = jnp.float32
    rows, width = hidden_in.shape
    ring_rows = RING * rows
    z_at = lax.axis_index("z")
    y_at = lax.axis_index("y")
    x_at = lax.axis_index("x_hi")
    core_at = lax.axis_index("core")
    my_index = (y_at * 2 + x_at) * 2 + core_at

    def columns(weight):
        part = weight.shape[1] // RING
        return lax.dynamic_slice_in_dim(weight, z_at * part, part, 1).astype(low)

    def gather(block):
        return lax.all_gather(block, GROUP_AXES, axis=0, tiled=True)

    own_places = lax.dynamic_slice_in_dim(positions, my_index * rows, rows)
    firsts = positions.reshape(BLOCKS, BLOCK)[:, 0]
    segments = segment_ids.reshape(BLOCKS, BLOCK)[:, 0]
    logical = firsts // BLOCK + jnp.maximum(segments - 1, 0) * 2
    numbers = jnp.arange(BLOCKS, dtype=jnp.int32)
    order = jnp.sum(jnp.where(logical[:, None] == numbers[None, :], numbers[:, None], 0), axis=0)
    notes = gather_z(jnp.concatenate([own_places, order, jnp.zeros((112,), jnp.int32)])[None])
    places = notes[:, :rows]
    order = lax.dynamic_index_in_dim(notes, y_at, 0, keepdims=False)[rows : rows + BLOCKS]

    gains = jnp.pad(
        jnp.stack([attn_gain, mlp_gain], axis=1).astype(low), ((0, 0), (0, HEAD_DIM - 2))
    )
    first_weights = gather(
        jnp.concatenate(
            [columns(query_weight), columns(key_weight), columns(value_weight), gains], axis=1
        )
    )
    attn_scale = first_weights[:, 1024].astype(f32)[None]
    mlp_scale = first_weights[:, 1025].astype(f32)[None]
    out_columns = columns(out_weight)
    out_come = shift(out_columns, "x_hi", 1, 2)
    gate_columns, up_columns, down_columns, out_come = together(
        gate_weight, up_weight, down_weight, out_come
    )
    gate_columns, up_columns = columns(gate_columns), columns(up_columns)
    mlp_columns = []
    for start in range(0, gate_columns.shape[1], FF_STEP):
        mlp_columns.append(gate_columns[:, start : start + FF_STEP])
        mlp_columns.append(up_columns[:, start : start + FF_STEP])
    mlp_weights = gather(jnp.concatenate(mlp_columns + [columns(down_columns)], axis=1))
    out_slice = gather_by_permutes(jnp.stack([out_columns, out_come]), y_at, x_at, core_at)

    hidden_blocks = ring_blocks(hidden_in)
    out_slice = after(out_slice, *hidden_blocks)
    out_left = shift(out_slice, "z", 1)
    out_right = shift(out_slice, "z", 3)
    frequency = rope_base ** (-2.0 * jnp.arange(HEAD_DIM // 2, dtype=f32) / HEAD_DIM)
    angles = places.astype(f32)[:, :, None] * frequency[None, None, :]
    cosine = jnp.cos(angles)
    sine = jnp.sin(angles)
    cosine = jnp.concatenate([cosine, cosine], axis=-1)
    sine = jnp.concatenate([-sine, sine], axis=-1)
    query_row = query_gain[None]
    key_row = key_gain[None]

    hidden_all = jnp.stack(hidden_blocks)
    first_in, qkv_pre, send = first_part(
        hidden_all, attn_scale, first_weights, cosine, sine, query_row, key_row
    )
    out_top = shift(out_left[: width // 2], "z", 1)
    out_bottom = shift(out_right[width // 2 :], "z", 3)
    arrived, out_left, out_right, out_top, out_bottom = together(
        to_heads(send), out_left, out_right, out_top, out_bottom
    )
    other_pair = shift(arrived[:, 1], "core", 1, 2)
    head_mixed, head_mixed_t, head_logs = attention_forward(order, core_at, arrived, other_pair)
    cot_own = after(cotangent, head_mixed)
    cot_left = shift(cot_own, "z", 1)
    cot_right = shift(cot_own, "z", 3)

    mixed_arrived, cot_left, cot_right = together(to_heads(head_mixed), cot_left, cot_right)
    half = rows // 2
    mixed_blocks = [mixed_arrived[:4]] + [
        shift(mixed_arrived[4 * (RING - j) : 4 * (RING - j) + 4], "z", j) for j in range(1, RING)
    ]
    out_opposite = jnp.concatenate([out_top, out_bottom], axis=0)
    out_weights = [out_slice, out_left, out_opposite, out_right]
    mixed_blocks, out_weights = together(mixed_blocks, out_weights)
    middle, second_in = middle_part(mixed_blocks, out_weights, hidden_in, mlp_scale)
    hidden = hidden_in.astype(f32)
    left = shift(second_in, "z", 1)
    right = shift(second_in, "z", 3)
    *held, own_part = mlp_blocks(0, [second_in], [cot_own], mlp_weights, ())
    held, own_part, left, right, cot_left, cot_right = together(
        held, own_part, left, right, cot_left, cot_right
    )
    top = shift(left[:half], "z", 1)
    bottom = shift(right[half:], "z", 3)
    cot_top = shift(cot_left[:half], "z", 1)
    cot_bottom = shift(cot_right[half:], "z", 3)
    *held, left_part, right_part = mlp_blocks(
        1, [left, right], [cot_left, cot_right], mlp_weights, held
    )
    left_back = send_back(left_part, 1)
    right_back = send_back(right_part, 3)
    held, top, bottom, cot_top, cot_bottom = together(held, top, bottom, cot_top, cot_bottom)
    *held, opposite_part = mlp_blocks(1, [top, bottom], [cot_top, cot_bottom], mlp_weights, held)
    opposite_back = send_back(opposite_part, 2)
    inner, both_grad, second_all, cot_all = held

    def pair_sum(keep, come):
        return (keep.astype(f32) + come.astype(f32)).astype(low)

    def to_owners(pair):
        return lax.all_to_all(pair, ("y", "x_hi"), 0, 0, tiled=True)

    def add_up(terms):
        return jnp.sum(terms.astype(f32), axis=0).astype(low)

    def over_x(share):
        return share, shift(share, "x_lo", 1, 2)

    def over_z(pair):
        share = pair_sum(*pair)
        return [share] + [shift(share, "z", r) for r in range(1, RING)]

    both_term = lax.dot_general(
        second_all.reshape(ring_rows, width),
        both_grad.reshape(ring_rows, 3072),
        contract_first,
        preferred_element_type=f32,
    ).astype(low)
    left_back, right_back, opposite_back, both_term, inner = together(
        left_back, right_back, opposite_back, both_term, inner
    )
    both_share = lax.psum_scatter(both_term, GROUP_AXES, scatter_dimension=0, tiled=True)

    middle_grad, own_low, mlp_gain_part, *grad_blocks = middle_back(
        (own_part, left_back, right_back, opposite_back),
        out_weights,
        middle,
        cotangent,
        mlp_scale,
    )
    grad_blocks = [grad_blocks[0]] + [shift(grad_blocks[RING - r], "z", r) for r in range(1, RING)]
    down_keep, down_give = pair_grad(core_at, [cot_all], inner)
    grad_blocks, down_keep, down_give, own_low, inner = together(
        grad_blocks, down_keep, down_give, own_low, inner
    )
    head_grads = to_heads(jnp.concatenate(grad_blocks, axis=0))
    low_left = shift(own_low, "z", 1)
    low_right = shift(own_low, "z", 3)
    down_sum = pair_sum(down_keep, shift(down_give, "core", 1, 2))
    mlp_own, mlp_opposite, mlp_left, mlp_right = mlp_out_part(inner, mlp_weights)
    head_grads, down_sum, low_left, low_right, own_low, mlp_opposite, mlp_left, mlp_right = together(
        head_grads, down_sum, low_left, low_right, own_low, mlp_opposite, mlp_left, mlp_right
    )
    mlp_left = send_back(mlp_left, 1)
    mlp_right = send_back(mlp_right, 3)
    down_terms = to_owners(down_sum)

    query_grad, grad_keep, grad_give = attention_backward(
        order, core_at, arrived, other_pair, head_grads, head_mixed_t, head_logs
    )
    query_grad, grad_keep, grad_give, mlp_left, mlp_right, own_low, mlp_opposite = together(
        query_grad, grad_keep, grad_give, mlp_left, mlp_right, own_low, mlp_opposite
    )
    low_opposite = shift(own_low, "z", 2)
    grads_send = lax.dynamic_update_slice_in_dim(
        query_grad, pair_sum(grad_keep, shift(grad_give, "core", 1, 2))[:, None], 1, 1
    )
    grads_send, down_terms = together(grads_send, down_terms)
    returned = to_heads(grads_send)
    down_pair = over_x(add_up(down_terms))
    out_keep, out_give = pair_grad(
        core_at, [own_low, low_left, low_opposite, low_right], mixed_arrived, by_heads=True
    )
    out_sum = pair_sum(out_keep, shift(out_give, "core", 1, 2))
    mlp_opposite = send_back(mlp_opposite, 2)
    returned, out_sum, mlp_opposite = together(returned, out_sum, mlp_opposite)
    out_terms = to_owners(out_sum)
    qkv_grad, qkv_keep, qkv_give, query_gain_part, key_gain_part = first_back(
        core_at, returned, qkv_pre, cosine, sine, query_row, key_row, first_in
    )
    qkv_grad, qkv_give, down_pair = together(qkv_grad, qkv_give, down_pair)
    qkv_come = shift(qkv_give, "core", 1, 2)
    *first_parts, gains_keep, gains_give = last_part(
        core_at,
        qkv_grad,
        first_weights,
        hidden_all,
        mlp_gain_part,
        query_gain_part,
        key_gain_part,
    )
    down_blocks = over_z(down_pair)
    first_parts, gains_give, qkv_come, out_terms, down_blocks, both_share = together(
        first_parts, gains_give, qkv_come, out_terms, down_blocks, both_share
    )
    gains_come = shift(gains_give, "core", 1, 2)
    first_own, first_left, first_top, first_bottom, first_right = first_parts
    first_top = shift(first_top, "z", 3)
    first_bottom = shift(first_bottom, "z", 1)
    qkv_terms = to_owners(
        jnp.concatenate([pair_sum(qkv_keep, qkv_come), pair_sum(gains_keep, gains_come)], axis=2)
    )
    both_pair = over_x(both_share)
    out_pair = over_x(add_up(out_terms))
    first_left = send_back(
        jnp.concatenate([pair_sum(first_left[:half], first_top), first_left[half:]], axis=0), 1
    )
    first_right = send_back(
        jnp.concatenate([first_right[:half], pair_sum(first_right[half:], first_bottom)], axis=0), 3
    )
    qkv_terms, out_pair, both_pair = together(qkv_terms, out_pair, both_pair)
    qkv_share = add_up(qkv_terms)
    both_sum = pair_sum(*both_pair)
    both_left = shift(both_sum, "z", 1)
    both_right = shift(both_sum, "z", 3)
    both_blocks = [both_sum, both_left, shift(both_sum, "z", 2), both_right]
    qkv_pair = over_x(qkv_share)
    output = (
        middle
        + mlp_own.astype(f32)
        + mlp_left.astype(f32)
        + mlp_right.astype(f32)
        + mlp_opposite.astype(f32)
    ).astype(low)
    first_grad = first_own.astype(f32) + first_left.astype(f32) + first_right.astype(f32)
    hidden_rms = inverse_rms(hidden)
    own_norm = hidden * hidden_rms
    scaled_first = first_grad * attn_scale
    hidden_grad = (
        middle_grad
        + hidden_rms
        * (scaled_first - own_norm * jnp.mean(scaled_first * own_norm, axis=-1, keepdims=True))
    ).astype(low)

    (down_grad_out,) = place(z_at, down_blocks, (1536,))
    gate_grad_out, up_grad_out = place(z_at, both_blocks, (1536, 1536), chunk=FF_STEP)
    (out_grad_out,) = place(z_at, over_z(out_pair), (512,))
    query_grad_out, key_grad_out, value_grad_out, gain_sum = place(
        z_at, over_z(qkv_pair), (512, 256, 256), summed=True
    )
    gain_sum = gain_sum[:, :4].T

    return (
        output,
        hidden_grad,
        gain_sum[0],
        gain_sum[2],
        gain_sum[3],
        query_grad_out,
        key_grad_out,
        value_grad_out,
        out_grad_out,
        gain_sum[1],
        gate_grad_out,
        up_grad_out,
        down_grad_out,
    )


def solution(mesh):
    fine = Mesh(mesh.devices.reshape(2, 4, 4, 2, 2), ALL_AXES)
    rep = ("x_lo", "z")
    row = P(ALL_AXES, None)
    part = P(GROUP_AXES)
    weight = P(GROUP_AXES, None)
    in_specs = (
        row,
        row,
        P(rep),
        P(rep),
        part,
        P(),
        P(),
        weight,
        weight,
        weight,
        weight,
        part,
        weight,
        weight,
        weight,
    )
    out_specs = (
        row,
        row,
        part,
        P(),
        P(),
        weight,
        weight,
        weight,
        weight,
        part,
        weight,
        weight,
        weight,
    )
    return jax.shard_map(local, mesh=fine, in_specs=in_specs, out_specs=out_specs, check_vma=False)
```

```python
import functools

import jax
import jax.numpy as jnp
from jax import lax
from jax.experimental import pallas as pl
from jax.experimental.pallas import tpu as pltpu
from jax.sharding import Mesh
from jax.sharding import PartitionSpec as P

HEAD_DIM = 128
RING = 4
BLOCK = 256
BLOCKS = 16
TILE = 512
TILES = 8
PROMPT_TILES = 6
FF_STEP = 512
VMEM_LIMIT = 60 * 1024 * 1024

norm_eps = 1e-06
rope_base = 1000000.0
score_scale = HEAD_DIM ** (-0.5)
score_scale_log2 = score_scale * 1.4426950408889634
contract_first = (((0,), (0,)), ((), ()))
contract_last = (((1,), (1,)), ((), ()))
GROUP_AXES = ("y", "x_hi", "core")
ALL_AXES = ("x_lo", "z", "y", "x_hi", "core")
low = jnp.bfloat16


def inverse_rms(values):
    return lax.rsqrt(jnp.mean(values * values, axis=-1, keepdims=True) + norm_eps)


def normalize(values):
    return values * inverse_rms(values)


def shift(values, axis, by, size=RING):
    return lax.ppermute(values, axis, [(i, (i + by) % size) for i in range(size)])


def gather_z(values):
    return jnp.concatenate(
        [values, shift(values, "z", 1), shift(values, "z", 2), shift(values, "z", 3)], axis=0
    )


def forward_kernel(
    order, core, own_a, own_b, other_a, other_b, mixed_ref, mixed_t_ref, log_ref, k_all, v_t, acc, total
):
    tile = pl.program_id(0)
    start = tile * TILE

    def take(keys, values):
        for half in range(2):
            rows = pl.ds(pl.multiple_of(start + half * BLOCK, BLOCK), BLOCK)
            k_all[rows, :] = keys[half]
            v_t[tile, :, half * BLOCK : (half + 1) * BLOCK] = (
                values[half].astype(jnp.float32).T.astype(low)
            )

    @pl.when(core[0] == 0)
    def _():
        take((own_a[0, 1], own_b[0, 1]), (other_a[0], other_b[0]))

    @pl.when(core[0] == 1)
    def _():
        take((other_a[0], other_b[0]), (own_a[0, 1], own_b[0, 1]))

    queries = jnp.concatenate([own_a[0, 0], own_b[0, 0]], axis=0)
    acc[...] = jnp.zeros_like(acc)
    total[...] = jnp.zeros_like(total)

    def chunk(at, masked):
        keys = k_all[pl.ds(pl.multiple_of(at * TILE, TILE), TILE), :]
        scores = lax.dot_general(keys, queries, contract_last, preferred_element_type=jnp.float32)
        weights = jnp.exp2(scores * score_scale_log2)
        if masked:
            key_row = lax.broadcasted_iota(jnp.int32, (TILE, TILE), 0)
            query_row = lax.broadcasted_iota(jnp.int32, (TILE, TILE), 1)
            weights = jnp.where(key_row <= query_row, weights, 0.0)
        total[...] += jnp.sum(weights, axis=0, keepdims=True)
        acc[...] += jnp.dot(v_t[at], weights.astype(low), preferred_element_type=jnp.float32)

    @pl.loop(0, jnp.minimum(tile, PROMPT_TILES))
    def _(at):
        chunk(at, False)

    chunk(tile, True)
    mixed_t = acc[...] / total[...]
    mixed_t_ref[0] = mixed_t
    log_ref[0] = jnp.log2(total[...])
    mixed = mixed_t.T.astype(low)
    mixed_ref[order[2 * tile]] = mixed[:BLOCK]
    mixed_ref[order[2 * tile + 1]] = mixed[BLOCK:]


def tile_specs(lead):
    return [
        pl.BlockSpec(
            (1, *lead, BLOCK, HEAD_DIM),
            functools.partial(
                lambda half, tile, order, core: (order[2 * tile + half],) + (0,) * (len(lead) + 2),
                half,
            ),
        )
        for half in range(2)
    ]


def attention_forward(order, core_at, arrived, other):
    whole = pl.BlockSpec(memory_space=pltpu.VMEM)
    turned = pl.BlockSpec((1, HEAD_DIM, TILE), lambda tile, order, core: (tile, 0, 0))
    line = pl.BlockSpec((1, 1, TILE), lambda tile, order, core: (tile, 0, 0))
    return pl.pallas_call(
        forward_kernel,
        out_shape=(
            jax.ShapeDtypeStruct((BLOCKS, BLOCK, HEAD_DIM), low),
            jax.ShapeDtypeStruct((TILES, HEAD_DIM, TILE), jnp.float32),
            jax.ShapeDtypeStruct((TILES, 1, TILE), jnp.float32),
        ),
        grid_spec=pltpu.PrefetchScalarGridSpec(
            num_scalar_prefetch=2,
            grid=(TILES,),
            in_specs=tile_specs((2,)) + tile_specs(()),
            out_specs=(whole, turned, line),
            scratch_shapes=[
                pltpu.VMEM((BLOCKS * BLOCK, HEAD_DIM), low),
                pltpu.VMEM((TILES, HEAD_DIM, TILE), low),
                pltpu.VMEM((HEAD_DIM, TILE), jnp.float32),
                pltpu.VMEM((1, TILE), jnp.float32),
            ],
        ),
        compiler_params=pltpu.CompilerParams(vmem_limit_bytes=VMEM_LIMIT),
        cost_estimate=pl.CostEstimate(
            flops=1024, bytes_accessed=1024, transcendentals=0
        ),
    )(order, core_at[None], arrived, arrived, other, other)


def backward_kernel(
    order, core, own_a, own_b, other_a, other_b, grad_a, grad_b, mixed_t_ref, log_ref,
    q_out, keep_out, give_out, k_all, v_all, k_t, q_acc, k_acc, v_acc,
):
    tile = pl.program_id(0)
    start = tile * TILE

    def take(keys, values):
        for half in range(2):
            rows = pl.ds(pl.multiple_of(start + half * BLOCK, BLOCK), BLOCK)
            k_all[rows, :] = keys[half]
            v_all[rows, :] = values[half]
            k_t[tile, :, half * BLOCK : (half + 1) * BLOCK] = (
                keys[half].astype(jnp.float32).T.astype(low)
            )

    @pl.when(core[0] == 0)
    def _():
        take((own_a[0, 1], own_b[0, 1]), (other_a[0], other_b[0]))

    @pl.when(core[0] == 1)
    def _():
        take((other_a[0], other_b[0]), (own_a[0, 1], own_b[0, 1]))

    rows = pl.ds(pl.multiple_of(start, TILE), TILE)
    k_acc[rows, :] = jnp.zeros((TILE, HEAD_DIM), jnp.float32)
    v_acc[rows, :] = jnp.zeros((TILE, HEAD_DIM), jnp.float32)
    queries = jnp.concatenate([own_a[0, 0], own_b[0, 0]], axis=0)
    grads = jnp.concatenate([grad_a[0], grad_b[0]], axis=0)
    grads_t = grads.astype(jnp.float32).T
    shared = jnp.sum(grads_t * mixed_t_ref[0], axis=0, keepdims=True)
    logs = log_ref[0]
    q_acc[...] = jnp.zeros_like(q_acc)

    def chunk(at, masked):
        rows = pl.ds(pl.multiple_of(at * TILE, TILE), TILE)
        scores = lax.dot_general(
            k_all[rows, :], queries, contract_last, preferred_element_type=jnp.float32
        )
        probs = jnp.exp2(scores * score_scale_log2 - logs)
        if masked:
            key_row = lax.broadcasted_iota(jnp.int32, (TILE, TILE), 0)
            query_row = lax.broadcasted_iota(jnp.int32, (TILE, TILE), 1)
            probs = jnp.where(key_row <= query_row, probs, 0.0)
        prob_grads = lax.dot_general(
            v_all[rows, :], grads, contract_last, preferred_element_type=jnp.float32
        )
        score_grads = (probs * (prob_grads - shared)).astype(low)
        v_acc[rows, :] += jnp.dot(probs.astype(low), grads, preferred_element_type=jnp.float32)
        k_acc[rows, :] += jnp.dot(score_grads, queries, preferred_element_type=jnp.float32)
        q_acc[...] += jnp.dot(k_t[at], score_grads, preferred_element_type=jnp.float32)

    @pl.loop(0, jnp.minimum(tile, PROMPT_TILES))
    def _(at):
        chunk(at, False)

    chunk(tile, True)
    query_grad = (q_acc[...] * score_scale).T.astype(low)
    q_out[order[2 * tile], 0] = query_grad[:BLOCK]
    q_out[order[2 * tile + 1], 0] = query_grad[BLOCK:]

    def give(keep_acc, keep_scale, give_acc, give_scale):
        for at in range(BLOCKS):
            rows = slice(at * BLOCK, (at + 1) * BLOCK)
            keep_out[order[at]] = (keep_acc[rows, :] * keep_scale).astype(low)
            give_out[order[at]] = (give_acc[rows, :] * give_scale).astype(low)

    @pl.when((tile == TILES - 1) & (core[0] == 0))
    def _():
        give(k_acc, score_scale, v_acc, 1.0)

    @pl.when((tile == TILES - 1) & (core[0] == 1))
    def _():
        give(v_acc, 1.0, k_acc, score_scale)


def attention_backward(order, core_at, arrived, other, grads, mixed_t, logs):
    whole = pl.BlockSpec(memory_space=pltpu.VMEM)
    rows = BLOCKS * BLOCK
    turned = pl.BlockSpec((1, HEAD_DIM, TILE), lambda tile, order, core: (tile, 0, 0))
    line = pl.BlockSpec((1, 1, TILE), lambda tile, order, core: (tile, 0, 0))
    return pl.pallas_call(
        backward_kernel,
        out_shape=(jax.ShapeDtypeStruct((BLOCKS, 2, BLOCK, HEAD_DIM), low),)
        + (jax.ShapeDtypeStruct((BLOCKS, BLOCK, HEAD_DIM), low),) * 2,
        grid_spec=pltpu.PrefetchScalarGridSpec(
            num_scalar_prefetch=2,
            grid=(TILES,),
            in_specs=tile_specs((2,)) + tile_specs(()) + tile_specs(()) + [turned, line],
            out_specs=(whole, whole, whole),
            scratch_shapes=[
                pltpu.VMEM((rows, HEAD_DIM), low),
                pltpu.VMEM((rows, HEAD_DIM), low),
                pltpu.VMEM((TILES, HEAD_DIM, TILE), low),
                pltpu.VMEM((HEAD_DIM, TILE), jnp.float32),
                pltpu.VMEM((rows, HEAD_DIM), jnp.float32),
                pltpu.VMEM((rows, HEAD_DIM), jnp.float32),
            ],
        ),
        compiler_params=pltpu.CompilerParams(vmem_limit_bytes=VMEM_LIMIT),
        cost_estimate=pl.CostEstimate(
            flops=1024, bytes_accessed=1024, transcendentals=0
        ),
    )(order, core_at[None], arrived, arrived, other, other, grads, grads, mixed_t, logs)


def mlp_kernel(parts, *refs):
    second_refs, cot_refs = refs[:parts], refs[parts : 2 * parts]
    both_weight_ref, down_ref = refs[2 * parts : 2 * parts + 2]
    count = refs[-1].shape[0] // BLOCK
    inner_ref, both_ref, second_out, cot_out = refs[-5 - count : -1 - count]
    grad_refs, acc = refs[-1 - count : -1], refs[-1]
    at = pl.program_id(0)
    step = down_ref.shape[1]
    rows, width = acc.shape

    @pl.when(at == 0)
    def _():
        for ins, out in ((second_refs, second_out), (cot_refs, cot_out)):
            start = 0
            for part in ins:
                size = part.shape[0]
                out[start // BLOCK, start % BLOCK : start % BLOCK + size, :] = part[...]
                start += size

    second = second_out[...].reshape(rows, width)
    both_act = jnp.dot(second, both_weight_ref[...], preferred_element_type=jnp.float32)
    inner_grad = jnp.dot(
        cot_out[...].reshape(rows, width), down_ref[...], preferred_element_type=jnp.float32
    )
    gate_act = both_act[:, :step]
    up_act = both_act[:, step:]
    sigmoid = 1.0 / (1.0 + jnp.exp(-gate_act))
    silu = gate_act * sigmoid
    inner_ref[...] = (silu * up_act).astype(low).reshape(inner_ref.shape)
    gate_grad = (inner_grad * up_act * (sigmoid * (1.0 + gate_act * (1.0 - sigmoid)))).astype(low)
    both_grad = jnp.concatenate([gate_grad, (inner_grad * silu).astype(low)], axis=1)
    both_ref[:, :, pl.ds(pl.multiple_of(at * 2 * step, 2 * step), 2 * step)] = both_grad.reshape(
        count, BLOCK, 2 * step
    )
    part = lax.dot_general(
        both_grad, both_weight_ref[...], contract_last, preferred_element_type=jnp.float32
    )
    last = pl.num_programs(0) - 1

    @pl.when(at == 0)
    def _():
        acc[...] = part

    @pl.when((at > 0) & (at < last))
    def _():
        acc[...] += part

    @pl.when(at == last)
    def _():
        total = (acc[...] + part).astype(low)
        for block, grad in enumerate(grad_refs):
            grad[...] = total[block * BLOCK : (block + 1) * BLOCK]


def mlp_blocks(place_at, seconds, cots, weights, held):
    rows = sum(second.shape[0] for second in seconds)
    width = seconds[0].shape[1]
    count = rows // BLOCK
    hidden_width = weights.shape[1] // 3
    step = FF_STEP
    steps = hidden_width // step
    ins = [
        pl.BlockSpec(value.shape, lambda c: (0, 0), pipeline_mode=pl.Buffered(1))
        for value in (*seconds, *cots)
    ]
    kept = pl.BlockSpec((count, BLOCK, step), lambda c: (place_at, 0, c))
    kept_both = pl.BlockSpec((count, BLOCK, 2 * hidden_width), lambda c: (place_at, 0, 0))
    kept_rows = pl.BlockSpec((count, BLOCK, width), lambda c: (place_at, 0, 0))
    rows_shape = jax.ShapeDtypeStruct((RING, BLOCK, width), low)
    return pl.pallas_call(
        functools.partial(mlp_kernel, len(seconds)),
        grid=(steps,),
        in_specs=ins
        + [
            pl.BlockSpec((width, 2 * step), lambda c: (0, c)),
            pl.BlockSpec((width, step), lambda c: (0, 2 * steps + c)),
        ]
        + [pl.BlockSpec(memory_space=pl.ANY)] * len(held),
        out_specs=(kept, kept_both, kept_rows, kept_rows)
        + (pl.BlockSpec((BLOCK, width), lambda c: (0, 0)),) * count,
        out_shape=(
            jax.ShapeDtypeStruct((RING, BLOCK, hidden_width), low),
            jax.ShapeDtypeStruct((RING, BLOCK, 2 * hidden_width), low),
            rows_shape,
            rows_shape,
        )
        + (jax.ShapeDtypeStruct((BLOCK, width), low),) * count,
        scratch_shapes=[pltpu.VMEM((rows, width), jnp.float32)],
        input_output_aliases={len(ins) + 2 + i: i for i in range(len(held))},
        compiler_params=pltpu.CompilerParams(vmem_limit_bytes=VMEM_LIMIT),
        cost_estimate=pl.CostEstimate(
            flops=2 * 5 * rows * width * hidden_width,
            bytes_accessed=2 * 3 * width * hidden_width,
            transcendentals=rows * hidden_width,
        ),
    )(*seconds, *cots, weights, weights, *held)


def mlp_out_kernel(inner_ref, weight_ref, *outs):
    inner = inner_ref[...].reshape(RING * BLOCK, inner_ref.shape[2])
    part = lax.dot_general(
        inner, weight_ref[...], contract_last, preferred_element_type=jnp.float32
    ).astype(low)
    for block, out in enumerate(outs):
        out[...] = part[block * BLOCK : (block + 1) * BLOCK]


def mlp_out_part(inner, weights):
    _, rows, hidden_width = inner.shape
    width = weights.shape[0]
    steps = 4
    return pl.pallas_call(
        mlp_out_kernel,
        grid=(steps,),
        in_specs=[
            pl.BlockSpec(inner.shape, lambda d: (0, 0, 0)),
            pl.BlockSpec((width // steps, hidden_width), lambda d: (d, 2)),
        ],
        out_specs=(pl.BlockSpec((rows, width // steps), lambda d: (0, d)),) * RING,
        out_shape=(jax.ShapeDtypeStruct((rows, width), low),) * RING,
        compiler_params=pltpu.CompilerParams(vmem_limit_bytes=VMEM_LIMIT),
        cost_estimate=pl.CostEstimate(flops=1024, bytes_accessed=1024, transcendentals=0),
    )(inner, weights)


def pair_grad(core_at, lefts, right, by_heads=False):
    width = lefts[0].shape[-1]
    outs = 512 if by_heads else right.shape[2]
    rows = RING * BLOCK

    def kernel(core_ref, *refs):
        left_refs = refs[: len(lefts)]
        right_ref, keep_ref = refs[len(lefts) : len(lefts) + 2]
        give_ref = refs[-1]
        if by_heads:
            all_ref = refs[-1]

            @pl.when(pl.program_id(0) == 0)
            def _():
                for r in range(RING):
                    for head in range(4):
                        all_ref[
                            r * BLOCK : (r + 1) * BLOCK, head * HEAD_DIM : (head + 1) * HEAD_DIM
                        ] = right_ref[4 * r + head]

            values = all_ref[...]
        else:
            values = right_ref[...].reshape(rows, outs)
        inputs = [ref[...].reshape(-1, 256) for ref in left_refs]
        inputs = inputs[0] if len(inputs) == 1 else jnp.concatenate(inputs, axis=0)
        term = lax.dot_general(
            inputs, values, contract_first, preferred_element_type=jnp.float32
        ).astype(low)
        if by_heads:
            keep_ref[...] = term
            return
        first_core = core_ref[0] == 0
        keep_ref[0] = jnp.where(first_core, term[:128], term[128:])
        give_ref[0] = jnp.where(first_core, term[128:], term[:128])

    def columns(value):
        lead = value.shape[:-1]
        return pl.BlockSpec((*lead, 256), lambda i: (0,) * len(lead) + (i,))

    half = pl.BlockSpec((1, 128, outs), lambda i: (i, 0, 0))
    return pl.pallas_call(
        kernel,
        grid=(width // 256,),
        in_specs=[pl.BlockSpec(memory_space=pltpu.SMEM)]
        + [columns(value) for value in lefts]
        + [pl.BlockSpec(right.shape, lambda i: (0, 0, 0))],
        out_specs=pl.BlockSpec((256, outs), lambda i: (i, 0)) if by_heads else (half, half),
        out_shape=jax.ShapeDtypeStruct((width, outs), low)
        if by_heads
        else (jax.ShapeDtypeStruct((width // 256, 128, outs), low),) * 2,
        scratch_shapes=[pltpu.VMEM((rows, 512), low)] * by_heads,
        compiler_params=pltpu.CompilerParams(vmem_limit_bytes=VMEM_LIMIT),
        cost_estimate=pl.CostEstimate(flops=1024, bytes_accessed=1024, transcendentals=0),
    )(core_at[None], *lefts, right)


def middle_kernel(*refs):
    mixed_refs, weight_refs = refs[:RING], refs[RING : 2 * RING]
    hidden_ref, gain_ref, middle_ref, second_ref = refs[2 * RING :]
    at = pl.program_id(0)
    step = weight_refs[0].shape[0]
    columns = pl.ds(pl.multiple_of(at * step, step), step)
    total = hidden_ref[:, columns].astype(jnp.float32)
    for mixed, weight in zip(mixed_refs, weight_refs):
        rows = jnp.concatenate([mixed[head] for head in range(4)], axis=1)
        total += lax.dot_general(
            rows, weight[...], contract_last, preferred_element_type=jnp.float32
        )
    middle_ref[:, columns] = total

    @pl.when(at == pl.num_programs(0) - 1)
    def _():
        second_ref[...] = (normalize(middle_ref[...]) * gain_ref[...]).astype(low)


def middle_part(mixed_blocks, weights, hidden, gain):
    rows, width = hidden.shape
    steps = 4
    whole = pl.BlockSpec((rows, width), lambda d: (0, 0))
    return pl.pallas_call(
        middle_kernel,
        grid=(steps,),
        in_specs=[pl.BlockSpec((4, rows, HEAD_DIM), lambda d: (0, 0, 0))] * RING
        + [pl.BlockSpec((width // steps, 512), lambda d: (d, 0))] * RING
        + [whole, pl.BlockSpec((1, width), lambda d: (0, 0))],
        out_specs=(whole, whole),
        out_shape=(
            jax.ShapeDtypeStruct((rows, width), jnp.float32),
            jax.ShapeDtypeStruct((rows, width), low),
        ),
        compiler_params=pltpu.CompilerParams(vmem_limit_bytes=32 * 1024 * 1024),
        cost_estimate=pl.CostEstimate(flops=1024, bytes_accessed=1024, transcendentals=0),
    )(*mixed_blocks, *weights, hidden, gain)


def middle_back_kernel(*refs):
    parts, weight_refs = refs[:RING], refs[RING : 2 * RING]
    middle_ref, cot_ref, gain_ref, grad_ref, low_ref, gain_out, *rest = refs[2 * RING :]
    outs, accs = rest[:RING], rest[RING:]
    at = pl.program_id(0)
    step = weight_refs[0].shape[0]

    @pl.when(at == 0)
    def _():
        second_grad = sum(part[...].astype(jnp.float32) for part in parts)
        middle = middle_ref[...]
        scale = inverse_rms(middle)
        normed = middle * scale
        gain_out[...] = jnp.sum(second_grad * normed, axis=0, keepdims=True)
        scaled = second_grad * gain_ref[...]
        grad = cot_ref[...].astype(jnp.float32) + scale * (
            scaled - normed * jnp.mean(scaled * normed, axis=-1, keepdims=True)
        )
        grad_ref[...] = grad
        low_ref[...] = grad.astype(low)
        for acc in accs:
            acc[...] = jnp.zeros_like(acc)

    rows = low_ref[:, pl.ds(pl.multiple_of(at * step, step), step)]
    for weight, acc in zip(weight_refs, accs):
        acc[...] += jnp.dot(rows, weight[...], preferred_element_type=jnp.float32)

    @pl.when(at == pl.num_programs(0) - 1)
    def _():
        for out, acc in zip(outs, accs):
            for head in range(4):
                out[head] = acc[:, head * HEAD_DIM : (head + 1) * HEAD_DIM].astype(low)


def middle_back(parts, weights, middle, cot, gain):
    rows, width = middle.shape
    steps = 4
    whole = pl.BlockSpec((rows, width), lambda d: (0, 0))
    row = pl.BlockSpec((1, width), lambda d: (0, 0))
    heads = pl.BlockSpec((4, rows, HEAD_DIM), lambda d: (0, 0, 0))
    return pl.pallas_call(
        middle_back_kernel,
        grid=(steps,),
        in_specs=[whole] * RING
        + [pl.BlockSpec((width // steps, 512), lambda d: (d, 0))] * RING
        + [whole, whole, row],
        out_specs=(whole, whole, row) + (heads,) * RING,
        out_shape=(
            jax.ShapeDtypeStruct((rows, width), jnp.float32),
            jax.ShapeDtypeStruct((rows, width), low),
            jax.ShapeDtypeStruct((1, width), jnp.float32),
        )
        + (jax.ShapeDtypeStruct((4, rows, HEAD_DIM), low),) * RING,
        scratch_shapes=[pltpu.VMEM((rows, 512), jnp.float32)] * RING,
        compiler_params=pltpu.CompilerParams(vmem_limit_bytes=40 * 1024 * 1024),
        cost_estimate=pl.CostEstimate(flops=1024, bytes_accessed=1024, transcendentals=0),
    )(*parts, *weights, middle, cot, gain)


def first_kernel(
    own_ref, left_ref, top_ref, bottom_ref, right_ref, weight_ref, gains_ref, cos_ref, sin_ref,
    query_gain, key_gain, hidden_ref, first_ref, pre_ref, send_ref, gain_out,
):
    at = pl.program_id(0)
    half = top_ref.shape[0]

    @pl.when(at == 0)
    def _():
        gain_out[...] = gains_ref[...].astype(jnp.float32).T[:8]
        hidden_ref[0] = own_ref[...]

    @pl.when(at == 1)
    def _():
        hidden_ref[0] = left_ref[...]

    @pl.when(at == 2)
    def _():
        hidden_ref[0, :half] = top_ref[...]
        hidden_ref[0, half:] = bottom_ref[...]

    @pl.when(at == 3)
    def _():
        hidden_ref[0] = right_ref[...]

    first = (normalize(hidden_ref[0].astype(jnp.float32)) * gain_out[0:1]).astype(low)
    first_ref[0] = first
    pre = jnp.dot(first, weight_ref[...], preferred_element_type=jnp.float32)
    pre_ref[0] = pre
    cosine = cos_ref[0]
    sine = sin_ref[0]

    def turned(head, gain):
        values = normalize(pre[:, head * HEAD_DIM : (head + 1) * HEAD_DIM]) * gain
        return (values * cosine + pltpu.roll(values, HEAD_DIM // 2, 1) * sine).astype(low)

    for head in range(4):
        send_ref[head, 0] = turned(head, query_gain[...])
    for head in range(2):
        send_ref[2 * head, 1] = turned(4 + head, key_gain[...])
        send_ref[2 * head + 1, 1] = pre[:, (6 + head) * HEAD_DIM : (7 + head) * HEAD_DIM].astype(low)


def first_part(blocks, weights, cosine, sine, query_gain, key_gain):
    rows, width = blocks[0].shape
    row = pl.BlockSpec((1, HEAD_DIM), lambda r: (0, 0))
    turn = pl.BlockSpec((1, rows, HEAD_DIM), lambda r: (r, 0, 0))
    return pl.pallas_call(
        first_kernel,
        grid=(RING,),
        in_specs=[pl.BlockSpec(block.shape, lambda r: (0, 0)) for block in blocks]
        + [
            pl.BlockSpec((width, 1024), lambda r: (0, 0)),
            pl.BlockSpec((width, HEAD_DIM), lambda r: (0, 8)),
            turn,
            turn,
            row,
            row,
        ],
        out_specs=(
            pl.BlockSpec((1, rows, width), lambda r: (r, 0, 0)),
            pl.BlockSpec((1, rows, width), lambda r: (r, 0, 0)),
            pl.BlockSpec((1, rows, 1024), lambda r: (r, 0, 0)),
            pl.BlockSpec((4, 2, rows, HEAD_DIM), lambda r: (r, 0, 0, 0)),
            pl.BlockSpec((8, width), lambda r: (0, 0)),
        ),
        out_shape=(
            jax.ShapeDtypeStruct((RING, rows, width), low),
            jax.ShapeDtypeStruct((RING, rows, width), low),
            jax.ShapeDtypeStruct((RING, rows, 1024), jnp.float32),
            jax.ShapeDtypeStruct((BLOCKS, 2, rows, HEAD_DIM), low),
            jax.ShapeDtypeStruct((8, width), jnp.float32),
        ),
        compiler_params=pltpu.CompilerParams(vmem_limit_bytes=VMEM_LIMIT),
        cost_estimate=pl.CostEstimate(
            flops=2 * RING * rows * width * 1024,
            bytes_accessed=20 * 1024 * 1024,
            transcendentals=0,
        ),
    )(*blocks, weights, weights, cosine, sine, query_gain, key_gain)


def first_back_kernel(
    core_ref, back_ref, pre_ref, cos_ref, sin_ref, query_gain, key_gain, first_ref,
    grad_ref, keep_ref, give_ref, query_sum, key_sum, all_grads,
):
    at = pl.program_id(0)
    rows = grad_ref.shape[1]
    cosine = cos_ref[0]
    sine = sin_ref[0]

    @pl.when(at == 0)
    def _():
        query_sum[...] = jnp.zeros_like(query_sum)
        key_sum[...] = jnp.zeros_like(key_sum)

    def back(grads, head, gain, sums):
        columns = slice(head * HEAD_DIM, (head + 1) * HEAD_DIM)
        values = pre_ref[0, :, columns]
        grads = grads.astype(jnp.float32)
        grads = grads * cosine - pltpu.roll(grads, HEAD_DIM // 2, 1) * sine
        scale = inverse_rms(values)
        normed = values * scale
        sums[...] += jnp.sum(grads * normed, axis=0, keepdims=True)
        scaled = grads * gain
        out = scale * (scaled - normed * jnp.mean(scaled * normed, axis=-1, keepdims=True))
        grad_ref[0, :, columns] = out.astype(low)

    for head in range(4):
        back(back_ref[head, 0], head, query_gain[...], query_sum)
    for head in range(2):
        back(back_ref[2 * head, 1], 4 + head, key_gain[...], key_sum)
        grad_ref[0, :, (6 + head) * HEAD_DIM : (7 + head) * HEAD_DIM] = back_ref[2 * head + 1, 1]
    all_grads[pl.ds(pl.multiple_of(at * rows, rows), rows), :] = grad_ref[0]

    @pl.when(at == RING - 1)
    def _():
        grads = all_grads[...]
        first_core = core_ref[0] == 0
        for pair in range(8):
            inputs = first_ref[:, :, pair * 256 : (pair + 1) * 256].reshape(RING * rows, 256)
            term = lax.dot_general(
                inputs, grads, contract_first, preferred_element_type=jnp.float32
            ).astype(low)
            keep_ref[pair] = jnp.where(first_core, term[:128], term[128:])
            give_ref[pair] = jnp.where(first_core, term[128:], term[:128])


def first_back(core_at, returned, pre, cosine, sine, query_gain, key_gain, first_in):
    _, rows, width = first_in.shape
    row = pl.BlockSpec((1, HEAD_DIM), lambda r: (0, 0))
    turn = pl.BlockSpec((1, rows, HEAD_DIM), lambda r: (r, 0, 0))
    wide = pl.BlockSpec((1, rows, 1024), lambda r: (r, 0, 0))
    half = pl.BlockSpec((8, 128, 1024), lambda r: (0, 0, 0))
    return pl.pallas_call(
        first_back_kernel,
        grid=(RING,),
        in_specs=[
            pl.BlockSpec(memory_space=pltpu.SMEM),
            pl.BlockSpec((4, 2, rows, HEAD_DIM), lambda r: (r, 0, 0, 0)),
            wide,
            turn,
            turn,
            row,
            row,
            pl.BlockSpec((RING, rows, width), lambda r: (0, 0, 0)),
        ],
        out_specs=(wide, half, half, row, row),
        out_shape=(
            jax.ShapeDtypeStruct((RING, rows, 1024), low),
            jax.ShapeDtypeStruct((8, 128, 1024), low),
            jax.ShapeDtypeStruct((8, 128, 1024), low),
            jax.ShapeDtypeStruct((1, HEAD_DIM), jnp.float32),
            jax.ShapeDtypeStruct((1, HEAD_DIM), jnp.float32),
        ),
        scratch_shapes=[pltpu.VMEM((RING * rows, 1024), low)],
        compiler_params=pltpu.CompilerParams(vmem_limit_bytes=VMEM_LIMIT),
        cost_estimate=pl.CostEstimate(flops=1024, bytes_accessed=1024, transcendentals=0),
    )(core_at[None], returned, pre, cosine, sine, query_gain, key_gain, first_in)


def last_kernel(
    core_ref, grad_ref, weight_ref, hidden_ref, mlp_ref, query_ref, key_ref,
    own_ref, left_a, left_b, top_ref, bottom_ref, right_a, right_b, keep_ref, give_ref, gain_acc,
):
    at = pl.program_id(0)
    width = hidden_ref.shape[2]
    part = lax.dot_general(
        grad_ref[0], weight_ref[...], contract_last, preferred_element_type=jnp.float32
    )
    half = top_ref.shape[0]
    @pl.when(at == 0)
    def _():
        own_ref[...] = part.astype(low)

    for r, first, second in ((1, left_a, left_b), (2, top_ref, bottom_ref), (3, right_a, right_b)):

        @pl.when(at == r)
        def _(first=first, second=second):
            first[...] = part[:half].astype(low)
            second[...] = part[half:].astype(low)

    normed = normalize(hidden_ref[0].astype(jnp.float32))
    gain = jnp.sum(part * normed, axis=0, keepdims=True)

    @pl.when(at == 0)
    def _():
        gain_acc[...] = gain

    @pl.when(at > 0)
    def _():
        gain_acc[...] += gain

    @pl.when(at == RING - 1)
    def _():
        lines = [
            gain_acc[...],
            mlp_ref[...],
            jnp.concatenate([query_ref[...]] * BLOCKS, axis=1),
            jnp.concatenate([key_ref[...]] * BLOCKS, axis=1),
            jnp.zeros((HEAD_DIM - 4, width), jnp.float32),
        ]
        turned = jnp.concatenate(lines, axis=0).T.astype(low)
        first_core = core_ref[0] == 0
        for pair in range(8):
            first = turned[pair * 256 : pair * 256 + 128]
            second = turned[pair * 256 + 128 : (pair + 1) * 256]
            keep_ref[pair] = jnp.where(first_core, first, second)
            give_ref[pair] = jnp.where(first_core, second, first)


def last_part(core_at, grads, weights, hidden_all, mlp_part, query_part, key_part):
    _, rows, width = hidden_all.shape
    block = pl.BlockSpec((rows, width), lambda r: (0, 0))
    small = pl.BlockSpec((rows // 2, width), lambda r: (0, 0))
    whole = jax.ShapeDtypeStruct((rows, width), low)
    part = jax.ShapeDtypeStruct((rows // 2, width), low)
    row = pl.BlockSpec((1, HEAD_DIM), lambda r: (0, 0))
    half = pl.BlockSpec((8, 128, HEAD_DIM), lambda r: (0, 0, 0))
    return pl.pallas_call(
        last_kernel,
        grid=(RING,),
        in_specs=[
            pl.BlockSpec(memory_space=pltpu.SMEM),
            pl.BlockSpec((1, rows, 1024), lambda r: (r, 0, 0)),
            pl.BlockSpec((width, 1024), lambda r: (0, 0)),
            pl.BlockSpec((1, rows, width), lambda r: (r, 0, 0)),
            pl.BlockSpec((1, width), lambda r: (0, 0)),
            row,
            row,
        ],
        out_specs=(block,) + (small,) * 6 + (half, half),
        out_shape=(whole,) + (part,) * 6
        + (jax.ShapeDtypeStruct((8, 128, HEAD_DIM), low),) * 2,
        scratch_shapes=[pltpu.VMEM((1, width), jnp.float32)],
        compiler_params=pltpu.CompilerParams(vmem_limit_bytes=VMEM_LIMIT),
        cost_estimate=pl.CostEstimate(flops=1024, bytes_accessed=1024, transcendentals=0),
    )(core_at[None], grads, weights, hidden_all, mlp_part, query_part, key_part)


def arrange_kernel(at_ref, own_ref, other_ref, out_ref):
    y_at, x_at, core_at = at_ref[0], at_ref[1], at_ref[2]
    for dy in range(RING):
        for dx in range(2):
            first = ((y_at - dy + RING) & 3) * 4 + (x_at ^ dx) * 2
            own = pl.multiple_of((first + core_at) * 128, 128)
            other = pl.multiple_of((first + 1 - core_at) * 128, 128)
            out_ref[pl.ds(own, 128), :] = own_ref[dy, dx]
            out_ref[pl.ds(other, 128), :] = other_ref[dy, dx]


def gather_by_permutes(pairs, y_at, x_at, core_at):
    own = jnp.stack(pairs)
    other = shift(own, "core", 1, 2)
    whole = pl.BlockSpec(memory_space=pltpu.VMEM)
    return pl.pallas_call(
        arrange_kernel,
        in_specs=[pl.BlockSpec(memory_space=pltpu.SMEM), whole, whole],
        out_specs=whole,
        out_shape=jax.ShapeDtypeStruct((BLOCKS * 128, own.shape[3]), own.dtype),
        compiler_params=pltpu.CompilerParams(vmem_limit_bytes=VMEM_LIMIT),
        cost_estimate=pl.CostEstimate(flops=1024, bytes_accessed=1024, transcendentals=0),
    )(jnp.stack([y_at, x_at, core_at]), own, other)


def pair_sums_kernel(keep_ref, come_ref, gains_keep, gains_come, out_ref):
    f32 = jnp.float32
    wide = keep_ref.shape[2]
    out_ref[0, :, :wide] = (keep_ref[0].astype(f32) + come_ref[0].astype(f32)).astype(low)
    out_ref[0, :, wide:] = (gains_keep[0].astype(f32) + gains_come[0].astype(f32)).astype(low)


def pair_sums(keep, come, gains_keep, gains_come):
    blocks, rows, wide = keep.shape
    large = pl.BlockSpec((1, rows, wide), lambda i: (i, 0, 0))
    small = pl.BlockSpec((1, rows, HEAD_DIM), lambda i: (i, 0, 0))
    return pl.pallas_call(
        pair_sums_kernel,
        grid=(blocks,),
        in_specs=[large, large, small, small],
        out_specs=pl.BlockSpec((1, rows, wide + HEAD_DIM), lambda i: (i, 0, 0)),
        out_shape=jax.ShapeDtypeStruct((blocks, rows, wide + HEAD_DIM), low),
        compiler_params=pltpu.CompilerParams(vmem_limit_bytes=VMEM_LIMIT),
        cost_estimate=pl.CostEstimate(flops=1024, bytes_accessed=1024, transcendentals=0),
    )(keep, come, gains_keep, gains_come)


def to_heads(send):
    return lax.all_to_all(send, GROUP_AXES, 0, 0, tiled=True)


def after(value, *others):
    return lax.optimization_barrier((value, others))[0]


def ring_blocks(values):
    half = values.shape[0] // 2
    left = shift(values, "z", 1)
    right = shift(values, "z", 3)
    opposite = jnp.concatenate(
        [shift(left[:half], "z", 1), shift(right[half:], "z", 3)], axis=0
    )
    return [values, left, opposite, right]


def together(*values):
    return lax.optimization_barrier(values)


def place(z_at, blocks, widths, chunk=None, summed=False):
    rows = blocks[0].shape[0]
    whole = pl.BlockSpec(memory_space=pltpu.VMEM)
    shapes = [RING * part for part in widths] + [HEAD_DIM] * summed

    def kernel(z_ref, *refs):
        ins, outs = refs[:RING], refs[RING:]
        for r in range(RING):
            slot = (z_ref[0] - r + RING) & 3
            start = 0
            for turn in range(widths[0] // chunk if chunk else 1):
                for out, part in zip(outs, widths):
                    size = chunk or part
                    at = pl.multiple_of(slot * part + turn * size, 128)
                    out[:, pl.ds(at, size)] = ins[r][:, start : start + size].astype(jnp.float32)
                    start += size
            if summed:
                columns = ins[r][:, start : start + HEAD_DIM].astype(jnp.float32)
                outs[-1][...] = columns if r == 0 else outs[-1][...] + columns

    return pl.pallas_call(
        kernel,
        in_specs=[pl.BlockSpec(memory_space=pltpu.SMEM)] + [whole] * RING,
        out_specs=tuple(whole for _ in shapes),
        out_shape=tuple(jax.ShapeDtypeStruct((rows, part), jnp.float32) for part in shapes),
        compiler_params=pltpu.CompilerParams(vmem_limit_bytes=VMEM_LIMIT),
        cost_estimate=pl.CostEstimate(flops=1024, bytes_accessed=1024, transcendentals=0),
    )(z_at[None], *blocks)


def send_back(block, r):
    return shift(block, "z", -r)


def local(
    hidden_in,
    cotangent,
    segment_ids,
    positions,
    attn_gain,
    query_gain,
    key_gain,
    query_weight,
    key_weight,
    value_weight,
    out_weight,
    mlp_gain,
    gate_weight,
    up_weight,
    down_weight,
):
    f32 = jnp.float32
    rows, width = hidden_in.shape
    ring_rows = RING * rows
    z_at = lax.axis_index("z")
    y_at = lax.axis_index("y")
    x_at = lax.axis_index("x_hi")
    core_at = lax.axis_index("core")
    my_index = (y_at * 2 + x_at) * 2 + core_at

    def columns(weight):
        part = weight.shape[1] // RING
        return lax.dynamic_slice_in_dim(weight, z_at * part, part, 1).astype(low)

    def gather(block):
        return lax.all_gather(block, GROUP_AXES, axis=0, tiled=True)

    own_places = lax.dynamic_slice_in_dim(positions, my_index * rows, rows)
    firsts = positions.reshape(BLOCKS, BLOCK)[:, 0]
    segments = segment_ids.reshape(BLOCKS, BLOCK)[:, 0]
    logical = firsts // BLOCK + jnp.maximum(segments - 1, 0) * 2
    numbers = jnp.arange(BLOCKS, dtype=jnp.int32)
    order = jnp.sum(jnp.where(logical[:, None] == numbers[None, :], numbers[:, None], 0), axis=0)
    notes = gather_z(jnp.concatenate([own_places, order, jnp.zeros((112,), jnp.int32)])[None])
    places = notes[:, :rows]
    order = lax.dynamic_index_in_dim(notes, y_at, 0, keepdims=False)[rows : rows + BLOCKS]

    gains = jnp.pad(
        jnp.stack([attn_gain, mlp_gain], axis=1).astype(low), ((0, 0), (0, HEAD_DIM - 2))
    )
    first_weights = gather(
        jnp.concatenate(
            [columns(query_weight), columns(key_weight), columns(value_weight), gains], axis=1
        )
    )
    out_columns = columns(out_weight)
    out_come = shift(out_columns, "x_hi", 1, 2)
    out_pairs = jnp.stack([out_columns, out_come])
    out_pairs = [out_pairs] + [shift(out_pairs, "y", r) for r in range(1, RING)]

    hidden_own = after(hidden_in, notes, out_come)
    hidden_left = shift(hidden_own, "z", 1)
    hidden_right = shift(hidden_own, "z", 3)
    gate_columns, up_columns, down_columns, hidden_left, hidden_right, out_pairs = together(
        gate_weight, up_weight, down_weight, hidden_left, hidden_right, out_pairs
    )
    out_slice = gather_by_permutes(out_pairs, y_at, x_at, core_at)
    gate_columns, up_columns = columns(gate_columns), columns(up_columns)
    mlp_columns = []
    for start in range(0, gate_columns.shape[1], FF_STEP):
        mlp_columns.append(gate_columns[:, start : start + FF_STEP])
        mlp_columns.append(up_columns[:, start : start + FF_STEP])
    mlp_weights = gather(jnp.concatenate(mlp_columns + [columns(down_columns)], axis=1))
    half = rows // 2
    hidden_blocks = [
        hidden_own,
        hidden_left,
        shift(hidden_left[:half], "z", 1),
        shift(hidden_right[half:], "z", 3),
        hidden_right,
    ]
    out_slice = after(out_slice, *hidden_blocks)
    out_left = shift(out_slice, "z", 1)
    out_right = shift(out_slice, "z", 3)
    frequency = rope_base ** (-2.0 * jnp.arange(HEAD_DIM // 2, dtype=f32) / HEAD_DIM)
    angles = places.astype(f32)[:, :, None] * frequency[None, None, :]
    cosine = jnp.cos(angles)
    sine = jnp.sin(angles)
    cosine = jnp.concatenate([cosine, cosine], axis=-1)
    sine = jnp.concatenate([-sine, sine], axis=-1)
    query_row = query_gain[None]
    key_row = key_gain[None]

    hidden_all, first_in, qkv_pre, send, gain_rows = first_part(
        hidden_blocks, first_weights, cosine, sine, query_row, key_row
    )
    attn_scale = gain_rows[0:1]
    mlp_scale = gain_rows[1:2]
    out_top = shift(out_left[: width // 2], "z", 1)
    out_bottom = shift(out_right[width // 2 :], "z", 3)
    arrived, out_left, out_right, out_top, out_bottom = together(
        to_heads(send), out_left, out_right, out_top, out_bottom
    )
    other_pair = shift(arrived[:, 1], "core", 1, 2)
    head_mixed, head_mixed_t, head_logs = attention_forward(order, core_at, arrived, other_pair)
    cot_own = after(cotangent, head_mixed)
    cot_left = shift(cot_own, "z", 1)
    cot_right = shift(cot_own, "z", 3)

    mixed_arrived, cot_left, cot_right = together(to_heads(head_mixed), cot_left, cot_right)
    mixed_blocks = [mixed_arrived[:4]] + [
        shift(mixed_arrived[4 * (RING - j) : 4 * (RING - j) + 4], "z", j) for j in range(1, RING)
    ]
    out_opposite = jnp.concatenate([out_top, out_bottom], axis=0)
    out_weights = [out_slice, out_left, out_opposite, out_right]
    mixed_blocks, out_weights = together(mixed_blocks, out_weights)
    middle, second_in, cot_opposite = together(
        *middle_part(mixed_blocks, out_weights, hidden_in, mlp_scale), shift(cot_own, "z", 2)
    )
    hidden = hidden_in.astype(f32)
    left = shift(second_in, "z", 1)
    right = shift(second_in, "z", 3)
    *held, own_part = mlp_blocks(0, [second_in], [cot_own], mlp_weights, ())
    held, own_part, left, right, second_in = together(held, own_part, left, right, second_in)
    opposite = shift(second_in, "z", 2)
    *held, left_part, right_part = mlp_blocks(
        1, [left, right], [cot_left, cot_right], mlp_weights, held
    )
    left_back = send_back(left_part, 1)
    right_back = send_back(right_part, 3)
    held, opposite = together(held, opposite)
    *held, opposite_part = mlp_blocks(1, [opposite], [cot_opposite], mlp_weights, held)
    opposite_back = send_back(opposite_part, 2)
    inner, both_grad, second_all, cot_all = held

    def pair_sum(keep, come):
        return (keep.astype(f32) + come.astype(f32)).astype(low)

    def to_owners(pair):
        return lax.all_to_all(pair, ("y", "x_hi"), 0, 0, tiled=True)

    def add_up(terms):
        return jnp.sum(terms.astype(f32), axis=0).astype(low)

    def over_x(share):
        return share, shift(share, "x_lo", 1, 2)

    def over_z(pair):
        share = pair_sum(*pair)
        return [share] + [shift(share, "z", r) for r in range(1, RING)]

    both_term = lax.dot_general(
        second_all.reshape(ring_rows, width),
        both_grad.reshape(ring_rows, 3072),
        contract_first,
        preferred_element_type=f32,
    ).astype(low)
    left_back, right_back, opposite_back, both_term, inner = together(
        left_back, right_back, opposite_back, both_term, inner
    )
    both_share = lax.psum_scatter(both_term, GROUP_AXES, scatter_dimension=0, tiled=True)

    middle_grad, own_low, mlp_gain_part, *grad_blocks = middle_back(
        (own_part, left_back, right_back, opposite_back),
        out_weights,
        middle,
        cotangent,
        mlp_scale,
    )
    grad_blocks = [grad_blocks[0]] + [shift(grad_blocks[RING - r], "z", r) for r in range(1, RING)]
    grad_blocks, own_low, inner = together(grad_blocks, own_low, inner)
    down_keep, down_give = pair_grad(core_at, [cot_all], inner)
    head_grads = to_heads(jnp.concatenate(grad_blocks, axis=0))
    low_left = shift(own_low, "z", 1)
    low_right = shift(own_low, "z", 3)
    down_sum = pair_sum(down_keep, shift(down_give, "core", 1, 2))
    mlp_own, mlp_opposite, mlp_left, mlp_right = mlp_out_part(
        after(inner, down_give), mlp_weights
    )
    head_grads, down_sum, low_left, low_right, own_low, mlp_opposite, mlp_left, mlp_right = together(
        head_grads, down_sum, low_left, low_right, own_low, mlp_opposite, mlp_left, mlp_right
    )
    mlp_left = send_back(mlp_left, 1)
    mlp_right = send_back(mlp_right, 3)
    down_terms = to_owners(down_sum)

    query_grad, grad_keep, grad_give = attention_backward(
        order, core_at, arrived, other_pair, head_grads, head_mixed_t, head_logs
    )
    query_grad, grad_keep, grad_give, mlp_left, mlp_right, own_low, mlp_opposite = together(
        query_grad, grad_keep, grad_give, mlp_left, mlp_right, own_low, mlp_opposite
    )
    low_opposite = shift(own_low, "z", 2)
    grads_send = lax.dynamic_update_slice_in_dim(
        query_grad, pair_sum(grad_keep, shift(grad_give, "core", 1, 2))[:, None], 1, 1
    )
    grads_send, down_terms = together(grads_send, down_terms)
    returned = to_heads(grads_send)
    down_pair = over_x(add_up(down_terms))
    out_term = pair_grad(
        core_at, [own_low, low_left, low_opposite, low_right], mixed_arrived, by_heads=True
    )
    mlp_opposite = send_back(mlp_opposite, 2)
    returned, both_share, out_term = together(returned, both_share, out_term)
    out_share = lax.psum_scatter(out_term, GROUP_AXES, scatter_dimension=0, tiled=True)
    both_pair = over_x(both_share)
    qkv_grad, qkv_keep, qkv_give, query_gain_part, key_gain_part = first_back(
        core_at, returned, qkv_pre, cosine, sine, query_row, key_row, first_in
    )
    qkv_grad, qkv_give, down_pair, both_pair = together(qkv_grad, qkv_give, down_pair, both_pair)
    both_sum = pair_sum(*both_pair)
    both_left = shift(both_sum, "z", 1)
    both_right = shift(both_sum, "z", 3)
    down_blocks = over_z(down_pair)
    qkv_come = shift(qkv_give, "core", 1, 2)
    *first_parts, gains_keep, gains_give = last_part(
        core_at,
        qkv_grad,
        first_weights,
        hidden_all,
        mlp_gain_part,
        query_gain_part,
        key_gain_part,
    )
    first_parts, gains_give, qkv_come, mlp_opposite, both_left, both_right, both_sum = together(
        first_parts, gains_give, qkv_come, mlp_opposite, both_left, both_right, both_sum
    )
    gains_come = shift(gains_give, "core", 1, 2)
    first_own, left_a, left_b, first_top, first_bottom, right_a, right_b = first_parts
    first_top = shift(first_top, "z", 3)
    first_bottom = shift(first_bottom, "z", 1)
    qkv_terms = to_owners(pair_sums(qkv_keep, qkv_come, gains_keep, gains_come))
    first_left = send_back(jnp.concatenate([pair_sum(left_a, first_top), left_b], axis=0), 1)
    first_right = send_back(jnp.concatenate([right_a, pair_sum(right_b, first_bottom)], axis=0), 3)
    both_opposite = shift(both_sum, "z", 2)
    qkv_terms, down_blocks, both_opposite = together(qkv_terms, down_blocks, both_opposite)
    out_pair = over_x(out_share)
    qkv_share = add_up(qkv_terms)
    both_blocks = [both_sum, both_left, both_opposite, both_right]
    qkv_pair = over_x(qkv_share)
    output = (
        middle
        + mlp_own.astype(f32)
        + mlp_left.astype(f32)
        + mlp_right.astype(f32)
        + mlp_opposite.astype(f32)
    ).astype(low)
    first_grad = first_own.astype(f32) + first_left.astype(f32) + first_right.astype(f32)
    hidden_rms = inverse_rms(hidden)
    own_norm = hidden * hidden_rms
    scaled_first = first_grad * attn_scale
    hidden_grad = (
        middle_grad
        + hidden_rms
        * (scaled_first - own_norm * jnp.mean(scaled_first * own_norm, axis=-1, keepdims=True))
    ).astype(low)

    (down_grad_out,) = place(z_at, down_blocks, (1536,))
    gate_grad_out, up_grad_out = place(z_at, both_blocks, (1536, 1536), chunk=FF_STEP)
    (out_grad_out,) = place(z_at, over_z(out_pair), (512,))
    query_grad_out, key_grad_out, value_grad_out, gain_sum = place(
        z_at, over_z(qkv_pair), (512, 256, 256), summed=True
    )
    gain_sum = gain_sum[:, :4].T

    return (
        output,
        hidden_grad,
        gain_sum[0],
        gain_sum[2],
        gain_sum[3],
        query_grad_out,
        key_grad_out,
        value_grad_out,
        out_grad_out,
        gain_sum[1],
        gate_grad_out,
        up_grad_out,
        down_grad_out,
    )


def solution(mesh):
    fine = Mesh(mesh.devices.reshape(2, 4, 4, 2, 2), ALL_AXES)
    rep = ("x_lo", "z")
    row = P(ALL_AXES, None)
    part = P(GROUP_AXES)
    weight = P(GROUP_AXES, None)
    in_specs = (
        row,
        row,
        P(rep),
        P(rep),
        part,
        P(),
        P(),
        weight,
        weight,
        weight,
        weight,
        part,
        weight,
        weight,
        weight,
    )
    out_specs = (
        row,
        row,
        part,
        P(),
        P(),
        weight,
        weight,
        weight,
        weight,
        part,
        weight,
        weight,
        weight,
    )
    return jax.shard_map(local, mesh=fine, in_specs=in_specs, out_specs=out_specs, check_vma=False)
```

```python
import functools

import jax
import jax.numpy as jnp
from jax import lax
from jax.experimental import pallas as pl
from jax.experimental.pallas import tpu as pltpu
from jax.sharding import Mesh
from jax.sharding import PartitionSpec as P

HEAD_DIM = 128
RING = 4
BLOCK = 256
BLOCKS = 16
TILE = 512
TILES = 8
PROMPT_TILES = 6
FF_STEP = 512
VMEM_LIMIT = 60 * 1024 * 1024

norm_eps = 1e-06
rope_base = 1000000.0
score_scale = HEAD_DIM ** (-0.5)
score_scale_log2 = score_scale * 1.4426950408889634
contract_first = (((0,), (0,)), ((), ()))
contract_last = (((1,), (1,)), ((), ()))
GROUP_AXES = ("y", "x_hi", "core")
ALL_AXES = ("x_lo", "z", "y", "x_hi", "core")
low = jnp.bfloat16


def inverse_rms(values):
    return lax.rsqrt(jnp.mean(values * values, axis=-1, keepdims=True) + norm_eps)


def normalize(values):
    return values * inverse_rms(values)


def shift(values, axis, by, size=RING):
    return lax.ppermute(values, axis, [(i, (i + by) % size) for i in range(size)])


def gather_z(values):
    return jnp.concatenate(
        [values, shift(values, "z", 1), shift(values, "z", 2), shift(values, "z", 3)], axis=0
    )


def forward_kernel(
    order, core, own_a, own_b, other_a, other_b, mixed_ref, mixed_t_ref, log_ref, k_all, v_t, acc, total
):
    tile = pl.program_id(0)
    start = tile * TILE

    def take(keys, values):
        for half in range(2):
            rows = pl.ds(pl.multiple_of(start + half * BLOCK, BLOCK), BLOCK)
            k_all[rows, :] = keys[half]
            v_t[tile, :, half * BLOCK : (half + 1) * BLOCK] = (
                values[half].astype(jnp.float32).T.astype(low)
            )

    @pl.when(core[0] == 0)
    def _():
        take((own_a[0, 1], own_b[0, 1]), (other_a[0], other_b[0]))

    @pl.when(core[0] == 1)
    def _():
        take((other_a[0], other_b[0]), (own_a[0, 1], own_b[0, 1]))

    queries = jnp.concatenate([own_a[0, 0], own_b[0, 0]], axis=0)
    acc[...] = jnp.zeros_like(acc)
    total[...] = jnp.zeros_like(total)

    def chunk(at, masked):
        keys = k_all[pl.ds(pl.multiple_of(at * TILE, TILE), TILE), :]
        scores = lax.dot_general(keys, queries, contract_last, preferred_element_type=jnp.float32)
        weights = jnp.exp2(scores * score_scale_log2)
        if masked:
            key_row = lax.broadcasted_iota(jnp.int32, (TILE, TILE), 0)
            query_row = lax.broadcasted_iota(jnp.int32, (TILE, TILE), 1)
            weights = jnp.where(key_row <= query_row, weights, 0.0)
        total[...] += jnp.sum(weights, axis=0, keepdims=True)
        acc[...] += jnp.dot(v_t[at], weights.astype(low), preferred_element_type=jnp.float32)

    @pl.loop(0, jnp.minimum(tile, PROMPT_TILES))
    def _(at):
        chunk(at, False)

    chunk(tile, True)
    mixed_t = acc[...] / total[...]
    mixed_t_ref[0] = mixed_t
    log_ref[0] = jnp.log2(total[...])
    mixed = mixed_t.T.astype(low)
    mixed_ref[order[2 * tile]] = mixed[:BLOCK]
    mixed_ref[order[2 * tile + 1]] = mixed[BLOCK:]


def tile_specs(lead):
    return [
        pl.BlockSpec(
            (1, *lead, BLOCK, HEAD_DIM),
            functools.partial(
                lambda half, tile, order, core: (order[2 * tile + half],) + (0,) * (len(lead) + 2),
                half,
            ),
        )
        for half in range(2)
    ]


def attention_forward(order, core_at, arrived, other):
    whole = pl.BlockSpec(memory_space=pltpu.VMEM)
    turned = pl.BlockSpec((1, HEAD_DIM, TILE), lambda tile, order, core: (tile, 0, 0))
    line = pl.BlockSpec((1, 1, TILE), lambda tile, order, core: (tile, 0, 0))
    return pl.pallas_call(
        forward_kernel,
        out_shape=(
            jax.ShapeDtypeStruct((BLOCKS, BLOCK, HEAD_DIM), low),
            jax.ShapeDtypeStruct((TILES, HEAD_DIM, TILE), jnp.float32),
            jax.ShapeDtypeStruct((TILES, 1, TILE), jnp.float32),
        ),
        grid_spec=pltpu.PrefetchScalarGridSpec(
            num_scalar_prefetch=2,
            grid=(TILES,),
            in_specs=tile_specs((2,)) + tile_specs(()),
            out_specs=(whole, turned, line),
            scratch_shapes=[
                pltpu.VMEM((BLOCKS * BLOCK, HEAD_DIM), low),
                pltpu.VMEM((TILES, HEAD_DIM, TILE), low),
                pltpu.VMEM((HEAD_DIM, TILE), jnp.float32),
                pltpu.VMEM((1, TILE), jnp.float32),
            ],
        ),
        compiler_params=pltpu.CompilerParams(vmem_limit_bytes=VMEM_LIMIT),
        cost_estimate=pl.CostEstimate(
            flops=1024, bytes_accessed=1024, transcendentals=0
        ),
    )(order, core_at[None], arrived, arrived, other, other)


def backward_kernel(
    order, core, own_a, own_b, other_a, other_b, grad_a, grad_b, mixed_t_ref, log_ref,
    q_out, keep_out, give_out, k_all, v_all, k_t, q_acc, k_acc, v_acc,
):
    tile = pl.program_id(0)
    start = tile * TILE

    def take(keys, values):
        for half in range(2):
            rows = pl.ds(pl.multiple_of(start + half * BLOCK, BLOCK), BLOCK)
            k_all[rows, :] = keys[half]
            v_all[rows, :] = values[half]
            k_t[tile, :, half * BLOCK : (half + 1) * BLOCK] = (
                keys[half].astype(jnp.float32).T.astype(low)
            )

    @pl.when(core[0] == 0)
    def _():
        take((own_a[0, 1], own_b[0, 1]), (other_a[0], other_b[0]))

    @pl.when(core[0] == 1)
    def _():
        take((other_a[0], other_b[0]), (own_a[0, 1], own_b[0, 1]))

    rows = pl.ds(pl.multiple_of(start, TILE), TILE)
    k_acc[rows, :] = jnp.zeros((TILE, HEAD_DIM), jnp.float32)
    v_acc[rows, :] = jnp.zeros((TILE, HEAD_DIM), jnp.float32)
    queries = jnp.concatenate([own_a[0, 0], own_b[0, 0]], axis=0)
    grads = jnp.concatenate([grad_a[0], grad_b[0]], axis=0)
    grads_t = grads.astype(jnp.float32).T
    shared = jnp.sum(grads_t * mixed_t_ref[0], axis=0, keepdims=True)
    logs = log_ref[0]
    q_acc[...] = jnp.zeros_like(q_acc)

    def chunk(at, masked):
        rows = pl.ds(pl.multiple_of(at * TILE, TILE), TILE)
        scores = lax.dot_general(
            k_all[rows, :], queries, contract_last, preferred_element_type=jnp.float32
        )
        probs = jnp.exp2(scores * score_scale_log2 - logs)
        if masked:
            key_row = lax.broadcasted_iota(jnp.int32, (TILE, TILE), 0)
            query_row = lax.broadcasted_iota(jnp.int32, (TILE, TILE), 1)
            probs = jnp.where(key_row <= query_row, probs, 0.0)
        prob_grads = lax.dot_general(
            v_all[rows, :], grads, contract_last, preferred_element_type=jnp.float32
        )
        score_grads = (probs * (prob_grads - shared)).astype(low)
        v_acc[rows, :] += jnp.dot(probs.astype(low), grads, preferred_element_type=jnp.float32)
        k_acc[rows, :] += jnp.dot(score_grads, queries, preferred_element_type=jnp.float32)
        q_acc[...] += jnp.dot(k_t[at], score_grads, preferred_element_type=jnp.float32)

    @pl.loop(0, jnp.minimum(tile, PROMPT_TILES))
    def _(at):
        chunk(at, False)

    chunk(tile, True)
    query_grad = (q_acc[...] * score_scale).T.astype(low)
    q_out[order[2 * tile], 0] = query_grad[:BLOCK]
    q_out[order[2 * tile + 1], 0] = query_grad[BLOCK:]

    def give(keep_acc, keep_scale, give_acc, give_scale):
        for at in range(BLOCKS):
            rows = slice(at * BLOCK, (at + 1) * BLOCK)
            keep_out[order[at]] = (keep_acc[rows, :] * keep_scale).astype(low)
            give_out[order[at]] = (give_acc[rows, :] * give_scale).astype(low)

    @pl.when((tile == TILES - 1) & (core[0] == 0))
    def _():
        give(k_acc, score_scale, v_acc, 1.0)

    @pl.when((tile == TILES - 1) & (core[0] == 1))
    def _():
        give(v_acc, 1.0, k_acc, score_scale)


def attention_backward(order, core_at, arrived, other, grads, mixed_t, logs):
    whole = pl.BlockSpec(memory_space=pltpu.VMEM)
    rows = BLOCKS * BLOCK
    turned = pl.BlockSpec((1, HEAD_DIM, TILE), lambda tile, order, core: (tile, 0, 0))
    line = pl.BlockSpec((1, 1, TILE), lambda tile, order, core: (tile, 0, 0))
    return pl.pallas_call(
        backward_kernel,
        out_shape=(jax.ShapeDtypeStruct((BLOCKS, 2, BLOCK, HEAD_DIM), low),)
        + (jax.ShapeDtypeStruct((BLOCKS, BLOCK, HEAD_DIM), low),) * 2,
        grid_spec=pltpu.PrefetchScalarGridSpec(
            num_scalar_prefetch=2,
            grid=(TILES,),
            in_specs=tile_specs((2,)) + tile_specs(()) + tile_specs(()) + [turned, line],
            out_specs=(whole, whole, whole),
            scratch_shapes=[
                pltpu.VMEM((rows, HEAD_DIM), low),
                pltpu.VMEM((rows, HEAD_DIM), low),
                pltpu.VMEM((TILES, HEAD_DIM, TILE), low),
                pltpu.VMEM((HEAD_DIM, TILE), jnp.float32),
                pltpu.VMEM((rows, HEAD_DIM), jnp.float32),
                pltpu.VMEM((rows, HEAD_DIM), jnp.float32),
            ],
        ),
        compiler_params=pltpu.CompilerParams(vmem_limit_bytes=VMEM_LIMIT),
        cost_estimate=pl.CostEstimate(
            flops=1024, bytes_accessed=1024, transcendentals=0
        ),
    )(order, core_at[None], arrived, arrived, other, other, grads, grads, mixed_t, logs)


def mlp_kernel(parts, cot_parts, *refs):
    second_refs, cot_refs = refs[:parts], refs[parts : parts + cot_parts]
    both_weight_ref, down_ref = refs[parts + cot_parts : parts + cot_parts + 2]
    count = refs[-1].shape[0] // BLOCK
    inner_ref, both_ref, second_out, cot_out = refs[-5 - count : -1 - count]
    grad_refs, acc = refs[-1 - count : -1], refs[-1]
    at = pl.program_id(0)
    step = down_ref.shape[1]
    rows, width = acc.shape

    @pl.when(at == 0)
    def _():
        for ins, out in ((second_refs, second_out), (cot_refs, cot_out)):
            start = 0
            for part in ins:
                size = part.shape[0]
                out[start // BLOCK, start % BLOCK : start % BLOCK + size, :] = part[...]
                start += size

    second = second_out[...].reshape(rows, width)
    both_act = jnp.dot(second, both_weight_ref[...], preferred_element_type=jnp.float32)
    inner_grad = jnp.dot(
        cot_out[...].reshape(rows, width), down_ref[...], preferred_element_type=jnp.float32
    )
    gate_act = both_act[:, :step]
    up_act = both_act[:, step:]
    sigmoid = 1.0 / (1.0 + jnp.exp(-gate_act))
    silu = gate_act * sigmoid
    inner_ref[...] = (silu * up_act).astype(low).reshape(inner_ref.shape)
    gate_grad = (inner_grad * up_act * (sigmoid * (1.0 + gate_act * (1.0 - sigmoid)))).astype(low)
    both_grad = jnp.concatenate([gate_grad, (inner_grad * silu).astype(low)], axis=1)
    both_ref[:, :, pl.ds(pl.multiple_of(at * 2 * step, 2 * step), 2 * step)] = both_grad.reshape(
        count, BLOCK, 2 * step
    )
    part = lax.dot_general(
        both_grad, both_weight_ref[...], contract_last, preferred_element_type=jnp.float32
    )
    last = pl.num_programs(0) - 1

    @pl.when(at == 0)
    def _():
        acc[...] = part

    @pl.when((at > 0) & (at < last))
    def _():
        acc[...] += part

    @pl.when(at == last)
    def _():
        total = (acc[...] + part).astype(low)
        for block, grad in enumerate(grad_refs):
            grad[...] = total[block * BLOCK : (block + 1) * BLOCK]


def mlp_blocks(place_at, seconds, cots, weights, held):
    rows = sum(second.shape[0] for second in seconds)
    width = seconds[0].shape[1]
    count = rows // BLOCK
    hidden_width = weights.shape[1] // 3
    step = FF_STEP
    steps = hidden_width // step
    ins = [
        pl.BlockSpec(value.shape, lambda c: (0, 0), pipeline_mode=pl.Buffered(1))
        for value in (*seconds, *cots)
    ]
    kept = pl.BlockSpec((count, BLOCK, step), lambda c: (place_at, 0, c))
    kept_both = pl.BlockSpec((count, BLOCK, 2 * hidden_width), lambda c: (place_at, 0, 0))
    kept_rows = pl.BlockSpec((count, BLOCK, width), lambda c: (place_at, 0, 0))
    rows_shape = jax.ShapeDtypeStruct((RING, BLOCK, width), low)
    return pl.pallas_call(
        functools.partial(mlp_kernel, len(seconds), len(cots)),
        grid=(steps,),
        in_specs=ins
        + [
            pl.BlockSpec((width, 2 * step), lambda c: (0, c)),
            pl.BlockSpec((width, step), lambda c: (0, 2 * steps + c)),
        ]
        + [pl.BlockSpec(memory_space=pl.ANY)] * len(held),
        out_specs=(kept, kept_both, kept_rows, kept_rows)
        + (pl.BlockSpec((BLOCK, width), lambda c: (0, 0)),) * count,
        out_shape=(
            jax.ShapeDtypeStruct((RING, BLOCK, hidden_width), low),
            jax.ShapeDtypeStruct((RING, BLOCK, 2 * hidden_width), low),
            rows_shape,
            rows_shape,
        )
        + (jax.ShapeDtypeStruct((BLOCK, width), low),) * count,
        scratch_shapes=[pltpu.VMEM((rows, width), jnp.float32)],
        input_output_aliases={len(ins) + 2 + i: i for i in range(len(held))},
        compiler_params=pltpu.CompilerParams(vmem_limit_bytes=VMEM_LIMIT),
        cost_estimate=pl.CostEstimate(
            flops=2 * 5 * rows * width * hidden_width,
            bytes_accessed=2 * 3 * width * hidden_width,
            transcendentals=rows * hidden_width,
        ),
    )(*seconds, *cots, weights, weights, *held)


def mlp_out_kernel(inner_ref, weight_ref, *outs):
    inner = inner_ref[...].reshape(RING * BLOCK, inner_ref.shape[2])
    part = lax.dot_general(
        inner, weight_ref[...], contract_last, preferred_element_type=jnp.float32
    ).astype(low)
    for block, out in enumerate(outs):
        out[...] = part[block * BLOCK : (block + 1) * BLOCK]


def mlp_out_part(inner, weights):
    _, rows, hidden_width = inner.shape
    width = weights.shape[0]
    steps = 4
    return pl.pallas_call(
        mlp_out_kernel,
        grid=(steps,),
        in_specs=[
            pl.BlockSpec(inner.shape, lambda d: (0, 0, 0)),
            pl.BlockSpec((width // steps, hidden_width), lambda d: (d, 2)),
        ],
        out_specs=(pl.BlockSpec((rows, width // steps), lambda d: (0, d)),) * RING,
        out_shape=(jax.ShapeDtypeStruct((rows, width), low),) * RING,
        compiler_params=pltpu.CompilerParams(vmem_limit_bytes=VMEM_LIMIT),
        cost_estimate=pl.CostEstimate(flops=1024, bytes_accessed=1024, transcendentals=0),
    )(inner, weights)


def pair_grad(core_at, lefts, right, by_heads=False):
    width = lefts[0].shape[-1]
    outs = 512 if by_heads else right.shape[2]
    rows = RING * BLOCK

    def kernel(core_ref, *refs):
        left_refs = refs[: len(lefts)]
        right_ref, keep_ref = refs[len(lefts) : len(lefts) + 2]
        give_ref = refs[-1]
        if by_heads:
            all_ref = refs[-1]

            @pl.when(pl.program_id(0) == 0)
            def _():
                for r in range(RING):
                    for head in range(4):
                        all_ref[
                            r * BLOCK : (r + 1) * BLOCK, head * HEAD_DIM : (head + 1) * HEAD_DIM
                        ] = right_ref[4 * r + head]

            values = all_ref[...]
        else:
            values = right_ref[...].reshape(rows, outs)
        inputs = [ref[...].reshape(-1, 256) for ref in left_refs]
        inputs = inputs[0] if len(inputs) == 1 else jnp.concatenate(inputs, axis=0)
        term = lax.dot_general(
            inputs, values, contract_first, preferred_element_type=jnp.float32
        ).astype(low)
        if by_heads:
            keep_ref[...] = term
            return
        first_core = core_ref[0] == 0
        keep_ref[0] = jnp.where(first_core, term[:128], term[128:])
        give_ref[0] = jnp.where(first_core, term[128:], term[:128])

    def columns(value):
        lead = value.shape[:-1]
        return pl.BlockSpec((*lead, 256), lambda i: (0,) * len(lead) + (i,))

    half = pl.BlockSpec((1, 128, outs), lambda i: (i, 0, 0))
    return pl.pallas_call(
        kernel,
        grid=(width // 256,),
        in_specs=[pl.BlockSpec(memory_space=pltpu.SMEM)]
        + [columns(value) for value in lefts]
        + [pl.BlockSpec(right.shape, lambda i: (0, 0, 0))],
        out_specs=pl.BlockSpec((256, outs), lambda i: (i, 0)) if by_heads else (half, half),
        out_shape=jax.ShapeDtypeStruct((width, outs), low)
        if by_heads
        else (jax.ShapeDtypeStruct((width // 256, 128, outs), low),) * 2,
        scratch_shapes=[pltpu.VMEM((rows, 512), low)] * by_heads,
        compiler_params=pltpu.CompilerParams(vmem_limit_bytes=VMEM_LIMIT),
        cost_estimate=pl.CostEstimate(flops=1024, bytes_accessed=1024, transcendentals=0),
    )(core_at[None], *lefts, right)


def middle_kernel(*refs):
    mixed_refs, weight_refs = refs[:RING], refs[RING : 2 * RING]
    hidden_ref, gain_ref, middle_ref, second_ref = refs[2 * RING :]
    at = pl.program_id(0)
    step = weight_refs[0].shape[0]
    columns = pl.ds(pl.multiple_of(at * step, step), step)
    total = hidden_ref[:, columns].astype(jnp.float32)
    for mixed, weight in zip(mixed_refs, weight_refs):
        rows = jnp.concatenate([mixed[head] for head in range(4)], axis=1)
        total += lax.dot_general(
            rows, weight[...], contract_last, preferred_element_type=jnp.float32
        )
    middle_ref[:, columns] = total

    @pl.when(at == pl.num_programs(0) - 1)
    def _():
        second_ref[...] = (normalize(middle_ref[...]) * gain_ref[...]).astype(low)


def middle_part(mixed_blocks, weights, hidden, gain):
    rows, width = hidden.shape
    steps = 4
    whole = pl.BlockSpec((rows, width), lambda d: (0, 0))
    return pl.pallas_call(
        middle_kernel,
        grid=(steps,),
        in_specs=[pl.BlockSpec((4, rows, HEAD_DIM), lambda d: (0, 0, 0))] * RING
        + [pl.BlockSpec((width // steps, 512), lambda d: (d, 0))] * RING
        + [whole, pl.BlockSpec((1, width), lambda d: (0, 0))],
        out_specs=(whole, whole),
        out_shape=(
            jax.ShapeDtypeStruct((rows, width), jnp.float32),
            jax.ShapeDtypeStruct((rows, width), low),
        ),
        compiler_params=pltpu.CompilerParams(vmem_limit_bytes=32 * 1024 * 1024),
        cost_estimate=pl.CostEstimate(flops=1024, bytes_accessed=1024, transcendentals=0),
    )(*mixed_blocks, *weights, hidden, gain)


def middle_back_kernel(*refs):
    parts, weight_refs = refs[:RING], refs[RING : 2 * RING]
    middle_ref, cot_ref, gain_ref, grad_ref, low_ref, gain_out, *rest = refs[2 * RING :]
    outs, accs = rest[:RING], rest[RING:]
    at = pl.program_id(0)
    step = weight_refs[0].shape[0]

    @pl.when(at == 0)
    def _():
        second_grad = sum(part[...].astype(jnp.float32) for part in parts)
        middle = middle_ref[...]
        scale = inverse_rms(middle)
        normed = middle * scale
        gain_out[...] = jnp.sum(second_grad * normed, axis=0, keepdims=True)
        scaled = second_grad * gain_ref[...]
        grad = cot_ref[...].astype(jnp.float32) + scale * (
            scaled - normed * jnp.mean(scaled * normed, axis=-1, keepdims=True)
        )
        grad_ref[...] = grad
        low_ref[...] = grad.astype(low)
        for acc in accs:
            acc[...] = jnp.zeros_like(acc)

    rows = low_ref[:, pl.ds(pl.multiple_of(at * step, step), step)]
    for weight, acc in zip(weight_refs, accs):
        acc[...] += jnp.dot(rows, weight[...], preferred_element_type=jnp.float32)

    @pl.when(at == pl.num_programs(0) - 1)
    def _():
        for out, acc in zip(outs, accs):
            for head in range(4):
                out[head] = acc[:, head * HEAD_DIM : (head + 1) * HEAD_DIM].astype(low)


def middle_back(parts, weights, middle, cot, gain):
    rows, width = middle.shape
    steps = 4
    whole = pl.BlockSpec((rows, width), lambda d: (0, 0))
    row = pl.BlockSpec((1, width), lambda d: (0, 0))
    heads = pl.BlockSpec((4, rows, HEAD_DIM), lambda d: (0, 0, 0))
    return pl.pallas_call(
        middle_back_kernel,
        grid=(steps,),
        in_specs=[whole] * RING
        + [pl.BlockSpec((width // steps, 512), lambda d: (d, 0))] * RING
        + [whole, whole, row],
        out_specs=(whole, whole, row) + (heads,) * RING,
        out_shape=(
            jax.ShapeDtypeStruct((rows, width), jnp.float32),
            jax.ShapeDtypeStruct((rows, width), low),
            jax.ShapeDtypeStruct((1, width), jnp.float32),
        )
        + (jax.ShapeDtypeStruct((4, rows, HEAD_DIM), low),) * RING,
        scratch_shapes=[pltpu.VMEM((rows, 512), jnp.float32)] * RING,
        compiler_params=pltpu.CompilerParams(vmem_limit_bytes=VMEM_LIMIT),
        cost_estimate=pl.CostEstimate(flops=1024, bytes_accessed=1024, transcendentals=0),
    )(*parts, *weights, middle, cot, gain)


def first_kernel(
    own_ref, left_ref, top_ref, bottom_ref, right_ref, weight_ref, gains_ref, cos_ref, sin_ref,
    query_gain, key_gain, hidden_ref, first_ref, pre_ref, send_ref, gain_out,
):
    at = pl.program_id(0)
    half = top_ref.shape[0]

    @pl.when(at == 0)
    def _():
        gain_out[...] = gains_ref[...].astype(jnp.float32).T[:8]
        hidden_ref[0] = own_ref[...]

    @pl.when(at == 1)
    def _():
        hidden_ref[0] = left_ref[...]

    @pl.when(at == 2)
    def _():
        hidden_ref[0, :half] = top_ref[...]
        hidden_ref[0, half:] = bottom_ref[...]

    @pl.when(at == 3)
    def _():
        hidden_ref[0] = right_ref[...]

    first = (normalize(hidden_ref[0].astype(jnp.float32)) * gain_out[0:1]).astype(low)
    first_ref[0] = first
    pre = jnp.dot(first, weight_ref[...], preferred_element_type=jnp.float32)
    pre_ref[0] = pre
    cosine = cos_ref[0]
    sine = sin_ref[0]

    def turned(head, gain):
        values = normalize(pre[:, head * HEAD_DIM : (head + 1) * HEAD_DIM]) * gain
        return (values * cosine + pltpu.roll(values, HEAD_DIM // 2, 1) * sine).astype(low)

    for head in range(4):
        send_ref[head, 0] = turned(head, query_gain[...])
    for head in range(2):
        send_ref[2 * head, 1] = turned(4 + head, key_gain[...])
        send_ref[2 * head + 1, 1] = pre[:, (6 + head) * HEAD_DIM : (7 + head) * HEAD_DIM].astype(low)


def first_part(blocks, weights, cosine, sine, query_gain, key_gain):
    rows, width = blocks[0].shape
    row = pl.BlockSpec((1, HEAD_DIM), lambda r: (0, 0))
    turn = pl.BlockSpec((1, rows, HEAD_DIM), lambda r: (r, 0, 0))
    return pl.pallas_call(
        first_kernel,
        grid=(RING,),
        in_specs=[pl.BlockSpec(block.shape, lambda r: (0, 0)) for block in blocks]
        + [
            pl.BlockSpec((width, 1024), lambda r: (0, 0)),
            pl.BlockSpec((width, HEAD_DIM), lambda r: (0, 8)),
            turn,
            turn,
            row,
            row,
        ],
        out_specs=(
            pl.BlockSpec((1, rows, width), lambda r: (r, 0, 0)),
            pl.BlockSpec((1, rows, width), lambda r: (r, 0, 0)),
            pl.BlockSpec((1, rows, 1024), lambda r: (r, 0, 0)),
            pl.BlockSpec((4, 2, rows, HEAD_DIM), lambda r: (r, 0, 0, 0)),
            pl.BlockSpec((8, width), lambda r: (0, 0)),
        ),
        out_shape=(
            jax.ShapeDtypeStruct((RING, rows, width), low),
            jax.ShapeDtypeStruct((RING, rows, width), low),
            jax.ShapeDtypeStruct((RING, rows, 1024), jnp.float32),
            jax.ShapeDtypeStruct((BLOCKS, 2, rows, HEAD_DIM), low),
            jax.ShapeDtypeStruct((8, width), jnp.float32),
        ),
        compiler_params=pltpu.CompilerParams(vmem_limit_bytes=VMEM_LIMIT),
        cost_estimate=pl.CostEstimate(
            flops=2 * RING * rows * width * 1024,
            bytes_accessed=20 * 1024 * 1024,
            transcendentals=0,
        ),
    )(*blocks, weights, weights, cosine, sine, query_gain, key_gain)


def first_back_kernel(
    core_ref, back_ref, pre_ref, cos_ref, sin_ref, query_gain, key_gain, first_ref,
    grad_ref, keep_ref, give_ref, query_sum, key_sum, all_grads,
):
    at = pl.program_id(0)
    rows = grad_ref.shape[1]
    cosine = cos_ref[0]
    sine = sin_ref[0]

    @pl.when(at == 0)
    def _():
        query_sum[...] = jnp.zeros_like(query_sum)
        key_sum[...] = jnp.zeros_like(key_sum)

    def back(grads, head, gain, sums):
        columns = slice(head * HEAD_DIM, (head + 1) * HEAD_DIM)
        values = pre_ref[0, :, columns]
        grads = grads.astype(jnp.float32)
        grads = grads * cosine - pltpu.roll(grads, HEAD_DIM // 2, 1) * sine
        scale = inverse_rms(values)
        normed = values * scale
        sums[...] += jnp.sum(grads * normed, axis=0, keepdims=True)
        scaled = grads * gain
        out = scale * (scaled - normed * jnp.mean(scaled * normed, axis=-1, keepdims=True))
        grad_ref[0, :, columns] = out.astype(low)

    for head in range(4):
        back(back_ref[head, 0], head, query_gain[...], query_sum)
    for head in range(2):
        back(back_ref[2 * head, 1], 4 + head, key_gain[...], key_sum)
        grad_ref[0, :, (6 + head) * HEAD_DIM : (7 + head) * HEAD_DIM] = back_ref[2 * head + 1, 1]
    all_grads[pl.ds(pl.multiple_of(at * rows, rows), rows), :] = grad_ref[0]

    @pl.when(at == RING - 1)
    def _():
        grads = all_grads[...]
        first_core = core_ref[0] == 0
        for pair in range(8):
            inputs = first_ref[:, :, pair * 256 : (pair + 1) * 256].reshape(RING * rows, 256)
            term = lax.dot_general(
                inputs, grads, contract_first, preferred_element_type=jnp.float32
            ).astype(low)
            keep_ref[pair] = jnp.where(first_core, term[:128], term[128:])
            give_ref[pair] = jnp.where(first_core, term[128:], term[:128])


def first_back(core_at, returned, pre, cosine, sine, query_gain, key_gain, first_in):
    _, rows, width = first_in.shape
    row = pl.BlockSpec((1, HEAD_DIM), lambda r: (0, 0))
    turn = pl.BlockSpec((1, rows, HEAD_DIM), lambda r: (r, 0, 0))
    wide = pl.BlockSpec((1, rows, 1024), lambda r: (r, 0, 0))
    half = pl.BlockSpec((8, 128, 1024), lambda r: (0, 0, 0))
    return pl.pallas_call(
        first_back_kernel,
        grid=(RING,),
        in_specs=[
            pl.BlockSpec(memory_space=pltpu.SMEM),
            pl.BlockSpec((4, 2, rows, HEAD_DIM), lambda r: (r, 0, 0, 0)),
            wide,
            turn,
            turn,
            row,
            row,
            pl.BlockSpec((RING, rows, width), lambda r: (0, 0, 0)),
        ],
        out_specs=(wide, half, half, row, row),
        out_shape=(
            jax.ShapeDtypeStruct((RING, rows, 1024), low),
            jax.ShapeDtypeStruct((8, 128, 1024), low),
            jax.ShapeDtypeStruct((8, 128, 1024), low),
            jax.ShapeDtypeStruct((1, HEAD_DIM), jnp.float32),
            jax.ShapeDtypeStruct((1, HEAD_DIM), jnp.float32),
        ),
        scratch_shapes=[pltpu.VMEM((RING * rows, 1024), low)],
        compiler_params=pltpu.CompilerParams(vmem_limit_bytes=VMEM_LIMIT),
        cost_estimate=pl.CostEstimate(flops=1024, bytes_accessed=1024, transcendentals=0),
    )(core_at[None], returned, pre, cosine, sine, query_gain, key_gain, first_in)


def last_kernel(
    core_ref, grad_ref, weight_ref, hidden_ref, mlp_ref, query_ref, key_ref,
    own_ref, left_a, left_b, top_ref, bottom_ref, right_a, right_b, keep_ref, give_ref, gain_acc,
):
    at = pl.program_id(0)
    width = hidden_ref.shape[2]
    part = lax.dot_general(
        grad_ref[0], weight_ref[...], contract_last, preferred_element_type=jnp.float32
    )
    half = top_ref.shape[0]
    @pl.when(at == 0)
    def _():
        own_ref[...] = part.astype(low)

    for r, first, second in ((1, left_a, left_b), (2, top_ref, bottom_ref), (3, right_a, right_b)):

        @pl.when(at == r)
        def _(first=first, second=second):
            first[...] = part[:half].astype(low)
            second[...] = part[half:].astype(low)

    normed = normalize(hidden_ref[0].astype(jnp.float32))
    gain = jnp.sum(part * normed, axis=0, keepdims=True)

    @pl.when(at == 0)
    def _():
        gain_acc[...] = gain

    @pl.when(at > 0)
    def _():
        gain_acc[...] += gain

    @pl.when(at == RING - 1)
    def _():
        lines = [
            gain_acc[...],
            mlp_ref[...],
            jnp.concatenate([query_ref[...]] * BLOCKS, axis=1),
            jnp.concatenate([key_ref[...]] * BLOCKS, axis=1),
            jnp.zeros((HEAD_DIM - 4, width), jnp.float32),
        ]
        turned = jnp.concatenate(lines, axis=0).T.astype(low)
        first_core = core_ref[0] == 0
        for pair in range(8):
            first = turned[pair * 256 : pair * 256 + 128]
            second = turned[pair * 256 + 128 : (pair + 1) * 256]
            keep_ref[pair] = jnp.where(first_core, first, second)
            give_ref[pair] = jnp.where(first_core, second, first)


def last_part(core_at, grads, weights, hidden_all, mlp_part, query_part, key_part):
    _, rows, width = hidden_all.shape
    block = pl.BlockSpec((rows, width), lambda r: (0, 0))
    small = pl.BlockSpec((rows // 2, width), lambda r: (0, 0))
    whole = jax.ShapeDtypeStruct((rows, width), low)
    part = jax.ShapeDtypeStruct((rows // 2, width), low)
    row = pl.BlockSpec((1, HEAD_DIM), lambda r: (0, 0))
    half = pl.BlockSpec((8, 128, HEAD_DIM), lambda r: (0, 0, 0))
    return pl.pallas_call(
        last_kernel,
        grid=(RING,),
        in_specs=[
            pl.BlockSpec(memory_space=pltpu.SMEM),
            pl.BlockSpec((1, rows, 1024), lambda r: (r, 0, 0)),
            pl.BlockSpec((width, 1024), lambda r: (0, 0)),
            pl.BlockSpec((1, rows, width), lambda r: (r, 0, 0)),
            pl.BlockSpec((1, width), lambda r: (0, 0)),
            row,
            row,
        ],
        out_specs=(block,) + (small,) * 6 + (half, half),
        out_shape=(whole,) + (part,) * 6
        + (jax.ShapeDtypeStruct((8, 128, HEAD_DIM), low),) * 2,
        scratch_shapes=[pltpu.VMEM((1, width), jnp.float32)],
        compiler_params=pltpu.CompilerParams(vmem_limit_bytes=VMEM_LIMIT),
        cost_estimate=pl.CostEstimate(flops=1024, bytes_accessed=1024, transcendentals=0),
    )(core_at[None], grads, weights, hidden_all, mlp_part, query_part, key_part)


def arrange_kernel(at_ref, own_ref, other_ref, out_ref):
    y_at, x_at, core_at = at_ref[0], at_ref[1], at_ref[2]
    for dy in range(RING):
        for dx in range(2):
            first = ((y_at - dy + RING) & 3) * 4 + (x_at ^ dx) * 2
            own = pl.multiple_of((first + core_at) * 128, 128)
            other = pl.multiple_of((first + 1 - core_at) * 128, 128)
            out_ref[pl.ds(own, 128), :] = own_ref[dy, dx]
            out_ref[pl.ds(other, 128), :] = other_ref[dy, dx]


def gather_by_permutes(pairs, y_at, x_at, core_at):
    own = jnp.stack(pairs)
    other = shift(own, "core", 1, 2)
    whole = pl.BlockSpec(memory_space=pltpu.VMEM)
    return pl.pallas_call(
        arrange_kernel,
        in_specs=[pl.BlockSpec(memory_space=pltpu.SMEM), whole, whole],
        out_specs=whole,
        out_shape=jax.ShapeDtypeStruct((BLOCKS * 128, own.shape[3]), own.dtype),
        compiler_params=pltpu.CompilerParams(vmem_limit_bytes=VMEM_LIMIT),
        cost_estimate=pl.CostEstimate(flops=1024, bytes_accessed=1024, transcendentals=0),
    )(jnp.stack([y_at, x_at, core_at]), own, other)


def pair_sums_kernel(keep_ref, come_ref, gains_keep, gains_come, out_ref):
    f32 = jnp.float32
    wide = keep_ref.shape[2]
    out_ref[0, :, :wide] = (keep_ref[0].astype(f32) + come_ref[0].astype(f32)).astype(low)
    out_ref[0, :, wide:] = (gains_keep[0].astype(f32) + gains_come[0].astype(f32)).astype(low)


def pair_sums(keep, come, gains_keep, gains_come):
    blocks, rows, wide = keep.shape
    large = pl.BlockSpec((1, rows, wide), lambda i: (i, 0, 0))
    small = pl.BlockSpec((1, rows, HEAD_DIM), lambda i: (i, 0, 0))
    return pl.pallas_call(
        pair_sums_kernel,
        grid=(blocks,),
        in_specs=[large, large, small, small],
        out_specs=pl.BlockSpec((1, rows, wide + HEAD_DIM), lambda i: (i, 0, 0)),
        out_shape=jax.ShapeDtypeStruct((blocks, rows, wide + HEAD_DIM), low),
        compiler_params=pltpu.CompilerParams(vmem_limit_bytes=VMEM_LIMIT),
        cost_estimate=pl.CostEstimate(flops=1024, bytes_accessed=1024, transcendentals=0),
    )(keep, come, gains_keep, gains_come)


def to_heads(send):
    return lax.all_to_all(send, GROUP_AXES, 0, 0, tiled=True)


def after(value, *others):
    return lax.optimization_barrier((value, others))[0]


def ring_blocks(values):
    half = values.shape[0] // 2
    left = shift(values, "z", 1)
    right = shift(values, "z", 3)
    opposite = jnp.concatenate(
        [shift(left[:half], "z", 1), shift(right[half:], "z", 3)], axis=0
    )
    return [values, left, opposite, right]


def together(*values):
    return lax.optimization_barrier(values)


def place(z_at, blocks, widths, chunk=None, summed=False):
    rows = blocks[0].shape[0]
    whole = pl.BlockSpec(memory_space=pltpu.VMEM)
    shapes = [RING * part for part in widths] + [HEAD_DIM] * summed

    def kernel(z_ref, *refs):
        ins, outs = refs[:RING], refs[RING:]
        for r in range(RING):
            slot = (z_ref[0] - r + RING) & 3
            start = 0
            for turn in range(widths[0] // chunk if chunk else 1):
                for out, part in zip(outs, widths):
                    size = chunk or part
                    at = pl.multiple_of(slot * part + turn * size, 128)
                    out[:, pl.ds(at, size)] = ins[r][:, start : start + size].astype(jnp.float32)
                    start += size
            if summed:
                columns = ins[r][:, start : start + HEAD_DIM].astype(jnp.float32)
                outs[-1][...] = columns if r == 0 else outs[-1][...] + columns

    return pl.pallas_call(
        kernel,
        in_specs=[pl.BlockSpec(memory_space=pltpu.SMEM)] + [whole] * RING,
        out_specs=tuple(whole for _ in shapes),
        out_shape=tuple(jax.ShapeDtypeStruct((rows, part), jnp.float32) for part in shapes),
        compiler_params=pltpu.CompilerParams(vmem_limit_bytes=VMEM_LIMIT),
        cost_estimate=pl.CostEstimate(flops=1024, bytes_accessed=1024, transcendentals=0),
    )(z_at[None], *blocks)


def send_back(block, r):
    return shift(block, "z", -r)


def local(
    hidden_in,
    cotangent,
    segment_ids,
    positions,
    attn_gain,
    query_gain,
    key_gain,
    query_weight,
    key_weight,
    value_weight,
    out_weight,
    mlp_gain,
    gate_weight,
    up_weight,
    down_weight,
):
    f32 = jnp.float32
    rows, width = hidden_in.shape
    ring_rows = RING * rows
    z_at = lax.axis_index("z")
    y_at = lax.axis_index("y")
    x_at = lax.axis_index("x_hi")
    core_at = lax.axis_index("core")
    my_index = (y_at * 2 + x_at) * 2 + core_at

    def columns(weight):
        part = weight.shape[1] // RING
        return lax.dynamic_slice_in_dim(weight, z_at * part, part, 1).astype(low)

    def gather(block):
        return lax.all_gather(block, GROUP_AXES, axis=0, tiled=True)

    own_places = lax.dynamic_slice_in_dim(positions, my_index * rows, rows)
    firsts = positions.reshape(BLOCKS, BLOCK)[:, 0]
    segments = segment_ids.reshape(BLOCKS, BLOCK)[:, 0]
    logical = firsts // BLOCK + jnp.maximum(segments - 1, 0) * 2
    numbers = jnp.arange(BLOCKS, dtype=jnp.int32)
    order = jnp.sum(jnp.where(logical[:, None] == numbers[None, :], numbers[:, None], 0), axis=0)
    notes = gather_z(jnp.concatenate([own_places, order, jnp.zeros((112,), jnp.int32)])[None])
    places = notes[:, :rows]
    order = lax.dynamic_index_in_dim(notes, y_at, 0, keepdims=False)[rows : rows + BLOCKS]

    gains = jnp.pad(
        jnp.stack([attn_gain, mlp_gain], axis=1).astype(low), ((0, 0), (0, HEAD_DIM - 2))
    )
    first_weights = gather(
        jnp.concatenate(
            [columns(query_weight), columns(key_weight), columns(value_weight), gains], axis=1
        )
    )
    out_columns = columns(out_weight)
    out_come = shift(out_columns, "x_hi", 1, 2)
    out_pairs = jnp.stack([out_columns, out_come])
    out_pairs = [out_pairs] + [shift(out_pairs, "y", r) for r in range(1, RING)]

    hidden_own = after(hidden_in, notes, out_come)
    hidden_left = shift(hidden_own, "z", 1)
    hidden_right = shift(hidden_own, "z", 3)
    gate_columns, up_columns, down_columns, hidden_left, hidden_right, out_pairs = together(
        gate_weight, up_weight, down_weight, hidden_left, hidden_right, out_pairs
    )
    out_slice = gather_by_permutes(out_pairs, y_at, x_at, core_at)
    gate_columns, up_columns = columns(gate_columns), columns(up_columns)
    mlp_columns = []
    for start in range(0, gate_columns.shape[1], FF_STEP):
        mlp_columns.append(gate_columns[:, start : start + FF_STEP])
        mlp_columns.append(up_columns[:, start : start + FF_STEP])
    mlp_weights = gather(jnp.concatenate(mlp_columns + [columns(down_columns)], axis=1))
    half = rows // 2
    hidden_blocks = [
        hidden_own,
        hidden_left,
        shift(hidden_left[:half], "z", 1),
        shift(hidden_right[half:], "z", 3),
        hidden_right,
    ]
    out_slice = after(out_slice, *hidden_blocks)
    out_left = shift(out_slice, "z", 1)
    out_right = shift(out_slice, "z", 3)
    frequency = rope_base ** (-2.0 * jnp.arange(HEAD_DIM // 2, dtype=f32) / HEAD_DIM)
    angles = places.astype(f32)[:, :, None] * frequency[None, None, :]
    cosine = jnp.cos(angles)
    sine = jnp.sin(angles)
    cosine = jnp.concatenate([cosine, cosine], axis=-1)
    sine = jnp.concatenate([-sine, sine], axis=-1)
    query_row = query_gain[None]
    key_row = key_gain[None]

    hidden_all, first_in, qkv_pre, send, gain_rows = first_part(
        hidden_blocks, first_weights, cosine, sine, query_row, key_row
    )
    attn_scale = gain_rows[0:1]
    mlp_scale = gain_rows[1:2]
    out_top = shift(out_left[: width // 2], "z", 1)
    out_bottom = shift(out_right[width // 2 :], "z", 3)
    arrived, out_left, out_right, out_top, out_bottom = together(
        to_heads(send), out_left, out_right, out_top, out_bottom
    )
    other_pair = shift(arrived[:, 1], "core", 1, 2)
    head_mixed, head_mixed_t, head_logs = attention_forward(order, core_at, arrived, other_pair)
    cot_own = after(cotangent, head_mixed)
    cot_left = shift(cot_own, "z", 1)
    cot_right = shift(cot_own, "z", 3)

    cot_top = shift(cot_left[:half], "z", 1)
    cot_bottom = shift(cot_right[half:], "z", 3)
    mixed_arrived, cot_left, cot_right, cot_top, cot_bottom = together(
        to_heads(head_mixed), cot_left, cot_right, cot_top, cot_bottom
    )
    mixed_blocks = [mixed_arrived[:4]] + [
        shift(mixed_arrived[4 * (RING - j) : 4 * (RING - j) + 4], "z", j) for j in range(1, RING)
    ]
    out_opposite = jnp.concatenate([out_top, out_bottom], axis=0)
    out_weights = [out_slice, out_left, out_opposite, out_right]
    mixed_blocks, out_weights = together(mixed_blocks, out_weights)
    middle, second_in = middle_part(mixed_blocks, out_weights, hidden_in, mlp_scale)
    hidden = hidden_in.astype(f32)
    left = shift(second_in, "z", 1)
    right = shift(second_in, "z", 3)
    *held, own_part = mlp_blocks(0, [second_in], [cot_own], mlp_weights, ())
    held, own_part, left, right, second_in = together(held, own_part, left, right, second_in)
    opposite = shift(second_in, "z", 2)
    *held, left_part, right_part = mlp_blocks(
        1, [left, right], [cot_left, cot_right], mlp_weights, held
    )
    left_back = send_back(left_part, 1)
    right_back = send_back(right_part, 3)
    held, opposite = together(held, opposite)
    *held, opposite_part = mlp_blocks(
        1, [opposite], [cot_top, cot_bottom], mlp_weights, held
    )
    opposite_back = send_back(opposite_part, 2)
    inner, both_grad, second_all, cot_all = held

    def pair_sum(keep, come):
        return (keep.astype(f32) + come.astype(f32)).astype(low)

    def to_owners(pair):
        return lax.all_to_all(pair, ("y", "x_hi"), 0, 0, tiled=True)

    def add_up(terms):
        return jnp.sum(terms.astype(f32), axis=0).astype(low)

    def over_x(share):
        return share, shift(share, "x_lo", 1, 2)

    def over_z(pair):
        share = pair_sum(*pair)
        return [share] + [shift(share, "z", r) for r in range(1, RING)]

    both_term = lax.dot_general(
        second_all.reshape(ring_rows, width),
        both_grad.reshape(ring_rows, 3072),
        contract_first,
        preferred_element_type=f32,
    ).astype(low)
    left_back, right_back, opposite_back, both_term, inner = together(
        left_back, right_back, opposite_back, both_term, inner
    )
    both_share = lax.psum_scatter(both_term, GROUP_AXES, scatter_dimension=0, tiled=True)

    middle_grad, own_low, mlp_gain_part, *grad_blocks = middle_back(
        (own_part, left_back, right_back, opposite_back),
        out_weights,
        middle,
        cotangent,
        mlp_scale,
    )
    grad_blocks = [grad_blocks[0]] + [shift(grad_blocks[RING - r], "z", r) for r in range(1, RING)]
    down_keep, down_give = pair_grad(core_at, [cot_all], inner)
    grad_blocks, down_keep, down_give, own_low, inner = together(
        grad_blocks, down_keep, down_give, own_low, inner
    )
    head_grads = to_heads(jnp.concatenate(grad_blocks, axis=0))
    low_left = shift(own_low, "z", 1)
    low_right = shift(own_low, "z", 3)
    down_sum = pair_sum(down_keep, shift(down_give, "core", 1, 2))
    mlp_own, mlp_opposite, mlp_left, mlp_right = mlp_out_part(inner, mlp_weights)
    head_grads, down_sum, low_left, low_right, own_low, mlp_opposite, mlp_left, mlp_right = together(
        head_grads, down_sum, low_left, low_right, own_low, mlp_opposite, mlp_left, mlp_right
    )
    low_opposite = shift(own_low, "z", 2)
    down_terms = to_owners(down_sum)

    query_grad, grad_keep, grad_give = attention_backward(
        order, core_at, arrived, other_pair, head_grads, head_mixed_t, head_logs
    )
    query_grad, grad_keep, grad_give, low_opposite, mlp_opposite, mlp_left, mlp_right = together(
        query_grad, grad_keep, grad_give, low_opposite, mlp_opposite, mlp_left, mlp_right
    )
    mlp_left = send_back(mlp_left, 1)
    mlp_right = send_back(mlp_right, 3)
    mlp_opposite = send_back(mlp_opposite, 2)
    grads_send = lax.dynamic_update_slice_in_dim(
        query_grad, pair_sum(grad_keep, shift(grad_give, "core", 1, 2))[:, None], 1, 1
    )
    grads_send, down_terms = together(grads_send, down_terms)
    returned = to_heads(grads_send)
    down_pair = over_x(add_up(down_terms))
    out_term = pair_grad(
        core_at, [own_low, low_left, low_opposite, low_right], mixed_arrived, by_heads=True
    )
    returned, both_share, out_term, down_pair, mlp_left, mlp_right, mlp_opposite = together(
        returned, both_share, out_term, down_pair, mlp_left, mlp_right, mlp_opposite
    )
    out_share = lax.psum_scatter(out_term, GROUP_AXES, scatter_dimension=0, tiled=True)
    both_pair = over_x(both_share)
    down_blocks = over_z(down_pair)
    qkv_grad, qkv_keep, qkv_give, query_gain_part, key_gain_part = first_back(
        core_at, returned, qkv_pre, cosine, sine, query_row, key_row, first_in
    )
    qkv_grad, qkv_give, down_blocks, both_pair = together(
        qkv_grad, qkv_give, down_blocks, both_pair
    )
    both_sum = pair_sum(*both_pair)
    both_left = shift(both_sum, "z", 1)
    both_right = shift(both_sum, "z", 3)
    qkv_come = shift(qkv_give, "core", 1, 2)
    *first_parts, gains_keep, gains_give = last_part(
        core_at,
        qkv_grad,
        first_weights,
        hidden_all,
        mlp_gain_part,
        query_gain_part,
        key_gain_part,
    )
    first_parts, gains_give, qkv_come, both_left, both_right, both_sum = together(
        first_parts, gains_give, qkv_come, both_left, both_right, both_sum
    )
    gains_come = shift(gains_give, "core", 1, 2)
    first_own, left_a, left_b, first_top, first_bottom, right_a, right_b = first_parts
    first_top = shift(first_top, "z", 3)
    first_bottom = shift(first_bottom, "z", 1)
    qkv_terms = to_owners(pair_sums(qkv_keep, qkv_come, gains_keep, gains_come))
    first_left = send_back(jnp.concatenate([pair_sum(left_a, first_top), left_b], axis=0), 1)
    first_right = send_back(jnp.concatenate([right_a, pair_sum(right_b, first_bottom)], axis=0), 3)
    both_opposite = shift(both_sum, "z", 2)
    qkv_terms, first_left, first_right, both_opposite = together(
        qkv_terms, first_left, first_right, both_opposite
    )
    qkv_share = add_up(qkv_terms)
    both_blocks = [both_sum, both_left, both_opposite, both_right]
    qkv_pair, out_share = together(over_x(qkv_share), out_share)
    out_pair = over_x(out_share)
    output = (
        middle
        + mlp_own.astype(f32)
        + mlp_left.astype(f32)
        + mlp_right.astype(f32)
        + mlp_opposite.astype(f32)
    ).astype(low)
    first_grad = first_own.astype(f32) + first_left.astype(f32) + first_right.astype(f32)
    hidden_rms = inverse_rms(hidden)
    own_norm = hidden * hidden_rms
    scaled_first = first_grad * attn_scale
    hidden_grad = (
        middle_grad
        + hidden_rms
        * (scaled_first - own_norm * jnp.mean(scaled_first * own_norm, axis=-1, keepdims=True))
    ).astype(low)

    (down_grad_out,) = place(z_at, down_blocks, (1536,))
    gate_grad_out, up_grad_out = place(z_at, both_blocks, (1536, 1536), chunk=FF_STEP)
    (out_grad_out,) = place(z_at, over_z(out_pair), (512,))
    query_grad_out, key_grad_out, value_grad_out, gain_sum = place(
        z_at, over_z(qkv_pair), (512, 256, 256), summed=True
    )
    gain_sum = gain_sum[:, :4].T

    return (
        output,
        hidden_grad,
        gain_sum[0],
        gain_sum[2],
        gain_sum[3],
        query_grad_out,
        key_grad_out,
        value_grad_out,
        out_grad_out,
        gain_sum[1],
        gate_grad_out,
        up_grad_out,
        down_grad_out,
    )


def solution(mesh):
    fine = Mesh(mesh.devices.reshape(2, 4, 4, 2, 2), ALL_AXES)
    rep = ("x_lo", "z")
    row = P(ALL_AXES, None)
    part = P(GROUP_AXES)
    weight = P(GROUP_AXES, None)
    in_specs = (
        row,
        row,
        P(rep),
        P(rep),
        part,
        P(),
        P(),
        weight,
        weight,
        weight,
        weight,
        part,
        weight,
        weight,
        weight,
    )
    out_specs = (
        row,
        row,
        part,
        P(),
        P(),
        weight,
        weight,
        weight,
        weight,
        part,
        weight,
        weight,
        weight,
    )
    return jax.shard_map(local, mesh=fine, in_specs=in_specs, out_specs=out_specs, check_vma=False)
```

```python
import functools

import jax
import jax.numpy as jnp
from jax import lax
from jax.experimental import pallas as pl
from jax.experimental.pallas import tpu as pltpu
from jax.sharding import Mesh
from jax.sharding import PartitionSpec as P

HEAD_DIM = 128
RING = 4
BLOCK = 256
BLOCKS = 16
TILE = 512
TILES = 8
PROMPT_TILES = 6
FF_STEP = 512
VMEM_LIMIT = 60 * 1024 * 1024

norm_eps = 1e-06
rope_base = 1000000.0
score_scale = HEAD_DIM ** (-0.5)
score_scale_log2 = score_scale * 1.4426950408889634
contract_first = (((0,), (0,)), ((), ()))
contract_last = (((1,), (1,)), ((), ()))
GROUP_AXES = ("y", "x_hi", "core")
ALL_AXES = ("x_lo", "z", "y", "x_hi", "core")
low = jnp.bfloat16


def inverse_rms(values):
    return lax.rsqrt(jnp.mean(values * values, axis=-1, keepdims=True) + norm_eps)


def normalize(values):
    return values * inverse_rms(values)


def shift(values, axis, by, size=RING):
    return lax.ppermute(values, axis, [(i, (i + by) % size) for i in range(size)])


def gather_z(values):
    return jnp.concatenate(
        [values, shift(values, "z", 1), shift(values, "z", 2), shift(values, "z", 3)], axis=0
    )


def forward_kernel(
    order, core, own_a, own_b, other_a, other_b, mixed_ref, mixed_t_ref, log_ref, k_all, v_t, acc, total
):
    tile = pl.program_id(0)
    start = tile * TILE

    def take(keys, values):
        for half in range(2):
            rows = pl.ds(pl.multiple_of(start + half * BLOCK, BLOCK), BLOCK)
            k_all[rows, :] = keys[half]
            v_t[tile, :, half * BLOCK : (half + 1) * BLOCK] = (
                values[half].astype(jnp.float32).T.astype(low)
            )

    @pl.when(core[0] == 0)
    def _():
        take((own_a[0, 1], own_b[0, 1]), (other_a[0], other_b[0]))

    @pl.when(core[0] == 1)
    def _():
        take((other_a[0], other_b[0]), (own_a[0, 1], own_b[0, 1]))

    queries = jnp.concatenate([own_a[0, 0], own_b[0, 0]], axis=0)
    acc[...] = jnp.zeros_like(acc)
    total[...] = jnp.zeros_like(total)

    def chunk(at, masked):
        keys = k_all[pl.ds(pl.multiple_of(at * TILE, TILE), TILE), :]
        scores = lax.dot_general(keys, queries, contract_last, preferred_element_type=jnp.float32)
        weights = jnp.exp2(scores * score_scale_log2)
        if masked:
            key_row = lax.broadcasted_iota(jnp.int32, (TILE, TILE), 0)
            query_row = lax.broadcasted_iota(jnp.int32, (TILE, TILE), 1)
            weights = jnp.where(key_row <= query_row, weights, 0.0)
        total[...] += jnp.sum(weights, axis=0, keepdims=True)
        acc[...] += jnp.dot(v_t[at], weights.astype(low), preferred_element_type=jnp.float32)

    @pl.loop(0, jnp.minimum(tile, PROMPT_TILES))
    def _(at):
        chunk(at, False)

    chunk(tile, True)
    mixed_t = acc[...] / total[...]
    mixed_t_ref[0] = mixed_t
    log_ref[0] = jnp.log2(total[...])
    mixed = mixed_t.T.astype(low)
    mixed_ref[order[2 * tile]] = mixed[:BLOCK]
    mixed_ref[order[2 * tile + 1]] = mixed[BLOCK:]


def tile_specs(lead):
    return [
        pl.BlockSpec(
            (1, *lead, BLOCK, HEAD_DIM),
            functools.partial(
                lambda half, tile, order, core: (order[2 * tile + half],) + (0,) * (len(lead) + 2),
                half,
            ),
        )
        for half in range(2)
    ]


def attention_forward(order, core_at, arrived, other):
    whole = pl.BlockSpec(memory_space=pltpu.VMEM)
    turned = pl.BlockSpec((1, HEAD_DIM, TILE), lambda tile, order, core: (tile, 0, 0))
    line = pl.BlockSpec((1, 1, TILE), lambda tile, order, core: (tile, 0, 0))
    return pl.pallas_call(
        forward_kernel,
        out_shape=(
            jax.ShapeDtypeStruct((BLOCKS, BLOCK, HEAD_DIM), low),
            jax.ShapeDtypeStruct((TILES, HEAD_DIM, TILE), jnp.float32),
            jax.ShapeDtypeStruct((TILES, 1, TILE), jnp.float32),
        ),
        grid_spec=pltpu.PrefetchScalarGridSpec(
            num_scalar_prefetch=2,
            grid=(TILES,),
            in_specs=tile_specs((2,)) + tile_specs(()),
            out_specs=(whole, turned, line),
            scratch_shapes=[
                pltpu.VMEM((BLOCKS * BLOCK, HEAD_DIM), low),
                pltpu.VMEM((TILES, HEAD_DIM, TILE), low),
                pltpu.VMEM((HEAD_DIM, TILE), jnp.float32),
                pltpu.VMEM((1, TILE), jnp.float32),
            ],
        ),
        compiler_params=pltpu.CompilerParams(vmem_limit_bytes=VMEM_LIMIT),
        cost_estimate=pl.CostEstimate(
            flops=1024, bytes_accessed=1024, transcendentals=0
        ),
    )(order, core_at[None], arrived, arrived, other, other)


def backward_kernel(
    order, core, own_a, own_b, other_a, other_b, grad_a, grad_b, mixed_t_ref, log_ref,
    q_out, keep_out, give_out, k_all, v_all, k_t, q_acc, k_acc, v_acc,
):
    tile = pl.program_id(0)
    start = tile * TILE

    def take(keys, values):
        for half in range(2):
            rows = pl.ds(pl.multiple_of(start + half * BLOCK, BLOCK), BLOCK)
            k_all[rows, :] = keys[half]
            v_all[rows, :] = values[half]
            k_t[tile, :, half * BLOCK : (half + 1) * BLOCK] = (
                keys[half].astype(jnp.float32).T.astype(low)
            )

    @pl.when(core[0] == 0)
    def _():
        take((own_a[0, 1], own_b[0, 1]), (other_a[0], other_b[0]))

    @pl.when(core[0] == 1)
    def _():
        take((other_a[0], other_b[0]), (own_a[0, 1], own_b[0, 1]))

    rows = pl.ds(pl.multiple_of(start, TILE), TILE)
    k_acc[rows, :] = jnp.zeros((TILE, HEAD_DIM), jnp.float32)
    v_acc[rows, :] = jnp.zeros((TILE, HEAD_DIM), jnp.float32)
    queries = jnp.concatenate([own_a[0, 0], own_b[0, 0]], axis=0)
    grads = jnp.concatenate([grad_a[0], grad_b[0]], axis=0)
    grads_t = grads.astype(jnp.float32).T
    shared = jnp.sum(grads_t * mixed_t_ref[0], axis=0, keepdims=True)
    logs = log_ref[0]
    q_acc[...] = jnp.zeros_like(q_acc)

    def chunk(at, masked):
        rows = pl.ds(pl.multiple_of(at * TILE, TILE), TILE)
        scores = lax.dot_general(
            k_all[rows, :], queries, contract_last, preferred_element_type=jnp.float32
        )
        probs = jnp.exp2(scores * score_scale_log2 - logs)
        if masked:
            key_row = lax.broadcasted_iota(jnp.int32, (TILE, TILE), 0)
            query_row = lax.broadcasted_iota(jnp.int32, (TILE, TILE), 1)
            probs = jnp.where(key_row <= query_row, probs, 0.0)
        prob_grads = lax.dot_general(
            v_all[rows, :], grads, contract_last, preferred_element_type=jnp.float32
        )
        score_grads = (probs * (prob_grads - shared)).astype(low)
        v_acc[rows, :] += jnp.dot(probs.astype(low), grads, preferred_element_type=jnp.float32)
        k_acc[rows, :] += jnp.dot(score_grads, queries, preferred_element_type=jnp.float32)
        q_acc[...] += jnp.dot(k_t[at], score_grads, preferred_element_type=jnp.float32)

    @pl.loop(0, jnp.minimum(tile, PROMPT_TILES))
    def _(at):
        chunk(at, False)

    chunk(tile, True)
    query_grad = (q_acc[...] * score_scale).T.astype(low)
    q_out[order[2 * tile], 0] = query_grad[:BLOCK]
    q_out[order[2 * tile + 1], 0] = query_grad[BLOCK:]

    def give(keep_acc, keep_scale, give_acc, give_scale):
        for at in range(BLOCKS):
            rows = slice(at * BLOCK, (at + 1) * BLOCK)
            keep_out[order[at]] = (keep_acc[rows, :] * keep_scale).astype(low)
            give_out[order[at]] = (give_acc[rows, :] * give_scale).astype(low)

    @pl.when((tile == TILES - 1) & (core[0] == 0))
    def _():
        give(k_acc, score_scale, v_acc, 1.0)

    @pl.when((tile == TILES - 1) & (core[0] == 1))
    def _():
        give(v_acc, 1.0, k_acc, score_scale)


def attention_backward(order, core_at, arrived, other, grads, mixed_t, logs):
    whole = pl.BlockSpec(memory_space=pltpu.VMEM)
    rows = BLOCKS * BLOCK
    turned = pl.BlockSpec((1, HEAD_DIM, TILE), lambda tile, order, core: (tile, 0, 0))
    line = pl.BlockSpec((1, 1, TILE), lambda tile, order, core: (tile, 0, 0))
    return pl.pallas_call(
        backward_kernel,
        out_shape=(jax.ShapeDtypeStruct((BLOCKS, 2, BLOCK, HEAD_DIM), low),)
        + (jax.ShapeDtypeStruct((BLOCKS, BLOCK, HEAD_DIM), low),) * 2,
        grid_spec=pltpu.PrefetchScalarGridSpec(
            num_scalar_prefetch=2,
            grid=(TILES,),
            in_specs=tile_specs((2,)) + tile_specs(()) + tile_specs(()) + [turned, line],
            out_specs=(whole, whole, whole),
            scratch_shapes=[
                pltpu.VMEM((rows, HEAD_DIM), low),
                pltpu.VMEM((rows, HEAD_DIM), low),
                pltpu.VMEM((TILES, HEAD_DIM, TILE), low),
                pltpu.VMEM((HEAD_DIM, TILE), jnp.float32),
                pltpu.VMEM((rows, HEAD_DIM), jnp.float32),
                pltpu.VMEM((rows, HEAD_DIM), jnp.float32),
            ],
        ),
        compiler_params=pltpu.CompilerParams(vmem_limit_bytes=VMEM_LIMIT),
        cost_estimate=pl.CostEstimate(
            flops=1024, bytes_accessed=1024, transcendentals=0
        ),
    )(order, core_at[None], arrived, arrived, other, other, grads, grads, mixed_t, logs)


def mlp_kernel(parts, cot_parts, *refs):
    second_refs, cot_refs = refs[:parts], refs[parts : parts + cot_parts]
    both_weight_ref, down_ref = refs[parts + cot_parts : parts + cot_parts + 2]
    count = refs[-1].shape[0] // BLOCK
    inner_ref, both_ref, second_out, cot_out = refs[-5 - count : -1 - count]
    grad_refs, acc = refs[-1 - count : -1], refs[-1]
    at = pl.program_id(0)
    step = down_ref.shape[1]
    rows, width = acc.shape

    @pl.when(at == 0)
    def _():
        for ins, out in ((second_refs, second_out), (cot_refs, cot_out)):
            start = 0
            for part in ins:
                size = part.shape[0]
                out[start // BLOCK, start % BLOCK : start % BLOCK + size, :] = part[...]
                start += size

    second = second_out[...].reshape(rows, width)
    both_act = jnp.dot(second, both_weight_ref[...], preferred_element_type=jnp.float32)
    inner_grad = jnp.dot(
        cot_out[...].reshape(rows, width), down_ref[...], preferred_element_type=jnp.float32
    )
    gate_act = both_act[:, :step]
    up_act = both_act[:, step:]
    sigmoid = 1.0 / (1.0 + jnp.exp(-gate_act))
    silu = gate_act * sigmoid
    inner_ref[...] = (silu * up_act).astype(low).reshape(inner_ref.shape)
    gate_grad = (inner_grad * up_act * (sigmoid * (1.0 + gate_act * (1.0 - sigmoid)))).astype(low)
    both_grad = jnp.concatenate([gate_grad, (inner_grad * silu).astype(low)], axis=1)
    both_ref[:, :, pl.ds(pl.multiple_of(at * 2 * step, 2 * step), 2 * step)] = both_grad.reshape(
        count, BLOCK, 2 * step
    )
    part = lax.dot_general(
        both_grad, both_weight_ref[...], contract_last, preferred_element_type=jnp.float32
    )
    last = pl.num_programs(0) - 1

    @pl.when(at == 0)
    def _():
        acc[...] = part

    @pl.when((at > 0) & (at < last))
    def _():
        acc[...] += part

    @pl.when(at == last)
    def _():
        total = (acc[...] + part).astype(low)
        for block, grad in enumerate(grad_refs):
            grad[...] = total[block * BLOCK : (block + 1) * BLOCK]


def mlp_blocks(place_at, seconds, cots, weights, held):
    rows = sum(second.shape[0] for second in seconds)
    width = seconds[0].shape[1]
    count = rows // BLOCK
    hidden_width = weights.shape[1] // 3
    step = FF_STEP
    steps = hidden_width // step
    ins = [
        pl.BlockSpec(value.shape, lambda c: (0, 0), pipeline_mode=pl.Buffered(1))
        for value in (*seconds, *cots)
    ]
    kept = pl.BlockSpec((count, BLOCK, step), lambda c: (place_at, 0, c))
    kept_both = pl.BlockSpec((count, BLOCK, 2 * hidden_width), lambda c: (place_at, 0, 0))
    kept_rows = pl.BlockSpec((count, BLOCK, width), lambda c: (place_at, 0, 0))
    rows_shape = jax.ShapeDtypeStruct((RING, BLOCK, width), low)
    return pl.pallas_call(
        functools.partial(mlp_kernel, len(seconds), len(cots)),
        grid=(steps,),
        in_specs=ins
        + [
            pl.BlockSpec((width, 2 * step), lambda c: (0, c)),
            pl.BlockSpec((width, step), lambda c: (0, 2 * steps + c)),
        ]
        + [pl.BlockSpec(memory_space=pl.ANY)] * len(held),
        out_specs=(kept, kept_both, kept_rows, kept_rows)
        + (pl.BlockSpec((BLOCK, width), lambda c: (0, 0)),) * count,
        out_shape=(
            jax.ShapeDtypeStruct((RING, BLOCK, hidden_width), low),
            jax.ShapeDtypeStruct((RING, BLOCK, 2 * hidden_width), low),
            rows_shape,
            rows_shape,
        )
        + (jax.ShapeDtypeStruct((BLOCK, width), low),) * count,
        scratch_shapes=[pltpu.VMEM((rows, width), jnp.float32)],
        input_output_aliases={len(ins) + 2 + i: i for i in range(len(held))},
        compiler_params=pltpu.CompilerParams(vmem_limit_bytes=VMEM_LIMIT),
        cost_estimate=pl.CostEstimate(
            flops=2 * 5 * rows * width * hidden_width,
            bytes_accessed=2 * 3 * width * hidden_width,
            transcendentals=rows * hidden_width,
        ),
    )(*seconds, *cots, weights, weights, *held)


def mlp_out_kernel(inner_ref, weight_ref, *outs):
    inner = inner_ref[...].reshape(RING * BLOCK, inner_ref.shape[2])
    part = lax.dot_general(
        inner, weight_ref[...], contract_last, preferred_element_type=jnp.float32
    ).astype(low)
    for block, out in enumerate(outs):
        out[...] = part[block * BLOCK : (block + 1) * BLOCK]


def mlp_out_part(inner, weights):
    _, rows, hidden_width = inner.shape
    width = weights.shape[0]
    steps = 4
    return pl.pallas_call(
        mlp_out_kernel,
        grid=(steps,),
        in_specs=[
            pl.BlockSpec(inner.shape, lambda d: (0, 0, 0)),
            pl.BlockSpec((width // steps, hidden_width), lambda d: (d, 2)),
        ],
        out_specs=(pl.BlockSpec((rows, width // steps), lambda d: (0, d)),) * RING,
        out_shape=(jax.ShapeDtypeStruct((rows, width), low),) * RING,
        compiler_params=pltpu.CompilerParams(vmem_limit_bytes=VMEM_LIMIT),
        cost_estimate=pl.CostEstimate(flops=1024, bytes_accessed=1024, transcendentals=0),
    )(inner, weights)


def pair_grad(core_at, lefts, right, by_heads=False):
    width = lefts[0].shape[-1]
    outs = 512 if by_heads else right.shape[2]
    rows = RING * BLOCK

    def kernel(core_ref, *refs):
        left_refs = refs[: len(lefts)]
        right_ref, keep_ref, give_ref = refs[len(lefts) : len(lefts) + 3]
        if by_heads:
            all_ref = refs[-1]

            @pl.when(pl.program_id(0) == 0)
            def _():
                for r in range(RING):
                    for head in range(4):
                        all_ref[
                            r * BLOCK : (r + 1) * BLOCK, head * HEAD_DIM : (head + 1) * HEAD_DIM
                        ] = right_ref[4 * r + head]

            values = all_ref[...]
        else:
            values = right_ref[...].reshape(rows, outs)
        inputs = [ref[...].reshape(-1, 256) for ref in left_refs]
        inputs = inputs[0] if len(inputs) == 1 else jnp.concatenate(inputs, axis=0)
        term = lax.dot_general(
            inputs, values, contract_first, preferred_element_type=jnp.float32
        ).astype(low)
        first_core = core_ref[0] == 0
        keep_ref[0] = jnp.where(first_core, term[:128], term[128:])
        give_ref[0] = jnp.where(first_core, term[128:], term[:128])

    def columns(value):
        lead = value.shape[:-1]
        return pl.BlockSpec((*lead, 256), lambda i: (0,) * len(lead) + (i,))

    half = pl.BlockSpec((1, 128, outs), lambda i: (i, 0, 0))
    return pl.pallas_call(
        kernel,
        grid=(width // 256,),
        in_specs=[pl.BlockSpec(memory_space=pltpu.SMEM)]
        + [columns(value) for value in lefts]
        + [pl.BlockSpec(right.shape, lambda i: (0, 0, 0))],
        out_specs=(half, half),
        out_shape=(jax.ShapeDtypeStruct((width // 256, 128, outs), low),) * 2,
        scratch_shapes=[pltpu.VMEM((rows, 512), low)] * by_heads,
        compiler_params=pltpu.CompilerParams(vmem_limit_bytes=VMEM_LIMIT),
        cost_estimate=pl.CostEstimate(flops=1024, bytes_accessed=1024, transcendentals=0),
    )(core_at[None], *lefts, right)


def middle_kernel(*refs):
    mixed_refs, weight_refs = refs[:RING], refs[RING : 2 * RING]
    hidden_ref, gain_ref, middle_ref, second_ref = refs[2 * RING :]
    at = pl.program_id(0)
    step = weight_refs[0].shape[0]
    columns = pl.ds(pl.multiple_of(at * step, step), step)
    total = hidden_ref[:, columns].astype(jnp.float32)
    for mixed, weight in zip(mixed_refs, weight_refs):
        rows = jnp.concatenate([mixed[head] for head in range(4)], axis=1)
        total += lax.dot_general(
            rows, weight[...], contract_last, preferred_element_type=jnp.float32
        )
    middle_ref[:, columns] = total

    @pl.when(at == pl.num_programs(0) - 1)
    def _():
        second_ref[...] = (normalize(middle_ref[...]) * gain_ref[...]).astype(low)


def middle_part(mixed_blocks, weights, hidden, gain):
    rows, width = hidden.shape
    steps = 4
    whole = pl.BlockSpec((rows, width), lambda d: (0, 0))
    return pl.pallas_call(
        middle_kernel,
        grid=(steps,),
        in_specs=[pl.BlockSpec((4, rows, HEAD_DIM), lambda d: (0, 0, 0))] * RING
        + [pl.BlockSpec((width // steps, 512), lambda d: (d, 0))] * RING
        + [whole, pl.BlockSpec((1, width), lambda d: (0, 0))],
        out_specs=(whole, whole),
        out_shape=(
            jax.ShapeDtypeStruct((rows, width), jnp.float32),
            jax.ShapeDtypeStruct((rows, width), low),
        ),
        compiler_params=pltpu.CompilerParams(vmem_limit_bytes=32 * 1024 * 1024),
        cost_estimate=pl.CostEstimate(flops=1024, bytes_accessed=1024, transcendentals=0),
    )(*mixed_blocks, *weights, hidden, gain)


def middle_back_kernel(*refs):
    parts, weight_refs = refs[:RING], refs[RING : 2 * RING]
    middle_ref, cot_ref, gain_ref, grad_ref, low_ref, gain_out, *rest = refs[2 * RING :]
    outs, accs = rest[:RING], rest[RING:]
    at = pl.program_id(0)
    step = weight_refs[0].shape[0]

    @pl.when(at == 0)
    def _():
        second_grad = sum(part[...].astype(jnp.float32) for part in parts)
        middle = middle_ref[...]
        scale = inverse_rms(middle)
        normed = middle * scale
        gain_out[...] = jnp.sum(second_grad * normed, axis=0, keepdims=True)
        scaled = second_grad * gain_ref[...]
        grad = cot_ref[...].astype(jnp.float32) + scale * (
            scaled - normed * jnp.mean(scaled * normed, axis=-1, keepdims=True)
        )
        grad_ref[...] = grad
        low_ref[...] = grad.astype(low)
        for acc in accs:
            acc[...] = jnp.zeros_like(acc)

    rows = low_ref[:, pl.ds(pl.multiple_of(at * step, step), step)]
    for weight, acc in zip(weight_refs, accs):
        acc[...] += jnp.dot(rows, weight[...], preferred_element_type=jnp.float32)

    @pl.when(at == pl.num_programs(0) - 1)
    def _():
        for out, acc in zip(outs, accs):
            for head in range(4):
                out[head] = acc[:, head * HEAD_DIM : (head + 1) * HEAD_DIM].astype(low)


def middle_back(parts, weights, middle, cot, gain):
    rows, width = middle.shape
    steps = 4
    whole = pl.BlockSpec((rows, width), lambda d: (0, 0))
    row = pl.BlockSpec((1, width), lambda d: (0, 0))
    heads = pl.BlockSpec((4, rows, HEAD_DIM), lambda d: (0, 0, 0))
    return pl.pallas_call(
        middle_back_kernel,
        grid=(steps,),
        in_specs=[whole] * RING
        + [pl.BlockSpec((width // steps, 512), lambda d: (d, 0))] * RING
        + [whole, whole, row],
        out_specs=(whole, whole, row) + (heads,) * RING,
        out_shape=(
            jax.ShapeDtypeStruct((rows, width), jnp.float32),
            jax.ShapeDtypeStruct((rows, width), low),
            jax.ShapeDtypeStruct((1, width), jnp.float32),
        )
        + (jax.ShapeDtypeStruct((4, rows, HEAD_DIM), low),) * RING,
        scratch_shapes=[pltpu.VMEM((rows, 512), jnp.float32)] * RING,
        compiler_params=pltpu.CompilerParams(vmem_limit_bytes=VMEM_LIMIT),
        cost_estimate=pl.CostEstimate(flops=1024, bytes_accessed=1024, transcendentals=0),
    )(*parts, *weights, middle, cot, gain)


def first_kernel(
    own_ref, left_ref, top_ref, bottom_ref, right_ref, weight_ref, gains_ref, cos_ref, sin_ref,
    query_gain, key_gain, hidden_ref, first_ref, pre_ref, send_ref, gain_out,
):
    at = pl.program_id(0)
    half = top_ref.shape[0]

    @pl.when(at == 0)
    def _():
        gain_out[...] = gains_ref[...].astype(jnp.float32).T[:8]
        hidden_ref[0] = own_ref[...]

    @pl.when(at == 1)
    def _():
        hidden_ref[0] = left_ref[...]

    @pl.when(at == 2)
    def _():
        hidden_ref[0, :half] = top_ref[...]
        hidden_ref[0, half:] = bottom_ref[...]

    @pl.when(at == 3)
    def _():
        hidden_ref[0] = right_ref[...]

    first = (normalize(hidden_ref[0].astype(jnp.float32)) * gain_out[0:1]).astype(low)
    first_ref[0] = first
    pre = jnp.dot(first, weight_ref[...], preferred_element_type=jnp.float32)
    pre_ref[0] = pre
    cosine = cos_ref[0]
    sine = sin_ref[0]

    def turned(head, gain):
        values = normalize(pre[:, head * HEAD_DIM : (head + 1) * HEAD_DIM]) * gain
        return (values * cosine + pltpu.roll(values, HEAD_DIM // 2, 1) * sine).astype(low)

    for head in range(4):
        send_ref[head, 0] = turned(head, query_gain[...])
    for head in range(2):
        send_ref[2 * head, 1] = turned(4 + head, key_gain[...])
        send_ref[2 * head + 1, 1] = pre[:, (6 + head) * HEAD_DIM : (7 + head) * HEAD_DIM].astype(low)


def first_part(blocks, weights, cosine, sine, query_gain, key_gain):
    rows, width = blocks[0].shape
    row = pl.BlockSpec((1, HEAD_DIM), lambda r: (0, 0))
    turn = pl.BlockSpec((1, rows, HEAD_DIM), lambda r: (r, 0, 0))
    return pl.pallas_call(
        first_kernel,
        grid=(RING,),
        in_specs=[pl.BlockSpec(block.shape, lambda r: (0, 0)) for block in blocks]
        + [
            pl.BlockSpec((width, 1024), lambda r: (0, 0)),
            pl.BlockSpec((width, HEAD_DIM), lambda r: (0, 8)),
            turn,
            turn,
            row,
            row,
        ],
        out_specs=(
            pl.BlockSpec((1, rows, width), lambda r: (r, 0, 0)),
            pl.BlockSpec((1, rows, width), lambda r: (r, 0, 0)),
            pl.BlockSpec((1, rows, 1024), lambda r: (r, 0, 0)),
            pl.BlockSpec((4, 2, rows, HEAD_DIM), lambda r: (r, 0, 0, 0)),
            pl.BlockSpec((8, width), lambda r: (0, 0)),
        ),
        out_shape=(
            jax.ShapeDtypeStruct((RING, rows, width), low),
            jax.ShapeDtypeStruct((RING, rows, width), low),
            jax.ShapeDtypeStruct((RING, rows, 1024), jnp.float32),
            jax.ShapeDtypeStruct((BLOCKS, 2, rows, HEAD_DIM), low),
            jax.ShapeDtypeStruct((8, width), jnp.float32),
        ),
        compiler_params=pltpu.CompilerParams(vmem_limit_bytes=VMEM_LIMIT),
        cost_estimate=pl.CostEstimate(
            flops=2 * RING * rows * width * 1024,
            bytes_accessed=20 * 1024 * 1024,
            transcendentals=0,
        ),
    )(*blocks, weights, weights, cosine, sine, query_gain, key_gain)


def first_back_kernel(
    core_ref, back_ref, pre_ref, cos_ref, sin_ref, query_gain, key_gain, first_ref,
    grad_ref, keep_ref, give_ref, query_sum, key_sum, all_grads,
):
    at = pl.program_id(0)
    rows = grad_ref.shape[1]
    cosine = cos_ref[0]
    sine = sin_ref[0]

    @pl.when(at == 0)
    def _():
        query_sum[...] = jnp.zeros_like(query_sum)
        key_sum[...] = jnp.zeros_like(key_sum)

    def back(grads, head, gain, sums):
        columns = slice(head * HEAD_DIM, (head + 1) * HEAD_DIM)
        values = pre_ref[0, :, columns]
        grads = grads.astype(jnp.float32)
        grads = grads * cosine - pltpu.roll(grads, HEAD_DIM // 2, 1) * sine
        scale = inverse_rms(values)
        normed = values * scale
        sums[...] += jnp.sum(grads * normed, axis=0, keepdims=True)
        scaled = grads * gain
        out = scale * (scaled - normed * jnp.mean(scaled * normed, axis=-1, keepdims=True))
        grad_ref[0, :, columns] = out.astype(low)

    for head in range(4):
        back(back_ref[head, 0], head, query_gain[...], query_sum)
    for head in range(2):
        back(back_ref[2 * head, 1], 4 + head, key_gain[...], key_sum)
        grad_ref[0, :, (6 + head) * HEAD_DIM : (7 + head) * HEAD_DIM] = back_ref[2 * head + 1, 1]
    all_grads[pl.ds(pl.multiple_of(at * rows, rows), rows), :] = grad_ref[0]

    @pl.when(at == RING - 1)
    def _():
        grads = all_grads[...]
        first_core = core_ref[0] == 0
        for pair in range(8):
            inputs = first_ref[:, :, pair * 256 : (pair + 1) * 256].reshape(RING * rows, 256)
            term = lax.dot_general(
                inputs, grads, contract_first, preferred_element_type=jnp.float32
            ).astype(low)
            keep_ref[pair] = jnp.where(first_core, term[:128], term[128:])
            give_ref[pair] = jnp.where(first_core, term[128:], term[:128])


def first_back(core_at, returned, pre, cosine, sine, query_gain, key_gain, first_in):
    _, rows, width = first_in.shape
    row = pl.BlockSpec((1, HEAD_DIM), lambda r: (0, 0))
    turn = pl.BlockSpec((1, rows, HEAD_DIM), lambda r: (r, 0, 0))
    wide = pl.BlockSpec((1, rows, 1024), lambda r: (r, 0, 0))
    half = pl.BlockSpec((8, 128, 1024), lambda r: (0, 0, 0))
    return pl.pallas_call(
        first_back_kernel,
        grid=(RING,),
        in_specs=[
            pl.BlockSpec(memory_space=pltpu.SMEM),
            pl.BlockSpec((4, 2, rows, HEAD_DIM), lambda r: (r, 0, 0, 0)),
            wide,
            turn,
            turn,
            row,
            row,
            pl.BlockSpec((RING, rows, width), lambda r: (0, 0, 0)),
        ],
        out_specs=(wide, half, half, row, row),
        out_shape=(
            jax.ShapeDtypeStruct((RING, rows, 1024), low),
            jax.ShapeDtypeStruct((8, 128, 1024), low),
            jax.ShapeDtypeStruct((8, 128, 1024), low),
            jax.ShapeDtypeStruct((1, HEAD_DIM), jnp.float32),
            jax.ShapeDtypeStruct((1, HEAD_DIM), jnp.float32),
        ),
        scratch_shapes=[pltpu.VMEM((RING * rows, 1024), low)],
        compiler_params=pltpu.CompilerParams(vmem_limit_bytes=VMEM_LIMIT),
        cost_estimate=pl.CostEstimate(flops=1024, bytes_accessed=1024, transcendentals=0),
    )(core_at[None], returned, pre, cosine, sine, query_gain, key_gain, first_in)


def last_kernel(
    core_ref, grad_ref, weight_ref, hidden_ref, mlp_ref, query_ref, key_ref,
    own_ref, left_a, left_b, top_ref, bottom_ref, right_a, right_b, keep_ref, give_ref, gain_acc,
):
    at = pl.program_id(0)
    width = hidden_ref.shape[2]
    part = lax.dot_general(
        grad_ref[0], weight_ref[...], contract_last, preferred_element_type=jnp.float32
    )
    half = top_ref.shape[0]
    @pl.when(at == 0)
    def _():
        own_ref[...] = part.astype(low)

    for r, first, second in ((1, left_a, left_b), (2, top_ref, bottom_ref), (3, right_a, right_b)):

        @pl.when(at == r)
        def _(first=first, second=second):
            first[...] = part[:half].astype(low)
            second[...] = part[half:].astype(low)

    normed = normalize(hidden_ref[0].astype(jnp.float32))
    gain = jnp.sum(part * normed, axis=0, keepdims=True)

    @pl.when(at == 0)
    def _():
        gain_acc[...] = gain

    @pl.when(at > 0)
    def _():
        gain_acc[...] += gain

    @pl.when(at == RING - 1)
    def _():
        lines = [
            gain_acc[...],
            mlp_ref[...],
            jnp.concatenate([query_ref[...]] * BLOCKS, axis=1),
            jnp.concatenate([key_ref[...]] * BLOCKS, axis=1),
            jnp.zeros((HEAD_DIM - 4, width), jnp.float32),
        ]
        turned = jnp.concatenate(lines, axis=0).T.astype(low)
        first_core = core_ref[0] == 0
        for pair in range(8):
            first = turned[pair * 256 : pair * 256 + 128]
            second = turned[pair * 256 + 128 : (pair + 1) * 256]
            keep_ref[pair] = jnp.where(first_core, first, second)
            give_ref[pair] = jnp.where(first_core, second, first)


def last_part(core_at, grads, weights, hidden_all, mlp_part, query_part, key_part):
    _, rows, width = hidden_all.shape
    block = pl.BlockSpec((rows, width), lambda r: (0, 0))
    small = pl.BlockSpec((rows // 2, width), lambda r: (0, 0))
    whole = jax.ShapeDtypeStruct((rows, width), low)
    part = jax.ShapeDtypeStruct((rows // 2, width), low)
    row = pl.BlockSpec((1, HEAD_DIM), lambda r: (0, 0))
    half = pl.BlockSpec((8, 128, HEAD_DIM), lambda r: (0, 0, 0))
    return pl.pallas_call(
        last_kernel,
        grid=(RING,),
        in_specs=[
            pl.BlockSpec(memory_space=pltpu.SMEM),
            pl.BlockSpec((1, rows, 1024), lambda r: (r, 0, 0)),
            pl.BlockSpec((width, 1024), lambda r: (0, 0)),
            pl.BlockSpec((1, rows, width), lambda r: (r, 0, 0)),
            pl.BlockSpec((1, width), lambda r: (0, 0)),
            row,
            row,
        ],
        out_specs=(block,) + (small,) * 6 + (half, half),
        out_shape=(whole,) + (part,) * 6
        + (jax.ShapeDtypeStruct((8, 128, HEAD_DIM), low),) * 2,
        scratch_shapes=[pltpu.VMEM((1, width), jnp.float32)],
        compiler_params=pltpu.CompilerParams(vmem_limit_bytes=VMEM_LIMIT),
        cost_estimate=pl.CostEstimate(flops=1024, bytes_accessed=1024, transcendentals=0),
    )(core_at[None], grads, weights, hidden_all, mlp_part, query_part, key_part)


def arrange_kernel(at_ref, own_ref, other_ref, out_ref):
    y_at, x_at, core_at = at_ref[0], at_ref[1], at_ref[2]
    for dy in range(RING):
        for dx in range(2):
            first = ((y_at - dy + RING) & 3) * 4 + (x_at ^ dx) * 2
            own = pl.multiple_of((first + core_at) * 128, 128)
            other = pl.multiple_of((first + 1 - core_at) * 128, 128)
            out_ref[pl.ds(own, 128), :] = own_ref[dy, dx]
            out_ref[pl.ds(other, 128), :] = other_ref[dy, dx]


def gather_by_permutes(pairs, y_at, x_at, core_at):
    own = jnp.stack(pairs)
    other = shift(own, "core", 1, 2)
    whole = pl.BlockSpec(memory_space=pltpu.VMEM)
    return pl.pallas_call(
        arrange_kernel,
        in_specs=[pl.BlockSpec(memory_space=pltpu.SMEM), whole, whole],
        out_specs=whole,
        out_shape=jax.ShapeDtypeStruct((BLOCKS * 128, own.shape[3]), own.dtype),
        compiler_params=pltpu.CompilerParams(vmem_limit_bytes=VMEM_LIMIT),
        cost_estimate=pl.CostEstimate(flops=1024, bytes_accessed=1024, transcendentals=0),
    )(jnp.stack([y_at, x_at, core_at]), own, other)


def pair_sums_kernel(keep_ref, come_ref, gains_keep, gains_come, out_ref):
    f32 = jnp.float32
    wide = keep_ref.shape[2]
    out_ref[:, :, :wide] = (keep_ref[...].astype(f32) + come_ref[...].astype(f32)).astype(low)
    out_ref[:, :, wide:] = (gains_keep[...].astype(f32) + gains_come[...].astype(f32)).astype(low)


def pair_sums(keep, come, more_keep, more_come):
    blocks, rows, wide = keep.shape
    narrow = more_keep.shape[2]
    large = pl.BlockSpec((4, rows, wide), lambda i: (i, 0, 0))
    small = pl.BlockSpec((4, rows, narrow), lambda i: (i, 0, 0))
    return pl.pallas_call(
        pair_sums_kernel,
        grid=(blocks // 4,),
        in_specs=[large, large, small, small],
        out_specs=pl.BlockSpec((4, rows, wide + narrow), lambda i: (i, 0, 0)),
        out_shape=jax.ShapeDtypeStruct((blocks, rows, wide + narrow), low),
        compiler_params=pltpu.CompilerParams(vmem_limit_bytes=VMEM_LIMIT),
        cost_estimate=pl.CostEstimate(flops=1024, bytes_accessed=1024, transcendentals=0),
    )(keep, come, more_keep, more_come)


def to_heads(send):
    return lax.all_to_all(send, GROUP_AXES, 0, 0, tiled=True)


def after(value, *others):
    return lax.optimization_barrier((value, others))[0]


def ring_blocks(values):
    half = values.shape[0] // 2
    left = shift(values, "z", 1)
    right = shift(values, "z", 3)
    opposite = jnp.concatenate(
        [shift(left[:half], "z", 1), shift(right[half:], "z", 3)], axis=0
    )
    return [values, left, opposite, right]


def together(*values):
    return lax.optimization_barrier(values)


def place(z_at, blocks, widths, chunk=None, summed=False):
    rows = blocks[0].shape[0]
    whole = pl.BlockSpec(memory_space=pltpu.VMEM)
    shapes = [RING * part for part in widths] + [HEAD_DIM] * summed

    def kernel(z_ref, *refs):
        ins, outs = refs[:RING], refs[RING:]
        for r in range(RING):
            slot = (z_ref[0] - r + RING) & 3
            start = 0
            for turn in range(widths[0] // chunk if chunk else 1):
                for out, part in zip(outs, widths):
                    size = chunk or part
                    at = pl.multiple_of(slot * part + turn * size, 128)
                    out[:, pl.ds(at, size)] = ins[r][:, start : start + size].astype(jnp.float32)
                    start += size
            if summed:
                columns = ins[r][:, start : start + HEAD_DIM].astype(jnp.float32)
                outs[-1][...] = columns if r == 0 else outs[-1][...] + columns

    return pl.pallas_call(
        kernel,
        in_specs=[pl.BlockSpec(memory_space=pltpu.SMEM)] + [whole] * RING,
        out_specs=tuple(whole for _ in shapes),
        out_shape=tuple(jax.ShapeDtypeStruct((rows, part), jnp.float32) for part in shapes),
        compiler_params=pltpu.CompilerParams(vmem_limit_bytes=VMEM_LIMIT),
        cost_estimate=pl.CostEstimate(flops=1024, bytes_accessed=1024, transcendentals=0),
    )(z_at[None], *blocks)


def send_back(block, r):
    return shift(block, "z", -r)


def local(
    hidden_in,
    cotangent,
    segment_ids,
    positions,
    attn_gain,
    query_gain,
    key_gain,
    query_weight,
    key_weight,
    value_weight,
    out_weight,
    mlp_gain,
    gate_weight,
    up_weight,
    down_weight,
):
    f32 = jnp.float32
    rows, width = hidden_in.shape
    ring_rows = RING * rows
    z_at = lax.axis_index("z")
    y_at = lax.axis_index("y")
    x_at = lax.axis_index("x_hi")
    core_at = lax.axis_index("core")
    my_index = (y_at * 2 + x_at) * 2 + core_at

    def columns(weight):
        part = weight.shape[1] // RING
        return lax.dynamic_slice_in_dim(weight, z_at * part, part, 1).astype(low)

    def gather(block):
        return lax.all_gather(block, GROUP_AXES, axis=0, tiled=True)

    own_places = lax.dynamic_slice_in_dim(positions, my_index * rows, rows)
    firsts = positions.reshape(BLOCKS, BLOCK)[:, 0]
    segments = segment_ids.reshape(BLOCKS, BLOCK)[:, 0]
    logical = firsts // BLOCK + jnp.maximum(segments - 1, 0) * 2
    numbers = jnp.arange(BLOCKS, dtype=jnp.int32)
    order = jnp.sum(jnp.where(logical[:, None] == numbers[None, :], numbers[:, None], 0), axis=0)
    notes = gather_z(jnp.concatenate([own_places, order, jnp.zeros((112,), jnp.int32)])[None])
    places = notes[:, :rows]
    order = lax.dynamic_index_in_dim(notes, y_at, 0, keepdims=False)[rows : rows + BLOCKS]

    gains = jnp.pad(
        jnp.stack([attn_gain, mlp_gain], axis=1).astype(low), ((0, 0), (0, HEAD_DIM - 2))
    )
    first_weights = gather(
        jnp.concatenate(
            [columns(query_weight), columns(key_weight), columns(value_weight), gains], axis=1
        )
    )
    out_columns = columns(out_weight)
    out_come = shift(out_columns, "x_hi", 1, 2)
    out_pairs = jnp.stack([out_columns, out_come])
    out_pairs = [out_pairs] + [shift(out_pairs, "y", r) for r in range(1, RING)]

    hidden_own = after(hidden_in, notes, out_come)
    hidden_left = shift(hidden_own, "z", 1)
    hidden_right = shift(hidden_own, "z", 3)
    gate_columns, up_columns, down_columns, hidden_left, hidden_right, out_pairs = together(
        gate_weight, up_weight, down_weight, hidden_left, hidden_right, out_pairs
    )
    out_slice = gather_by_permutes(out_pairs, y_at, x_at, core_at)
    gate_columns, up_columns = columns(gate_columns), columns(up_columns)
    mlp_columns = []
    for start in range(0, gate_columns.shape[1], FF_STEP):
        mlp_columns.append(gate_columns[:, start : start + FF_STEP])
        mlp_columns.append(up_columns[:, start : start + FF_STEP])
    mlp_weights = gather(jnp.concatenate(mlp_columns + [columns(down_columns)], axis=1))
    half = rows // 2
    hidden_blocks = [
        hidden_own,
        hidden_left,
        shift(hidden_left[:half], "z", 1),
        shift(hidden_right[half:], "z", 3),
        hidden_right,
    ]
    out_slice = after(out_slice, *hidden_blocks)
    out_left = shift(out_slice, "z", 1)
    out_right = shift(out_slice, "z", 3)
    frequency = rope_base ** (-2.0 * jnp.arange(HEAD_DIM // 2, dtype=f32) / HEAD_DIM)
    angles = places.astype(f32)[:, :, None] * frequency[None, None, :]
    cosine = jnp.cos(angles)
    sine = jnp.sin(angles)
    cosine = jnp.concatenate([cosine, cosine], axis=-1)
    sine = jnp.concatenate([-sine, sine], axis=-1)
    query_row = query_gain[None]
    key_row = key_gain[None]

    hidden_all, first_in, qkv_pre, send, gain_rows = first_part(
        hidden_blocks, first_weights, cosine, sine, query_row, key_row
    )
    attn_scale = gain_rows[0:1]
    mlp_scale = gain_rows[1:2]
    arrived, out_left, out_right = together(to_heads(send), out_left, out_right)
    other_pair = shift(arrived[:, 1], "core", 1, 2)
    head_mixed, head_mixed_t, head_logs = attention_forward(order, core_at, arrived, other_pair)
    out_top = shift(out_left[: width // 2], "z", 1)
    out_bottom = shift(out_right[width // 2 :], "z", 3)
    head_mixed, head_mixed_t, head_logs, out_top, out_bottom = together(
        head_mixed, head_mixed_t, head_logs, out_top, out_bottom
    )
    cot_own = after(cotangent, head_mixed)
    cot_left = shift(cot_own, "z", 1)
    cot_right = shift(cot_own, "z", 3)

    cot_top = shift(cot_left[:half], "z", 1)
    cot_bottom = shift(cot_right[half:], "z", 3)
    mixed_arrived, cot_left, cot_right, cot_top, cot_bottom = together(
        to_heads(head_mixed), cot_left, cot_right, cot_top, cot_bottom
    )
    mixed_blocks = [mixed_arrived[:4]] + [
        shift(mixed_arrived[4 * (RING - j) : 4 * (RING - j) + 4], "z", j) for j in range(1, RING)
    ]
    out_opposite = jnp.concatenate([out_top, out_bottom], axis=0)
    out_weights = [out_slice, out_left, out_opposite, out_right]
    mixed_blocks, out_weights = together(mixed_blocks, out_weights)
    middle, second_in = middle_part(mixed_blocks, out_weights, hidden_in, mlp_scale)
    hidden = hidden_in.astype(f32)
    left = shift(second_in, "z", 1)
    right = shift(second_in, "z", 3)
    *held, own_part = mlp_blocks(0, [second_in], [cot_own], mlp_weights, ())
    held, own_part, left, right, second_in = together(held, own_part, left, right, second_in)
    opposite = shift(second_in, "z", 2)
    *held, left_part, right_part = mlp_blocks(
        1, [left, right], [cot_left, cot_right], mlp_weights, held
    )
    left_back = send_back(left_part, 1)
    right_back = send_back(right_part, 3)
    held, opposite = together(held, opposite)
    *held, opposite_part = mlp_blocks(
        1, [opposite], [cot_top, cot_bottom], mlp_weights, held
    )
    opposite_back = send_back(opposite_part, 2)
    inner, both_grad, second_all, cot_all = held

    def pair_sum(keep, come):
        return (keep.astype(f32) + come.astype(f32)).astype(low)

    def to_owners(pair):
        return lax.all_to_all(pair, ("y", "x_hi"), 0, 0, tiled=True)

    def add_up(terms):
        return jnp.sum(terms.astype(f32), axis=0).astype(low)

    def over_x(share):
        return share, shift(share, "x_lo", 1, 2)

    def over_z(pair):
        share = pair_sum(*pair)
        return [share] + [shift(share, "z", r) for r in range(1, RING)]

    both_term = lax.dot_general(
        second_all.reshape(ring_rows, width),
        both_grad.reshape(ring_rows, 3072),
        contract_first,
        preferred_element_type=f32,
    ).astype(low)
    left_back, right_back, opposite_back, both_term, inner = together(
        left_back, right_back, opposite_back, both_term, inner
    )
    both_share = lax.psum_scatter(both_term, GROUP_AXES, scatter_dimension=0, tiled=True)

    middle_grad, own_low, mlp_gain_part, *grad_blocks = middle_back(
        (own_part, left_back, right_back, opposite_back),
        out_weights,
        middle,
        cotangent,
        mlp_scale,
    )
    grad_blocks = [grad_blocks[0]] + [shift(grad_blocks[RING - r], "z", r) for r in range(1, RING)]
    down_keep, down_give = pair_grad(core_at, [cot_all], inner)
    grad_blocks, down_keep, down_give, own_low, inner = together(
        grad_blocks, down_keep, down_give, own_low, inner
    )
    head_grads = to_heads(jnp.concatenate(grad_blocks, axis=0))
    low_left = shift(own_low, "z", 1)
    low_right = shift(own_low, "z", 3)
    mlp_own, mlp_opposite, mlp_left, mlp_right = mlp_out_part(inner, mlp_weights)
    head_grads, low_left, low_right, own_low, mlp_opposite, mlp_left, mlp_right = together(
        head_grads, low_left, low_right, own_low, mlp_opposite, mlp_left, mlp_right
    )
    mlp_left = send_back(mlp_left, 1)
    mlp_right = send_back(mlp_right, 3)

    query_grad, grad_keep, grad_give = attention_backward(
        order, core_at, arrived, other_pair, head_grads, head_mixed_t, head_logs
    )
    query_grad, grad_keep, grad_give, mlp_left, mlp_right, own_low, mlp_opposite, down_give = together(
        query_grad, grad_keep, grad_give, mlp_left, mlp_right, own_low, mlp_opposite, down_give
    )
    low_opposite = shift(own_low, "z", 2)
    mlp_opposite = send_back(after(mlp_opposite, low_opposite), 2)
    grads_send = lax.dynamic_update_slice_in_dim(
        query_grad, pair_sum(grad_keep, shift(grad_give, "core", 1, 2))[:, None], 1, 1
    )
    returned = to_heads(grads_send)
    out_keep, out_give = pair_grad(
        core_at, [own_low, low_left, low_opposite, low_right], mixed_arrived, by_heads=True
    )
    down_sum = pair_sums(
        down_keep,
        shift(down_give, "core", 1, 2),
        out_keep,
        shift(out_give, "core", 1, 2),
    )
    returned, both_share, down_sum = together(returned, both_share, down_sum)
    both_pair = over_x(both_share)
    down_terms = to_owners(down_sum)
    qkv_grad, qkv_keep, qkv_give, query_gain_part, key_gain_part = first_back(
        core_at, returned, qkv_pre, cosine, sine, query_row, key_row, first_in
    )
    qkv_grad, qkv_give, both_pair, mlp_opposite = together(
        qkv_grad, qkv_give, both_pair, mlp_opposite
    )
    both_sum = pair_sum(*both_pair)
    both_left = shift(both_sum, "z", 1)
    both_right = shift(both_sum, "z", 3)
    qkv_come = shift(qkv_give, "core", 1, 2)
    *first_parts, gains_keep, gains_give = last_part(
        core_at,
        qkv_grad,
        first_weights,
        hidden_all,
        mlp_gain_part,
        query_gain_part,
        key_gain_part,
    )
    first_parts, gains_give, qkv_come, both_left, both_right, both_sum, down_terms = together(
        first_parts, gains_give, qkv_come, both_left, both_right, both_sum, down_terms
    )
    down_pair = over_x(add_up(down_terms))
    gains_come = shift(gains_give, "core", 1, 2)
    first_own, left_a, left_b, first_top, first_bottom, right_a, right_b = first_parts
    first_top = shift(first_top, "z", 3)
    first_bottom = shift(first_bottom, "z", 1)
    qkv_terms = to_owners(pair_sums(qkv_keep, qkv_come, gains_keep, gains_come))
    first_left = send_back(jnp.concatenate([pair_sum(left_a, first_top), left_b], axis=0), 1)
    first_right = send_back(jnp.concatenate([right_a, pair_sum(right_b, first_bottom)], axis=0), 3)
    both_opposite = shift(both_sum, "z", 2)
    qkv_terms, first_left, first_right, both_opposite, down_pair = together(
        qkv_terms, first_left, first_right, both_opposite, down_pair
    )
    down_blocks = over_z(down_pair)
    qkv_share = add_up(qkv_terms)
    both_blocks = [both_sum, both_left, both_opposite, both_right]
    qkv_pair = over_x(qkv_share)
    output = (
        middle
        + mlp_own.astype(f32)
        + mlp_left.astype(f32)
        + mlp_right.astype(f32)
        + mlp_opposite.astype(f32)
    ).astype(low)
    first_grad = first_own.astype(f32) + first_left.astype(f32) + first_right.astype(f32)
    hidden_rms = inverse_rms(hidden)
    own_norm = hidden * hidden_rms
    scaled_first = first_grad * attn_scale
    hidden_grad = (
        middle_grad
        + hidden_rms
        * (scaled_first - own_norm * jnp.mean(scaled_first * own_norm, axis=-1, keepdims=True))
    ).astype(low)

    down_grad_out, out_grad_out = place(z_at, down_blocks, (1536, 512))
    gate_grad_out, up_grad_out = place(z_at, both_blocks, (1536, 1536), chunk=FF_STEP)
    query_grad_out, key_grad_out, value_grad_out, gain_sum = place(
        z_at, over_z(qkv_pair), (512, 256, 256), summed=True
    )
    gain_sum = gain_sum[:, :4].T

    return (
        output,
        hidden_grad,
        gain_sum[0],
        gain_sum[2],
        gain_sum[3],
        query_grad_out,
        key_grad_out,
        value_grad_out,
        out_grad_out,
        gain_sum[1],
        gate_grad_out,
        up_grad_out,
        down_grad_out,
    )


def solution(mesh):
    fine = Mesh(mesh.devices.reshape(2, 4, 4, 2, 2), ALL_AXES)
    rep = ("x_lo", "z")
    row = P(ALL_AXES, None)
    part = P(GROUP_AXES)
    weight = P(GROUP_AXES, None)
    in_specs = (
        row,
        row,
        P(rep),
        P(rep),
        part,
        P(),
        P(),
        weight,
        weight,
        weight,
        weight,
        part,
        weight,
        weight,
        weight,
    )
    out_specs = (
        row,
        row,
        part,
        P(),
        P(),
        weight,
        weight,
        weight,
        weight,
        part,
        weight,
        weight,
        weight,
    )
    return jax.shard_map(local, mesh=fine, in_specs=in_specs, out_specs=out_specs, check_vma=False)
```

```python
import functools

import jax
import jax.numpy as jnp
from jax import lax
from jax.experimental import pallas as pl
from jax.experimental.pallas import tpu as pltpu
from jax.sharding import Mesh
from jax.sharding import PartitionSpec as P

HEAD_DIM = 128
RING = 4
BLOCK = 256
BLOCKS = 16
TILE = 512
TILES = 8
PROMPT_TILES = 6
FF_STEP = 512
VMEM_LIMIT = 60 * 1024 * 1024

norm_eps = 1e-06
rope_base = 1000000.0
score_scale = HEAD_DIM ** (-0.5)
score_scale_log2 = score_scale * 1.4426950408889634
contract_first = (((0,), (0,)), ((), ()))
contract_last = (((1,), (1,)), ((), ()))
GROUP_AXES = ("y", "x_hi", "core")
ALL_AXES = ("x_lo", "z", "y", "x_hi", "core")
low = jnp.bfloat16


def inverse_rms(values):
    return lax.rsqrt(jnp.mean(values * values, axis=-1, keepdims=True) + norm_eps)


def normalize(values):
    return values * inverse_rms(values)


def shift(values, axis, by, size=RING):
    return lax.ppermute(values, axis, [(i, (i + by) % size) for i in range(size)])


def gather_z(values):
    return jnp.concatenate(
        [values, shift(values, "z", 1), shift(values, "z", 2), shift(values, "z", 3)], axis=0
    )


def forward_kernel(
    order, core, own_a, own_b, other_a, other_b, mixed_ref, mixed_t_ref, log_ref, k_all, v_t, acc, total
):
    tile = pl.program_id(0)
    start = tile * TILE

    def take(keys, values):
        for half in range(2):
            rows = pl.ds(pl.multiple_of(start + half * BLOCK, BLOCK), BLOCK)
            k_all[rows, :] = keys[half]
            v_t[tile, :, half * BLOCK : (half + 1) * BLOCK] = (
                values[half].astype(jnp.float32).T.astype(low)
            )

    @pl.when(core[0] == 0)
    def _():
        take((own_a[0, 1], own_b[0, 1]), (other_a[0], other_b[0]))

    @pl.when(core[0] == 1)
    def _():
        take((other_a[0], other_b[0]), (own_a[0, 1], own_b[0, 1]))

    queries = jnp.concatenate([own_a[0, 0], own_b[0, 0]], axis=0)
    acc[...] = jnp.zeros_like(acc)
    total[...] = jnp.zeros_like(total)

    def chunk(at, masked):
        keys = k_all[pl.ds(pl.multiple_of(at * TILE, TILE), TILE), :]
        scores = lax.dot_general(keys, queries, contract_last, preferred_element_type=jnp.float32)
        weights = jnp.exp2(scores * score_scale_log2)
        if masked:
            key_row = lax.broadcasted_iota(jnp.int32, (TILE, TILE), 0)
            query_row = lax.broadcasted_iota(jnp.int32, (TILE, TILE), 1)
            weights = jnp.where(key_row <= query_row, weights, 0.0)
        total[...] += jnp.sum(weights, axis=0, keepdims=True)
        acc[...] += jnp.dot(v_t[at], weights.astype(low), preferred_element_type=jnp.float32)

    @pl.loop(0, jnp.minimum(tile, PROMPT_TILES))
    def _(at):
        chunk(at, False)

    chunk(tile, True)
    mixed_t = acc[...] / total[...]
    mixed_t_ref[0] = mixed_t
    log_ref[0] = jnp.log2(total[...])
    mixed = mixed_t.T.astype(low)
    mixed_ref[order[2 * tile]] = mixed[:BLOCK]
    mixed_ref[order[2 * tile + 1]] = mixed[BLOCK:]


def tile_specs(lead):
    return [
        pl.BlockSpec(
            (1, *lead, BLOCK, HEAD_DIM),
            functools.partial(
                lambda half, tile, order, core: (order[2 * tile + half],) + (0,) * (len(lead) + 2),
                half,
            ),
        )
        for half in range(2)
    ]


def attention_forward(order, core_at, arrived, other):
    whole = pl.BlockSpec(memory_space=pltpu.VMEM)
    turned = pl.BlockSpec((1, HEAD_DIM, TILE), lambda tile, order, core: (tile, 0, 0))
    line = pl.BlockSpec((1, 1, TILE), lambda tile, order, core: (tile, 0, 0))
    return pl.pallas_call(
        forward_kernel,
        out_shape=(
            jax.ShapeDtypeStruct((BLOCKS, BLOCK, HEAD_DIM), low),
            jax.ShapeDtypeStruct((TILES, HEAD_DIM, TILE), jnp.float32),
            jax.ShapeDtypeStruct((TILES, 1, TILE), jnp.float32),
        ),
        grid_spec=pltpu.PrefetchScalarGridSpec(
            num_scalar_prefetch=2,
            grid=(TILES,),
            in_specs=tile_specs((2,)) + tile_specs(()),
            out_specs=(whole, turned, line),
            scratch_shapes=[
                pltpu.VMEM((BLOCKS * BLOCK, HEAD_DIM), low),
                pltpu.VMEM((TILES, HEAD_DIM, TILE), low),
                pltpu.VMEM((HEAD_DIM, TILE), jnp.float32),
                pltpu.VMEM((1, TILE), jnp.float32),
            ],
        ),
        compiler_params=pltpu.CompilerParams(vmem_limit_bytes=VMEM_LIMIT),
        cost_estimate=pl.CostEstimate(
            flops=1024, bytes_accessed=1024, transcendentals=0
        ),
    )(order, core_at[None], arrived, arrived, other, other)


def backward_kernel(
    order, core, own_a, own_b, other_a, other_b, grad_a, grad_b, mixed_t_ref, log_ref,
    q_out, keep_out, give_out, k_all, v_all, k_t, q_acc, k_acc, v_acc,
):
    tile = pl.program_id(0)
    start = tile * TILE

    def take(keys, values):
        for half in range(2):
            rows = pl.ds(pl.multiple_of(start + half * BLOCK, BLOCK), BLOCK)
            k_all[rows, :] = keys[half]
            v_all[rows, :] = values[half]
            k_t[tile, :, half * BLOCK : (half + 1) * BLOCK] = (
                keys[half].astype(jnp.float32).T.astype(low)
            )

    @pl.when(core[0] == 0)
    def _():
        take((own_a[0, 1], own_b[0, 1]), (other_a[0], other_b[0]))

    @pl.when(core[0] == 1)
    def _():
        take((other_a[0], other_b[0]), (own_a[0, 1], own_b[0, 1]))

    rows = pl.ds(pl.multiple_of(start, TILE), TILE)
    k_acc[rows, :] = jnp.zeros((TILE, HEAD_DIM), jnp.float32)
    v_acc[rows, :] = jnp.zeros((TILE, HEAD_DIM), jnp.float32)
    queries = jnp.concatenate([own_a[0, 0], own_b[0, 0]], axis=0)
    grads = jnp.concatenate([grad_a[0], grad_b[0]], axis=0)
    grads_t = grads.astype(jnp.float32).T
    shared = jnp.sum(grads_t * mixed_t_ref[0], axis=0, keepdims=True)
    logs = log_ref[0]
    q_acc[...] = jnp.zeros_like(q_acc)

    def chunk(at, masked):
        rows = pl.ds(pl.multiple_of(at * TILE, TILE), TILE)
        scores = lax.dot_general(
            k_all[rows, :], queries, contract_last, preferred_element_type=jnp.float32
        )
        probs = jnp.exp2(scores * score_scale_log2 - logs)
        if masked:
            key_row = lax.broadcasted_iota(jnp.int32, (TILE, TILE), 0)
            query_row = lax.broadcasted_iota(jnp.int32, (TILE, TILE), 1)
            probs = jnp.where(key_row <= query_row, probs, 0.0)
        prob_grads = lax.dot_general(
            v_all[rows, :], grads, contract_last, preferred_element_type=jnp.float32
        )
        score_grads = (probs * (prob_grads - shared)).astype(low)
        v_acc[rows, :] += jnp.dot(probs.astype(low), grads, preferred_element_type=jnp.float32)
        k_acc[rows, :] += jnp.dot(score_grads, queries, preferred_element_type=jnp.float32)
        q_acc[...] += jnp.dot(k_t[at], score_grads, preferred_element_type=jnp.float32)

    @pl.loop(0, jnp.minimum(tile, PROMPT_TILES))
    def _(at):
        chunk(at, False)

    chunk(tile, True)
    query_grad = (q_acc[...] * score_scale).T.astype(low)
    q_out[order[2 * tile], 0] = query_grad[:BLOCK]
    q_out[order[2 * tile + 1], 0] = query_grad[BLOCK:]

    def give(keep_acc, keep_scale, give_acc, give_scale):
        for at in range(BLOCKS):
            rows = slice(at * BLOCK, (at + 1) * BLOCK)
            keep_out[order[at]] = (keep_acc[rows, :] * keep_scale).astype(low)
            give_out[order[at]] = (give_acc[rows, :] * give_scale).astype(low)

    @pl.when((tile == TILES - 1) & (core[0] == 0))
    def _():
        give(k_acc, score_scale, v_acc, 1.0)

    @pl.when((tile == TILES - 1) & (core[0] == 1))
    def _():
        give(v_acc, 1.0, k_acc, score_scale)


def attention_backward(order, core_at, arrived, other, grads, mixed_t, logs):
    whole = pl.BlockSpec(memory_space=pltpu.VMEM)
    rows = BLOCKS * BLOCK
    turned = pl.BlockSpec((1, HEAD_DIM, TILE), lambda tile, order, core: (tile, 0, 0))
    line = pl.BlockSpec((1, 1, TILE), lambda tile, order, core: (tile, 0, 0))
    return pl.pallas_call(
        backward_kernel,
        out_shape=(jax.ShapeDtypeStruct((BLOCKS, 2, BLOCK, HEAD_DIM), low),)
        + (jax.ShapeDtypeStruct((BLOCKS, BLOCK, HEAD_DIM), low),) * 2,
        grid_spec=pltpu.PrefetchScalarGridSpec(
            num_scalar_prefetch=2,
            grid=(TILES,),
            in_specs=tile_specs((2,)) + tile_specs(()) + tile_specs(()) + [turned, line],
            out_specs=(whole, whole, whole),
            scratch_shapes=[
                pltpu.VMEM((rows, HEAD_DIM), low),
                pltpu.VMEM((rows, HEAD_DIM), low),
                pltpu.VMEM((TILES, HEAD_DIM, TILE), low),
                pltpu.VMEM((HEAD_DIM, TILE), jnp.float32),
                pltpu.VMEM((rows, HEAD_DIM), jnp.float32),
                pltpu.VMEM((rows, HEAD_DIM), jnp.float32),
            ],
        ),
        compiler_params=pltpu.CompilerParams(vmem_limit_bytes=VMEM_LIMIT),
        cost_estimate=pl.CostEstimate(
            flops=1024, bytes_accessed=1024, transcendentals=0
        ),
    )(order, core_at[None], arrived, arrived, other, other, grads, grads, mixed_t, logs)


def mlp_kernel(parts, cot_parts, *refs):
    second_refs, cot_refs = refs[:parts], refs[parts : parts + cot_parts]
    both_weight_ref, down_ref = refs[parts + cot_parts : parts + cot_parts + 2]
    count = refs[-1].shape[0] // BLOCK
    inner_ref, both_ref, second_out, cot_out = refs[-5 - count : -1 - count]
    grad_refs, acc = refs[-1 - count : -1], refs[-1]
    at = pl.program_id(0)
    step = down_ref.shape[1]
    rows, width = acc.shape

    @pl.when(at == 0)
    def _():
        for ins, out in ((second_refs, second_out), (cot_refs, cot_out)):
            start = 0
            for part in ins:
                size = part.shape[0]
                out[start // BLOCK, start % BLOCK : start % BLOCK + size, :] = part[...]
                start += size

    second = second_out[...].reshape(rows, width)
    both_act = jnp.dot(second, both_weight_ref[...], preferred_element_type=jnp.float32)
    inner_grad = jnp.dot(
        cot_out[...].reshape(rows, width), down_ref[...], preferred_element_type=jnp.float32
    )
    gate_act = both_act[:, :step]
    up_act = both_act[:, step:]
    sigmoid = 1.0 / (1.0 + jnp.exp(-gate_act))
    silu = gate_act * sigmoid
    inner_ref[...] = (silu * up_act).astype(low).reshape(inner_ref.shape)
    gate_grad = (inner_grad * up_act * (sigmoid * (1.0 + gate_act * (1.0 - sigmoid)))).astype(low)
    both_grad = jnp.concatenate([gate_grad, (inner_grad * silu).astype(low)], axis=1)
    both_ref[:, :, pl.ds(pl.multiple_of(at * 2 * step, 2 * step), 2 * step)] = both_grad.reshape(
        count, BLOCK, 2 * step
    )
    part = lax.dot_general(
        both_grad, both_weight_ref[...], contract_last, preferred_element_type=jnp.float32
    )
    last = pl.num_programs(0) - 1

    @pl.when(at == 0)
    def _():
        acc[...] = part

    @pl.when((at > 0) & (at < last))
    def _():
        acc[...] += part

    @pl.when(at == last)
    def _():
        total = (acc[...] + part).astype(low)
        for block, grad in enumerate(grad_refs):
            grad[...] = total[block * BLOCK : (block + 1) * BLOCK]


def mlp_blocks(place_at, seconds, cots, weights, held):
    rows = sum(second.shape[0] for second in seconds)
    width = seconds[0].shape[1]
    count = rows // BLOCK
    hidden_width = weights.shape[1] // 3
    step = FF_STEP
    steps = hidden_width // step
    ins = [
        pl.BlockSpec(value.shape, lambda c: (0, 0), pipeline_mode=pl.Buffered(1))
        for value in (*seconds, *cots)
    ]
    kept = pl.BlockSpec((count, BLOCK, step), lambda c: (place_at, 0, c))
    kept_both = pl.BlockSpec((count, BLOCK, 2 * hidden_width), lambda c: (place_at, 0, 0))
    kept_rows = pl.BlockSpec((count, BLOCK, width), lambda c: (place_at, 0, 0))
    rows_shape = jax.ShapeDtypeStruct((RING, BLOCK, width), low)
    return pl.pallas_call(
        functools.partial(mlp_kernel, len(seconds), len(cots)),
        grid=(steps,),
        in_specs=ins
        + [
            pl.BlockSpec((width, 2 * step), lambda c: (0, c)),
            pl.BlockSpec((width, step), lambda c: (0, 2 * steps + c)),
        ]
        + [pl.BlockSpec(memory_space=pl.ANY)] * len(held),
        out_specs=(kept, kept_both, kept_rows, kept_rows)
        + (pl.BlockSpec((BLOCK, width), lambda c: (0, 0)),) * count,
        out_shape=(
            jax.ShapeDtypeStruct((RING, BLOCK, hidden_width), low),
            jax.ShapeDtypeStruct((RING, BLOCK, 2 * hidden_width), low),
            rows_shape,
            rows_shape,
        )
        + (jax.ShapeDtypeStruct((BLOCK, width), low),) * count,
        scratch_shapes=[pltpu.VMEM((rows, width), jnp.float32)],
        input_output_aliases={len(ins) + 2 + i: i for i in range(len(held))},
        compiler_params=pltpu.CompilerParams(vmem_limit_bytes=VMEM_LIMIT),
        cost_estimate=pl.CostEstimate(
            flops=2 * 5 * rows * width * hidden_width,
            bytes_accessed=2 * 3 * width * hidden_width,
            transcendentals=rows * hidden_width,
        ),
    )(*seconds, *cots, weights, weights, *held)


def mlp_out_kernel(inner_ref, weight_ref, *outs):
    inner = inner_ref[...].reshape(RING * BLOCK, inner_ref.shape[2])
    part = lax.dot_general(
        inner, weight_ref[...], contract_last, preferred_element_type=jnp.float32
    ).astype(low)
    for block, out in enumerate(outs):
        out[...] = part[block * BLOCK : (block + 1) * BLOCK]


def mlp_out_part(inner, weights):
    _, rows, hidden_width = inner.shape
    width = weights.shape[0]
    steps = 4
    return pl.pallas_call(
        mlp_out_kernel,
        grid=(steps,),
        in_specs=[
            pl.BlockSpec(inner.shape, lambda d: (0, 0, 0)),
            pl.BlockSpec((width // steps, hidden_width), lambda d: (d, 2)),
        ],
        out_specs=(pl.BlockSpec((rows, width // steps), lambda d: (0, d)),) * RING,
        out_shape=(jax.ShapeDtypeStruct((rows, width), low),) * RING,
        compiler_params=pltpu.CompilerParams(vmem_limit_bytes=VMEM_LIMIT),
        cost_estimate=pl.CostEstimate(flops=1024, bytes_accessed=1024, transcendentals=0),
    )(inner, weights)


def pair_grad(core_at, lefts, right, by_heads=False):
    width = lefts[0].shape[-1]
    outs = 512 if by_heads else right.shape[2]
    rows = RING * BLOCK

    def kernel(core_ref, *refs):
        left_refs = refs[: len(lefts)]
        right_ref, keep_ref, give_ref = refs[len(lefts) : len(lefts) + 3]
        if by_heads:
            all_ref = refs[-1]

            @pl.when(pl.program_id(0) == 0)
            def _():
                for r in range(RING):
                    for head in range(4):
                        all_ref[
                            r * BLOCK : (r + 1) * BLOCK, head * HEAD_DIM : (head + 1) * HEAD_DIM
                        ] = right_ref[4 * r + head]

            values = all_ref[...]
        else:
            values = right_ref[...].reshape(rows, outs)
        inputs = [ref[...].reshape(-1, 256) for ref in left_refs]
        inputs = inputs[0] if len(inputs) == 1 else jnp.concatenate(inputs, axis=0)
        term = lax.dot_general(
            inputs, values, contract_first, preferred_element_type=jnp.float32
        ).astype(low)
        first_core = core_ref[0] == 0
        keep_ref[0] = jnp.where(first_core, term[:128], term[128:])
        give_ref[0] = jnp.where(first_core, term[128:], term[:128])

    def columns(value):
        lead = value.shape[:-1]
        return pl.BlockSpec((*lead, 256), lambda i: (0,) * len(lead) + (i,))

    half = pl.BlockSpec((1, 128, outs), lambda i: (i, 0, 0))
    return pl.pallas_call(
        kernel,
        grid=(width // 256,),
        in_specs=[pl.BlockSpec(memory_space=pltpu.SMEM)]
        + [columns(value) for value in lefts]
        + [pl.BlockSpec(right.shape, lambda i: (0, 0, 0))],
        out_specs=(half, half),
        out_shape=(jax.ShapeDtypeStruct((width // 256, 128, outs), low),) * 2,
        scratch_shapes=[pltpu.VMEM((rows, 512), low)] * by_heads,
        compiler_params=pltpu.CompilerParams(vmem_limit_bytes=VMEM_LIMIT),
        cost_estimate=pl.CostEstimate(flops=1024, bytes_accessed=1024, transcendentals=0),
    )(core_at[None], *lefts, right)


def middle_kernel(*refs):
    mixed_refs, weight_refs = refs[:RING], refs[RING : 2 * RING]
    hidden_ref, gain_ref, middle_ref, second_ref = refs[2 * RING :]
    at = pl.program_id(0)
    step = weight_refs[0].shape[0]
    columns = pl.ds(pl.multiple_of(at * step, step), step)
    total = hidden_ref[:, columns].astype(jnp.float32)
    for mixed, weight in zip(mixed_refs, weight_refs):
        rows = jnp.concatenate([mixed[head] for head in range(4)], axis=1)
        total += lax.dot_general(
            rows, weight[...], contract_last, preferred_element_type=jnp.float32
        )
    middle_ref[:, columns] = total

    @pl.when(at == pl.num_programs(0) - 1)
    def _():
        second_ref[...] = (normalize(middle_ref[...]) * gain_ref[...]).astype(low)


def middle_part(mixed_blocks, weights, hidden, gain):
    rows, width = hidden.shape
    steps = 4
    whole = pl.BlockSpec((rows, width), lambda d: (0, 0))
    return pl.pallas_call(
        middle_kernel,
        grid=(steps,),
        in_specs=[pl.BlockSpec((4, rows, HEAD_DIM), lambda d: (0, 0, 0))] * RING
        + [pl.BlockSpec((width // steps, 512), lambda d: (d, 0))] * RING
        + [whole, pl.BlockSpec((1, width), lambda d: (0, 0))],
        out_specs=(whole, whole),
        out_shape=(
            jax.ShapeDtypeStruct((rows, width), jnp.float32),
            jax.ShapeDtypeStruct((rows, width), low),
        ),
        compiler_params=pltpu.CompilerParams(vmem_limit_bytes=32 * 1024 * 1024),
        cost_estimate=pl.CostEstimate(flops=1024, bytes_accessed=1024, transcendentals=0),
    )(*mixed_blocks, *weights, hidden, gain)


def middle_back_kernel(*refs):
    parts, weight_refs = refs[:RING], refs[RING : 2 * RING]
    middle_ref, cot_ref, gain_ref, grad_ref, low_ref, gain_out, *rest = refs[2 * RING :]
    outs, accs = rest[:RING], rest[RING:]
    at = pl.program_id(0)
    step = weight_refs[0].shape[0]

    @pl.when(at == 0)
    def _():
        second_grad = sum(part[...].astype(jnp.float32) for part in parts)
        middle = middle_ref[...]
        scale = inverse_rms(middle)
        normed = middle * scale
        gain_out[...] = jnp.sum(second_grad * normed, axis=0, keepdims=True)
        scaled = second_grad * gain_ref[...]
        grad = cot_ref[...].astype(jnp.float32) + scale * (
            scaled - normed * jnp.mean(scaled * normed, axis=-1, keepdims=True)
        )
        grad_ref[...] = grad
        low_ref[...] = grad.astype(low)
        for acc in accs:
            acc[...] = jnp.zeros_like(acc)

    rows = low_ref[:, pl.ds(pl.multiple_of(at * step, step), step)]
    for weight, acc in zip(weight_refs, accs):
        acc[...] += jnp.dot(rows, weight[...], preferred_element_type=jnp.float32)

    @pl.when(at == pl.num_programs(0) - 1)
    def _():
        for out, acc in zip(outs, accs):
            for head in range(4):
                out[head] = acc[:, head * HEAD_DIM : (head + 1) * HEAD_DIM].astype(low)


def middle_back(parts, weights, middle, cot, gain):
    rows, width = middle.shape
    steps = 4
    whole = pl.BlockSpec((rows, width), lambda d: (0, 0))
    row = pl.BlockSpec((1, width), lambda d: (0, 0))
    heads = pl.BlockSpec((4, rows, HEAD_DIM), lambda d: (0, 0, 0))
    return pl.pallas_call(
        middle_back_kernel,
        grid=(steps,),
        in_specs=[whole] * RING
        + [pl.BlockSpec((width // steps, 512), lambda d: (d, 0))] * RING
        + [whole, whole, row],
        out_specs=(whole, whole, row) + (heads,) * RING,
        out_shape=(
            jax.ShapeDtypeStruct((rows, width), jnp.float32),
            jax.ShapeDtypeStruct((rows, width), low),
            jax.ShapeDtypeStruct((1, width), jnp.float32),
        )
        + (jax.ShapeDtypeStruct((4, rows, HEAD_DIM), low),) * RING,
        scratch_shapes=[pltpu.VMEM((rows, 512), jnp.float32)] * RING,
        compiler_params=pltpu.CompilerParams(vmem_limit_bytes=VMEM_LIMIT),
        cost_estimate=pl.CostEstimate(flops=1024, bytes_accessed=1024, transcendentals=0),
    )(*parts, *weights, middle, cot, gain)


def first_kernel(
    own_ref, left_ref, top_ref, bottom_ref, right_ref, weight_ref, gains_ref, cos_ref, sin_ref,
    query_gain, key_gain, hidden_ref, first_ref, pre_ref, send_ref, gain_out,
):
    at = pl.program_id(0)
    half = top_ref.shape[0]

    @pl.when(at == 0)
    def _():
        gain_out[...] = gains_ref[...].astype(jnp.float32).T[:8]
        hidden_ref[0] = own_ref[...]

    @pl.when(at == 1)
    def _():
        hidden_ref[0] = left_ref[...]

    @pl.when(at == 2)
    def _():
        hidden_ref[0, :half] = top_ref[...]
        hidden_ref[0, half:] = bottom_ref[...]

    @pl.when(at == 3)
    def _():
        hidden_ref[0] = right_ref[...]

    first = (normalize(hidden_ref[0].astype(jnp.float32)) * gain_out[0:1]).astype(low)
    first_ref[0] = first
    pre = jnp.dot(first, weight_ref[...], preferred_element_type=jnp.float32)
    pre_ref[0] = pre
    cosine = cos_ref[0]
    sine = sin_ref[0]

    def turned(head, gain):
        values = normalize(pre[:, head * HEAD_DIM : (head + 1) * HEAD_DIM]) * gain
        return (values * cosine + pltpu.roll(values, HEAD_DIM // 2, 1) * sine).astype(low)

    for head in range(4):
        send_ref[head, 0] = turned(head, query_gain[...])
    for head in range(2):
        send_ref[2 * head, 1] = turned(4 + head, key_gain[...])
        send_ref[2 * head + 1, 1] = pre[:, (6 + head) * HEAD_DIM : (7 + head) * HEAD_DIM].astype(low)


def first_part(blocks, weights, cosine, sine, query_gain, key_gain):
    rows, width = blocks[0].shape
    row = pl.BlockSpec((1, HEAD_DIM), lambda r: (0, 0))
    turn = pl.BlockSpec((1, rows, HEAD_DIM), lambda r: (r, 0, 0))
    return pl.pallas_call(
        first_kernel,
        grid=(RING,),
        in_specs=[pl.BlockSpec(block.shape, lambda r: (0, 0)) for block in blocks]
        + [
            pl.BlockSpec((width, 1024), lambda r: (0, 0)),
            pl.BlockSpec((width, HEAD_DIM), lambda r: (0, 8)),
            turn,
            turn,
            row,
            row,
        ],
        out_specs=(
            pl.BlockSpec((1, rows, width), lambda r: (r, 0, 0)),
            pl.BlockSpec((1, rows, width), lambda r: (r, 0, 0)),
            pl.BlockSpec((1, rows, 1024), lambda r: (r, 0, 0)),
            pl.BlockSpec((4, 2, rows, HEAD_DIM), lambda r: (r, 0, 0, 0)),
            pl.BlockSpec((8, width), lambda r: (0, 0)),
        ),
        out_shape=(
            jax.ShapeDtypeStruct((RING, rows, width), low),
            jax.ShapeDtypeStruct((RING, rows, width), low),
            jax.ShapeDtypeStruct((RING, rows, 1024), jnp.float32),
            jax.ShapeDtypeStruct((BLOCKS, 2, rows, HEAD_DIM), low),
            jax.ShapeDtypeStruct((8, width), jnp.float32),
        ),
        compiler_params=pltpu.CompilerParams(vmem_limit_bytes=VMEM_LIMIT),
        cost_estimate=pl.CostEstimate(
            flops=2 * RING * rows * width * 1024,
            bytes_accessed=20 * 1024 * 1024,
            transcendentals=0,
        ),
    )(*blocks, weights, weights, cosine, sine, query_gain, key_gain)


def first_back_kernel(
    core_ref, back_ref, pre_ref, cos_ref, sin_ref, query_gain, key_gain, first_ref,
    grad_ref, keep_ref, give_ref, query_sum, key_sum, all_grads,
):
    at = pl.program_id(0)
    rows = grad_ref.shape[1]
    cosine = cos_ref[0]
    sine = sin_ref[0]

    @pl.when(at == 0)
    def _():
        query_sum[...] = jnp.zeros_like(query_sum)
        key_sum[...] = jnp.zeros_like(key_sum)

    def back(grads, head, gain, sums):
        columns = slice(head * HEAD_DIM, (head + 1) * HEAD_DIM)
        values = pre_ref[0, :, columns]
        grads = grads.astype(jnp.float32)
        grads = grads * cosine - pltpu.roll(grads, HEAD_DIM // 2, 1) * sine
        scale = inverse_rms(values)
        normed = values * scale
        sums[...] += jnp.sum(grads * normed, axis=0, keepdims=True)
        scaled = grads * gain
        out = scale * (scaled - normed * jnp.mean(scaled * normed, axis=-1, keepdims=True))
        grad_ref[0, :, columns] = out.astype(low)

    for head in range(4):
        back(back_ref[head, 0], head, query_gain[...], query_sum)
    for head in range(2):
        back(back_ref[2 * head, 1], 4 + head, key_gain[...], key_sum)
        grad_ref[0, :, (6 + head) * HEAD_DIM : (7 + head) * HEAD_DIM] = back_ref[2 * head + 1, 1]
    all_grads[pl.ds(pl.multiple_of(at * rows, rows), rows), :] = grad_ref[0]

    @pl.when(at == RING - 1)
    def _():
        grads = all_grads[...]
        first_core = core_ref[0] == 0
        for pair in range(8):
            inputs = first_ref[:, :, pair * 256 : (pair + 1) * 256].reshape(RING * rows, 256)
            term = lax.dot_general(
                inputs, grads, contract_first, preferred_element_type=jnp.float32
            ).astype(low)
            keep_ref[pair] = jnp.where(first_core, term[:128], term[128:])
            give_ref[pair] = jnp.where(first_core, term[128:], term[:128])


def first_back(core_at, returned, pre, cosine, sine, query_gain, key_gain, first_in):
    _, rows, width = first_in.shape
    row = pl.BlockSpec((1, HEAD_DIM), lambda r: (0, 0))
    turn = pl.BlockSpec((1, rows, HEAD_DIM), lambda r: (r, 0, 0))
    wide = pl.BlockSpec((1, rows, 1024), lambda r: (r, 0, 0))
    half = pl.BlockSpec((8, 128, 1024), lambda r: (0, 0, 0))
    return pl.pallas_call(
        first_back_kernel,
        grid=(RING,),
        in_specs=[
            pl.BlockSpec(memory_space=pltpu.SMEM),
            pl.BlockSpec((4, 2, rows, HEAD_DIM), lambda r: (r, 0, 0, 0)),
            wide,
            turn,
            turn,
            row,
            row,
            pl.BlockSpec((RING, rows, width), lambda r: (0, 0, 0)),
        ],
        out_specs=(wide, half, half, row, row),
        out_shape=(
            jax.ShapeDtypeStruct((RING, rows, 1024), low),
            jax.ShapeDtypeStruct((8, 128, 1024), low),
            jax.ShapeDtypeStruct((8, 128, 1024), low),
            jax.ShapeDtypeStruct((1, HEAD_DIM), jnp.float32),
            jax.ShapeDtypeStruct((1, HEAD_DIM), jnp.float32),
        ),
        scratch_shapes=[pltpu.VMEM((RING * rows, 1024), low)],
        compiler_params=pltpu.CompilerParams(vmem_limit_bytes=VMEM_LIMIT),
        cost_estimate=pl.CostEstimate(flops=1024, bytes_accessed=1024, transcendentals=0),
    )(core_at[None], returned, pre, cosine, sine, query_gain, key_gain, first_in)


def last_kernel(
    core_ref, grad_ref, weight_ref, hidden_ref, mlp_ref, query_ref, key_ref,
    own_ref, left_a, left_b, top_ref, bottom_ref, right_a, right_b, keep_ref, give_ref, gain_acc,
):
    at = pl.program_id(0)
    width = hidden_ref.shape[2]
    part = lax.dot_general(
        grad_ref[0], weight_ref[...], contract_last, preferred_element_type=jnp.float32
    )
    half = top_ref.shape[0]
    @pl.when(at == 0)
    def _():
        own_ref[...] = part.astype(low)

    for r, first, second in ((1, left_a, left_b), (2, top_ref, bottom_ref), (3, right_a, right_b)):

        @pl.when(at == r)
        def _(first=first, second=second):
            first[...] = part[:half].astype(low)
            second[...] = part[half:].astype(low)

    normed = normalize(hidden_ref[0].astype(jnp.float32))
    gain = jnp.sum(part * normed, axis=0, keepdims=True)

    @pl.when(at == 0)
    def _():
        gain_acc[...] = gain

    @pl.when(at > 0)
    def _():
        gain_acc[...] += gain

    @pl.when(at == RING - 1)
    def _():
        lines = [
            gain_acc[...],
            mlp_ref[...],
            jnp.concatenate([query_ref[...]] * BLOCKS, axis=1),
            jnp.concatenate([key_ref[...]] * BLOCKS, axis=1),
            jnp.zeros((HEAD_DIM - 4, width), jnp.float32),
        ]
        turned = jnp.concatenate(lines, axis=0).T.astype(low)
        first_core = core_ref[0] == 0
        for pair in range(8):
            first = turned[pair * 256 : pair * 256 + 128]
            second = turned[pair * 256 + 128 : (pair + 1) * 256]
            keep_ref[pair] = jnp.where(first_core, first, second)
            give_ref[pair] = jnp.where(first_core, second, first)


def last_part(core_at, grads, weights, hidden_all, mlp_part, query_part, key_part):
    _, rows, width = hidden_all.shape
    block = pl.BlockSpec((rows, width), lambda r: (0, 0))
    small = pl.BlockSpec((rows // 2, width), lambda r: (0, 0))
    whole = jax.ShapeDtypeStruct((rows, width), low)
    part = jax.ShapeDtypeStruct((rows // 2, width), low)
    row = pl.BlockSpec((1, HEAD_DIM), lambda r: (0, 0))
    half = pl.BlockSpec((8, 128, HEAD_DIM), lambda r: (0, 0, 0))
    return pl.pallas_call(
        last_kernel,
        grid=(RING,),
        in_specs=[
            pl.BlockSpec(memory_space=pltpu.SMEM),
            pl.BlockSpec((1, rows, 1024), lambda r: (r, 0, 0)),
            pl.BlockSpec((width, 1024), lambda r: (0, 0)),
            pl.BlockSpec((1, rows, width), lambda r: (r, 0, 0)),
            pl.BlockSpec((1, width), lambda r: (0, 0)),
            row,
            row,
        ],
        out_specs=(block,) + (small,) * 6 + (half, half),
        out_shape=(whole,) + (part,) * 6
        + (jax.ShapeDtypeStruct((8, 128, HEAD_DIM), low),) * 2,
        scratch_shapes=[pltpu.VMEM((1, width), jnp.float32)],
        compiler_params=pltpu.CompilerParams(vmem_limit_bytes=VMEM_LIMIT),
        cost_estimate=pl.CostEstimate(flops=1024, bytes_accessed=1024, transcendentals=0),
    )(core_at[None], grads, weights, hidden_all, mlp_part, query_part, key_part)


def arrange_kernel(at_ref, own_ref, other_ref, out_ref):
    y_at, x_at, core_at = at_ref[0], at_ref[1], at_ref[2]
    for dy in range(RING):
        for dx in range(2):
            first = ((y_at - dy + RING) & 3) * 4 + (x_at ^ dx) * 2
            own = pl.multiple_of((first + core_at) * 128, 128)
            other = pl.multiple_of((first + 1 - core_at) * 128, 128)
            out_ref[pl.ds(own, 128), :] = own_ref[dy, dx]
            out_ref[pl.ds(other, 128), :] = other_ref[dy, dx]


def gather_by_permutes(pairs, y_at, x_at, core_at):
    own = jnp.stack(pairs)
    other = shift(own, "core", 1, 2)
    whole = pl.BlockSpec(memory_space=pltpu.VMEM)
    return pl.pallas_call(
        arrange_kernel,
        in_specs=[pl.BlockSpec(memory_space=pltpu.SMEM), whole, whole],
        out_specs=whole,
        out_shape=jax.ShapeDtypeStruct((BLOCKS * 128, own.shape[3]), own.dtype),
        compiler_params=pltpu.CompilerParams(vmem_limit_bytes=VMEM_LIMIT),
        cost_estimate=pl.CostEstimate(flops=1024, bytes_accessed=1024, transcendentals=0),
    )(jnp.stack([y_at, x_at, core_at]), own, other)


def pair_sums_kernel(keep_ref, come_ref, gains_keep, gains_come, out_ref):
    f32 = jnp.float32
    wide = keep_ref.shape[2]
    out_ref[:, :, :wide] = (keep_ref[...].astype(f32) + come_ref[...].astype(f32)).astype(low)
    out_ref[:, :, wide:] = (gains_keep[...].astype(f32) + gains_come[...].astype(f32)).astype(low)


def pair_sums(keep, come, more_keep, more_come):
    blocks, rows, wide = keep.shape
    narrow = more_keep.shape[2]
    large = pl.BlockSpec((4, rows, wide), lambda i: (i, 0, 0))
    small = pl.BlockSpec((4, rows, narrow), lambda i: (i, 0, 0))
    return pl.pallas_call(
        pair_sums_kernel,
        grid=(blocks // 4,),
        in_specs=[large, large, small, small],
        out_specs=pl.BlockSpec((4, rows, wide + narrow), lambda i: (i, 0, 0)),
        out_shape=jax.ShapeDtypeStruct((blocks, rows, wide + narrow), low),
        compiler_params=pltpu.CompilerParams(vmem_limit_bytes=VMEM_LIMIT),
        cost_estimate=pl.CostEstimate(flops=1024, bytes_accessed=1024, transcendentals=0),
    )(keep, come, more_keep, more_come)


def to_heads(send):
    return lax.all_to_all(send, GROUP_AXES, 0, 0, tiled=True)


def after(value, *others):
    return lax.optimization_barrier((value, others))[0]


def ring_blocks(values):
    half = values.shape[0] // 2
    left = shift(values, "z", 1)
    right = shift(values, "z", 3)
    opposite = jnp.concatenate(
        [shift(left[:half], "z", 1), shift(right[half:], "z", 3)], axis=0
    )
    return [values, left, opposite, right]


def together(*values):
    return lax.optimization_barrier(values)


def place(z_at, blocks, widths, chunk=None, summed=False):
    rows = blocks[0].shape[0]
    whole = pl.BlockSpec(memory_space=pltpu.VMEM)
    shapes = [RING * part for part in widths] + [HEAD_DIM] * summed

    def kernel(z_ref, *refs):
        ins, outs = refs[:RING], refs[RING:]
        for r in range(RING):
            slot = (z_ref[0] - r + RING) & 3
            start = 0
            for turn in range(widths[0] // chunk if chunk else 1):
                for out, part in zip(outs, widths):
                    size = chunk or part
                    at = pl.multiple_of(slot * part + turn * size, 128)
                    out[:, pl.ds(at, size)] = ins[r][:, start : start + size].astype(jnp.float32)
                    start += size
            if summed:
                columns = ins[r][:, start : start + HEAD_DIM].astype(jnp.float32)
                outs[-1][...] = columns if r == 0 else outs[-1][...] + columns

    return pl.pallas_call(
        kernel,
        in_specs=[pl.BlockSpec(memory_space=pltpu.SMEM)] + [whole] * RING,
        out_specs=tuple(whole for _ in shapes),
        out_shape=tuple(jax.ShapeDtypeStruct((rows, part), jnp.float32) for part in shapes),
        compiler_params=pltpu.CompilerParams(vmem_limit_bytes=VMEM_LIMIT),
        cost_estimate=pl.CostEstimate(flops=1024, bytes_accessed=1024, transcendentals=0),
    )(z_at[None], *blocks)


def send_back(block, r):
    return shift(block, "z", -r)


def local(
    hidden_in,
    cotangent,
    segment_ids,
    positions,
    attn_gain,
    query_gain,
    key_gain,
    query_weight,
    key_weight,
    value_weight,
    out_weight,
    mlp_gain,
    gate_weight,
    up_weight,
    down_weight,
):
    f32 = jnp.float32
    rows, width = hidden_in.shape
    ring_rows = RING * rows
    z_at = lax.axis_index("z")
    y_at = lax.axis_index("y")
    x_at = lax.axis_index("x_hi")
    core_at = lax.axis_index("core")
    my_index = (y_at * 2 + x_at) * 2 + core_at

    def columns(weight):
        part = weight.shape[1] // RING
        return lax.dynamic_slice_in_dim(weight, z_at * part, part, 1).astype(low)

    def gather(block):
        return lax.all_gather(block, GROUP_AXES, axis=0, tiled=True)

    own_places = lax.dynamic_slice_in_dim(positions, my_index * rows, rows)
    firsts = positions.reshape(BLOCKS, BLOCK)[:, 0]
    segments = segment_ids.reshape(BLOCKS, BLOCK)[:, 0]
    logical = firsts // BLOCK + jnp.maximum(segments - 1, 0) * 2
    numbers = jnp.arange(BLOCKS, dtype=jnp.int32)
    order = jnp.sum(jnp.where(logical[:, None] == numbers[None, :], numbers[:, None], 0), axis=0)
    notes = gather_z(jnp.concatenate([own_places, order, jnp.zeros((112,), jnp.int32)])[None])
    places = notes[:, :rows]
    order = lax.dynamic_index_in_dim(notes, y_at, 0, keepdims=False)[rows : rows + BLOCKS]

    gains = jnp.pad(
        jnp.stack([attn_gain, mlp_gain], axis=1).astype(low), ((0, 0), (0, HEAD_DIM - 2))
    )
    first_weights = gather(
        jnp.concatenate(
            [columns(query_weight), columns(key_weight), columns(value_weight), gains], axis=1
        )
    )
    out_columns = columns(out_weight)
    out_come = shift(out_columns, "x_hi", 1, 2)
    out_pairs = jnp.stack([out_columns, out_come])
    out_pairs = [out_pairs] + [shift(out_pairs, "y", r) for r in range(1, RING)]

    hidden_own = after(hidden_in, notes, out_come)
    hidden_left = shift(hidden_own, "z", 1)
    hidden_right = shift(hidden_own, "z", 3)
    gate_columns, up_columns, down_columns, hidden_left, hidden_right, out_pairs = together(
        gate_weight, up_weight, down_weight, hidden_left, hidden_right, out_pairs
    )
    out_slice = gather_by_permutes(out_pairs, y_at, x_at, core_at)
    gate_columns, up_columns = columns(gate_columns), columns(up_columns)
    mlp_columns = []
    for start in range(0, gate_columns.shape[1], FF_STEP):
        mlp_columns.append(gate_columns[:, start : start + FF_STEP])
        mlp_columns.append(up_columns[:, start : start + FF_STEP])
    mlp_weights = gather(jnp.concatenate(mlp_columns + [columns(down_columns)], axis=1))
    half = rows // 2
    hidden_blocks = [
        hidden_own,
        hidden_left,
        shift(hidden_left[:half], "z", 1),
        shift(hidden_right[half:], "z", 3),
        hidden_right,
    ]
    out_slice = after(out_slice, *hidden_blocks)
    out_left = shift(out_slice, "z", 1)
    out_right = shift(out_slice, "z", 3)
    frequency = rope_base ** (-2.0 * jnp.arange(HEAD_DIM // 2, dtype=f32) / HEAD_DIM)
    angles = places.astype(f32)[:, :, None] * frequency[None, None, :]
    cosine = jnp.cos(angles)
    sine = jnp.sin(angles)
    cosine = jnp.concatenate([cosine, cosine], axis=-1)
    sine = jnp.concatenate([-sine, sine], axis=-1)
    query_row = query_gain[None]
    key_row = key_gain[None]

    hidden_all, first_in, qkv_pre, send, gain_rows = first_part(
        hidden_blocks, first_weights, cosine, sine, query_row, key_row
    )
    attn_scale = gain_rows[0:1]
    mlp_scale = gain_rows[1:2]
    arrived, out_left, out_right = together(to_heads(send), out_left, out_right)
    other_pair = shift(arrived[:, 1], "core", 1, 2)
    head_mixed, head_mixed_t, head_logs = attention_forward(order, core_at, arrived, other_pair)
    out_top = shift(out_left[: width // 2], "z", 1)
    out_bottom = shift(out_right[width // 2 :], "z", 3)
    head_mixed, head_mixed_t, head_logs, out_top, out_bottom = together(
        head_mixed, head_mixed_t, head_logs, out_top, out_bottom
    )
    cot_own = after(cotangent, head_mixed)
    cot_left = shift(cot_own, "z", 1)
    cot_right = shift(cot_own, "z", 3)

    cot_top = shift(cot_left[:half], "z", 1)
    cot_bottom = shift(cot_right[half:], "z", 3)
    mixed_arrived, cot_left, cot_right, cot_top, cot_bottom = together(
        to_heads(head_mixed), cot_left, cot_right, cot_top, cot_bottom
    )
    mixed_blocks = [mixed_arrived[:4]] + [
        shift(mixed_arrived[4 * (RING - j) : 4 * (RING - j) + 4], "z", j) for j in range(1, RING)
    ]
    out_opposite = jnp.concatenate([out_top, out_bottom], axis=0)
    out_weights = [out_slice, out_left, out_opposite, out_right]
    mixed_blocks, out_weights = together(mixed_blocks, out_weights)
    middle, second_in = middle_part(mixed_blocks, out_weights, hidden_in, mlp_scale)
    hidden = hidden_in.astype(f32)
    left = shift(second_in, "z", 1)
    right = shift(second_in, "z", 3)
    *held, own_part = mlp_blocks(0, [second_in], [cot_own], mlp_weights, ())
    held, own_part, left, right, second_in = together(held, own_part, left, right, second_in)
    opposite = shift(second_in, "z", 2)
    *held, left_part, right_part = mlp_blocks(
        1, [left, right], [cot_left, cot_right], mlp_weights, held
    )
    left_back = send_back(left_part, 1)
    right_back = send_back(right_part, 3)
    held, opposite = together(held, opposite)
    *held, opposite_part = mlp_blocks(
        1, [opposite], [cot_top, cot_bottom], mlp_weights, held
    )
    opposite_back = send_back(opposite_part, 2)
    inner, both_grad, second_all, cot_all = held

    def pair_sum(keep, come):
        return (keep.astype(f32) + come.astype(f32)).astype(low)

    def to_owners(pair):
        return lax.all_to_all(pair, ("y", "x_hi"), 0, 0, tiled=True)

    def add_up(terms):
        return jnp.sum(terms.astype(f32), axis=0).astype(low)

    def over_x(share):
        return share, shift(share, "x_lo", 1, 2)

    def over_z(pair):
        share = pair_sum(*pair)
        return [share] + [shift(share, "z", r) for r in range(1, RING)]

    both_term = lax.dot_general(
        second_all.reshape(ring_rows, width),
        both_grad.reshape(ring_rows, 3072),
        contract_first,
        preferred_element_type=f32,
    ).astype(low)
    left_back, right_back, opposite_back, both_term, inner = together(
        left_back, right_back, opposite_back, both_term, inner
    )
    both_share = lax.psum_scatter(both_term, GROUP_AXES, scatter_dimension=0, tiled=True)

    middle_grad, own_low, mlp_gain_part, *grad_blocks = middle_back(
        (own_part, left_back, right_back, opposite_back),
        out_weights,
        middle,
        cotangent,
        mlp_scale,
    )
    grad_blocks = [grad_blocks[0]] + [shift(grad_blocks[RING - r], "z", r) for r in range(1, RING)]
    down_keep, down_give = pair_grad(core_at, [cot_all], inner)
    grad_blocks, down_keep, down_give, own_low, inner = together(
        grad_blocks, down_keep, down_give, own_low, inner
    )
    head_grads = to_heads(jnp.concatenate(grad_blocks, axis=0))
    low_left = shift(own_low, "z", 1)
    low_right = shift(own_low, "z", 3)
    mlp_own, mlp_opposite, mlp_left, mlp_right = mlp_out_part(inner, mlp_weights)
    head_grads, low_left, low_right, own_low, mlp_opposite, mlp_left, mlp_right = together(
        head_grads, low_left, low_right, own_low, mlp_opposite, mlp_left, mlp_right
    )
    mlp_left = send_back(mlp_left, 1)
    mlp_right = send_back(mlp_right, 3)

    query_grad, grad_keep, grad_give = attention_backward(
        order, core_at, arrived, other_pair, head_grads, head_mixed_t, head_logs
    )
    query_grad, grad_keep, grad_give, mlp_left, mlp_right, own_low, mlp_opposite, down_give = together(
        query_grad, grad_keep, grad_give, mlp_left, mlp_right, own_low, mlp_opposite, down_give
    )
    low_opposite = shift(own_low, "z", 2)
    mlp_opposite = send_back(after(mlp_opposite, low_opposite), 2)
    grads_send = lax.dynamic_update_slice_in_dim(
        query_grad, pair_sum(grad_keep, shift(grad_give, "core", 1, 2))[:, None], 1, 1
    )
    returned = to_heads(grads_send)
    out_keep, out_give = pair_grad(
        core_at, [own_low, low_left, low_opposite, low_right], mixed_arrived, by_heads=True
    )
    down_sum = pair_sums(
        down_keep,
        shift(down_give, "core", 1, 2),
        out_keep,
        shift(out_give, "core", 1, 2),
    )
    returned, both_share, down_sum = together(returned, both_share, down_sum)
    both_pair = over_x(both_share)
    down_terms = lax.all_to_all(
        down_sum.reshape(RING, 2, 128, down_sum.shape[2]), "y", 0, 0, tiled=True
    )
    qkv_grad, qkv_keep, qkv_give, query_gain_part, key_gain_part = first_back(
        core_at, returned, qkv_pre, cosine, sine, query_row, key_row, first_in
    )
    qkv_grad, qkv_give, both_pair, mlp_opposite = together(
        qkv_grad, qkv_give, both_pair, mlp_opposite
    )
    both_sum = pair_sum(*both_pair)
    both_left = shift(both_sum, "z", 1)
    both_right = shift(both_sum, "z", 3)
    qkv_come = shift(qkv_give, "core", 1, 2)
    *first_parts, gains_keep, gains_give = last_part(
        core_at,
        qkv_grad,
        first_weights,
        hidden_all,
        mlp_gain_part,
        query_gain_part,
        key_gain_part,
    )
    first_parts, gains_give, qkv_come, both_left, both_right, both_sum = together(
        first_parts, gains_give, qkv_come, both_left, both_right, both_sum
    )
    down_halves = add_up(down_terms)
    down_keep = lax.dynamic_index_in_dim(down_halves, x_at, 0, keepdims=False)
    down_give = lax.dynamic_index_in_dim(down_halves, 1 - x_at, 0, keepdims=False)
    down_come = lax.ppermute(down_give, ("x_lo", "x_hi"), [(i, 3 - i) for i in range(4)])
    down_pair = over_x(pair_sum(down_keep, down_come))
    gains_come = shift(gains_give, "core", 1, 2)
    first_own, left_a, left_b, first_top, first_bottom, right_a, right_b = first_parts
    first_top = shift(first_top, "z", 3)
    first_bottom = shift(first_bottom, "z", 1)
    qkv_terms = to_owners(pair_sums(qkv_keep, qkv_come, gains_keep, gains_come))
    first_left = send_back(jnp.concatenate([pair_sum(left_a, first_top), left_b], axis=0), 1)
    first_right = send_back(jnp.concatenate([right_a, pair_sum(right_b, first_bottom)], axis=0), 3)
    both_opposite = shift(both_sum, "z", 2)
    qkv_terms, first_left, first_right, both_opposite, down_pair = together(
        qkv_terms, first_left, first_right, both_opposite, down_pair
    )
    down_blocks = over_z(down_pair)
    qkv_share = add_up(qkv_terms)
    both_blocks = [both_sum, both_left, both_opposite, both_right]
    qkv_pair = over_x(qkv_share)
    output = (
        middle
        + mlp_own.astype(f32)
        + mlp_left.astype(f32)
        + mlp_right.astype(f32)
        + mlp_opposite.astype(f32)
    ).astype(low)
    first_grad = first_own.astype(f32) + first_left.astype(f32) + first_right.astype(f32)
    hidden_rms = inverse_rms(hidden)
    own_norm = hidden * hidden_rms
    scaled_first = first_grad * attn_scale
    hidden_grad = (
        middle_grad
        + hidden_rms
        * (scaled_first - own_norm * jnp.mean(scaled_first * own_norm, axis=-1, keepdims=True))
    ).astype(low)

    down_grad_out, out_grad_out = place(z_at, down_blocks, (1536, 512))
    gate_grad_out, up_grad_out = place(z_at, both_blocks, (1536, 1536), chunk=FF_STEP)
    query_grad_out, key_grad_out, value_grad_out, gain_sum = place(
        z_at, over_z(qkv_pair), (512, 256, 256), summed=True
    )
    gain_sum = gain_sum[:, :4].T

    return (
        output,
        hidden_grad,
        gain_sum[0],
        gain_sum[2],
        gain_sum[3],
        query_grad_out,
        key_grad_out,
        value_grad_out,
        out_grad_out,
        gain_sum[1],
        gate_grad_out,
        up_grad_out,
        down_grad_out,
    )


def solution(mesh):
    fine = Mesh(mesh.devices.reshape(2, 4, 4, 2, 2), ALL_AXES)
    rep = ("x_lo", "z")
    row = P(ALL_AXES, None)
    part = P(GROUP_AXES)
    weight = P(GROUP_AXES, None)
    in_specs = (
        row,
        row,
        P(rep),
        P(rep),
        part,
        P(),
        P(),
        weight,
        weight,
        weight,
        weight,
        part,
        weight,
        weight,
        weight,
    )
    out_specs = (
        row,
        row,
        part,
        P(),
        P(),
        weight,
        weight,
        weight,
        weight,
        part,
        weight,
        weight,
        weight,
    )
    return jax.shard_map(local, mesh=fine, in_specs=in_specs, out_specs=out_specs, check_vma=False)
```

```python
import functools

import jax
import jax.numpy as jnp
from jax import lax
from jax.experimental import pallas as pl
from jax.experimental.pallas import tpu as pltpu
from jax.sharding import Mesh
from jax.sharding import PartitionSpec as P

HEAD_DIM = 128
RING = 4
BLOCK = 256
BLOCKS = 16
TILE = 512
TILES = 8
PROMPT_TILES = 6
FF_STEP = 512
VMEM_LIMIT = 60 * 1024 * 1024

norm_eps = 1e-06
rope_base = 1000000.0
score_scale = HEAD_DIM ** (-0.5)
score_scale_log2 = score_scale * 1.4426950408889634
contract_first = (((0,), (0,)), ((), ()))
contract_last = (((1,), (1,)), ((), ()))
GROUP_AXES = ("y", "x_hi", "core")
ALL_AXES = ("x_lo", "z", "y", "x_hi", "core")
low = jnp.bfloat16


def inverse_rms(values):
    return lax.rsqrt(jnp.mean(values * values, axis=-1, keepdims=True) + norm_eps)


def normalize(values):
    return values * inverse_rms(values)


def shift(values, axis, by, size=RING):
    return lax.ppermute(values, axis, [(i, (i + by) % size) for i in range(size)])


def gather_z(values):
    return jnp.concatenate(
        [values, shift(values, "z", 1), shift(values, "z", 2), shift(values, "z", 3)], axis=0
    )


def forward_kernel(
    order, core, own_a, own_b, other_a, other_b, mixed_ref, mixed_t_ref, log_ref, k_all, v_t, acc, total
):
    tile = pl.program_id(0)
    start = tile * TILE

    def take(keys, values):
        for half in range(2):
            rows = pl.ds(pl.multiple_of(start + half * BLOCK, BLOCK), BLOCK)
            k_all[rows, :] = keys[half]
            v_t[tile, :, half * BLOCK : (half + 1) * BLOCK] = (
                values[half].astype(jnp.float32).T.astype(low)
            )

    @pl.when(core[0] == 0)
    def _():
        take((own_a[0, 1], own_b[0, 1]), (other_a[0], other_b[0]))

    @pl.when(core[0] == 1)
    def _():
        take((other_a[0], other_b[0]), (own_a[0, 1], own_b[0, 1]))

    queries = jnp.concatenate([own_a[0, 0], own_b[0, 0]], axis=0)
    acc[...] = jnp.zeros_like(acc)
    total[...] = jnp.zeros_like(total)

    def chunk(at, masked):
        keys = k_all[pl.ds(pl.multiple_of(at * TILE, TILE), TILE), :]
        scores = lax.dot_general(keys, queries, contract_last, preferred_element_type=jnp.float32)
        weights = jnp.exp2(scores * score_scale_log2)
        if masked:
            key_row = lax.broadcasted_iota(jnp.int32, (TILE, TILE), 0)
            query_row = lax.broadcasted_iota(jnp.int32, (TILE, TILE), 1)
            weights = jnp.where(key_row <= query_row, weights, 0.0)
        total[...] += jnp.sum(weights, axis=0, keepdims=True)
        acc[...] += jnp.dot(v_t[at], weights.astype(low), preferred_element_type=jnp.float32)

    full = jnp.minimum(tile, PROMPT_TILES)
    for count in range(PROMPT_TILES + 1):

        @pl.when(full == count)
        def _(count=count):
            for at in range(count):
                chunk(at, False)
            chunk(tile, True)

    mixed_t = acc[...] / total[...]
    mixed_t_ref[0] = mixed_t
    log_ref[0] = jnp.log2(total[...])
    mixed = mixed_t.T.astype(low)
    mixed_ref[order[2 * tile]] = mixed[:BLOCK]
    mixed_ref[order[2 * tile + 1]] = mixed[BLOCK:]


def tile_specs(lead):
    return [
        pl.BlockSpec(
            (1, *lead, BLOCK, HEAD_DIM),
            functools.partial(
                lambda half, tile, order, core: (order[2 * tile + half],) + (0,) * (len(lead) + 2),
                half,
            ),
        )
        for half in range(2)
    ]


def attention_forward(order, core_at, arrived, other):
    whole = pl.BlockSpec(memory_space=pltpu.VMEM)
    turned = pl.BlockSpec((1, HEAD_DIM, TILE), lambda tile, order, core: (tile, 0, 0))
    line = pl.BlockSpec((1, 1, TILE), lambda tile, order, core: (tile, 0, 0))
    return pl.pallas_call(
        forward_kernel,
        out_shape=(
            jax.ShapeDtypeStruct((BLOCKS, BLOCK, HEAD_DIM), low),
            jax.ShapeDtypeStruct((TILES, HEAD_DIM, TILE), jnp.float32),
            jax.ShapeDtypeStruct((TILES, 1, TILE), jnp.float32),
        ),
        grid_spec=pltpu.PrefetchScalarGridSpec(
            num_scalar_prefetch=2,
            grid=(TILES,),
            in_specs=tile_specs((2,)) + tile_specs(()),
            out_specs=(whole, turned, line),
            scratch_shapes=[
                pltpu.VMEM((BLOCKS * BLOCK, HEAD_DIM), low),
                pltpu.VMEM((TILES, HEAD_DIM, TILE), low),
                pltpu.VMEM((HEAD_DIM, TILE), jnp.float32),
                pltpu.VMEM((1, TILE), jnp.float32),
            ],
        ),
        compiler_params=pltpu.CompilerParams(vmem_limit_bytes=VMEM_LIMIT),
        cost_estimate=pl.CostEstimate(
            flops=1024, bytes_accessed=1024, transcendentals=0
        ),
    )(order, core_at[None], arrived, arrived, other, other)


def backward_kernel(
    order, core, own_a, own_b, other_a, other_b, grad_a, grad_b, mixed_t_ref, log_ref,
    q_out, keep_out, give_out, k_all, v_all, k_t, q_acc, k_acc, v_acc,
):
    tile = pl.program_id(0)
    start = tile * TILE

    def take(keys, values):
        for half in range(2):
            rows = pl.ds(pl.multiple_of(start + half * BLOCK, BLOCK), BLOCK)
            k_all[rows, :] = keys[half]
            v_all[rows, :] = values[half]
            k_t[tile, :, half * BLOCK : (half + 1) * BLOCK] = (
                keys[half].astype(jnp.float32).T.astype(low)
            )

    @pl.when(core[0] == 0)
    def _():
        take((own_a[0, 1], own_b[0, 1]), (other_a[0], other_b[0]))

    @pl.when(core[0] == 1)
    def _():
        take((other_a[0], other_b[0]), (own_a[0, 1], own_b[0, 1]))

    rows = pl.ds(pl.multiple_of(start, TILE), TILE)
    k_acc[rows, :] = jnp.zeros((TILE, HEAD_DIM), jnp.float32)
    v_acc[rows, :] = jnp.zeros((TILE, HEAD_DIM), jnp.float32)
    queries = jnp.concatenate([own_a[0, 0], own_b[0, 0]], axis=0)
    grads = jnp.concatenate([grad_a[0], grad_b[0]], axis=0)
    grads_t = grads.astype(jnp.float32).T
    shared = jnp.sum(grads_t * mixed_t_ref[0], axis=0, keepdims=True)
    logs = log_ref[0]
    q_acc[...] = jnp.zeros_like(q_acc)

    def chunk(at, masked):
        rows = pl.ds(pl.multiple_of(at * TILE, TILE), TILE)
        scores = lax.dot_general(
            k_all[rows, :], queries, contract_last, preferred_element_type=jnp.float32
        )
        probs = jnp.exp2(scores * score_scale_log2 - logs)
        if masked:
            key_row = lax.broadcasted_iota(jnp.int32, (TILE, TILE), 0)
            query_row = lax.broadcasted_iota(jnp.int32, (TILE, TILE), 1)
            probs = jnp.where(key_row <= query_row, probs, 0.0)
        prob_grads = lax.dot_general(
            v_all[rows, :], grads, contract_last, preferred_element_type=jnp.float32
        )
        score_grads = (probs * (prob_grads - shared)).astype(low)
        v_acc[rows, :] += jnp.dot(probs.astype(low), grads, preferred_element_type=jnp.float32)
        k_acc[rows, :] += jnp.dot(score_grads, queries, preferred_element_type=jnp.float32)
        q_acc[...] += jnp.dot(k_t[at], score_grads, preferred_element_type=jnp.float32)

    full = jnp.minimum(tile, PROMPT_TILES)
    for count in range(PROMPT_TILES + 1):

        @pl.when(full == count)
        def _(count=count):
            for at in range(count):
                chunk(at, False)
            chunk(tile, True)

    query_grad = (q_acc[...] * score_scale).T.astype(low)
    q_out[order[2 * tile], 0] = query_grad[:BLOCK]
    q_out[order[2 * tile + 1], 0] = query_grad[BLOCK:]

    def give(keep_acc, keep_scale, give_acc, give_scale):
        for at in range(BLOCKS):
            rows = slice(at * BLOCK, (at + 1) * BLOCK)
            keep_out[order[at]] = (keep_acc[rows, :] * keep_scale).astype(low)
            give_out[order[at]] = (give_acc[rows, :] * give_scale).astype(low)

    @pl.when((tile == TILES - 1) & (core[0] == 0))
    def _():
        give(k_acc, score_scale, v_acc, 1.0)

    @pl.when((tile == TILES - 1) & (core[0] == 1))
    def _():
        give(v_acc, 1.0, k_acc, score_scale)


def attention_backward(order, core_at, arrived, other, grads, mixed_t, logs):
    whole = pl.BlockSpec(memory_space=pltpu.VMEM)
    rows = BLOCKS * BLOCK
    turned = pl.BlockSpec((1, HEAD_DIM, TILE), lambda tile, order, core: (tile, 0, 0))
    line = pl.BlockSpec((1, 1, TILE), lambda tile, order, core: (tile, 0, 0))
    return pl.pallas_call(
        backward_kernel,
        out_shape=(jax.ShapeDtypeStruct((BLOCKS, 2, BLOCK, HEAD_DIM), low),)
        + (jax.ShapeDtypeStruct((BLOCKS, BLOCK, HEAD_DIM), low),) * 2,
        grid_spec=pltpu.PrefetchScalarGridSpec(
            num_scalar_prefetch=2,
            grid=(TILES,),
            in_specs=tile_specs((2,)) + tile_specs(()) + tile_specs(()) + [turned, line],
            out_specs=(whole, whole, whole),
            scratch_shapes=[
                pltpu.VMEM((rows, HEAD_DIM), low),
                pltpu.VMEM((rows, HEAD_DIM), low),
                pltpu.VMEM((TILES, HEAD_DIM, TILE), low),
                pltpu.VMEM((HEAD_DIM, TILE), jnp.float32),
                pltpu.VMEM((rows, HEAD_DIM), jnp.float32),
                pltpu.VMEM((rows, HEAD_DIM), jnp.float32),
            ],
        ),
        compiler_params=pltpu.CompilerParams(vmem_limit_bytes=VMEM_LIMIT),
        cost_estimate=pl.CostEstimate(
            flops=1024, bytes_accessed=1024, transcendentals=0
        ),
    )(order, core_at[None], arrived, arrived, other, other, grads, grads, mixed_t, logs)


def mlp_kernel(parts, cot_parts, *refs):
    second_refs, cot_refs = refs[:parts], refs[parts : parts + cot_parts]
    both_weight_ref, down_ref = refs[parts + cot_parts : parts + cot_parts + 2]
    count = refs[-1].shape[0] // BLOCK
    inner_ref, both_ref, second_out, cot_out = refs[-5 - count : -1 - count]
    grad_refs, acc = refs[-1 - count : -1], refs[-1]
    at = pl.program_id(0)
    step = down_ref.shape[1]
    rows, width = acc.shape

    @pl.when(at == 0)
    def _():
        for ins, out in ((second_refs, second_out), (cot_refs, cot_out)):
            start = 0
            for part in ins:
                size = part.shape[0]
                out[start // BLOCK, start % BLOCK : start % BLOCK + size, :] = part[...]
                start += size

    second = second_out[...].reshape(rows, width)
    both_act = jnp.dot(second, both_weight_ref[...], preferred_element_type=jnp.float32)
    inner_grad = jnp.dot(
        cot_out[...].reshape(rows, width), down_ref[...], preferred_element_type=jnp.float32
    )
    gate_act = both_act[:, :step]
    up_act = both_act[:, step:]
    sigmoid = 1.0 / (1.0 + jnp.exp(-gate_act))
    silu = gate_act * sigmoid
    inner_ref[...] = (silu * up_act).astype(low).reshape(inner_ref.shape)
    gate_grad = (inner_grad * up_act * (sigmoid * (1.0 + gate_act * (1.0 - sigmoid)))).astype(low)
    both_grad = jnp.concatenate([gate_grad, (inner_grad * silu).astype(low)], axis=1)
    both_ref[:, :, pl.ds(pl.multiple_of(at * 2 * step, 2 * step), 2 * step)] = both_grad.reshape(
        count, BLOCK, 2 * step
    )
    part = lax.dot_general(
        both_grad, both_weight_ref[...], contract_last, preferred_element_type=jnp.float32
    )
    last = pl.num_programs(0) - 1

    @pl.when(at == 0)
    def _():
        acc[...] = part

    @pl.when((at > 0) & (at < last))
    def _():
        acc[...] += part

    @pl.when(at == last)
    def _():
        total = (acc[...] + part).astype(low)
        for block, grad in enumerate(grad_refs):
            grad[...] = total[block * BLOCK : (block + 1) * BLOCK]


def mlp_blocks(place_at, seconds, cots, weights, held):
    rows = sum(second.shape[0] for second in seconds)
    width = seconds[0].shape[1]
    count = rows // BLOCK
    hidden_width = weights.shape[1] // 3
    step = FF_STEP
    steps = hidden_width // step
    ins = [
        pl.BlockSpec(value.shape, lambda c: (0, 0), pipeline_mode=pl.Buffered(1))
        for value in (*seconds, *cots)
    ]
    kept = pl.BlockSpec((count, BLOCK, step), lambda c: (place_at, 0, c))
    kept_both = pl.BlockSpec((count, BLOCK, 2 * hidden_width), lambda c: (place_at, 0, 0))
    kept_rows = pl.BlockSpec((count, BLOCK, width), lambda c: (place_at, 0, 0))
    rows_shape = jax.ShapeDtypeStruct((RING, BLOCK, width), low)
    return pl.pallas_call(
        functools.partial(mlp_kernel, len(seconds), len(cots)),
        grid=(steps,),
        in_specs=ins
        + [
            pl.BlockSpec((width, 2 * step), lambda c: (0, c)),
            pl.BlockSpec((width, step), lambda c: (0, 2 * steps + c)),
        ]
        + [pl.BlockSpec(memory_space=pl.ANY)] * len(held),
        out_specs=(kept, kept_both, kept_rows, kept_rows)
        + (pl.BlockSpec((BLOCK, width), lambda c: (0, 0)),) * count,
        out_shape=(
            jax.ShapeDtypeStruct((RING, BLOCK, hidden_width), low),
            jax.ShapeDtypeStruct((RING, BLOCK, 2 * hidden_width), low),
            rows_shape,
            rows_shape,
        )
        + (jax.ShapeDtypeStruct((BLOCK, width), low),) * count,
        scratch_shapes=[pltpu.VMEM((rows, width), jnp.float32)],
        input_output_aliases={len(ins) + 2 + i: i for i in range(len(held))},
        compiler_params=pltpu.CompilerParams(vmem_limit_bytes=VMEM_LIMIT),
        cost_estimate=pl.CostEstimate(
            flops=2 * 5 * rows * width * hidden_width,
            bytes_accessed=2 * 3 * width * hidden_width,
            transcendentals=rows * hidden_width,
        ),
    )(*seconds, *cots, weights, weights, *held)


def mlp_out_kernel(inner_ref, weight_ref, *outs):
    inner = inner_ref[...].reshape(RING * BLOCK, inner_ref.shape[2])
    part = lax.dot_general(
        inner, weight_ref[...], contract_last, preferred_element_type=jnp.float32
    ).astype(low)
    for block, out in enumerate(outs):
        out[...] = part[block * BLOCK : (block + 1) * BLOCK]


def mlp_out_part(inner, weights):
    _, rows, hidden_width = inner.shape
    width = weights.shape[0]
    steps = 4
    return pl.pallas_call(
        mlp_out_kernel,
        grid=(steps,),
        in_specs=[
            pl.BlockSpec(inner.shape, lambda d: (0, 0, 0)),
            pl.BlockSpec((width // steps, hidden_width), lambda d: (d, 2)),
        ],
        out_specs=(pl.BlockSpec((rows, width // steps), lambda d: (0, d)),) * RING,
        out_shape=(jax.ShapeDtypeStruct((rows, width), low),) * RING,
        compiler_params=pltpu.CompilerParams(vmem_limit_bytes=VMEM_LIMIT),
        cost_estimate=pl.CostEstimate(flops=1024, bytes_accessed=1024, transcendentals=0),
    )(inner, weights)


def pair_grad(core_at, lefts, right, by_heads=False):
    width = lefts[0].shape[-1]
    outs = 512 if by_heads else right.shape[2]
    rows = RING * BLOCK

    def kernel(core_ref, *refs):
        left_refs = refs[: len(lefts)]
        right_ref, keep_ref, give_ref = refs[len(lefts) : len(lefts) + 3]
        if by_heads:
            all_ref = refs[-1]

            @pl.when(pl.program_id(0) == 0)
            def _():
                for r in range(RING):
                    for head in range(4):
                        all_ref[
                            r * BLOCK : (r + 1) * BLOCK, head * HEAD_DIM : (head + 1) * HEAD_DIM
                        ] = right_ref[4 * r + head]

            values = all_ref[...]
        else:
            values = right_ref[...].reshape(rows, outs)
        inputs = [ref[...].reshape(-1, 256) for ref in left_refs]
        inputs = inputs[0] if len(inputs) == 1 else jnp.concatenate(inputs, axis=0)
        term = lax.dot_general(
            inputs, values, contract_first, preferred_element_type=jnp.float32
        ).astype(low)
        first_core = core_ref[0] == 0
        keep_ref[0] = jnp.where(first_core, term[:128], term[128:])
        give_ref[0] = jnp.where(first_core, term[128:], term[:128])

    def columns(value):
        lead = value.shape[:-1]
        return pl.BlockSpec((*lead, 256), lambda i: (0,) * len(lead) + (i,))

    half = pl.BlockSpec((1, 128, outs), lambda i: (i, 0, 0))
    return pl.pallas_call(
        kernel,
        grid=(width // 256,),
        in_specs=[pl.BlockSpec(memory_space=pltpu.SMEM)]
        + [columns(value) for value in lefts]
        + [pl.BlockSpec(right.shape, lambda i: (0, 0, 0))],
        out_specs=(half, half),
        out_shape=(jax.ShapeDtypeStruct((width // 256, 128, outs), low),) * 2,
        scratch_shapes=[pltpu.VMEM((rows, 512), low)] * by_heads,
        compiler_params=pltpu.CompilerParams(vmem_limit_bytes=VMEM_LIMIT),
        cost_estimate=pl.CostEstimate(flops=1024, bytes_accessed=1024, transcendentals=0),
    )(core_at[None], *lefts, right)


def middle_kernel(*refs):
    mixed_refs, weight_refs = refs[:RING], refs[RING : 2 * RING]
    hidden_ref, gain_ref, middle_ref, second_ref = refs[2 * RING :]
    at = pl.program_id(0)
    step = weight_refs[0].shape[0]
    columns = pl.ds(pl.multiple_of(at * step, step), step)
    total = hidden_ref[:, columns].astype(jnp.float32)
    for mixed, weight in zip(mixed_refs, weight_refs):
        rows = jnp.concatenate([mixed[head] for head in range(4)], axis=1)
        total += lax.dot_general(
            rows, weight[...], contract_last, preferred_element_type=jnp.float32
        )
    middle_ref[:, columns] = total

    @pl.when(at == pl.num_programs(0) - 1)
    def _():
        second_ref[...] = (normalize(middle_ref[...]) * gain_ref[...]).astype(low)


def middle_part(mixed_blocks, weights, hidden, gain):
    rows, width = hidden.shape
    steps = 4
    whole = pl.BlockSpec((rows, width), lambda d: (0, 0))
    return pl.pallas_call(
        middle_kernel,
        grid=(steps,),
        in_specs=[pl.BlockSpec((4, rows, HEAD_DIM), lambda d: (0, 0, 0))] * RING
        + [pl.BlockSpec((width // steps, 512), lambda d: (d, 0))] * RING
        + [whole, pl.BlockSpec((1, width), lambda d: (0, 0))],
        out_specs=(whole, whole),
        out_shape=(
            jax.ShapeDtypeStruct((rows, width), jnp.float32),
            jax.ShapeDtypeStruct((rows, width), low),
        ),
        compiler_params=pltpu.CompilerParams(vmem_limit_bytes=32 * 1024 * 1024),
        cost_estimate=pl.CostEstimate(flops=1024, bytes_accessed=1024, transcendentals=0),
    )(*mixed_blocks, *weights, hidden, gain)


def middle_back_kernel(*refs):
    parts, weight_refs = refs[:RING], refs[RING : 2 * RING]
    middle_ref, cot_ref, gain_ref, grad_ref, low_ref, gain_out, *rest = refs[2 * RING :]
    outs, accs = rest[:RING], rest[RING:]
    at = pl.program_id(0)
    step = weight_refs[0].shape[0]

    @pl.when(at == 0)
    def _():
        second_grad = sum(part[...].astype(jnp.float32) for part in parts)
        middle = middle_ref[...]
        scale = inverse_rms(middle)
        normed = middle * scale
        gain_out[...] = jnp.sum(second_grad * normed, axis=0, keepdims=True)
        scaled = second_grad * gain_ref[...]
        grad = cot_ref[...].astype(jnp.float32) + scale * (
            scaled - normed * jnp.mean(scaled * normed, axis=-1, keepdims=True)
        )
        grad_ref[...] = grad
        low_ref[...] = grad.astype(low)
        for acc in accs:
            acc[...] = jnp.zeros_like(acc)

    rows = low_ref[:, pl.ds(pl.multiple_of(at * step, step), step)]
    for weight, acc in zip(weight_refs, accs):
        acc[...] += jnp.dot(rows, weight[...], preferred_element_type=jnp.float32)

    @pl.when(at == pl.num_programs(0) - 1)
    def _():
        for out, acc in zip(outs, accs):
            for head in range(4):
                out[head] = acc[:, head * HEAD_DIM : (head + 1) * HEAD_DIM].astype(low)


def middle_back(parts, weights, middle, cot, gain):
    rows, width = middle.shape
    steps = 4
    whole = pl.BlockSpec((rows, width), lambda d: (0, 0))
    row = pl.BlockSpec((1, width), lambda d: (0, 0))
    heads = pl.BlockSpec((4, rows, HEAD_DIM), lambda d: (0, 0, 0))
    return pl.pallas_call(
        middle_back_kernel,
        grid=(steps,),
        in_specs=[whole] * RING
        + [pl.BlockSpec((width // steps, 512), lambda d: (d, 0))] * RING
        + [whole, whole, row],
        out_specs=(whole, whole, row) + (heads,) * RING,
        out_shape=(
            jax.ShapeDtypeStruct((rows, width), jnp.float32),
            jax.ShapeDtypeStruct((rows, width), low),
            jax.ShapeDtypeStruct((1, width), jnp.float32),
        )
        + (jax.ShapeDtypeStruct((4, rows, HEAD_DIM), low),) * RING,
        scratch_shapes=[pltpu.VMEM((rows, 512), jnp.float32)] * RING,
        compiler_params=pltpu.CompilerParams(vmem_limit_bytes=VMEM_LIMIT),
        cost_estimate=pl.CostEstimate(flops=1024, bytes_accessed=1024, transcendentals=0),
    )(*parts, *weights, middle, cot, gain)


def first_kernel(
    own_ref, left_ref, top_ref, bottom_ref, right_ref, weight_ref, gains_ref, cos_ref, sin_ref,
    query_gain, key_gain, hidden_ref, first_ref, pre_ref, send_ref, gain_out,
):
    at = pl.program_id(0)
    half = top_ref.shape[0]

    @pl.when(at == 0)
    def _():
        gain_out[...] = gains_ref[...].astype(jnp.float32).T[:8]
        hidden_ref[0] = own_ref[...]

    @pl.when(at == 1)
    def _():
        hidden_ref[0] = left_ref[...]

    @pl.when(at == 2)
    def _():
        hidden_ref[0, :half] = top_ref[...]
        hidden_ref[0, half:] = bottom_ref[...]

    @pl.when(at == 3)
    def _():
        hidden_ref[0] = right_ref[...]

    first = (normalize(hidden_ref[0].astype(jnp.float32)) * gain_out[0:1]).astype(low)
    first_ref[0] = first
    pre = jnp.dot(first, weight_ref[...], preferred_element_type=jnp.float32)
    pre_ref[0] = pre
    cosine = cos_ref[0]
    sine = sin_ref[0]

    def turned(head, gain):
        values = normalize(pre[:, head * HEAD_DIM : (head + 1) * HEAD_DIM]) * gain
        return (values * cosine + pltpu.roll(values, HEAD_DIM // 2, 1) * sine).astype(low)

    for head in range(4):
        send_ref[head, 0] = turned(head, query_gain[...])
    for head in range(2):
        send_ref[2 * head, 1] = turned(4 + head, key_gain[...])
        send_ref[2 * head + 1, 1] = pre[:, (6 + head) * HEAD_DIM : (7 + head) * HEAD_DIM].astype(low)


def first_part(blocks, weights, cosine, sine, query_gain, key_gain):
    rows, width = blocks[0].shape
    row = pl.BlockSpec((1, HEAD_DIM), lambda r: (0, 0))
    turn = pl.BlockSpec((1, rows, HEAD_DIM), lambda r: (r, 0, 0))
    return pl.pallas_call(
        first_kernel,
        grid=(RING,),
        in_specs=[pl.BlockSpec(block.shape, lambda r: (0, 0)) for block in blocks]
        + [
            pl.BlockSpec((width, 1024), lambda r: (0, 0)),
            pl.BlockSpec((width, HEAD_DIM), lambda r: (0, 8)),
            turn,
            turn,
            row,
            row,
        ],
        out_specs=(
            pl.BlockSpec((1, rows, width), lambda r: (r, 0, 0)),
            pl.BlockSpec((1, rows, width), lambda r: (r, 0, 0)),
            pl.BlockSpec((1, rows, 1024), lambda r: (r, 0, 0)),
            pl.BlockSpec((4, 2, rows, HEAD_DIM), lambda r: (r, 0, 0, 0)),
            pl.BlockSpec((8, width), lambda r: (0, 0)),
        ),
        out_shape=(
            jax.ShapeDtypeStruct((RING, rows, width), low),
            jax.ShapeDtypeStruct((RING, rows, width), low),
            jax.ShapeDtypeStruct((RING, rows, 1024), jnp.float32),
            jax.ShapeDtypeStruct((BLOCKS, 2, rows, HEAD_DIM), low),
            jax.ShapeDtypeStruct((8, width), jnp.float32),
        ),
        compiler_params=pltpu.CompilerParams(vmem_limit_bytes=VMEM_LIMIT),
        cost_estimate=pl.CostEstimate(
            flops=2 * RING * rows * width * 1024,
            bytes_accessed=20 * 1024 * 1024,
            transcendentals=0,
        ),
    )(*blocks, weights, weights, cosine, sine, query_gain, key_gain)


def first_back_kernel(
    core_ref, back_ref, pre_ref, cos_ref, sin_ref, query_gain, key_gain, first_ref,
    grad_ref, keep_ref, give_ref, query_sum, key_sum, all_grads,
):
    at = pl.program_id(0)
    rows = grad_ref.shape[1]
    cosine = cos_ref[0]
    sine = sin_ref[0]

    @pl.when(at == 0)
    def _():
        query_sum[...] = jnp.zeros_like(query_sum)
        key_sum[...] = jnp.zeros_like(key_sum)

    def back(grads, head, gain, sums):
        columns = slice(head * HEAD_DIM, (head + 1) * HEAD_DIM)
        values = pre_ref[0, :, columns]
        grads = grads.astype(jnp.float32)
        grads = grads * cosine - pltpu.roll(grads, HEAD_DIM // 2, 1) * sine
        scale = inverse_rms(values)
        normed = values * scale
        sums[...] += jnp.sum(grads * normed, axis=0, keepdims=True)
        scaled = grads * gain
        out = scale * (scaled - normed * jnp.mean(scaled * normed, axis=-1, keepdims=True))
        grad_ref[0, :, columns] = out.astype(low)

    for head in range(4):
        back(back_ref[head, 0], head, query_gain[...], query_sum)
    for head in range(2):
        back(back_ref[2 * head, 1], 4 + head, key_gain[...], key_sum)
        grad_ref[0, :, (6 + head) * HEAD_DIM : (7 + head) * HEAD_DIM] = back_ref[2 * head + 1, 1]
    all_grads[pl.ds(pl.multiple_of(at * rows, rows), rows), :] = grad_ref[0]

    @pl.when(at == RING - 1)
    def _():
        grads = all_grads[...]
        first_core = core_ref[0] == 0
        for pair in range(8):
            inputs = first_ref[:, :, pair * 256 : (pair + 1) * 256].reshape(RING * rows, 256)
            term = lax.dot_general(
                inputs, grads, contract_first, preferred_element_type=jnp.float32
            ).astype(low)
            keep_ref[pair] = jnp.where(first_core, term[:128], term[128:])
            give_ref[pair] = jnp.where(first_core, term[128:], term[:128])


def first_back(core_at, returned, pre, cosine, sine, query_gain, key_gain, first_in):
    _, rows, width = first_in.shape
    row = pl.BlockSpec((1, HEAD_DIM), lambda r: (0, 0))
    turn = pl.BlockSpec((1, rows, HEAD_DIM), lambda r: (r, 0, 0))
    wide = pl.BlockSpec((1, rows, 1024), lambda r: (r, 0, 0))
    half = pl.BlockSpec((8, 128, 1024), lambda r: (0, 0, 0))
    return pl.pallas_call(
        first_back_kernel,
        grid=(RING,),
        in_specs=[
            pl.BlockSpec(memory_space=pltpu.SMEM),
            pl.BlockSpec((4, 2, rows, HEAD_DIM), lambda r: (r, 0, 0, 0)),
            wide,
            turn,
            turn,
            row,
            row,
            pl.BlockSpec((RING, rows, width), lambda r: (0, 0, 0)),
        ],
        out_specs=(wide, half, half, row, row),
        out_shape=(
            jax.ShapeDtypeStruct((RING, rows, 1024), low),
            jax.ShapeDtypeStruct((8, 128, 1024), low),
            jax.ShapeDtypeStruct((8, 128, 1024), low),
            jax.ShapeDtypeStruct((1, HEAD_DIM), jnp.float32),
            jax.ShapeDtypeStruct((1, HEAD_DIM), jnp.float32),
        ),
        scratch_shapes=[pltpu.VMEM((RING * rows, 1024), low)],
        compiler_params=pltpu.CompilerParams(vmem_limit_bytes=VMEM_LIMIT),
        cost_estimate=pl.CostEstimate(flops=1024, bytes_accessed=1024, transcendentals=0),
    )(core_at[None], returned, pre, cosine, sine, query_gain, key_gain, first_in)


def last_kernel(
    core_ref, grad_ref, weight_ref, hidden_ref, mlp_ref, query_ref, key_ref,
    own_ref, left_a, left_b, top_ref, bottom_ref, right_a, right_b, keep_ref, give_ref, gain_acc,
):
    at = pl.program_id(0)
    width = hidden_ref.shape[2]
    part = lax.dot_general(
        grad_ref[0], weight_ref[...], contract_last, preferred_element_type=jnp.float32
    )
    half = top_ref.shape[0]
    @pl.when(at == 0)
    def _():
        own_ref[...] = part.astype(low)

    for r, first, second in ((1, left_a, left_b), (2, top_ref, bottom_ref), (3, right_a, right_b)):

        @pl.when(at == r)
        def _(first=first, second=second):
            first[...] = part[:half].astype(low)
            second[...] = part[half:].astype(low)

    normed = normalize(hidden_ref[0].astype(jnp.float32))
    gain = jnp.sum(part * normed, axis=0, keepdims=True)

    @pl.when(at == 0)
    def _():
        gain_acc[...] = gain

    @pl.when(at > 0)
    def _():
        gain_acc[...] += gain

    @pl.when(at == RING - 1)
    def _():
        lines = [
            gain_acc[...],
            mlp_ref[...],
            jnp.concatenate([query_ref[...]] * BLOCKS, axis=1),
            jnp.concatenate([key_ref[...]] * BLOCKS, axis=1),
            jnp.zeros((HEAD_DIM - 4, width), jnp.float32),
        ]
        turned = jnp.concatenate(lines, axis=0).T.astype(low)
        first_core = core_ref[0] == 0
        for pair in range(8):
            first = turned[pair * 256 : pair * 256 + 128]
            second = turned[pair * 256 + 128 : (pair + 1) * 256]
            keep_ref[pair] = jnp.where(first_core, first, second)
            give_ref[pair] = jnp.where(first_core, second, first)


def last_part(core_at, grads, weights, hidden_all, mlp_part, query_part, key_part):
    _, rows, width = hidden_all.shape
    block = pl.BlockSpec((rows, width), lambda r: (0, 0))
    small = pl.BlockSpec((rows // 2, width), lambda r: (0, 0))
    whole = jax.ShapeDtypeStruct((rows, width), low)
    part = jax.ShapeDtypeStruct((rows // 2, width), low)
    row = pl.BlockSpec((1, HEAD_DIM), lambda r: (0, 0))
    half = pl.BlockSpec((8, 128, HEAD_DIM), lambda r: (0, 0, 0))
    return pl.pallas_call(
        last_kernel,
        grid=(RING,),
        in_specs=[
            pl.BlockSpec(memory_space=pltpu.SMEM),
            pl.BlockSpec((1, rows, 1024), lambda r: (r, 0, 0)),
            pl.BlockSpec((width, 1024), lambda r: (0, 0)),
            pl.BlockSpec((1, rows, width), lambda r: (r, 0, 0)),
            pl.BlockSpec((1, width), lambda r: (0, 0)),
            row,
            row,
        ],
        out_specs=(block,) + (small,) * 6 + (half, half),
        out_shape=(whole,) + (part,) * 6
        + (jax.ShapeDtypeStruct((8, 128, HEAD_DIM), low),) * 2,
        scratch_shapes=[pltpu.VMEM((1, width), jnp.float32)],
        compiler_params=pltpu.CompilerParams(vmem_limit_bytes=VMEM_LIMIT),
        cost_estimate=pl.CostEstimate(flops=1024, bytes_accessed=1024, transcendentals=0),
    )(core_at[None], grads, weights, hidden_all, mlp_part, query_part, key_part)


def arrange_kernel(at_ref, own_ref, other_ref, out_ref):
    y_at, x_at, core_at = at_ref[0], at_ref[1], at_ref[2]
    for dy in range(RING):
        for dx in range(2):
            first = ((y_at - dy + RING) & 3) * 4 + (x_at ^ dx) * 2
            own = pl.multiple_of((first + core_at) * 128, 128)
            other = pl.multiple_of((first + 1 - core_at) * 128, 128)
            out_ref[pl.ds(own, 128), :] = own_ref[dy, dx]
            out_ref[pl.ds(other, 128), :] = other_ref[dy, dx]


def gather_by_permutes(pairs, y_at, x_at, core_at):
    own = jnp.stack(pairs)
    other = shift(own, "core", 1, 2)
    whole = pl.BlockSpec(memory_space=pltpu.VMEM)
    return pl.pallas_call(
        arrange_kernel,
        in_specs=[pl.BlockSpec(memory_space=pltpu.SMEM), whole, whole],
        out_specs=whole,
        out_shape=jax.ShapeDtypeStruct((BLOCKS * 128, own.shape[3]), own.dtype),
        compiler_params=pltpu.CompilerParams(vmem_limit_bytes=VMEM_LIMIT),
        cost_estimate=pl.CostEstimate(flops=1024, bytes_accessed=1024, transcendentals=0),
    )(jnp.stack([y_at, x_at, core_at]), own, other)


def pair_sums_kernel(keep_ref, come_ref, gains_keep, gains_come, out_ref):
    f32 = jnp.float32
    wide = keep_ref.shape[2]
    out_ref[:, :, :wide] = (keep_ref[...].astype(f32) + come_ref[...].astype(f32)).astype(low)
    out_ref[:, :, wide:] = (gains_keep[...].astype(f32) + gains_come[...].astype(f32)).astype(low)


def pair_sums(keep, come, more_keep, more_come):
    blocks, rows, wide = keep.shape
    narrow = more_keep.shape[2]
    large = pl.BlockSpec((4, rows, wide), lambda i: (i, 0, 0))
    small = pl.BlockSpec((4, rows, narrow), lambda i: (i, 0, 0))
    return pl.pallas_call(
        pair_sums_kernel,
        grid=(blocks // 4,),
        in_specs=[large, large, small, small],
        out_specs=pl.BlockSpec((4, rows, wide + narrow), lambda i: (i, 0, 0)),
        out_shape=jax.ShapeDtypeStruct((blocks, rows, wide + narrow), low),
        compiler_params=pltpu.CompilerParams(vmem_limit_bytes=VMEM_LIMIT),
        cost_estimate=pl.CostEstimate(flops=1024, bytes_accessed=1024, transcendentals=0),
    )(keep, come, more_keep, more_come)


def to_heads(send):
    return lax.all_to_all(send, GROUP_AXES, 0, 0, tiled=True)


def after(value, *others):
    return lax.optimization_barrier((value, others))[0]


def ring_blocks(values):
    half = values.shape[0] // 2
    left = shift(values, "z", 1)
    right = shift(values, "z", 3)
    opposite = jnp.concatenate(
        [shift(left[:half], "z", 1), shift(right[half:], "z", 3)], axis=0
    )
    return [values, left, opposite, right]


def together(*values):
    return lax.optimization_barrier(values)


def place(z_at, blocks, widths, chunk=None, summed=False):
    rows = blocks[0].shape[0]
    whole = pl.BlockSpec(memory_space=pltpu.VMEM)
    shapes = [RING * part for part in widths] + [HEAD_DIM] * summed

    def kernel(z_ref, *refs):
        ins, outs = refs[:RING], refs[RING:]
        for r in range(RING):
            slot = (z_ref[0] - r + RING) & 3
            start = 0
            for turn in range(widths[0] // chunk if chunk else 1):
                for out, part in zip(outs, widths):
                    size = chunk or part
                    at = pl.multiple_of(slot * part + turn * size, 128)
                    out[:, pl.ds(at, size)] = ins[r][:, start : start + size].astype(jnp.float32)
                    start += size
            if summed:
                columns = ins[r][:, start : start + HEAD_DIM].astype(jnp.float32)
                outs[-1][...] = columns if r == 0 else outs[-1][...] + columns

    return pl.pallas_call(
        kernel,
        in_specs=[pl.BlockSpec(memory_space=pltpu.SMEM)] + [whole] * RING,
        out_specs=tuple(whole for _ in shapes),
        out_shape=tuple(jax.ShapeDtypeStruct((rows, part), jnp.float32) for part in shapes),
        compiler_params=pltpu.CompilerParams(vmem_limit_bytes=VMEM_LIMIT),
        cost_estimate=pl.CostEstimate(flops=1024, bytes_accessed=1024, transcendentals=0),
    )(z_at[None], *blocks)


def send_back(block, r):
    return shift(block, "z", -r)


def local(
    hidden_in,
    cotangent,
    segment_ids,
    positions,
    attn_gain,
    query_gain,
    key_gain,
    query_weight,
    key_weight,
    value_weight,
    out_weight,
    mlp_gain,
    gate_weight,
    up_weight,
    down_weight,
):
    f32 = jnp.float32
    rows, width = hidden_in.shape
    ring_rows = RING * rows
    z_at = lax.axis_index("z")
    y_at = lax.axis_index("y")
    x_at = lax.axis_index("x_hi")
    core_at = lax.axis_index("core")
    my_index = (y_at * 2 + x_at) * 2 + core_at

    def columns(weight):
        part = weight.shape[1] // RING
        return lax.dynamic_slice_in_dim(weight, z_at * part, part, 1).astype(low)

    def gather(block):
        return lax.all_gather(block, GROUP_AXES, axis=0, tiled=True)

    own_places = lax.dynamic_slice_in_dim(positions, my_index * rows, rows)
    firsts = positions.reshape(BLOCKS, BLOCK)[:, 0]
    segments = segment_ids.reshape(BLOCKS, BLOCK)[:, 0]
    logical = firsts // BLOCK + jnp.maximum(segments - 1, 0) * 2
    numbers = jnp.arange(BLOCKS, dtype=jnp.int32)
    order = jnp.sum(jnp.where(logical[:, None] == numbers[None, :], numbers[:, None], 0), axis=0)
    notes = gather_z(jnp.concatenate([own_places, order, jnp.zeros((112,), jnp.int32)])[None])
    places = notes[:, :rows]
    order = lax.dynamic_index_in_dim(notes, y_at, 0, keepdims=False)[rows : rows + BLOCKS]

    gains = jnp.pad(
        jnp.stack([attn_gain, mlp_gain], axis=1).astype(low), ((0, 0), (0, HEAD_DIM - 2))
    )
    first_weights = gather(
        jnp.concatenate(
            [columns(query_weight), columns(key_weight), columns(value_weight), gains], axis=1
        )
    )
    out_columns = columns(out_weight)
    out_come = shift(out_columns, "x_hi", 1, 2)
    out_pairs = jnp.stack([out_columns, out_come])
    out_pairs = [out_pairs] + [shift(out_pairs, "y", r) for r in range(1, RING)]

    hidden_own = after(hidden_in, notes, out_come)
    hidden_left = shift(hidden_own, "z", 1)
    hidden_right = shift(hidden_own, "z", 3)
    gate_columns, up_columns, down_columns, hidden_left, hidden_right, out_pairs = together(
        gate_weight, up_weight, down_weight, hidden_left, hidden_right, out_pairs
    )
    out_slice = gather_by_permutes(out_pairs, y_at, x_at, core_at)
    gate_columns, up_columns = columns(gate_columns), columns(up_columns)
    mlp_columns = []
    for start in range(0, gate_columns.shape[1], FF_STEP):
        mlp_columns.append(gate_columns[:, start : start + FF_STEP])
        mlp_columns.append(up_columns[:, start : start + FF_STEP])
    mlp_weights = gather(jnp.concatenate(mlp_columns + [columns(down_columns)], axis=1))
    half = rows // 2
    hidden_blocks = [
        hidden_own,
        hidden_left,
        shift(hidden_left[:half], "z", 1),
        shift(hidden_right[half:], "z", 3),
        hidden_right,
    ]
    out_slice = after(out_slice, *hidden_blocks)
    out_left = shift(out_slice, "z", 1)
    out_right = shift(out_slice, "z", 3)
    frequency = rope_base ** (-2.0 * jnp.arange(HEAD_DIM // 2, dtype=f32) / HEAD_DIM)
    angles = places.astype(f32)[:, :, None] * frequency[None, None, :]
    cosine = jnp.cos(angles)
    sine = jnp.sin(angles)
    cosine = jnp.concatenate([cosine, cosine], axis=-1)
    sine = jnp.concatenate([-sine, sine], axis=-1)
    query_row = query_gain[None]
    key_row = key_gain[None]

    hidden_all, first_in, qkv_pre, send, gain_rows = first_part(
        hidden_blocks, first_weights, cosine, sine, query_row, key_row
    )
    attn_scale = gain_rows[0:1]
    mlp_scale = gain_rows[1:2]
    arrived, out_left, out_right = together(to_heads(send), out_left, out_right)
    other_pair = shift(arrived[:, 1], "core", 1, 2)
    head_mixed, head_mixed_t, head_logs = attention_forward(order, core_at, arrived, other_pair)
    out_top = shift(out_left[: width // 2], "z", 1)
    out_bottom = shift(out_right[width // 2 :], "z", 3)
    head_mixed, head_mixed_t, head_logs, out_top, out_bottom = together(
        head_mixed, head_mixed_t, head_logs, out_top, out_bottom
    )
    cot_own = after(cotangent, head_mixed)
    cot_left = shift(cot_own, "z", 1)
    cot_right = shift(cot_own, "z", 3)

    cot_top = shift(cot_left[:half], "z", 1)
    cot_bottom = shift(cot_right[half:], "z", 3)
    mixed_arrived, cot_left, cot_right, cot_top, cot_bottom = together(
        to_heads(head_mixed), cot_left, cot_right, cot_top, cot_bottom
    )
    mixed_blocks = [mixed_arrived[:4]] + [
        shift(mixed_arrived[4 * (RING - j) : 4 * (RING - j) + 4], "z", j) for j in range(1, RING)
    ]
    out_opposite = jnp.concatenate([out_top, out_bottom], axis=0)
    out_weights = [out_slice, out_left, out_opposite, out_right]
    mixed_blocks, out_weights = together(mixed_blocks, out_weights)
    middle, second_in = middle_part(mixed_blocks, out_weights, hidden_in, mlp_scale)
    hidden = hidden_in.astype(f32)
    left = shift(second_in, "z", 1)
    right = shift(second_in, "z", 3)
    *held, own_part = mlp_blocks(0, [second_in], [cot_own], mlp_weights, ())
    held, own_part, left, right, second_in = together(held, own_part, left, right, second_in)
    opposite = shift(second_in, "z", 2)
    *held, left_part, right_part = mlp_blocks(
        1, [left, right], [cot_left, cot_right], mlp_weights, held
    )
    left_back = send_back(left_part, 1)
    right_back = send_back(right_part, 3)
    held, opposite = together(held, opposite)
    *held, opposite_part = mlp_blocks(
        1, [opposite], [cot_top, cot_bottom], mlp_weights, held
    )
    opposite_back = send_back(opposite_part, 2)
    inner, both_grad, second_all, cot_all = held

    def pair_sum(keep, come):
        return (keep.astype(f32) + come.astype(f32)).astype(low)

    def along_y(pair):
        return lax.all_to_all(pair.reshape(RING, 2, 128, pair.shape[2]), "y", 0, 0, tiled=True)

    def along_x(halves):
        keep = lax.dynamic_index_in_dim(halves, x_at, 0, keepdims=False)
        give = lax.dynamic_index_in_dim(halves, 1 - x_at, 0, keepdims=False)
        return keep, lax.ppermute(give, ("x_lo", "x_hi"), [(i, 3 - i) for i in range(4)])

    def add_up(terms):
        return jnp.sum(terms.astype(f32), axis=0).astype(low)

    def over_x(share):
        return share, shift(share, "x_lo", 1, 2)

    def over_z(pair):
        share = pair_sum(*pair)
        return [share] + [shift(share, "z", r) for r in range(1, RING)]

    both_term = lax.dot_general(
        second_all.reshape(ring_rows, width),
        both_grad.reshape(ring_rows, 3072),
        contract_first,
        preferred_element_type=f32,
    ).astype(low)
    left_back, right_back, opposite_back, both_term, inner = together(
        left_back, right_back, opposite_back, both_term, inner
    )
    both_share = lax.psum_scatter(both_term, GROUP_AXES, scatter_dimension=0, tiled=True)

    middle_grad, own_low, mlp_gain_part, *grad_blocks = middle_back(
        (own_part, left_back, right_back, opposite_back),
        out_weights,
        middle,
        cotangent,
        mlp_scale,
    )
    grad_blocks = [grad_blocks[0]] + [shift(grad_blocks[RING - r], "z", r) for r in range(1, RING)]
    down_keep, down_give = pair_grad(core_at, [cot_all], inner)
    grad_blocks, down_keep, down_give, own_low, inner = together(
        grad_blocks, down_keep, down_give, own_low, inner
    )
    head_grads = to_heads(jnp.concatenate(grad_blocks, axis=0))
    low_left = shift(own_low, "z", 1)
    low_right = shift(own_low, "z", 3)
    mlp_own, mlp_opposite, mlp_left, mlp_right = mlp_out_part(inner, mlp_weights)
    head_grads, low_left, low_right, own_low, mlp_opposite, mlp_left, mlp_right = together(
        head_grads, low_left, low_right, own_low, mlp_opposite, mlp_left, mlp_right
    )
    mlp_left = send_back(mlp_left, 1)
    mlp_right = send_back(mlp_right, 3)

    query_grad, grad_keep, grad_give = attention_backward(
        order, core_at, arrived, other_pair, head_grads, head_mixed_t, head_logs
    )
    query_grad, grad_keep, grad_give, mlp_left, mlp_right, own_low, mlp_opposite, down_give = together(
        query_grad, grad_keep, grad_give, mlp_left, mlp_right, own_low, mlp_opposite, down_give
    )
    low_opposite = shift(own_low, "z", 2)
    mlp_opposite = send_back(after(mlp_opposite, low_opposite), 2)
    grads_send = lax.dynamic_update_slice_in_dim(
        query_grad, pair_sum(grad_keep, shift(grad_give, "core", 1, 2))[:, None], 1, 1
    )
    returned = to_heads(grads_send)
    out_keep, out_give = pair_grad(
        core_at, [own_low, low_left, low_opposite, low_right], mixed_arrived, by_heads=True
    )
    down_sum = pair_sums(
        down_keep,
        shift(down_give, "core", 1, 2),
        out_keep,
        shift(out_give, "core", 1, 2),
    )
    returned, both_share, down_sum = together(returned, both_share, down_sum)
    both_pair = over_x(both_share)
    down_terms = along_y(down_sum)
    qkv_grad, qkv_keep, qkv_give, query_gain_part, key_gain_part = first_back(
        core_at, returned, qkv_pre, cosine, sine, query_row, key_row, first_in
    )
    qkv_grad, qkv_give, both_pair, mlp_opposite = together(
        qkv_grad, qkv_give, both_pair, mlp_opposite
    )
    both_sum = pair_sum(*both_pair)
    both_left = shift(both_sum, "z", 1)
    both_right = shift(both_sum, "z", 3)
    qkv_come = shift(qkv_give, "core", 1, 2)
    *first_parts, gains_keep, gains_give = last_part(
        core_at,
        qkv_grad,
        first_weights,
        hidden_all,
        mlp_gain_part,
        query_gain_part,
        key_gain_part,
    )
    first_parts, gains_give, qkv_come, both_left, both_right, both_sum = together(
        first_parts, gains_give, qkv_come, both_left, both_right, both_sum
    )
    down_pair = over_x(pair_sum(*along_x(add_up(down_terms))))
    gains_come = shift(gains_give, "core", 1, 2)
    first_own, left_a, left_b, first_top, first_bottom, right_a, right_b = first_parts
    first_top = shift(first_top, "z", 3)
    first_bottom = shift(first_bottom, "z", 1)
    qkv_terms = along_y(pair_sums(qkv_keep, qkv_come, gains_keep, gains_come))
    first_left = send_back(jnp.concatenate([pair_sum(left_a, first_top), left_b], axis=0), 1)
    first_right = send_back(jnp.concatenate([right_a, pair_sum(right_b, first_bottom)], axis=0), 3)
    both_opposite = shift(both_sum, "z", 2)
    qkv_terms, first_left, first_right, both_opposite, down_pair = together(
        qkv_terms, first_left, first_right, both_opposite, down_pair
    )
    down_blocks = over_z(down_pair)
    qkv_share = pair_sum(*along_x(add_up(qkv_terms)))
    both_blocks = [both_sum, both_left, both_opposite, both_right]
    qkv_pair = over_x(qkv_share)
    output = (
        middle
        + mlp_own.astype(f32)
        + mlp_left.astype(f32)
        + mlp_right.astype(f32)
        + mlp_opposite.astype(f32)
    ).astype(low)
    first_grad = first_own.astype(f32) + first_left.astype(f32) + first_right.astype(f32)
    hidden_rms = inverse_rms(hidden)
    own_norm = hidden * hidden_rms
    scaled_first = first_grad * attn_scale
    hidden_grad = (
        middle_grad
        + hidden_rms
        * (scaled_first - own_norm * jnp.mean(scaled_first * own_norm, axis=-1, keepdims=True))
    ).astype(low)

    down_grad_out, out_grad_out = place(z_at, down_blocks, (1536, 512))
    gate_grad_out, up_grad_out = place(z_at, both_blocks, (1536, 1536), chunk=FF_STEP)
    query_grad_out, key_grad_out, value_grad_out, gain_sum = place(
        z_at, over_z(qkv_pair), (512, 256, 256), summed=True
    )
    gain_sum = gain_sum[:, :4].T

    return (
        output,
        hidden_grad,
        gain_sum[0],
        gain_sum[2],
        gain_sum[3],
        query_grad_out,
        key_grad_out,
        value_grad_out,
        out_grad_out,
        gain_sum[1],
        gate_grad_out,
        up_grad_out,
        down_grad_out,
    )


def solution(mesh):
    fine = Mesh(mesh.devices.reshape(2, 4, 4, 2, 2), ALL_AXES)
    rep = ("x_lo", "z")
    row = P(ALL_AXES, None)
    part = P(GROUP_AXES)
    weight = P(GROUP_AXES, None)
    in_specs = (
        row,
        row,
        P(rep),
        P(rep),
        part,
        P(),
        P(),
        weight,
        weight,
        weight,
        weight,
        part,
        weight,
        weight,
        weight,
    )
    out_specs = (
        row,
        row,
        part,
        P(),
        P(),
        weight,
        weight,
        weight,
        weight,
        part,
        weight,
        weight,
        weight,
    )
    return jax.shard_map(local, mesh=fine, in_specs=in_specs, out_specs=out_specs, check_vma=False)
```

```python
import functools

import jax
import jax.numpy as jnp
from jax import lax
from jax.experimental import pallas as pl
from jax.experimental.pallas import tpu as pltpu
from jax.sharding import Mesh
from jax.sharding import PartitionSpec as P

HEAD_DIM = 128
RING = 4
BLOCK = 256
BLOCKS = 16
TILE = 512
TILES = 8
PROMPT_TILES = 6
FF_STEP = 512
VMEM_LIMIT = 60 * 1024 * 1024

norm_eps = 1e-06
rope_base = 1000000.0
score_scale = HEAD_DIM ** (-0.5)
score_scale_log2 = score_scale * 1.4426950408889634
contract_first = (((0,), (0,)), ((), ()))
contract_last = (((1,), (1,)), ((), ()))
GROUP_AXES = ("y", "x_hi", "core")
ALL_AXES = ("x_lo", "z", "y", "x_hi", "core")
low = jnp.bfloat16


def inverse_rms(values):
    return lax.rsqrt(jnp.mean(values * values, axis=-1, keepdims=True) + norm_eps)


def normalize(values):
    return values * inverse_rms(values)


def shift(values, axis, by, size=RING):
    return lax.ppermute(values, axis, [(i, (i + by) % size) for i in range(size)])


def gather_z(values):
    return jnp.concatenate(
        [values, shift(values, "z", 1), shift(values, "z", 2), shift(values, "z", 3)], axis=0
    )


def forward_kernel(
    order, core, own_a, own_b, other_a, other_b, mixed_ref, mixed_t_ref, log_ref, k_all, v_t, acc, total
):
    tile = pl.program_id(0)
    start = tile * TILE

    def take(keys, values):
        for half in range(2):
            rows = pl.ds(pl.multiple_of(start + half * BLOCK, BLOCK), BLOCK)
            k_all[rows, :] = keys[half]
            v_t[tile, :, half * BLOCK : (half + 1) * BLOCK] = (
                values[half].astype(jnp.float32).T.astype(low)
            )

    @pl.when(core[0] == 0)
    def _():
        take((own_a[0, 1], own_b[0, 1]), (other_a[0], other_b[0]))

    @pl.when(core[0] == 1)
    def _():
        take((other_a[0], other_b[0]), (own_a[0, 1], own_b[0, 1]))

    queries = jnp.concatenate([own_a[0, 0], own_b[0, 0]], axis=0)
    acc[...] = jnp.zeros_like(acc)
    total[...] = jnp.zeros_like(total)

    def chunk(at, masked):
        keys = k_all[pl.ds(pl.multiple_of(at * TILE, TILE), TILE), :]
        scores = lax.dot_general(keys, queries, contract_last, preferred_element_type=jnp.float32)
        weights = jnp.exp2(scores * score_scale_log2)
        if masked:
            key_row = lax.broadcasted_iota(jnp.int32, (TILE, TILE), 0)
            query_row = lax.broadcasted_iota(jnp.int32, (TILE, TILE), 1)
            weights = jnp.where(key_row <= query_row, weights, 0.0)
        total[...] += jnp.sum(weights, axis=0, keepdims=True)
        acc[...] += jnp.dot(v_t[at], weights.astype(low), preferred_element_type=jnp.float32)

    full = jnp.minimum(tile, PROMPT_TILES)
    for count in range(PROMPT_TILES + 1):

        @pl.when(full == count)
        def _(count=count):
            for at in range(count):
                chunk(at, False)
            chunk(tile, True)

    mixed_t = acc[...] / total[...]
    mixed_t_ref[0] = mixed_t
    log_ref[0] = jnp.log2(total[...])
    mixed = mixed_t.T.astype(low)
    mixed_ref[order[2 * tile]] = mixed[:BLOCK]
    mixed_ref[order[2 * tile + 1]] = mixed[BLOCK:]


def tile_specs(lead):
    return [
        pl.BlockSpec(
            (1, *lead, BLOCK, HEAD_DIM),
            functools.partial(
                lambda half, tile, order, core: (order[2 * tile + half],) + (0,) * (len(lead) + 2),
                half,
            ),
        )
        for half in range(2)
    ]


def attention_forward(order, core_at, arrived, other):
    whole = pl.BlockSpec(memory_space=pltpu.VMEM)
    turned = pl.BlockSpec((1, HEAD_DIM, TILE), lambda tile, order, core: (tile, 0, 0))
    line = pl.BlockSpec((1, 1, TILE), lambda tile, order, core: (tile, 0, 0))
    return pl.pallas_call(
        forward_kernel,
        out_shape=(
            jax.ShapeDtypeStruct((BLOCKS, BLOCK, HEAD_DIM), low),
            jax.ShapeDtypeStruct((TILES, HEAD_DIM, TILE), jnp.float32),
            jax.ShapeDtypeStruct((TILES, 1, TILE), jnp.float32),
        ),
        grid_spec=pltpu.PrefetchScalarGridSpec(
            num_scalar_prefetch=2,
            grid=(TILES,),
            in_specs=tile_specs((2,)) + tile_specs(()),
            out_specs=(whole, turned, line),
            scratch_shapes=[
                pltpu.VMEM((BLOCKS * BLOCK, HEAD_DIM), low),
                pltpu.VMEM((TILES, HEAD_DIM, TILE), low),
                pltpu.VMEM((HEAD_DIM, TILE), jnp.float32),
                pltpu.VMEM((1, TILE), jnp.float32),
            ],
        ),
        compiler_params=pltpu.CompilerParams(vmem_limit_bytes=VMEM_LIMIT),
        cost_estimate=pl.CostEstimate(
            flops=1024, bytes_accessed=1024, transcendentals=0
        ),
    )(order, core_at[None], arrived, arrived, other, other)


def backward_kernel(
    order, core, own_a, own_b, other_a, other_b, grad_a, grad_b, mixed_t_ref, log_ref,
    q_out, keep_out, give_out, k_all, v_all, k_t, q_acc, k_acc, v_acc,
):
    tile = pl.program_id(0)
    start = tile * TILE

    def take(keys, values):
        for half in range(2):
            rows = pl.ds(pl.multiple_of(start + half * BLOCK, BLOCK), BLOCK)
            k_all[rows, :] = keys[half]
            v_all[rows, :] = values[half]
            k_t[tile, :, half * BLOCK : (half + 1) * BLOCK] = (
                keys[half].astype(jnp.float32).T.astype(low)
            )

    @pl.when(core[0] == 0)
    def _():
        take((own_a[0, 1], own_b[0, 1]), (other_a[0], other_b[0]))

    @pl.when(core[0] == 1)
    def _():
        take((other_a[0], other_b[0]), (own_a[0, 1], own_b[0, 1]))

    rows = pl.ds(pl.multiple_of(start, TILE), TILE)
    k_acc[rows, :] = jnp.zeros((TILE, HEAD_DIM), jnp.float32)
    v_acc[rows, :] = jnp.zeros((TILE, HEAD_DIM), jnp.float32)
    queries = jnp.concatenate([own_a[0, 0], own_b[0, 0]], axis=0)
    grads = jnp.concatenate([grad_a[0], grad_b[0]], axis=0)
    grads_t = grads.astype(jnp.float32).T
    shared = jnp.sum(grads_t * mixed_t_ref[0], axis=0, keepdims=True)
    logs = log_ref[0]
    q_acc[...] = jnp.zeros_like(q_acc)

    def chunk(at, masked):
        rows = pl.ds(pl.multiple_of(at * TILE, TILE), TILE)
        scores = lax.dot_general(
            k_all[rows, :], queries, contract_last, preferred_element_type=jnp.float32
        )
        probs = jnp.exp2(scores * score_scale_log2 - logs)
        if masked:
            key_row = lax.broadcasted_iota(jnp.int32, (TILE, TILE), 0)
            query_row = lax.broadcasted_iota(jnp.int32, (TILE, TILE), 1)
            probs = jnp.where(key_row <= query_row, probs, 0.0)
        prob_grads = lax.dot_general(
            v_all[rows, :], grads, contract_last, preferred_element_type=jnp.float32
        )
        score_grads = (probs * (prob_grads - shared)).astype(low)
        v_acc[rows, :] += jnp.dot(probs.astype(low), grads, preferred_element_type=jnp.float32)
        k_acc[rows, :] += jnp.dot(score_grads, queries, preferred_element_type=jnp.float32)
        q_acc[...] += jnp.dot(k_t[at], score_grads, preferred_element_type=jnp.float32)

    full = jnp.minimum(tile, PROMPT_TILES)
    for count in range(PROMPT_TILES + 1):

        @pl.when(full == count)
        def _(count=count):
            for at in range(count):
                chunk(at, False)
            chunk(tile, True)

    query_grad = (q_acc[...] * score_scale).T.astype(low)
    q_out[order[2 * tile], 0] = query_grad[:BLOCK]
    q_out[order[2 * tile + 1], 0] = query_grad[BLOCK:]

    def give(keep_acc, keep_scale, give_acc, give_scale):
        for at in range(BLOCKS):
            rows = slice(at * BLOCK, (at + 1) * BLOCK)
            keep_out[order[at]] = (keep_acc[rows, :] * keep_scale).astype(low)
            give_out[order[at]] = (give_acc[rows, :] * give_scale).astype(low)

    @pl.when((tile == TILES - 1) & (core[0] == 0))
    def _():
        give(k_acc, score_scale, v_acc, 1.0)

    @pl.when((tile == TILES - 1) & (core[0] == 1))
    def _():
        give(v_acc, 1.0, k_acc, score_scale)


def attention_backward(order, core_at, arrived, other, grads, mixed_t, logs):
    whole = pl.BlockSpec(memory_space=pltpu.VMEM)
    rows = BLOCKS * BLOCK
    turned = pl.BlockSpec((1, HEAD_DIM, TILE), lambda tile, order, core: (tile, 0, 0))
    line = pl.BlockSpec((1, 1, TILE), lambda tile, order, core: (tile, 0, 0))
    return pl.pallas_call(
        backward_kernel,
        out_shape=(jax.ShapeDtypeStruct((BLOCKS, 2, BLOCK, HEAD_DIM), low),)
        + (jax.ShapeDtypeStruct((BLOCKS, BLOCK, HEAD_DIM), low),) * 2,
        grid_spec=pltpu.PrefetchScalarGridSpec(
            num_scalar_prefetch=2,
            grid=(TILES,),
            in_specs=tile_specs((2,)) + tile_specs(()) + tile_specs(()) + [turned, line],
            out_specs=(whole, whole, whole),
            scratch_shapes=[
                pltpu.VMEM((rows, HEAD_DIM), low),
                pltpu.VMEM((rows, HEAD_DIM), low),
                pltpu.VMEM((TILES, HEAD_DIM, TILE), low),
                pltpu.VMEM((HEAD_DIM, TILE), jnp.float32),
                pltpu.VMEM((rows, HEAD_DIM), jnp.float32),
                pltpu.VMEM((rows, HEAD_DIM), jnp.float32),
            ],
        ),
        compiler_params=pltpu.CompilerParams(vmem_limit_bytes=VMEM_LIMIT),
        cost_estimate=pl.CostEstimate(
            flops=1024, bytes_accessed=1024, transcendentals=0
        ),
    )(order, core_at[None], arrived, arrived, other, other, grads, grads, mixed_t, logs)


def mlp_kernel(parts, cot_parts, *refs):
    second_refs, cot_refs = refs[:parts], refs[parts : parts + cot_parts]
    both_weight_ref, down_ref = refs[parts + cot_parts : parts + cot_parts + 2]
    count = refs[-1].shape[0] // BLOCK
    inner_ref, both_ref, second_out, cot_out = refs[-5 - count : -1 - count]
    grad_refs, acc = refs[-1 - count : -1], refs[-1]
    at = pl.program_id(0)
    step = down_ref.shape[1]
    rows, width = acc.shape

    @pl.when(at == 0)
    def _():
        for ins, out in ((second_refs, second_out), (cot_refs, cot_out)):
            start = 0
            for part in ins:
                size = part.shape[0]
                out[start // BLOCK, start % BLOCK : start % BLOCK + size, :] = part[...]
                start += size

    second = second_out[...].reshape(rows, width)
    both_act = jnp.dot(second, both_weight_ref[...], preferred_element_type=jnp.float32)
    inner_grad = jnp.dot(
        cot_out[...].reshape(rows, width), down_ref[...], preferred_element_type=jnp.float32
    )
    gate_act = both_act[:, :step]
    up_act = both_act[:, step:]
    sigmoid = 1.0 / (1.0 + jnp.exp(-gate_act))
    silu = gate_act * sigmoid
    inner_ref[...] = (silu * up_act).astype(low).reshape(inner_ref.shape)
    gate_grad = (inner_grad * up_act * (sigmoid * (1.0 + gate_act * (1.0 - sigmoid)))).astype(low)
    both_grad = jnp.concatenate([gate_grad, (inner_grad * silu).astype(low)], axis=1)
    both_ref[:, :, pl.ds(pl.multiple_of(at * 2 * step, 2 * step), 2 * step)] = both_grad.reshape(
        count, BLOCK, 2 * step
    )
    part = lax.dot_general(
        both_grad, both_weight_ref[...], contract_last, preferred_element_type=jnp.float32
    )
    last = pl.num_programs(0) - 1

    @pl.when(at == 0)
    def _():
        acc[...] = part

    @pl.when((at > 0) & (at < last))
    def _():
        acc[...] += part

    @pl.when(at == last)
    def _():
        total = (acc[...] + part).astype(low)
        for block, grad in enumerate(grad_refs):
            grad[...] = total[block * BLOCK : (block + 1) * BLOCK]


def mlp_blocks(place_at, seconds, cots, weights, held):
    rows = sum(second.shape[0] for second in seconds)
    width = seconds[0].shape[1]
    count = rows // BLOCK
    hidden_width = weights.shape[1] // 3
    step = FF_STEP
    steps = hidden_width // step
    ins = [
        pl.BlockSpec(value.shape, lambda c: (0, 0), pipeline_mode=pl.Buffered(1))
        for value in (*seconds, *cots)
    ]
    kept = pl.BlockSpec((count, BLOCK, step), lambda c: (place_at, 0, c))
    kept_both = pl.BlockSpec((count, BLOCK, 2 * hidden_width), lambda c: (place_at, 0, 0))
    kept_rows = pl.BlockSpec((count, BLOCK, width), lambda c: (place_at, 0, 0))
    rows_shape = jax.ShapeDtypeStruct((RING, BLOCK, width), low)
    return pl.pallas_call(
        functools.partial(mlp_kernel, len(seconds), len(cots)),
        grid=(steps,),
        in_specs=ins
        + [
            pl.BlockSpec((width, 2 * step), lambda c: (0, c)),
            pl.BlockSpec((width, step), lambda c: (0, 2 * steps + c)),
        ]
        + [pl.BlockSpec(memory_space=pl.ANY)] * len(held),
        out_specs=(kept, kept_both, kept_rows, kept_rows)
        + (pl.BlockSpec((BLOCK, width), lambda c: (0, 0)),) * count,
        out_shape=(
            jax.ShapeDtypeStruct((RING, BLOCK, hidden_width), low),
            jax.ShapeDtypeStruct((RING, BLOCK, 2 * hidden_width), low),
            rows_shape,
            rows_shape,
        )
        + (jax.ShapeDtypeStruct((BLOCK, width), low),) * count,
        scratch_shapes=[pltpu.VMEM((rows, width), jnp.float32)],
        input_output_aliases={len(ins) + 2 + i: i for i in range(len(held))},
        compiler_params=pltpu.CompilerParams(vmem_limit_bytes=VMEM_LIMIT),
        cost_estimate=pl.CostEstimate(
            flops=2 * 5 * rows * width * hidden_width,
            bytes_accessed=2 * 3 * width * hidden_width,
            transcendentals=rows * hidden_width,
        ),
    )(*seconds, *cots, weights, weights, *held)


def mlp_out_kernel(inner_ref, weight_ref, *outs):
    inner = inner_ref[...].reshape(RING * BLOCK, inner_ref.shape[2])
    part = lax.dot_general(
        inner, weight_ref[...], contract_last, preferred_element_type=jnp.float32
    ).astype(low)
    for block, out in enumerate(outs):
        out[...] = part[block * BLOCK : (block + 1) * BLOCK]


def mlp_out_part(inner, weights):
    _, rows, hidden_width = inner.shape
    width = weights.shape[0]
    steps = 4
    return pl.pallas_call(
        mlp_out_kernel,
        grid=(steps,),
        in_specs=[
            pl.BlockSpec(inner.shape, lambda d: (0, 0, 0)),
            pl.BlockSpec((width // steps, hidden_width), lambda d: (d, 2)),
        ],
        out_specs=(pl.BlockSpec((rows, width // steps), lambda d: (0, d)),) * RING,
        out_shape=(jax.ShapeDtypeStruct((rows, width), low),) * RING,
        compiler_params=pltpu.CompilerParams(vmem_limit_bytes=VMEM_LIMIT),
        cost_estimate=pl.CostEstimate(flops=1024, bytes_accessed=1024, transcendentals=0),
    )(inner, weights)


def pair_grad(core_at, lefts, right, by_heads=False):
    width = lefts[0].shape[-1]
    outs = 512 if by_heads else right.shape[2]
    rows = RING * BLOCK

    def kernel(core_ref, *refs):
        left_refs = refs[: len(lefts)]
        right_ref, keep_ref, give_ref = refs[len(lefts) : len(lefts) + 3]
        if by_heads:
            all_ref = refs[-1]

            @pl.when(pl.program_id(0) == 0)
            def _():
                for r in range(RING):
                    for head in range(4):
                        all_ref[
                            r * BLOCK : (r + 1) * BLOCK, head * HEAD_DIM : (head + 1) * HEAD_DIM
                        ] = right_ref[4 * r + head]

            values = all_ref[...]
        else:
            values = right_ref[...].reshape(rows, outs)
        inputs = [ref[...].reshape(-1, 256) for ref in left_refs]
        inputs = inputs[0] if len(inputs) == 1 else jnp.concatenate(inputs, axis=0)
        term = lax.dot_general(
            inputs, values, contract_first, preferred_element_type=jnp.float32
        ).astype(low)
        first_core = core_ref[0] == 0
        keep_ref[0] = jnp.where(first_core, term[:128], term[128:])
        give_ref[0] = jnp.where(first_core, term[128:], term[:128])

    def columns(value):
        lead = value.shape[:-1]
        return pl.BlockSpec((*lead, 256), lambda i: (0,) * len(lead) + (i,))

    half = pl.BlockSpec((1, 128, outs), lambda i: (i, 0, 0))
    return pl.pallas_call(
        kernel,
        grid=(width // 256,),
        in_specs=[pl.BlockSpec(memory_space=pltpu.SMEM)]
        + [columns(value) for value in lefts]
        + [pl.BlockSpec(right.shape, lambda i: (0, 0, 0))],
        out_specs=(half, half),
        out_shape=(jax.ShapeDtypeStruct((width // 256, 128, outs), low),) * 2,
        scratch_shapes=[pltpu.VMEM((rows, 512), low)] * by_heads,
        compiler_params=pltpu.CompilerParams(vmem_limit_bytes=VMEM_LIMIT),
        cost_estimate=pl.CostEstimate(flops=1024, bytes_accessed=1024, transcendentals=0),
    )(core_at[None], *lefts, right)


def middle_kernel(*refs):
    mixed_refs, weight_refs = refs[:RING], refs[RING : 2 * RING]
    hidden_ref, gain_ref, middle_ref, second_ref = refs[2 * RING :]
    at = pl.program_id(0)
    step = weight_refs[0].shape[0]
    columns = pl.ds(pl.multiple_of(at * step, step), step)
    total = hidden_ref[:, columns].astype(jnp.float32)
    for mixed, weight in zip(mixed_refs, weight_refs):
        rows = jnp.concatenate([mixed[head] for head in range(4)], axis=1)
        total += lax.dot_general(
            rows, weight[...], contract_last, preferred_element_type=jnp.float32
        )
    middle_ref[:, columns] = total

    @pl.when(at == pl.num_programs(0) - 1)
    def _():
        second_ref[...] = (normalize(middle_ref[...]) * gain_ref[...]).astype(low)


def middle_part(mixed_blocks, weights, hidden, gain):
    rows, width = hidden.shape
    steps = 4
    whole = pl.BlockSpec((rows, width), lambda d: (0, 0))
    return pl.pallas_call(
        middle_kernel,
        grid=(steps,),
        in_specs=[pl.BlockSpec((4, rows, HEAD_DIM), lambda d: (0, 0, 0))] * RING
        + [pl.BlockSpec((width // steps, 512), lambda d: (d, 0))] * RING
        + [whole, pl.BlockSpec((1, width), lambda d: (0, 0))],
        out_specs=(whole, whole),
        out_shape=(
            jax.ShapeDtypeStruct((rows, width), jnp.float32),
            jax.ShapeDtypeStruct((rows, width), low),
        ),
        compiler_params=pltpu.CompilerParams(vmem_limit_bytes=32 * 1024 * 1024),
        cost_estimate=pl.CostEstimate(flops=1024, bytes_accessed=1024, transcendentals=0),
    )(*mixed_blocks, *weights, hidden, gain)


def middle_back_kernel(*refs):
    parts, weight_refs = refs[:RING], refs[RING : 2 * RING]
    middle_ref, cot_ref, gain_ref, grad_ref, low_ref, gain_out, *rest = refs[2 * RING :]
    outs, accs = rest[:RING], rest[RING:]
    at = pl.program_id(0)
    step = weight_refs[0].shape[0]

    @pl.when(at == 0)
    def _():
        second_grad = sum(part[...].astype(jnp.float32) for part in parts)
        middle = middle_ref[...]
        scale = inverse_rms(middle)
        normed = middle * scale
        gain_out[...] = jnp.sum(second_grad * normed, axis=0, keepdims=True)
        scaled = second_grad * gain_ref[...]
        grad = cot_ref[...].astype(jnp.float32) + scale * (
            scaled - normed * jnp.mean(scaled * normed, axis=-1, keepdims=True)
        )
        grad_ref[...] = grad
        low_ref[...] = grad.astype(low)
        for acc in accs:
            acc[...] = jnp.zeros_like(acc)

    rows = low_ref[:, pl.ds(pl.multiple_of(at * step, step), step)]
    for weight, acc in zip(weight_refs, accs):
        acc[...] += jnp.dot(rows, weight[...], preferred_element_type=jnp.float32)

    @pl.when(at == pl.num_programs(0) - 1)
    def _():
        for out, acc in zip(outs, accs):
            for head in range(4):
                out[head] = acc[:, head * HEAD_DIM : (head + 1) * HEAD_DIM].astype(low)


def middle_back(parts, weights, middle, cot, gain):
    rows, width = middle.shape
    steps = 4
    whole = pl.BlockSpec((rows, width), lambda d: (0, 0))
    row = pl.BlockSpec((1, width), lambda d: (0, 0))
    heads = pl.BlockSpec((4, rows, HEAD_DIM), lambda d: (0, 0, 0))
    return pl.pallas_call(
        middle_back_kernel,
        grid=(steps,),
        in_specs=[whole] * RING
        + [pl.BlockSpec((width // steps, 512), lambda d: (d, 0))] * RING
        + [whole, whole, row],
        out_specs=(whole, whole, row) + (heads,) * RING,
        out_shape=(
            jax.ShapeDtypeStruct((rows, width), jnp.float32),
            jax.ShapeDtypeStruct((rows, width), low),
            jax.ShapeDtypeStruct((1, width), jnp.float32),
        )
        + (jax.ShapeDtypeStruct((4, rows, HEAD_DIM), low),) * RING,
        scratch_shapes=[pltpu.VMEM((rows, 512), jnp.float32)] * RING,
        compiler_params=pltpu.CompilerParams(vmem_limit_bytes=VMEM_LIMIT),
        cost_estimate=pl.CostEstimate(flops=1024, bytes_accessed=1024, transcendentals=0),
    )(*parts, *weights, middle, cot, gain)


def first_kernel(
    own_ref, left_ref, top_ref, bottom_ref, right_ref, weight_ref, gains_ref, cos_ref, sin_ref,
    query_gain, key_gain, hidden_ref, first_ref, pre_ref, send_ref, gain_out,
):
    at = pl.program_id(0)
    half = top_ref.shape[0]

    @pl.when(at == 0)
    def _():
        gain_out[...] = gains_ref[...].astype(jnp.float32).T[:8]
        hidden_ref[0] = own_ref[...]

    @pl.when(at == 1)
    def _():
        hidden_ref[0] = left_ref[...]

    @pl.when(at == 2)
    def _():
        hidden_ref[0, :half] = top_ref[...]
        hidden_ref[0, half:] = bottom_ref[...]

    @pl.when(at == 3)
    def _():
        hidden_ref[0] = right_ref[...]

    first = (normalize(hidden_ref[0].astype(jnp.float32)) * gain_out[0:1]).astype(low)
    first_ref[0] = first
    pre = jnp.dot(first, weight_ref[...], preferred_element_type=jnp.float32)
    pre_ref[0] = pre
    cosine = cos_ref[0]
    sine = sin_ref[0]

    def turned(head, gain):
        values = normalize(pre[:, head * HEAD_DIM : (head + 1) * HEAD_DIM]) * gain
        return (values * cosine + pltpu.roll(values, HEAD_DIM // 2, 1) * sine).astype(low)

    for head in range(4):
        send_ref[head, 0] = turned(head, query_gain[...])
    for head in range(2):
        send_ref[2 * head, 1] = turned(4 + head, key_gain[...])
        send_ref[2 * head + 1, 1] = pre[:, (6 + head) * HEAD_DIM : (7 + head) * HEAD_DIM].astype(low)


def first_part(blocks, weights, cosine, sine, query_gain, key_gain):
    rows, width = blocks[0].shape
    row = pl.BlockSpec((1, HEAD_DIM), lambda r: (0, 0))
    turn = pl.BlockSpec((1, rows, HEAD_DIM), lambda r: (r, 0, 0))
    return pl.pallas_call(
        first_kernel,
        grid=(RING,),
        in_specs=[pl.BlockSpec(block.shape, lambda r: (0, 0)) for block in blocks]
        + [
            pl.BlockSpec((width, 1024), lambda r: (0, 0)),
            pl.BlockSpec((width, HEAD_DIM), lambda r: (0, 8)),
            turn,
            turn,
            row,
            row,
        ],
        out_specs=(
            pl.BlockSpec((1, rows, width), lambda r: (r, 0, 0)),
            pl.BlockSpec((1, rows, width), lambda r: (r, 0, 0)),
            pl.BlockSpec((1, rows, 1024), lambda r: (r, 0, 0)),
            pl.BlockSpec((4, 2, rows, HEAD_DIM), lambda r: (r, 0, 0, 0)),
            pl.BlockSpec((8, width), lambda r: (0, 0)),
        ),
        out_shape=(
            jax.ShapeDtypeStruct((RING, rows, width), low),
            jax.ShapeDtypeStruct((RING, rows, width), low),
            jax.ShapeDtypeStruct((RING, rows, 1024), jnp.float32),
            jax.ShapeDtypeStruct((BLOCKS, 2, rows, HEAD_DIM), low),
            jax.ShapeDtypeStruct((8, width), jnp.float32),
        ),
        compiler_params=pltpu.CompilerParams(vmem_limit_bytes=VMEM_LIMIT),
        cost_estimate=pl.CostEstimate(
            flops=2 * RING * rows * width * 1024,
            bytes_accessed=20 * 1024 * 1024,
            transcendentals=0,
        ),
    )(*blocks, weights, weights, cosine, sine, query_gain, key_gain)


def first_back_kernel(
    core_ref, back_ref, pre_ref, cos_ref, sin_ref, query_gain, key_gain, first_ref,
    grad_ref, keep_ref, give_ref, query_sum, key_sum, all_grads,
):
    at = pl.program_id(0)
    rows = grad_ref.shape[1]
    cosine = cos_ref[0]
    sine = sin_ref[0]

    @pl.when(at == 0)
    def _():
        query_sum[...] = jnp.zeros_like(query_sum)
        key_sum[...] = jnp.zeros_like(key_sum)

    def back(grads, head, gain, sums):
        columns = slice(head * HEAD_DIM, (head + 1) * HEAD_DIM)
        values = pre_ref[0, :, columns]
        grads = grads.astype(jnp.float32)
        grads = grads * cosine - pltpu.roll(grads, HEAD_DIM // 2, 1) * sine
        scale = inverse_rms(values)
        normed = values * scale
        sums[...] += jnp.sum(grads * normed, axis=0, keepdims=True)
        scaled = grads * gain
        out = scale * (scaled - normed * jnp.mean(scaled * normed, axis=-1, keepdims=True))
        grad_ref[0, :, columns] = out.astype(low)

    for head in range(4):
        back(back_ref[head, 0], head, query_gain[...], query_sum)
    for head in range(2):
        back(back_ref[2 * head, 1], 4 + head, key_gain[...], key_sum)
        grad_ref[0, :, (6 + head) * HEAD_DIM : (7 + head) * HEAD_DIM] = back_ref[2 * head + 1, 1]
    all_grads[pl.ds(pl.multiple_of(at * rows, rows), rows), :] = grad_ref[0]

    @pl.when(at == RING - 1)
    def _():
        grads = all_grads[...]
        first_core = core_ref[0] == 0
        for pair in range(8):
            inputs = first_ref[:, :, pair * 256 : (pair + 1) * 256].reshape(RING * rows, 256)
            term = lax.dot_general(
                inputs, grads, contract_first, preferred_element_type=jnp.float32
            ).astype(low)
            keep_ref[pair] = jnp.where(first_core, term[:128], term[128:])
            give_ref[pair] = jnp.where(first_core, term[128:], term[:128])


def first_back(core_at, returned, pre, cosine, sine, query_gain, key_gain, first_in):
    _, rows, width = first_in.shape
    row = pl.BlockSpec((1, HEAD_DIM), lambda r: (0, 0))
    turn = pl.BlockSpec((1, rows, HEAD_DIM), lambda r: (r, 0, 0))
    wide = pl.BlockSpec((1, rows, 1024), lambda r: (r, 0, 0))
    half = pl.BlockSpec((8, 128, 1024), lambda r: (0, 0, 0))
    return pl.pallas_call(
        first_back_kernel,
        grid=(RING,),
        in_specs=[
            pl.BlockSpec(memory_space=pltpu.SMEM),
            pl.BlockSpec((4, 2, rows, HEAD_DIM), lambda r: (r, 0, 0, 0)),
            wide,
            turn,
            turn,
            row,
            row,
            pl.BlockSpec((RING, rows, width), lambda r: (0, 0, 0)),
        ],
        out_specs=(wide, half, half, row, row),
        out_shape=(
            jax.ShapeDtypeStruct((RING, rows, 1024), low),
            jax.ShapeDtypeStruct((8, 128, 1024), low),
            jax.ShapeDtypeStruct((8, 128, 1024), low),
            jax.ShapeDtypeStruct((1, HEAD_DIM), jnp.float32),
            jax.ShapeDtypeStruct((1, HEAD_DIM), jnp.float32),
        ),
        scratch_shapes=[pltpu.VMEM((RING * rows, 1024), low)],
        compiler_params=pltpu.CompilerParams(vmem_limit_bytes=VMEM_LIMIT),
        cost_estimate=pl.CostEstimate(flops=1024, bytes_accessed=1024, transcendentals=0),
    )(core_at[None], returned, pre, cosine, sine, query_gain, key_gain, first_in)


def last_kernel(
    core_ref, grad_ref, weight_ref, hidden_ref, mlp_ref, query_ref, key_ref,
    own_ref, left_a, left_b, top_ref, bottom_ref, right_a, right_b, keep_ref, give_ref, gain_acc,
):
    at = pl.program_id(0)
    width = hidden_ref.shape[2]
    part = lax.dot_general(
        grad_ref[0], weight_ref[...], contract_last, preferred_element_type=jnp.float32
    )
    half = top_ref.shape[0]
    @pl.when(at == 0)
    def _():
        own_ref[...] = part.astype(low)

    for r, first, second in ((1, left_a, left_b), (2, top_ref, bottom_ref), (3, right_a, right_b)):

        @pl.when(at == r)
        def _(first=first, second=second):
            first[...] = part[:half].astype(low)
            second[...] = part[half:].astype(low)

    normed = normalize(hidden_ref[0].astype(jnp.float32))
    gain = jnp.sum(part * normed, axis=0, keepdims=True)

    @pl.when(at == 0)
    def _():
        gain_acc[...] = gain

    @pl.when(at > 0)
    def _():
        gain_acc[...] += gain

    @pl.when(at == RING - 1)
    def _():
        lines = [
            gain_acc[...],
            mlp_ref[...],
            jnp.concatenate([query_ref[...]] * BLOCKS, axis=1),
            jnp.concatenate([key_ref[...]] * BLOCKS, axis=1),
            jnp.zeros((HEAD_DIM - 4, width), jnp.float32),
        ]
        turned = jnp.concatenate(lines, axis=0).T.astype(low)
        first_core = core_ref[0] == 0
        for pair in range(8):
            first = turned[pair * 256 : pair * 256 + 128]
            second = turned[pair * 256 + 128 : (pair + 1) * 256]
            keep_ref[pair] = jnp.where(first_core, first, second)
            give_ref[pair] = jnp.where(first_core, second, first)


def last_part(core_at, grads, weights, hidden_all, mlp_part, query_part, key_part):
    _, rows, width = hidden_all.shape
    block = pl.BlockSpec((rows, width), lambda r: (0, 0))
    small = pl.BlockSpec((rows // 2, width), lambda r: (0, 0))
    whole = jax.ShapeDtypeStruct((rows, width), low)
    part = jax.ShapeDtypeStruct((rows // 2, width), low)
    row = pl.BlockSpec((1, HEAD_DIM), lambda r: (0, 0))
    half = pl.BlockSpec((8, 128, HEAD_DIM), lambda r: (0, 0, 0))
    return pl.pallas_call(
        last_kernel,
        grid=(RING,),
        in_specs=[
            pl.BlockSpec(memory_space=pltpu.SMEM),
            pl.BlockSpec((1, rows, 1024), lambda r: (r, 0, 0)),
            pl.BlockSpec((width, 1024), lambda r: (0, 0)),
            pl.BlockSpec((1, rows, width), lambda r: (r, 0, 0)),
            pl.BlockSpec((1, width), lambda r: (0, 0)),
            row,
            row,
        ],
        out_specs=(block,) + (small,) * 6 + (half, half),
        out_shape=(whole,) + (part,) * 6
        + (jax.ShapeDtypeStruct((8, 128, HEAD_DIM), low),) * 2,
        scratch_shapes=[pltpu.VMEM((1, width), jnp.float32)],
        compiler_params=pltpu.CompilerParams(vmem_limit_bytes=VMEM_LIMIT),
        cost_estimate=pl.CostEstimate(flops=1024, bytes_accessed=1024, transcendentals=0),
    )(core_at[None], grads, weights, hidden_all, mlp_part, query_part, key_part)


def arrange_kernel(at_ref, own_ref, other_ref, out_ref):
    y_at, x_at, core_at = at_ref[0], at_ref[1], at_ref[2]
    for dy in range(RING):
        for dx in range(2):
            first = ((y_at - dy + RING) & 3) * 4 + (x_at ^ dx) * 2
            own = pl.multiple_of((first + core_at) * 128, 128)
            other = pl.multiple_of((first + 1 - core_at) * 128, 128)
            out_ref[pl.ds(own, 128), :] = own_ref[dy, dx]
            out_ref[pl.ds(other, 128), :] = other_ref[dy, dx]


def gather_by_permutes(pairs, y_at, x_at, core_at):
    own = jnp.stack(pairs)
    other = shift(own, "core", 1, 2)
    whole = pl.BlockSpec(memory_space=pltpu.VMEM)
    return pl.pallas_call(
        arrange_kernel,
        in_specs=[pl.BlockSpec(memory_space=pltpu.SMEM), whole, whole],
        out_specs=whole,
        out_shape=jax.ShapeDtypeStruct((BLOCKS * 128, own.shape[3]), own.dtype),
        compiler_params=pltpu.CompilerParams(vmem_limit_bytes=VMEM_LIMIT),
        cost_estimate=pl.CostEstimate(flops=1024, bytes_accessed=1024, transcendentals=0),
    )(jnp.stack([y_at, x_at, core_at]), own, other)


def pair_sums_kernel(keep_ref, come_ref, gains_keep, gains_come, out_ref):
    f32 = jnp.float32
    wide = keep_ref.shape[2]
    out_ref[:, :, :wide] = (keep_ref[...].astype(f32) + come_ref[...].astype(f32)).astype(low)
    out_ref[:, :, wide:] = (gains_keep[...].astype(f32) + gains_come[...].astype(f32)).astype(low)


def pair_sums(keep, come, more_keep, more_come):
    blocks, rows, wide = keep.shape
    narrow = more_keep.shape[2]
    large = pl.BlockSpec((4, rows, wide), lambda i: (i, 0, 0))
    small = pl.BlockSpec((4, rows, narrow), lambda i: (i, 0, 0))
    return pl.pallas_call(
        pair_sums_kernel,
        grid=(blocks // 4,),
        in_specs=[large, large, small, small],
        out_specs=pl.BlockSpec((4, rows, wide + narrow), lambda i: (i, 0, 0)),
        out_shape=jax.ShapeDtypeStruct((blocks, rows, wide + narrow), low),
        compiler_params=pltpu.CompilerParams(vmem_limit_bytes=VMEM_LIMIT),
        cost_estimate=pl.CostEstimate(flops=1024, bytes_accessed=1024, transcendentals=0),
    )(keep, come, more_keep, more_come)


def to_heads(send):
    return lax.all_to_all(send, GROUP_AXES, 0, 0, tiled=True)


def after(value, *others):
    return lax.optimization_barrier((value, others))[0]


def ring_blocks(values):
    half = values.shape[0] // 2
    left = shift(values, "z", 1)
    right = shift(values, "z", 3)
    opposite = jnp.concatenate(
        [shift(left[:half], "z", 1), shift(right[half:], "z", 3)], axis=0
    )
    return [values, left, opposite, right]


def together(*values):
    return lax.optimization_barrier(values)


def place(z_at, blocks, widths, chunk=None, summed=False):
    rows = blocks[0].shape[0]
    whole = pl.BlockSpec(memory_space=pltpu.VMEM)
    shapes = [RING * part for part in widths] + [HEAD_DIM] * summed

    def kernel(z_ref, *refs):
        ins, outs = refs[:RING], refs[RING:]
        for r in range(RING):
            slot = (z_ref[0] - r + RING) & 3
            start = 0
            for turn in range(widths[0] // chunk if chunk else 1):
                for out, part in zip(outs, widths):
                    size = chunk or part
                    at = pl.multiple_of(slot * part + turn * size, 128)
                    out[:, pl.ds(at, size)] = ins[r][:, start : start + size].astype(jnp.float32)
                    start += size
            if summed:
                columns = ins[r][:, start : start + HEAD_DIM].astype(jnp.float32)
                outs[-1][...] = columns if r == 0 else outs[-1][...] + columns

    return pl.pallas_call(
        kernel,
        in_specs=[pl.BlockSpec(memory_space=pltpu.SMEM)] + [whole] * RING,
        out_specs=tuple(whole for _ in shapes),
        out_shape=tuple(jax.ShapeDtypeStruct((rows, part), jnp.float32) for part in shapes),
        compiler_params=pltpu.CompilerParams(vmem_limit_bytes=VMEM_LIMIT),
        cost_estimate=pl.CostEstimate(flops=1024, bytes_accessed=1024, transcendentals=0),
    )(z_at[None], *blocks)


def send_back(block, r):
    return shift(block, "z", -r)


def local(
    hidden_in,
    cotangent,
    segment_ids,
    positions,
    attn_gain,
    query_gain,
    key_gain,
    query_weight,
    key_weight,
    value_weight,
    out_weight,
    mlp_gain,
    gate_weight,
    up_weight,
    down_weight,
):
    f32 = jnp.float32
    rows, width = hidden_in.shape
    ring_rows = RING * rows
    z_at = lax.axis_index("z")
    y_at = lax.axis_index("y")
    x_at = lax.axis_index("x_hi")
    core_at = lax.axis_index("core")
    my_index = (y_at * 2 + x_at) * 2 + core_at

    def columns(weight):
        part = weight.shape[1] // RING
        return lax.dynamic_slice_in_dim(weight, z_at * part, part, 1).astype(low)

    def gather(block):
        return lax.all_gather(block, GROUP_AXES, axis=0, tiled=True)

    own_places = lax.dynamic_slice_in_dim(positions, my_index * rows, rows)
    firsts = positions.reshape(BLOCKS, BLOCK)[:, 0]
    segments = segment_ids.reshape(BLOCKS, BLOCK)[:, 0]
    logical = firsts // BLOCK + jnp.maximum(segments - 1, 0) * 2
    numbers = jnp.arange(BLOCKS, dtype=jnp.int32)
    order = jnp.sum(jnp.where(logical[:, None] == numbers[None, :], numbers[:, None], 0), axis=0)
    notes = gather_z(jnp.concatenate([own_places, order, jnp.zeros((112,), jnp.int32)])[None])
    places = notes[:, :rows]
    order = lax.dynamic_index_in_dim(notes, y_at, 0, keepdims=False)[rows : rows + BLOCKS]

    gains = jnp.pad(
        jnp.stack([attn_gain, mlp_gain], axis=1).astype(low), ((0, 0), (0, HEAD_DIM - 2))
    )
    first_weights = gather(
        jnp.concatenate(
            [columns(query_weight), columns(key_weight), columns(value_weight), gains], axis=1
        )
    )
    out_columns = columns(out_weight)
    out_come = shift(out_columns, "x_hi", 1, 2)
    out_pairs = jnp.stack([out_columns, out_come])
    out_pairs = [out_pairs] + [shift(out_pairs, "y", r) for r in range(1, RING)]

    hidden_own = after(hidden_in, notes, out_come)
    hidden_left = shift(hidden_own, "z", 1)
    hidden_right = shift(hidden_own, "z", 3)
    gate_columns, up_columns, down_columns, hidden_left, hidden_right, out_pairs = together(
        gate_weight, up_weight, down_weight, hidden_left, hidden_right, out_pairs
    )
    out_slice = gather_by_permutes(out_pairs, y_at, x_at, core_at)
    gate_columns, up_columns = columns(gate_columns), columns(up_columns)
    mlp_columns = []
    for start in range(0, gate_columns.shape[1], FF_STEP):
        mlp_columns.append(gate_columns[:, start : start + FF_STEP])
        mlp_columns.append(up_columns[:, start : start + FF_STEP])
    mlp_weights = gather(jnp.concatenate(mlp_columns + [columns(down_columns)], axis=1))
    half = rows // 2
    hidden_blocks = [
        hidden_own,
        hidden_left,
        shift(hidden_left[:half], "z", 1),
        shift(hidden_right[half:], "z", 3),
        hidden_right,
    ]
    out_slice = after(out_slice, *hidden_blocks)
    out_left = shift(out_slice, "z", 1)
    out_right = shift(out_slice, "z", 3)
    frequency = rope_base ** (-2.0 * jnp.arange(HEAD_DIM // 2, dtype=f32) / HEAD_DIM)
    angles = places.astype(f32)[:, :, None] * frequency[None, None, :]
    cosine = jnp.cos(angles)
    sine = jnp.sin(angles)
    cosine = jnp.concatenate([cosine, cosine], axis=-1)
    sine = jnp.concatenate([-sine, sine], axis=-1)
    query_row = query_gain[None]
    key_row = key_gain[None]

    hidden_all, first_in, qkv_pre, send, gain_rows = first_part(
        hidden_blocks, first_weights, cosine, sine, query_row, key_row
    )
    attn_scale = gain_rows[0:1]
    mlp_scale = gain_rows[1:2]
    arrived, out_left, out_right = together(to_heads(send), out_left, out_right)
    other_pair = shift(arrived[:, 1], "core", 1, 2)
    head_mixed, head_mixed_t, head_logs = attention_forward(order, core_at, arrived, other_pair)
    out_top = shift(out_left[: width // 2], "z", 1)
    out_bottom = shift(out_right[width // 2 :], "z", 3)
    head_mixed, head_mixed_t, head_logs, out_top, out_bottom = together(
        head_mixed, head_mixed_t, head_logs, out_top, out_bottom
    )
    cot_own = after(cotangent, head_mixed)
    cot_left = shift(cot_own, "z", 1)
    cot_right = shift(cot_own, "z", 3)

    cot_top = shift(cot_left[:half], "z", 1)
    cot_bottom = shift(cot_right[half:], "z", 3)
    mixed_arrived, cot_left, cot_right, cot_top, cot_bottom = together(
        to_heads(head_mixed), cot_left, cot_right, cot_top, cot_bottom
    )
    mixed_blocks = [mixed_arrived[:4]] + [
        shift(mixed_arrived[4 * (RING - j) : 4 * (RING - j) + 4], "z", j) for j in range(1, RING)
    ]
    out_opposite = jnp.concatenate([out_top, out_bottom], axis=0)
    out_weights = [out_slice, out_left, out_opposite, out_right]
    mixed_blocks, out_weights = together(mixed_blocks, out_weights)
    middle, second_in = middle_part(mixed_blocks, out_weights, hidden_in, mlp_scale)
    hidden = hidden_in.astype(f32)
    left = shift(second_in, "z", 1)
    right = shift(second_in, "z", 3)
    *held, own_part = mlp_blocks(0, [second_in], [cot_own], mlp_weights, ())
    held, own_part, left, right, second_in = together(held, own_part, left, right, second_in)
    opposite = shift(second_in, "z", 2)
    *held, left_part, right_part = mlp_blocks(
        1, [left, right], [cot_left, cot_right], mlp_weights, held
    )
    left_back = send_back(left_part, 1)
    right_back = send_back(right_part, 3)
    held, opposite = together(held, opposite)
    *held, opposite_part = mlp_blocks(
        1, [opposite], [cot_top, cot_bottom], mlp_weights, held
    )
    opposite_back = send_back(opposite_part, 2)
    inner, both_grad, second_all, cot_all = held

    def pair_sum(keep, come):
        return (keep.astype(f32) + come.astype(f32)).astype(low)

    def along_y(pair):
        return lax.all_to_all(pair.reshape(RING, 2, 128, pair.shape[2]), "y", 0, 0, tiled=True)

    def along_x(halves):
        keep = lax.dynamic_index_in_dim(halves, x_at, 0, keepdims=False)
        give = lax.dynamic_index_in_dim(halves, 1 - x_at, 0, keepdims=False)
        return keep, lax.ppermute(give, ("x_lo", "x_hi"), [(i, 3 - i) for i in range(4)])

    def add_up(terms):
        return jnp.sum(terms.astype(f32), axis=0).astype(low)

    def over_x(share):
        return share, shift(share, "x_lo", 1, 2)

    def over_z(pair):
        share = pair_sum(*pair)
        return [share] + [shift(share, "z", r) for r in range(1, RING)]

    both_term = lax.dot_general(
        second_all.reshape(ring_rows, width),
        both_grad.reshape(ring_rows, 3072),
        contract_first,
        preferred_element_type=f32,
    ).astype(low)
    left_back, right_back, opposite_back, both_term, inner = together(
        left_back, right_back, opposite_back, both_term, inner
    )
    both_share = lax.psum_scatter(both_term, GROUP_AXES, scatter_dimension=0, tiled=True)

    middle_grad, own_low, mlp_gain_part, *grad_blocks = middle_back(
        (own_part, left_back, right_back, opposite_back),
        out_weights,
        middle,
        cotangent,
        mlp_scale,
    )
    grad_blocks = [grad_blocks[0]] + [shift(grad_blocks[RING - r], "z", r) for r in range(1, RING)]
    down_keep, down_give = pair_grad(core_at, [cot_all], inner)
    grad_blocks, down_keep, down_give, own_low, inner = together(
        grad_blocks, down_keep, down_give, own_low, inner
    )
    head_grads = to_heads(jnp.concatenate(grad_blocks, axis=0))
    low_left = shift(own_low, "z", 1)
    low_right = shift(own_low, "z", 3)
    mlp_own, mlp_opposite, mlp_left, mlp_right = mlp_out_part(inner, mlp_weights)
    head_grads, low_left, low_right, own_low, mlp_opposite, mlp_left, mlp_right = together(
        head_grads, low_left, low_right, own_low, mlp_opposite, mlp_left, mlp_right
    )
    mlp_left = send_back(mlp_left, 1)
    mlp_right = send_back(mlp_right, 3)

    query_grad, grad_keep, grad_give = attention_backward(
        order, core_at, arrived, other_pair, head_grads, head_mixed_t, head_logs
    )
    query_grad, grad_keep, grad_give, mlp_left, mlp_right, own_low, mlp_opposite, down_give = together(
        query_grad, grad_keep, grad_give, mlp_left, mlp_right, own_low, mlp_opposite, down_give
    )
    low_opposite = shift(own_low, "z", 2)
    mlp_opposite = send_back(after(mlp_opposite, low_opposite), 2)
    grads_send = lax.dynamic_update_slice_in_dim(
        query_grad, pair_sum(grad_keep, shift(grad_give, "core", 1, 2))[:, None], 1, 1
    )
    returned = to_heads(grads_send)
    out_keep, out_give = pair_grad(
        core_at, [own_low, low_left, low_opposite, low_right], mixed_arrived, by_heads=True
    )
    down_sum = pair_sums(
        down_keep,
        shift(down_give, "core", 1, 2),
        out_keep,
        shift(out_give, "core", 1, 2),
    )
    returned, both_share, down_sum = together(returned, both_share, down_sum)
    both_pair = over_x(both_share)
    down_terms = along_y(down_sum)
    qkv_grad, qkv_keep, qkv_give, query_gain_part, key_gain_part = first_back(
        core_at, returned, qkv_pre, cosine, sine, query_row, key_row, first_in
    )
    qkv_grad, qkv_give, both_pair, mlp_opposite = together(
        qkv_grad, qkv_give, both_pair, mlp_opposite
    )
    both_sum = pair_sum(*both_pair)
    both_left = shift(both_sum, "z", 1)
    both_right = shift(both_sum, "z", 3)
    qkv_come = shift(qkv_give, "core", 1, 2)
    *first_parts, gains_keep, gains_give = last_part(
        core_at,
        qkv_grad,
        first_weights,
        hidden_all,
        mlp_gain_part,
        query_gain_part,
        key_gain_part,
    )
    first_parts, gains_give, qkv_come, both_left, both_right, both_sum = together(
        first_parts, gains_give, qkv_come, both_left, both_right, both_sum
    )
    down_pair = over_x(pair_sum(*along_x(add_up(down_terms))))
    gains_come = shift(gains_give, "core", 1, 2)
    first_own, left_a, left_b, first_top, first_bottom, right_a, right_b = first_parts
    first_top = shift(first_top, "z", 3)
    first_bottom = shift(first_bottom, "z", 1)
    qkv_terms = along_y(pair_sums(qkv_keep, qkv_come, gains_keep, gains_come))
    first_left = send_back(jnp.concatenate([pair_sum(left_a, first_top), left_b], axis=0), 1)
    first_right = send_back(jnp.concatenate([right_a, pair_sum(right_b, first_bottom)], axis=0), 3)
    both_opposite = shift(both_sum, "z", 2)
    down_blocks = over_z(down_pair)
    qkv_share = pair_sum(*along_x(add_up(qkv_terms)))
    both_blocks = [both_sum, both_left, both_opposite, both_right]
    qkv_pair, down_blocks = together(over_x(qkv_share), down_blocks)
    output = (
        middle
        + after(mlp_own, first_top).astype(f32)
        + mlp_left.astype(f32)
        + mlp_right.astype(f32)
        + mlp_opposite.astype(f32)
    ).astype(low)
    first_grad = first_own.astype(f32) + first_left.astype(f32) + first_right.astype(f32)
    hidden_rms = inverse_rms(hidden)
    own_norm = hidden * hidden_rms
    scaled_first = first_grad * attn_scale
    hidden_grad = (
        middle_grad
        + hidden_rms
        * (scaled_first - own_norm * jnp.mean(scaled_first * own_norm, axis=-1, keepdims=True))
    ).astype(low)

    down_grad_out, out_grad_out = place(z_at, down_blocks, (1536, 512))
    gate_grad_out, up_grad_out = place(z_at, both_blocks, (1536, 1536), chunk=FF_STEP)
    query_grad_out, key_grad_out, value_grad_out, gain_sum = place(
        z_at, over_z(qkv_pair), (512, 256, 256), summed=True
    )
    gain_sum = gain_sum[:, :4].T

    return (
        output,
        hidden_grad,
        gain_sum[0],
        gain_sum[2],
        gain_sum[3],
        query_grad_out,
        key_grad_out,
        value_grad_out,
        out_grad_out,
        gain_sum[1],
        gate_grad_out,
        up_grad_out,
        down_grad_out,
    )


def solution(mesh):
    fine = Mesh(mesh.devices.reshape(2, 4, 4, 2, 2), ALL_AXES)
    rep = ("x_lo", "z")
    row = P(ALL_AXES, None)
    part = P(GROUP_AXES)
    weight = P(GROUP_AXES, None)
    in_specs = (
        row,
        row,
        P(rep),
        P(rep),
        part,
        P(),
        P(),
        weight,
        weight,
        weight,
        weight,
        part,
        weight,
        weight,
        weight,
    )
    out_specs = (
        row,
        row,
        part,
        P(),
        P(),
        weight,
        weight,
        weight,
        weight,
        part,
        weight,
        weight,
        weight,
    )
    return jax.shard_map(local, mesh=fine, in_specs=in_specs, out_specs=out_specs, check_vma=False)
```

```python
import functools

import jax
import jax.numpy as jnp
from jax import lax
from jax.experimental import pallas as pl
from jax.experimental.pallas import tpu as pltpu
from jax.sharding import Mesh
from jax.sharding import PartitionSpec as P

HEAD_DIM = 128
RING = 4
BLOCK = 256
BLOCKS = 16
TILE = 512
TILES = 8
PROMPT_TILES = 6
FF_STEP = 512
VMEM_LIMIT = 60 * 1024 * 1024

norm_eps = 1e-06
rope_base = 1000000.0
score_scale = HEAD_DIM ** (-0.5)
score_scale_log2 = score_scale * 1.4426950408889634
contract_first = (((0,), (0,)), ((), ()))
contract_last = (((1,), (1,)), ((), ()))
GROUP_AXES = ("y", "x_hi", "core")
ALL_AXES = ("x_lo", "z", "y", "x_hi", "core")
low = jnp.bfloat16


def inverse_rms(values):
    return lax.rsqrt(jnp.mean(values * values, axis=-1, keepdims=True) + norm_eps)


def normalize(values):
    return values * inverse_rms(values)


def shift(values, axis, by, size=RING):
    return lax.ppermute(values, axis, [(i, (i + by) % size) for i in range(size)])


def gather_z(values):
    return jnp.concatenate(
        [values, shift(values, "z", 1), shift(values, "z", 2), shift(values, "z", 3)], axis=0
    )


def forward_kernel(
    order, core, own_a, own_b, other_a, other_b, mixed_ref, mixed_t_ref, log_ref, k_all, v_t, acc, total
):
    tile = pl.program_id(0)
    start = tile * TILE

    def take(keys, values):
        for half in range(2):
            rows = pl.ds(pl.multiple_of(start + half * BLOCK, BLOCK), BLOCK)
            k_all[rows, :] = keys[half]
            v_t[tile, :, half * BLOCK : (half + 1) * BLOCK] = (
                values[half].astype(jnp.float32).T.astype(low)
            )

    @pl.when(core[0] == 0)
    def _():
        take((own_a[0, 1], own_b[0, 1]), (other_a[0], other_b[0]))

    @pl.when(core[0] == 1)
    def _():
        take((other_a[0], other_b[0]), (own_a[0, 1], own_b[0, 1]))

    queries = jnp.concatenate([own_a[0, 0], own_b[0, 0]], axis=0)
    acc[...] = jnp.zeros_like(acc)
    total[...] = jnp.zeros_like(total)

    def chunk(at, masked):
        keys = k_all[pl.ds(pl.multiple_of(at * TILE, TILE), TILE), :]
        scores = lax.dot_general(keys, queries, contract_last, preferred_element_type=jnp.float32)
        weights = jnp.exp2(scores * score_scale_log2)
        if masked:
            key_row = lax.broadcasted_iota(jnp.int32, (TILE, TILE), 0)
            query_row = lax.broadcasted_iota(jnp.int32, (TILE, TILE), 1)
            weights = jnp.where(key_row <= query_row, weights, 0.0)
        total[...] += jnp.sum(weights, axis=0, keepdims=True)
        acc[...] += jnp.dot(v_t[at], weights.astype(low), preferred_element_type=jnp.float32)

    full = jnp.minimum(tile, PROMPT_TILES)
    for count in range(PROMPT_TILES + 1):

        @pl.when(full == count)
        def _(count=count):
            for at in range(count):
                chunk(at, False)
            chunk(tile, True)

    mixed_t = acc[...] / total[...]
    mixed_t_ref[0] = mixed_t
    log_ref[0] = jnp.log2(total[...])
    mixed = mixed_t.T.astype(low)
    mixed_ref[order[2 * tile]] = mixed[:BLOCK]
    mixed_ref[order[2 * tile + 1]] = mixed[BLOCK:]


def tile_specs(lead):
    return [
        pl.BlockSpec(
            (1, *lead, BLOCK, HEAD_DIM),
            functools.partial(
                lambda half, tile, order, core: (order[2 * tile + half],) + (0,) * (len(lead) + 2),
                half,
            ),
        )
        for half in range(2)
    ]


def attention_forward(order, core_at, arrived, other):
    whole = pl.BlockSpec(memory_space=pltpu.VMEM)
    turned = pl.BlockSpec((1, HEAD_DIM, TILE), lambda tile, order, core: (tile, 0, 0))
    line = pl.BlockSpec((1, 1, TILE), lambda tile, order, core: (tile, 0, 0))
    return pl.pallas_call(
        forward_kernel,
        out_shape=(
            jax.ShapeDtypeStruct((BLOCKS, BLOCK, HEAD_DIM), low),
            jax.ShapeDtypeStruct((TILES, HEAD_DIM, TILE), jnp.float32),
            jax.ShapeDtypeStruct((TILES, 1, TILE), jnp.float32),
        ),
        grid_spec=pltpu.PrefetchScalarGridSpec(
            num_scalar_prefetch=2,
            grid=(TILES,),
            in_specs=tile_specs((2,)) + tile_specs(()),
            out_specs=(whole, turned, line),
            scratch_shapes=[
                pltpu.VMEM((BLOCKS * BLOCK, HEAD_DIM), low),
                pltpu.VMEM((TILES, HEAD_DIM, TILE), low),
                pltpu.VMEM((HEAD_DIM, TILE), jnp.float32),
                pltpu.VMEM((1, TILE), jnp.float32),
            ],
        ),
        compiler_params=pltpu.CompilerParams(vmem_limit_bytes=VMEM_LIMIT),
        cost_estimate=pl.CostEstimate(
            flops=1024, bytes_accessed=1024, transcendentals=0
        ),
    )(order, core_at[None], arrived, arrived, other, other)


def backward_kernel(
    order, core, own_a, own_b, other_a, other_b, grad_a, grad_b, mixed_t_ref, log_ref,
    q_out, keep_out, give_out, k_all, v_all, k_t, q_acc, k_acc, v_acc,
):
    tile = pl.program_id(0)
    start = tile * TILE

    def take(keys, values):
        for half in range(2):
            rows = pl.ds(pl.multiple_of(start + half * BLOCK, BLOCK), BLOCK)
            k_all[rows, :] = keys[half]
            v_all[rows, :] = values[half]
            k_t[tile, :, half * BLOCK : (half + 1) * BLOCK] = (
                keys[half].astype(jnp.float32).T.astype(low)
            )

    @pl.when(core[0] == 0)
    def _():
        take((own_a[0, 1], own_b[0, 1]), (other_a[0], other_b[0]))

    @pl.when(core[0] == 1)
    def _():
        take((other_a[0], other_b[0]), (own_a[0, 1], own_b[0, 1]))

    rows = pl.ds(pl.multiple_of(start, TILE), TILE)
    k_acc[rows, :] = jnp.zeros((TILE, HEAD_DIM), jnp.float32)
    v_acc[rows, :] = jnp.zeros((TILE, HEAD_DIM), jnp.float32)
    queries = jnp.concatenate([own_a[0, 0], own_b[0, 0]], axis=0)
    grads = jnp.concatenate([grad_a[0], grad_b[0]], axis=0)
    grads_t = grads.astype(jnp.float32).T
    shared = jnp.sum(grads_t * mixed_t_ref[0], axis=0, keepdims=True)
    logs = log_ref[0]
    q_acc[...] = jnp.zeros_like(q_acc)

    def chunk(at, masked):
        rows = pl.ds(pl.multiple_of(at * TILE, TILE), TILE)
        scores = lax.dot_general(
            k_all[rows, :], queries, contract_last, preferred_element_type=jnp.float32
        )
        probs = jnp.exp2(scores * score_scale_log2 - logs)
        if masked:
            key_row = lax.broadcasted_iota(jnp.int32, (TILE, TILE), 0)
            query_row = lax.broadcasted_iota(jnp.int32, (TILE, TILE), 1)
            probs = jnp.where(key_row <= query_row, probs, 0.0)
        prob_grads = lax.dot_general(
            v_all[rows, :], grads, contract_last, preferred_element_type=jnp.float32
        )
        score_grads = (probs * (prob_grads - shared)).astype(low)
        v_acc[rows, :] += jnp.dot(probs.astype(low), grads, preferred_element_type=jnp.float32)
        k_acc[rows, :] += jnp.dot(score_grads, queries, preferred_element_type=jnp.float32)
        q_acc[...] += jnp.dot(k_t[at], score_grads, preferred_element_type=jnp.float32)

    full = jnp.minimum(tile, PROMPT_TILES)
    for count in range(PROMPT_TILES + 1):

        @pl.when(full == count)
        def _(count=count):
            for at in range(count):
                chunk(at, False)
            chunk(tile, True)

    query_grad = (q_acc[...] * score_scale).T.astype(low)
    q_out[order[2 * tile], 0] = query_grad[:BLOCK]
    q_out[order[2 * tile + 1], 0] = query_grad[BLOCK:]

    def give(keep_acc, keep_scale, give_acc, give_scale):
        for at in range(BLOCKS):
            rows = slice(at * BLOCK, (at + 1) * BLOCK)
            keep_out[order[at]] = (keep_acc[rows, :] * keep_scale).astype(low)
            give_out[order[at]] = (give_acc[rows, :] * give_scale).astype(low)

    @pl.when((tile == TILES - 1) & (core[0] == 0))
    def _():
        give(k_acc, score_scale, v_acc, 1.0)

    @pl.when((tile == TILES - 1) & (core[0] == 1))
    def _():
        give(v_acc, 1.0, k_acc, score_scale)


def attention_backward(order, core_at, arrived, other, grads, mixed_t, logs):
    whole = pl.BlockSpec(memory_space=pltpu.VMEM)
    rows = BLOCKS * BLOCK
    turned = pl.BlockSpec((1, HEAD_DIM, TILE), lambda tile, order, core: (tile, 0, 0))
    line = pl.BlockSpec((1, 1, TILE), lambda tile, order, core: (tile, 0, 0))
    return pl.pallas_call(
        backward_kernel,
        out_shape=(jax.ShapeDtypeStruct((BLOCKS, 2, BLOCK, HEAD_DIM), low),)
        + (jax.ShapeDtypeStruct((BLOCKS, BLOCK, HEAD_DIM), low),) * 2,
        grid_spec=pltpu.PrefetchScalarGridSpec(
            num_scalar_prefetch=2,
            grid=(TILES,),
            in_specs=tile_specs((2,)) + tile_specs(()) + tile_specs(()) + [turned, line],
            out_specs=(whole, whole, whole),
            scratch_shapes=[
                pltpu.VMEM((rows, HEAD_DIM), low),
                pltpu.VMEM((rows, HEAD_DIM), low),
                pltpu.VMEM((TILES, HEAD_DIM, TILE), low),
                pltpu.VMEM((HEAD_DIM, TILE), jnp.float32),
                pltpu.VMEM((rows, HEAD_DIM), jnp.float32),
                pltpu.VMEM((rows, HEAD_DIM), jnp.float32),
            ],
        ),
        compiler_params=pltpu.CompilerParams(vmem_limit_bytes=VMEM_LIMIT),
        cost_estimate=pl.CostEstimate(
            flops=1024, bytes_accessed=1024, transcendentals=0
        ),
    )(order, core_at[None], arrived, arrived, other, other, grads, grads, mixed_t, logs)


def mlp_kernel(parts, cot_parts, *refs):
    second_refs, cot_refs = refs[:parts], refs[parts : parts + cot_parts]
    both_weight_ref, down_ref = refs[parts + cot_parts : parts + cot_parts + 2]
    count = refs[-1].shape[0] // BLOCK
    inner_ref, both_ref, second_out, cot_out = refs[-5 - count : -1 - count]
    grad_refs, acc = refs[-1 - count : -1], refs[-1]
    at = pl.program_id(0)
    step = down_ref.shape[1]
    rows, width = acc.shape

    @pl.when(at == 0)
    def _():
        for ins, out in ((second_refs, second_out), (cot_refs, cot_out)):
            start = 0
            for part in ins:
                size = part.shape[0]
                out[start // BLOCK, start % BLOCK : start % BLOCK + size, :] = part[...]
                start += size

    second = second_out[...].reshape(rows, width)
    both_act = jnp.dot(second, both_weight_ref[...], preferred_element_type=jnp.float32)
    inner_grad = jnp.dot(
        cot_out[...].reshape(rows, width), down_ref[...], preferred_element_type=jnp.float32
    )
    gate_act = both_act[:, :step]
    up_act = both_act[:, step:]
    sigmoid = 1.0 / (1.0 + jnp.exp(-gate_act))
    silu = gate_act * sigmoid
    inner_ref[...] = (silu * up_act).astype(low).reshape(inner_ref.shape)
    gate_grad = (inner_grad * up_act * (sigmoid * (1.0 + gate_act * (1.0 - sigmoid)))).astype(low)
    both_grad = jnp.concatenate([gate_grad, (inner_grad * silu).astype(low)], axis=1)
    both_ref[:, :, pl.ds(pl.multiple_of(at * 2 * step, 2 * step), 2 * step)] = both_grad.reshape(
        count, BLOCK, 2 * step
    )
    part = lax.dot_general(
        both_grad, both_weight_ref[...], contract_last, preferred_element_type=jnp.float32
    )
    last = pl.num_programs(0) - 1

    @pl.when(at == 0)
    def _():
        acc[...] = part

    @pl.when((at > 0) & (at < last))
    def _():
        acc[...] += part

    @pl.when(at == last)
    def _():
        total = (acc[...] + part).astype(low)
        for block, grad in enumerate(grad_refs):
            grad[...] = total[block * BLOCK : (block + 1) * BLOCK]


def mlp_blocks(place_at, seconds, cots, weights, held):
    rows = sum(second.shape[0] for second in seconds)
    width = seconds[0].shape[1]
    count = rows // BLOCK
    hidden_width = weights.shape[1] // 3
    step = FF_STEP
    steps = hidden_width // step
    ins = [
        pl.BlockSpec(value.shape, lambda c: (0, 0), pipeline_mode=pl.Buffered(1))
        for value in (*seconds, *cots)
    ]
    kept = pl.BlockSpec((count, BLOCK, step), lambda c: (place_at, 0, c))
    kept_both = pl.BlockSpec((count, BLOCK, 2 * hidden_width), lambda c: (place_at, 0, 0))
    kept_rows = pl.BlockSpec((count, BLOCK, width), lambda c: (place_at, 0, 0))
    rows_shape = jax.ShapeDtypeStruct((RING, BLOCK, width), low)
    return pl.pallas_call(
        functools.partial(mlp_kernel, len(seconds), len(cots)),
        grid=(steps,),
        in_specs=ins
        + [
            pl.BlockSpec((width, 2 * step), lambda c: (0, c)),
            pl.BlockSpec((width, step), lambda c: (0, 2 * steps + c)),
        ]
        + [pl.BlockSpec(memory_space=pl.ANY)] * len(held),
        out_specs=(kept, kept_both, kept_rows, kept_rows)
        + (pl.BlockSpec((BLOCK, width), lambda c: (0, 0)),) * count,
        out_shape=(
            jax.ShapeDtypeStruct((RING, BLOCK, hidden_width), low),
            jax.ShapeDtypeStruct((RING, BLOCK, 2 * hidden_width), low),
            rows_shape,
            rows_shape,
        )
        + (jax.ShapeDtypeStruct((BLOCK, width), low),) * count,
        scratch_shapes=[pltpu.VMEM((rows, width), jnp.float32)],
        input_output_aliases={len(ins) + 2 + i: i for i in range(len(held))},
        compiler_params=pltpu.CompilerParams(vmem_limit_bytes=VMEM_LIMIT),
        cost_estimate=pl.CostEstimate(
            flops=2 * 5 * rows * width * hidden_width,
            bytes_accessed=2 * 3 * width * hidden_width,
            transcendentals=rows * hidden_width,
        ),
    )(*seconds, *cots, weights, weights, *held)


def mlp_out_kernel(inner_ref, weight_ref, *outs):
    inner = inner_ref[...].reshape(RING * BLOCK, inner_ref.shape[2])
    part = lax.dot_general(
        inner, weight_ref[...], contract_last, preferred_element_type=jnp.float32
    ).astype(low)
    for block, out in enumerate(outs):
        out[...] = part[block * BLOCK : (block + 1) * BLOCK]


def mlp_out_part(inner, weights):
    _, rows, hidden_width = inner.shape
    width = weights.shape[0]
    steps = 4
    return pl.pallas_call(
        mlp_out_kernel,
        grid=(steps,),
        in_specs=[
            pl.BlockSpec(inner.shape, lambda d: (0, 0, 0)),
            pl.BlockSpec((width // steps, hidden_width), lambda d: (d, 2)),
        ],
        out_specs=(pl.BlockSpec((rows, width // steps), lambda d: (0, d)),) * RING,
        out_shape=(jax.ShapeDtypeStruct((rows, width), low),) * RING,
        compiler_params=pltpu.CompilerParams(vmem_limit_bytes=VMEM_LIMIT),
        cost_estimate=pl.CostEstimate(flops=1024, bytes_accessed=1024, transcendentals=0),
    )(inner, weights)


def pair_grad(core_at, lefts, right, by_heads=False):
    width = lefts[0].shape[-1]
    outs = 512 if by_heads else right.shape[2]
    rows = RING * BLOCK

    def kernel(core_ref, *refs):
        left_refs = refs[: len(lefts)]
        right_ref, keep_ref, give_ref = refs[len(lefts) : len(lefts) + 3]
        if by_heads:
            all_ref = refs[-1]

            @pl.when(pl.program_id(0) == 0)
            def _():
                for r in range(RING):
                    for head in range(4):
                        all_ref[
                            r * BLOCK : (r + 1) * BLOCK, head * HEAD_DIM : (head + 1) * HEAD_DIM
                        ] = right_ref[4 * r + head]

            values = all_ref[...]
        else:
            values = right_ref[...].reshape(rows, outs)
        inputs = [ref[...].reshape(-1, 256) for ref in left_refs]
        inputs = inputs[0] if len(inputs) == 1 else jnp.concatenate(inputs, axis=0)
        term = lax.dot_general(
            inputs, values, contract_first, preferred_element_type=jnp.float32
        ).astype(low)
        first_core = core_ref[0] == 0
        keep_ref[0] = jnp.where(first_core, term[:128], term[128:])
        give_ref[0] = jnp.where(first_core, term[128:], term[:128])

    def columns(value):
        lead = value.shape[:-1]
        return pl.BlockSpec((*lead, 256), lambda i: (0,) * len(lead) + (i,))

    half = pl.BlockSpec((1, 128, outs), lambda i: (i, 0, 0))
    return pl.pallas_call(
        kernel,
        grid=(width // 256,),
        in_specs=[pl.BlockSpec(memory_space=pltpu.SMEM)]
        + [columns(value) for value in lefts]
        + [pl.BlockSpec(right.shape, lambda i: (0, 0, 0))],
        out_specs=(half, half),
        out_shape=(jax.ShapeDtypeStruct((width // 256, 128, outs), low),) * 2,
        scratch_shapes=[pltpu.VMEM((rows, 512), low)] * by_heads,
        compiler_params=pltpu.CompilerParams(vmem_limit_bytes=VMEM_LIMIT),
        cost_estimate=pl.CostEstimate(
            flops=0 if by_heads else 2 * rows * width * outs, bytes_accessed=1024, transcendentals=0
        ),
    )(core_at[None], *lefts, right)


def middle_kernel(*refs):
    mixed_refs, weight_refs = refs[:RING], refs[RING : 2 * RING]
    hidden_ref, gain_ref, middle_ref, second_ref = refs[2 * RING :]
    at = pl.program_id(0)
    step = weight_refs[0].shape[0]
    columns = pl.ds(pl.multiple_of(at * step, step), step)
    total = hidden_ref[:, columns].astype(jnp.float32)
    for mixed, weight in zip(mixed_refs, weight_refs):
        rows = jnp.concatenate([mixed[head] for head in range(4)], axis=1)
        total += lax.dot_general(
            rows, weight[...], contract_last, preferred_element_type=jnp.float32
        )
    middle_ref[:, columns] = total

    @pl.when(at == pl.num_programs(0) - 1)
    def _():
        second_ref[...] = (normalize(middle_ref[...]) * gain_ref[...]).astype(low)


def middle_part(mixed_blocks, weights, hidden, gain):
    rows, width = hidden.shape
    steps = 4
    whole = pl.BlockSpec((rows, width), lambda d: (0, 0))
    return pl.pallas_call(
        middle_kernel,
        grid=(steps,),
        in_specs=[pl.BlockSpec((4, rows, HEAD_DIM), lambda d: (0, 0, 0))] * RING
        + [pl.BlockSpec((width // steps, 512), lambda d: (d, 0))] * RING
        + [whole, pl.BlockSpec((1, width), lambda d: (0, 0))],
        out_specs=(whole, whole),
        out_shape=(
            jax.ShapeDtypeStruct((rows, width), jnp.float32),
            jax.ShapeDtypeStruct((rows, width), low),
        ),
        compiler_params=pltpu.CompilerParams(vmem_limit_bytes=32 * 1024 * 1024),
        cost_estimate=pl.CostEstimate(flops=1024, bytes_accessed=1024, transcendentals=0),
    )(*mixed_blocks, *weights, hidden, gain)


def middle_back_kernel(*refs):
    parts, weight_refs = refs[:RING], refs[RING : 2 * RING]
    middle_ref, cot_ref, gain_ref, grad_ref, low_ref, gain_out, *rest = refs[2 * RING :]
    outs, accs = rest[:RING], rest[RING:]
    at = pl.program_id(0)
    step = weight_refs[0].shape[0]

    @pl.when(at == 0)
    def _():
        second_grad = sum(part[...].astype(jnp.float32) for part in parts)
        middle = middle_ref[...]
        scale = inverse_rms(middle)
        normed = middle * scale
        gain_out[...] = jnp.sum(second_grad * normed, axis=0, keepdims=True)
        scaled = second_grad * gain_ref[...]
        grad = cot_ref[...].astype(jnp.float32) + scale * (
            scaled - normed * jnp.mean(scaled * normed, axis=-1, keepdims=True)
        )
        grad_ref[...] = grad
        low_ref[...] = grad.astype(low)
        for acc in accs:
            acc[...] = jnp.zeros_like(acc)

    rows = low_ref[:, pl.ds(pl.multiple_of(at * step, step), step)]
    for weight, acc in zip(weight_refs, accs):
        acc[...] += jnp.dot(rows, weight[...], preferred_element_type=jnp.float32)

    @pl.when(at == pl.num_programs(0) - 1)
    def _():
        for out, acc in zip(outs, accs):
            for head in range(4):
                out[head] = acc[:, head * HEAD_DIM : (head + 1) * HEAD_DIM].astype(low)


def middle_back(parts, weights, middle, cot, gain):
    rows, width = middle.shape
    steps = 4
    whole = pl.BlockSpec((rows, width), lambda d: (0, 0))
    row = pl.BlockSpec((1, width), lambda d: (0, 0))
    heads = pl.BlockSpec((4, rows, HEAD_DIM), lambda d: (0, 0, 0))
    return pl.pallas_call(
        middle_back_kernel,
        grid=(steps,),
        in_specs=[whole] * RING
        + [pl.BlockSpec((width // steps, 512), lambda d: (d, 0))] * RING
        + [whole, whole, row],
        out_specs=(whole, whole, row) + (heads,) * RING,
        out_shape=(
            jax.ShapeDtypeStruct((rows, width), jnp.float32),
            jax.ShapeDtypeStruct((rows, width), low),
            jax.ShapeDtypeStruct((1, width), jnp.float32),
        )
        + (jax.ShapeDtypeStruct((4, rows, HEAD_DIM), low),) * RING,
        scratch_shapes=[pltpu.VMEM((rows, 512), jnp.float32)] * RING,
        compiler_params=pltpu.CompilerParams(vmem_limit_bytes=VMEM_LIMIT),
        cost_estimate=pl.CostEstimate(flops=1024, bytes_accessed=1024, transcendentals=0),
    )(*parts, *weights, middle, cot, gain)


def first_kernel(
    own_ref, left_ref, top_ref, bottom_ref, right_ref, weight_ref, gains_ref, cos_ref, sin_ref,
    query_gain, key_gain, hidden_ref, first_ref, pre_ref, send_ref, gain_out,
):
    at = pl.program_id(0)
    half = top_ref.shape[0]

    @pl.when(at == 0)
    def _():
        gain_out[...] = gains_ref[...].astype(jnp.float32).T[:8]
        hidden_ref[0] = own_ref[...]

    @pl.when(at == 1)
    def _():
        hidden_ref[0] = left_ref[...]

    @pl.when(at == 2)
    def _():
        hidden_ref[0, :half] = top_ref[...]
        hidden_ref[0, half:] = bottom_ref[...]

    @pl.when(at == 3)
    def _():
        hidden_ref[0] = right_ref[...]

    first = (normalize(hidden_ref[0].astype(jnp.float32)) * gain_out[0:1]).astype(low)
    first_ref[0] = first
    pre = jnp.dot(first, weight_ref[...], preferred_element_type=jnp.float32)
    pre_ref[0] = pre
    cosine = cos_ref[0]
    sine = sin_ref[0]

    def turned(head, gain):
        values = normalize(pre[:, head * HEAD_DIM : (head + 1) * HEAD_DIM]) * gain
        return (values * cosine + pltpu.roll(values, HEAD_DIM // 2, 1) * sine).astype(low)

    for head in range(4):
        send_ref[head, 0] = turned(head, query_gain[...])
    for head in range(2):
        send_ref[2 * head, 1] = turned(4 + head, key_gain[...])
        send_ref[2 * head + 1, 1] = pre[:, (6 + head) * HEAD_DIM : (7 + head) * HEAD_DIM].astype(low)


def first_part(blocks, weights, cosine, sine, query_gain, key_gain):
    rows, width = blocks[0].shape
    row = pl.BlockSpec((1, HEAD_DIM), lambda r: (0, 0))
    turn = pl.BlockSpec((1, rows, HEAD_DIM), lambda r: (r, 0, 0))
    return pl.pallas_call(
        first_kernel,
        grid=(RING,),
        in_specs=[pl.BlockSpec(block.shape, lambda r: (0, 0)) for block in blocks]
        + [
            pl.BlockSpec((width, 1024), lambda r: (0, 0)),
            pl.BlockSpec((width, HEAD_DIM), lambda r: (0, 8)),
            turn,
            turn,
            row,
            row,
        ],
        out_specs=(
            pl.BlockSpec((1, rows, width), lambda r: (r, 0, 0)),
            pl.BlockSpec((1, rows, width), lambda r: (r, 0, 0)),
            pl.BlockSpec((1, rows, 1024), lambda r: (r, 0, 0)),
            pl.BlockSpec((4, 2, rows, HEAD_DIM), lambda r: (r, 0, 0, 0)),
            pl.BlockSpec((8, width), lambda r: (0, 0)),
        ),
        out_shape=(
            jax.ShapeDtypeStruct((RING, rows, width), low),
            jax.ShapeDtypeStruct((RING, rows, width), low),
            jax.ShapeDtypeStruct((RING, rows, 1024), jnp.float32),
            jax.ShapeDtypeStruct((BLOCKS, 2, rows, HEAD_DIM), low),
            jax.ShapeDtypeStruct((8, width), jnp.float32),
        ),
        compiler_params=pltpu.CompilerParams(vmem_limit_bytes=VMEM_LIMIT),
        cost_estimate=pl.CostEstimate(
            flops=2 * RING * rows * width * 1024,
            bytes_accessed=20 * 1024 * 1024,
            transcendentals=0,
        ),
    )(*blocks, weights, weights, cosine, sine, query_gain, key_gain)


def first_back_kernel(
    core_ref, back_ref, pre_ref, cos_ref, sin_ref, query_gain, key_gain, first_ref,
    grad_ref, keep_ref, give_ref, query_sum, key_sum, all_grads,
):
    at = pl.program_id(0)
    rows = grad_ref.shape[1]
    cosine = cos_ref[0]
    sine = sin_ref[0]

    @pl.when(at == 0)
    def _():
        query_sum[...] = jnp.zeros_like(query_sum)
        key_sum[...] = jnp.zeros_like(key_sum)

    def back(grads, head, gain, sums):
        columns = slice(head * HEAD_DIM, (head + 1) * HEAD_DIM)
        values = pre_ref[0, :, columns]
        grads = grads.astype(jnp.float32)
        grads = grads * cosine - pltpu.roll(grads, HEAD_DIM // 2, 1) * sine
        scale = inverse_rms(values)
        normed = values * scale
        sums[...] += jnp.sum(grads * normed, axis=0, keepdims=True)
        scaled = grads * gain
        out = scale * (scaled - normed * jnp.mean(scaled * normed, axis=-1, keepdims=True))
        grad_ref[0, :, columns] = out.astype(low)

    for head in range(4):
        back(back_ref[head, 0], head, query_gain[...], query_sum)
    for head in range(2):
        back(back_ref[2 * head, 1], 4 + head, key_gain[...], key_sum)
        grad_ref[0, :, (6 + head) * HEAD_DIM : (7 + head) * HEAD_DIM] = back_ref[2 * head + 1, 1]
    all_grads[pl.ds(pl.multiple_of(at * rows, rows), rows), :] = grad_ref[0]

    @pl.when(at == RING - 1)
    def _():
        grads = all_grads[...]
        first_core = core_ref[0] == 0
        for pair in range(8):
            inputs = first_ref[:, :, pair * 256 : (pair + 1) * 256].reshape(RING * rows, 256)
            term = lax.dot_general(
                inputs, grads, contract_first, preferred_element_type=jnp.float32
            ).astype(low)
            keep_ref[pair] = jnp.where(first_core, term[:128], term[128:])
            give_ref[pair] = jnp.where(first_core, term[128:], term[:128])


def first_back(core_at, returned, pre, cosine, sine, query_gain, key_gain, first_in):
    _, rows, width = first_in.shape
    row = pl.BlockSpec((1, HEAD_DIM), lambda r: (0, 0))
    turn = pl.BlockSpec((1, rows, HEAD_DIM), lambda r: (r, 0, 0))
    wide = pl.BlockSpec((1, rows, 1024), lambda r: (r, 0, 0))
    half = pl.BlockSpec((8, 128, 1024), lambda r: (0, 0, 0))
    return pl.pallas_call(
        first_back_kernel,
        grid=(RING,),
        in_specs=[
            pl.BlockSpec(memory_space=pltpu.SMEM),
            pl.BlockSpec((4, 2, rows, HEAD_DIM), lambda r: (r, 0, 0, 0)),
            wide,
            turn,
            turn,
            row,
            row,
            pl.BlockSpec((RING, rows, width), lambda r: (0, 0, 0)),
        ],
        out_specs=(wide, half, half, row, row),
        out_shape=(
            jax.ShapeDtypeStruct((RING, rows, 1024), low),
            jax.ShapeDtypeStruct((8, 128, 1024), low),
            jax.ShapeDtypeStruct((8, 128, 1024), low),
            jax.ShapeDtypeStruct((1, HEAD_DIM), jnp.float32),
            jax.ShapeDtypeStruct((1, HEAD_DIM), jnp.float32),
        ),
        scratch_shapes=[pltpu.VMEM((RING * rows, 1024), low)],
        compiler_params=pltpu.CompilerParams(vmem_limit_bytes=VMEM_LIMIT),
        cost_estimate=pl.CostEstimate(flops=1024, bytes_accessed=1024, transcendentals=0),
    )(core_at[None], returned, pre, cosine, sine, query_gain, key_gain, first_in)


def last_kernel(
    core_ref, grad_ref, weight_ref, hidden_ref, mlp_ref, query_ref, key_ref,
    own_ref, left_a, left_b, top_ref, bottom_ref, right_a, right_b, keep_ref, give_ref, gain_acc,
):
    at = pl.program_id(0)
    width = hidden_ref.shape[2]
    part = lax.dot_general(
        grad_ref[0], weight_ref[...], contract_last, preferred_element_type=jnp.float32
    )
    half = top_ref.shape[0]
    @pl.when(at == 0)
    def _():
        own_ref[...] = part.astype(low)

    for r, first, second in ((1, left_a, left_b), (2, top_ref, bottom_ref), (3, right_a, right_b)):

        @pl.when(at == r)
        def _(first=first, second=second):
            first[...] = part[:half].astype(low)
            second[...] = part[half:].astype(low)

    normed = normalize(hidden_ref[0].astype(jnp.float32))
    gain = jnp.sum(part * normed, axis=0, keepdims=True)

    @pl.when(at == 0)
    def _():
        gain_acc[...] = gain

    @pl.when(at > 0)
    def _():
        gain_acc[...] += gain

    @pl.when(at == RING - 1)
    def _():
        lines = [
            gain_acc[...],
            mlp_ref[...],
            jnp.concatenate([query_ref[...]] * BLOCKS, axis=1),
            jnp.concatenate([key_ref[...]] * BLOCKS, axis=1),
            jnp.zeros((HEAD_DIM - 4, width), jnp.float32),
        ]
        turned = jnp.concatenate(lines, axis=0).T.astype(low)
        first_core = core_ref[0] == 0
        for pair in range(8):
            first = turned[pair * 256 : pair * 256 + 128]
            second = turned[pair * 256 + 128 : (pair + 1) * 256]
            keep_ref[pair] = jnp.where(first_core, first, second)
            give_ref[pair] = jnp.where(first_core, second, first)


def last_part(core_at, grads, weights, hidden_all, mlp_part, query_part, key_part):
    _, rows, width = hidden_all.shape
    block = pl.BlockSpec((rows, width), lambda r: (0, 0))
    small = pl.BlockSpec((rows // 2, width), lambda r: (0, 0))
    whole = jax.ShapeDtypeStruct((rows, width), low)
    part = jax.ShapeDtypeStruct((rows // 2, width), low)
    row = pl.BlockSpec((1, HEAD_DIM), lambda r: (0, 0))
    half = pl.BlockSpec((8, 128, HEAD_DIM), lambda r: (0, 0, 0))
    return pl.pallas_call(
        last_kernel,
        grid=(RING,),
        in_specs=[
            pl.BlockSpec(memory_space=pltpu.SMEM),
            pl.BlockSpec((1, rows, 1024), lambda r: (r, 0, 0)),
            pl.BlockSpec((width, 1024), lambda r: (0, 0)),
            pl.BlockSpec((1, rows, width), lambda r: (r, 0, 0)),
            pl.BlockSpec((1, width), lambda r: (0, 0)),
            row,
            row,
        ],
        out_specs=(block,) + (small,) * 6 + (half, half),
        out_shape=(whole,) + (part,) * 6
        + (jax.ShapeDtypeStruct((8, 128, HEAD_DIM), low),) * 2,
        scratch_shapes=[pltpu.VMEM((1, width), jnp.float32)],
        compiler_params=pltpu.CompilerParams(vmem_limit_bytes=VMEM_LIMIT),
        cost_estimate=pl.CostEstimate(flops=1024, bytes_accessed=1024, transcendentals=0),
    )(core_at[None], grads, weights, hidden_all, mlp_part, query_part, key_part)


def arrange_kernel(at_ref, own_ref, other_ref, out_ref):
    y_at, x_at, core_at = at_ref[0], at_ref[1], at_ref[2]
    for dy in range(RING):
        for dx in range(2):
            first = ((y_at - dy + RING) & 3) * 4 + (x_at ^ dx) * 2
            own = pl.multiple_of((first + core_at) * 128, 128)
            other = pl.multiple_of((first + 1 - core_at) * 128, 128)
            out_ref[pl.ds(own, 128), :] = own_ref[dy, dx]
            out_ref[pl.ds(other, 128), :] = other_ref[dy, dx]


def gather_by_permutes(pairs, y_at, x_at, core_at):
    own = jnp.stack(pairs)
    other = shift(own, "core", 1, 2)
    whole = pl.BlockSpec(memory_space=pltpu.VMEM)
    return pl.pallas_call(
        arrange_kernel,
        in_specs=[pl.BlockSpec(memory_space=pltpu.SMEM), whole, whole],
        out_specs=whole,
        out_shape=jax.ShapeDtypeStruct((BLOCKS * 128, own.shape[3]), own.dtype),
        compiler_params=pltpu.CompilerParams(vmem_limit_bytes=VMEM_LIMIT),
        cost_estimate=pl.CostEstimate(flops=1024, bytes_accessed=1024, transcendentals=0),
    )(jnp.stack([y_at, x_at, core_at]), own, other)


def pair_sums_kernel(keep_ref, come_ref, gains_keep, gains_come, out_ref):
    f32 = jnp.float32
    wide = keep_ref.shape[2]
    out_ref[:, :, :wide] = (keep_ref[...].astype(f32) + come_ref[...].astype(f32)).astype(low)
    out_ref[:, :, wide:] = (gains_keep[...].astype(f32) + gains_come[...].astype(f32)).astype(low)


def pair_sums(keep, come, more_keep, more_come):
    blocks, rows, wide = keep.shape
    narrow = more_keep.shape[2]
    large = pl.BlockSpec((4, rows, wide), lambda i: (i, 0, 0))
    small = pl.BlockSpec((4, rows, narrow), lambda i: (i, 0, 0))
    return pl.pallas_call(
        pair_sums_kernel,
        grid=(blocks // 4,),
        in_specs=[large, large, small, small],
        out_specs=pl.BlockSpec((4, rows, wide + narrow), lambda i: (i, 0, 0)),
        out_shape=jax.ShapeDtypeStruct((blocks, rows, wide + narrow), low),
        compiler_params=pltpu.CompilerParams(vmem_limit_bytes=VMEM_LIMIT),
        cost_estimate=pl.CostEstimate(flops=1024, bytes_accessed=1024, transcendentals=0),
    )(keep, come, more_keep, more_come)


def to_heads(send):
    return lax.all_to_all(send, GROUP_AXES, 0, 0, tiled=True)


def after(value, *others):
    return lax.optimization_barrier((value, others))[0]


def ring_blocks(values):
    half = values.shape[0] // 2
    left = shift(values, "z", 1)
    right = shift(values, "z", 3)
    opposite = jnp.concatenate(
        [shift(left[:half], "z", 1), shift(right[half:], "z", 3)], axis=0
    )
    return [values, left, opposite, right]


def together(*values):
    return lax.optimization_barrier(values)


def place(z_at, blocks, widths, chunk=None, summed=False):
    rows = blocks[0].shape[0]
    whole = pl.BlockSpec(memory_space=pltpu.VMEM)
    shapes = [RING * part for part in widths] + [HEAD_DIM] * summed

    def kernel(z_ref, *refs):
        ins, outs = refs[:RING], refs[RING:]
        for r in range(RING):
            slot = (z_ref[0] - r + RING) & 3
            start = 0
            for turn in range(widths[0] // chunk if chunk else 1):
                for out, part in zip(outs, widths):
                    size = chunk or part
                    at = pl.multiple_of(slot * part + turn * size, 128)
                    out[:, pl.ds(at, size)] = ins[r][:, start : start + size].astype(jnp.float32)
                    start += size
            if summed:
                columns = ins[r][:, start : start + HEAD_DIM].astype(jnp.float32)
                outs[-1][...] = columns if r == 0 else outs[-1][...] + columns

    return pl.pallas_call(
        kernel,
        in_specs=[pl.BlockSpec(memory_space=pltpu.SMEM)] + [whole] * RING,
        out_specs=tuple(whole for _ in shapes),
        out_shape=tuple(jax.ShapeDtypeStruct((rows, part), jnp.float32) for part in shapes),
        compiler_params=pltpu.CompilerParams(vmem_limit_bytes=VMEM_LIMIT),
        cost_estimate=pl.CostEstimate(flops=1024, bytes_accessed=1024, transcendentals=0),
    )(z_at[None], *blocks)


def send_back(block, r):
    return shift(block, "z", -r)


def local(
    hidden_in,
    cotangent,
    segment_ids,
    positions,
    attn_gain,
    query_gain,
    key_gain,
    query_weight,
    key_weight,
    value_weight,
    out_weight,
    mlp_gain,
    gate_weight,
    up_weight,
    down_weight,
):
    f32 = jnp.float32
    rows, width = hidden_in.shape
    ring_rows = RING * rows
    z_at = lax.axis_index("z")
    y_at = lax.axis_index("y")
    x_at = lax.axis_index("x_hi")
    core_at = lax.axis_index("core")
    my_index = (y_at * 2 + x_at) * 2 + core_at

    def columns(weight):
        part = weight.shape[1] // RING
        return lax.dynamic_slice_in_dim(weight, z_at * part, part, 1).astype(low)

    def gather(block):
        return lax.all_gather(block, GROUP_AXES, axis=0, tiled=True)

    own_places = lax.dynamic_slice_in_dim(positions, my_index * rows, rows)
    firsts = positions.reshape(BLOCKS, BLOCK)[:, 0]
    segments = segment_ids.reshape(BLOCKS, BLOCK)[:, 0]
    logical = firsts // BLOCK + jnp.maximum(segments - 1, 0) * 2
    numbers = jnp.arange(BLOCKS, dtype=jnp.int32)
    order = jnp.sum(jnp.where(logical[:, None] == numbers[None, :], numbers[:, None], 0), axis=0)
    notes = gather_z(jnp.concatenate([own_places, order, jnp.zeros((112,), jnp.int32)])[None])
    places = notes[:, :rows]
    order = lax.dynamic_index_in_dim(notes, y_at, 0, keepdims=False)[rows : rows + BLOCKS]

    gains = jnp.pad(
        jnp.stack([attn_gain, mlp_gain], axis=1).astype(low), ((0, 0), (0, HEAD_DIM - 2))
    )
    first_weights = gather(
        jnp.concatenate(
            [columns(query_weight), columns(key_weight), columns(value_weight), gains], axis=1
        )
    )
    out_columns = columns(out_weight)
    out_come = shift(out_columns, "x_hi", 1, 2)
    out_pairs = jnp.stack([out_columns, out_come])
    out_pairs = [out_pairs] + [shift(out_pairs, "y", r) for r in range(1, RING)]

    hidden_own = after(hidden_in, notes, out_come)
    hidden_left = shift(hidden_own, "z", 1)
    hidden_right = shift(hidden_own, "z", 3)
    gate_columns, up_columns, down_columns, hidden_left, hidden_right, out_pairs = together(
        gate_weight, up_weight, down_weight, hidden_left, hidden_right, out_pairs
    )
    out_slice = gather_by_permutes(out_pairs, y_at, x_at, core_at)
    gate_columns, up_columns = columns(gate_columns), columns(up_columns)
    mlp_columns = []
    for start in range(0, gate_columns.shape[1], FF_STEP):
        mlp_columns.append(gate_columns[:, start : start + FF_STEP])
        mlp_columns.append(up_columns[:, start : start + FF_STEP])
    mlp_weights = gather(jnp.concatenate(mlp_columns + [columns(down_columns)], axis=1))
    half = rows // 2
    hidden_blocks = [
        hidden_own,
        hidden_left,
        shift(hidden_left[:half], "z", 1),
        shift(hidden_right[half:], "z", 3),
        hidden_right,
    ]
    out_slice = after(out_slice, *hidden_blocks)
    out_left = shift(out_slice, "z", 1)
    out_right = shift(out_slice, "z", 3)
    frequency = rope_base ** (-2.0 * jnp.arange(HEAD_DIM // 2, dtype=f32) / HEAD_DIM)
    angles = places.astype(f32)[:, :, None] * frequency[None, None, :]
    cosine = jnp.cos(angles)
    sine = jnp.sin(angles)
    cosine = jnp.concatenate([cosine, cosine], axis=-1)
    sine = jnp.concatenate([-sine, sine], axis=-1)
    query_row = query_gain[None]
    key_row = key_gain[None]

    hidden_all, first_in, qkv_pre, send, gain_rows = first_part(
        hidden_blocks, first_weights, cosine, sine, query_row, key_row
    )
    attn_scale = gain_rows[0:1]
    mlp_scale = gain_rows[1:2]
    arrived, out_left, out_right = together(to_heads(send), out_left, out_right)
    other_pair = shift(arrived[:, 1], "core", 1, 2)
    head_mixed, head_mixed_t, head_logs = attention_forward(order, core_at, arrived, other_pair)
    out_top = shift(out_left[: width // 2], "z", 1)
    out_bottom = shift(out_right[width // 2 :], "z", 3)
    head_mixed, head_mixed_t, head_logs, out_top, out_bottom = together(
        head_mixed, head_mixed_t, head_logs, out_top, out_bottom
    )
    cot_own = after(cotangent, head_mixed)
    cot_left = shift(cot_own, "z", 1)
    cot_right = shift(cot_own, "z", 3)

    cot_top = shift(cot_left[:half], "z", 1)
    cot_bottom = shift(cot_right[half:], "z", 3)
    mixed_arrived, cot_left, cot_right, cot_top, cot_bottom = together(
        to_heads(head_mixed), cot_left, cot_right, cot_top, cot_bottom
    )
    mixed_blocks = [mixed_arrived[:4]] + [
        shift(mixed_arrived[4 * (RING - j) : 4 * (RING - j) + 4], "z", j) for j in range(1, RING)
    ]
    out_opposite = jnp.concatenate([out_top, out_bottom], axis=0)
    out_weights = [out_slice, out_left, out_opposite, out_right]
    mixed_blocks, out_weights = together(mixed_blocks, out_weights)
    middle, second_in = middle_part(mixed_blocks, out_weights, hidden_in, mlp_scale)
    hidden = hidden_in.astype(f32)
    left = shift(second_in, "z", 1)
    right = shift(second_in, "z", 3)
    *held, own_part = mlp_blocks(0, [second_in], [cot_own], mlp_weights, ())
    held, own_part, left, right, second_in = together(held, own_part, left, right, second_in)
    opposite = shift(second_in, "z", 2)
    *held, left_part, right_part = mlp_blocks(
        1, [left, right], [cot_left, cot_right], mlp_weights, held
    )
    left_back = send_back(left_part, 1)
    right_back = send_back(right_part, 3)
    held, opposite = together(held, opposite)
    *held, opposite_part = mlp_blocks(
        1, [opposite], [cot_top, cot_bottom], mlp_weights, held
    )
    opposite_back = send_back(opposite_part, 2)
    inner, both_grad, second_all, cot_all = held

    def pair_sum(keep, come):
        return (keep.astype(f32) + come.astype(f32)).astype(low)

    def along_y(pair):
        return lax.all_to_all(pair.reshape(RING, 2, 128, pair.shape[2]), "y", 0, 0, tiled=True)

    def along_x(halves):
        keep = lax.dynamic_index_in_dim(halves, x_at, 0, keepdims=False)
        give = lax.dynamic_index_in_dim(halves, 1 - x_at, 0, keepdims=False)
        return keep, lax.ppermute(give, ("x_lo", "x_hi"), [(i, 3 - i) for i in range(4)])

    def add_up(terms):
        return jnp.sum(terms.astype(f32), axis=0).astype(low)

    def over_x(share):
        return share, shift(share, "x_lo", 1, 2)

    def over_z(pair):
        share = pair_sum(*pair)
        return [share] + [shift(share, "z", r) for r in range(1, RING)]

    both_term = lax.dot_general(
        second_all.reshape(ring_rows, width),
        both_grad.reshape(ring_rows, 3072),
        contract_first,
        preferred_element_type=f32,
    ).astype(low)
    left_back, right_back, opposite_back, both_term, inner = together(
        left_back, right_back, opposite_back, both_term, inner
    )
    both_share = lax.psum_scatter(both_term, GROUP_AXES, scatter_dimension=0, tiled=True)

    middle_grad, own_low, mlp_gain_part, *grad_blocks = middle_back(
        (own_part, left_back, right_back, opposite_back),
        out_weights,
        middle,
        cotangent,
        mlp_scale,
    )
    grad_blocks = [grad_blocks[0]] + [shift(grad_blocks[RING - r], "z", r) for r in range(1, RING)]
    grad_blocks, own_low, inner = together(grad_blocks, own_low, inner)
    down_keep, down_give = pair_grad(core_at, [cot_all], inner)
    head_grads = to_heads(jnp.concatenate(grad_blocks, axis=0))
    low_left = shift(own_low, "z", 1)
    low_right = shift(own_low, "z", 3)
    mlp_own, mlp_opposite, mlp_left, mlp_right = mlp_out_part(inner, mlp_weights)
    head_grads, low_left, low_right, own_low, mlp_opposite, mlp_left, mlp_right, down_give = together(
        head_grads, low_left, low_right, own_low, mlp_opposite, mlp_left, mlp_right, down_give
    )
    mlp_left = send_back(mlp_left, 1)
    mlp_right = send_back(mlp_right, 3)

    query_grad, grad_keep, grad_give = attention_backward(
        order, core_at, arrived, other_pair, head_grads, head_mixed_t, head_logs
    )
    query_grad, grad_keep, grad_give, mlp_left, mlp_right, own_low, mlp_opposite, down_give = together(
        query_grad, grad_keep, grad_give, mlp_left, mlp_right, own_low, mlp_opposite, down_give
    )
    low_opposite = shift(own_low, "z", 2)
    mlp_opposite = send_back(after(mlp_opposite, low_opposite), 2)
    grads_send = lax.dynamic_update_slice_in_dim(
        query_grad, pair_sum(grad_keep, shift(grad_give, "core", 1, 2))[:, None], 1, 1
    )
    returned = to_heads(grads_send)
    out_keep, out_give = pair_grad(
        core_at, [own_low, low_left, low_opposite, low_right], mixed_arrived, by_heads=True
    )
    down_sum = pair_sums(
        down_keep,
        shift(down_give, "core", 1, 2),
        out_keep,
        shift(out_give, "core", 1, 2),
    )
    returned, both_share, down_sum = together(returned, both_share, down_sum)
    both_pair = over_x(both_share)
    down_terms = along_y(down_sum)
    qkv_grad, qkv_keep, qkv_give, query_gain_part, key_gain_part = first_back(
        core_at, returned, qkv_pre, cosine, sine, query_row, key_row, first_in
    )
    qkv_grad, qkv_give, both_pair, mlp_opposite = together(
        qkv_grad, qkv_give, both_pair, mlp_opposite
    )
    both_sum = pair_sum(*both_pair)
    both_left = shift(both_sum, "z", 1)
    both_right = shift(both_sum, "z", 3)
    qkv_come = shift(qkv_give, "core", 1, 2)
    *first_parts, gains_keep, gains_give = last_part(
        core_at,
        qkv_grad,
        first_weights,
        hidden_all,
        mlp_gain_part,
        query_gain_part,
        key_gain_part,
    )
    first_parts, gains_give, qkv_come, both_left, both_right, both_sum = together(
        first_parts, gains_give, qkv_come, both_left, both_right, both_sum
    )
    down_pair = over_x(pair_sum(*along_x(add_up(down_terms))))
    gains_come = shift(gains_give, "core", 1, 2)
    first_own, left_a, left_b, first_top, first_bottom, right_a, right_b = first_parts
    first_top = shift(first_top, "z", 3)
    first_bottom = shift(first_bottom, "z", 1)
    qkv_terms = along_y(pair_sums(qkv_keep, qkv_come, gains_keep, gains_come))
    first_left = send_back(jnp.concatenate([pair_sum(left_a, first_top), left_b], axis=0), 1)
    first_right = send_back(jnp.concatenate([right_a, pair_sum(right_b, first_bottom)], axis=0), 3)
    both_opposite = shift(both_sum, "z", 2)
    down_blocks = over_z(down_pair)
    qkv_share = pair_sum(*along_x(add_up(qkv_terms)))
    both_blocks = [both_sum, both_left, both_opposite, both_right]
    qkv_pair = over_x(qkv_share)
    output = (
        middle
        + after(mlp_own, first_top).astype(f32)
        + mlp_left.astype(f32)
        + mlp_right.astype(f32)
        + mlp_opposite.astype(f32)
    ).astype(low)
    first_grad = first_own.astype(f32) + first_left.astype(f32) + first_right.astype(f32)
    hidden_rms = inverse_rms(hidden)
    own_norm = hidden * hidden_rms
    scaled_first = first_grad * attn_scale
    hidden_grad = (
        middle_grad
        + hidden_rms
        * (scaled_first - own_norm * jnp.mean(scaled_first * own_norm, axis=-1, keepdims=True))
    ).astype(low)

    down_grad_out, out_grad_out = place(z_at, down_blocks, (1536, 512))
    gate_grad_out, up_grad_out = place(z_at, both_blocks, (1536, 1536), chunk=FF_STEP)
    query_grad_out, key_grad_out, value_grad_out, gain_sum = place(
        z_at, over_z(qkv_pair), (512, 256, 256), summed=True
    )
    gain_sum = gain_sum[:, :4].T

    return (
        output,
        hidden_grad,
        gain_sum[0],
        gain_sum[2],
        gain_sum[3],
        query_grad_out,
        key_grad_out,
        value_grad_out,
        out_grad_out,
        gain_sum[1],
        gate_grad_out,
        up_grad_out,
        down_grad_out,
    )


def solution(mesh):
    fine = Mesh(mesh.devices.reshape(2, 4, 4, 2, 2), ALL_AXES)
    rep = ("x_lo", "z")
    row = P(ALL_AXES, None)
    part = P(GROUP_AXES)
    weight = P(GROUP_AXES, None)
    in_specs = (
        row,
        row,
        P(rep),
        P(rep),
        part,
        P(),
        P(),
        weight,
        weight,
        weight,
        weight,
        part,
        weight,
        weight,
        weight,
    )
    out_specs = (
        row,
        row,
        part,
        P(),
        P(),
        weight,
        weight,
        weight,
        weight,
        part,
        weight,
        weight,
        weight,
    )
    return jax.shard_map(local, mesh=fine, in_specs=in_specs, out_specs=out_specs, check_vma=False)
```
